32 devices in a mesh: dp: 16 (over z, x, core), mp: 2 (over y).
Axes of the slice: x: 2, y: 2, z: 4, core: 2. Of those that a mesh axis runs over, the one named last changes fastest.
Arguments:
- tokens: bfloat16 [16, 1089, 768], P('dp'), may hold values from -6 to 6
- cotangent: bfloat16 [16, 1089, 768], P('dp'), may hold values from -6 to 6
- long_flag: int32 [16], P('dp'), may hold values from 0 to 1, as said below
- token_mask: int32 [16, 1089], P('dp'), may hold values from 0 to 1, as said below
- bucket_line: int32 [16, 1089, 1089], P('dp'), may hold values from 0 to 31
- bucket_across: int32 [16, 1089, 1089], P('dp'), may hold values from 0 to 63
- bucket_down: int32 [16, 1089, 1089], P('dp'), may hold values from 0 to 63
- project_weight: bfloat16 [3, 768, 768], P(None, None, 'mp'), may hold values from -0.21875 to 0.21875
- project_bias: bfloat16 [2, 768], P(None, 'mp'), may hold values from -4 to 4
- table_line: bfloat16 [32, 12], P(None, 'mp'), may hold values from -6 to 6
- table_across: bfloat16 [64, 12], P(None, 'mp'), may hold values from -6 to 6
- table_down: bfloat16 [64, 12], P(None, 'mp'), may hold values from -6 to 6
- output_weight: bfloat16 [768, 768], P('mp'), may hold values from -1.75 to 1.75
- output_bias: bfloat16 [768], replicated, may hold values from -4 to 4
- first_gain: float32 [768], replicated, may hold values from 0.5 to 1.5
- first_shift: float32 [768], replicated, may hold values from -4 to 4
- expand_weight: bfloat16 [768, 3072], P(None, 'mp'), may hold values from -0.21875 to 0.21875
- expand_bias: bfloat16 [3072], P('mp'), may hold values from -4 to 4
- reduce_weight: bfloat16 [3072, 768], P('mp'), may hold values from -0.109375 to 0.109375
- reduce_bias: bfloat16 [768], replicated, may hold values from -4 to 4
- second_gain: float32 [768], replicated, may hold values from 0.5 to 1.5
- second_shift: float32 [768], replicated, may hold values from -4 to 4
Outputs:
- layer_out: bfloat16 [16, 1089, 768], P('dp')
- input_grad: float32 [16, 1089, 768], P('dp', None, 'mp')
- project_weight_grad: float32 [3, 768, 768], P(None, None, 'mp')
- project_bias_grad: float32 [2, 768], P(None, 'mp')
- table_line_grad: float32 [32, 12], P(None, 'mp')
- table_across_grad: float32 [64, 12], P(None, 'mp')
- table_down_grad: float32 [64, 12], P(None, 'mp')
- output_weight_grad: float32 [768, 768], P('mp')
- output_bias_grad: float32 [768], replicated
- first_gain_grad: float32 [768], P('mp')
- first_shift_grad: float32 [768], P('mp')
- expand_weight_grad: float32 [768, 3072], P(None, 'mp')
- expand_bias_grad: float32 [3072], P('mp')
- reduce_weight_grad: float32 [3072, 768], P('mp')
- reduce_bias_grad: float32 [768], replicated
- second_gain_grad: float32 [768], replicated
- second_shift_grad: float32 [768], replicated
The draws below stay inside these ranges and needn't reach their ends.
Inputs may be any that keep to these rules, and one draw needn't show every extreme that they name: `long_flag`: 1 marks an item of the long bucket (1089 rows), 0 one of the short bucket (709 rows); both kinds occur. `token_mask`: 1 on an item's first rows and 0 after them; an item of the long bucket has more than 709 ones; an item of the short bucket has 532 ones or more, and its ones may run past row 709; some item of each bucket has ones on all 1089 rows.
All inputs are finite; a program needn't handle non-finite values.
Results may differ from the reference program's by a relative error of at most 0.014.
Values may be sent and summed in bfloat16 or wider, within the bound.
A program may use at most 256 MiB of HBM per device.

```python
import jax
import jax.numpy as jnp
from jax import lax

D = 768
HEADS = 12
FF = 3072
BUCKETS_1D = 32
BUCKETS_2D = 64
LONG = 1089
SHORT = 709
ITEMS = 16


def item_draw(key):
    item_index = jnp.arange(ITEMS, dtype=jnp.int32)
    coin_flip = jax.random.randint(jax.random.fold_in(key, 11), (ITEMS,), 0, 2).astype(jnp.int32)
    long_mark = jnp.where(item_index % 8 == 0, 1, jnp.where(item_index % 8 == 4, 0, coin_flip)).astype(jnp.int32)
    longest_cut = min(SHORT // 4, LONG - SHORT - 1)
    cut_rows = jax.random.randint(jax.random.fold_in(key, 12), (ITEMS,), 0, longest_cut + 1).astype(jnp.int32)
    cut_rows = jnp.where(item_index % 4 == 0, 0, cut_rows)
    short_rows = jax.random.randint(jax.random.fold_in(key, 13), (ITEMS,), SHORT - SHORT // 4, LONG + 1).astype(jnp.int32)
    short_rows = jnp.where(item_index % 8 == 4, LONG, short_rows)
    length = jnp.where(long_mark > 0, LONG - cut_rows, short_rows).astype(jnp.int32)
    return (long_mark, length)


def draw_long_flag(key, part):
    long_mark, length = item_draw(key)
    return long_mark


def draw_token_mask(key, part):
    long_mark, length = item_draw(key)
    positions = jnp.arange(LONG, dtype=jnp.int32)
    return (positions[None, :] < length[:, None]).astype(jnp.int32)


def place_ends(drawn, stream_key, least, top_value):
    place = [jax.random.randint(jax.random.fold_in(stream_key, axis), (), 0, length) for axis, length in enumerate(drawn.shape)]
    widest = drawn.shape.index(max(drawn.shape))
    next_to = place[:widest] + [(place[widest] + 1) % drawn.shape[widest]] + place[widest + 1:]
    return drawn.at[tuple(place)].set(least).at[tuple(next_to)].set(top_value)


def shard_levels(rng, extent, pieces, low, high):
    loudness = 1.0
    for axis_at, blocks in pieces:
        heights = jax.random.uniform(jax.random.fold_in(jax.random.fold_in(rng, 6), axis_at), (blocks,), jnp.float32, low / len(pieces), high / len(pieces))
        loudness = loudness * jnp.repeat(jnp.exp(heights), extent[axis_at] // blocks).reshape((-1,) + (1,) * (len(extent) - 1 - axis_at))
    return loudness


def scatter_about(rng, shape, scale, bound, pieces=(), kind=jnp.bfloat16):
    values = jax.random.normal(rng, shape, jnp.float32) * scale
    if len(pieces) > 0:
        values = shard_levels(rng, shape, pieces, -0.22, 0.18) * values
    return jnp.clip(values, min=-bound, max=bound).astype(kind)


def setup_inputs(seed: int = 0) -> dict:
    key_list = jax.random.split(jax.random.key(seed), 23)
    return {
        "tokens": scatter_about(key_list[0], (ITEMS, LONG, D), 1.0, 6.0, ((0, 16),)),
        "cotangent": scatter_about(key_list[1], (ITEMS, LONG, D), 1.0, 6.0, ((0, 16),)),
        "long_flag": draw_long_flag(jax.random.fold_in(key_list[22], 71), 0),
        "token_mask": draw_token_mask(jax.random.fold_in(key_list[22], 71), 0),
        "bucket_line": place_ends(jax.random.randint(key_list[4], (ITEMS, LONG, LONG), 0, BUCKETS_1D), jax.random.fold_in(key_list[4], 1), 0, BUCKETS_1D - 1).astype(jnp.int32),
        "bucket_across": place_ends(jax.random.randint(key_list[5], (ITEMS, LONG, LONG), 0, BUCKETS_2D), jax.random.fold_in(key_list[5], 1), 0, BUCKETS_2D - 1).astype(jnp.int32),
        "bucket_down": place_ends(jax.random.randint(key_list[6], (ITEMS, LONG, LONG), 0, BUCKETS_2D), jax.random.fold_in(key_list[6], 1), 0, BUCKETS_2D - 1).astype(jnp.int32),
        "project_weight": scatter_about(key_list[7], (3, D, D), D ** -0.5, 0.21875, ((2, 2),)),
        "project_bias": scatter_about(key_list[8], (2, D), 0.3, 4.0, ((1, 2),)),
        "table_line": scatter_about(key_list[9], (BUCKETS_1D, HEADS), 0.8, 6.0, ((1, 2),)),
        "table_across": scatter_about(key_list[10], (BUCKETS_2D, HEADS), 0.8, 6.0, ((1, 2),)),
        "table_down": scatter_about(key_list[11], (BUCKETS_2D, HEADS), 0.8, 6.0, ((1, 2),)),
        "output_weight": scatter_about(key_list[12], (D, D), (D // 64) ** -0.5, 1.75, ((0, 2),)),
        "output_bias": scatter_about(key_list[13], (D,), 0.3, 4.0),
        "first_gain": jnp.clip(1.0 + 0.1 * jax.random.normal(key_list[14], (D,), jnp.float32), 0.5, 1.5),
        "first_shift": scatter_about(key_list[15], (D,), 0.3, 4.0, (), jnp.float32),
        "expand_weight": scatter_about(key_list[16], (D, FF), D ** -0.5, 0.21875, ((1, 2),)),
        "expand_bias": scatter_about(key_list[17], (FF,), 0.3, 4.0, ((0, 2),)),
        "reduce_weight": scatter_about(key_list[18], (FF, D), FF ** -0.5, 0.109375, ((0, 2),)),
        "reduce_bias": scatter_about(key_list[19], (D,), 0.3, 4.0),
        "second_gain": jnp.clip(1.0 + 0.1 * jax.random.normal(key_list[20], (D,), jnp.float32), 0.5, 1.5),
        "second_shift": scatter_about(key_list[21], (D,), 0.3, 4.0, (), jnp.float32),
    }


highest = lax.Precision.HIGHEST
large_negative = -1000000000.0
norm_epsilon = 1e-05

@jax.custom_vjp
def low(v):
    return lax.optimization_barrier(v.astype(jnp.bfloat16)).astype(jnp.float32)

@jax.custom_vjp
def low_back(v):
    return v

def low_keep(v):
    return (low(v), None)

def low_pass(kept, grad):
    return (grad,)

def back_keep(v):
    return (v, None)

def back_low(kept, grad):
    return (low(grad),)
low.defvjp(low_keep, low_pass)
low_back.defvjp(back_keep, back_low)

def layer_norm(values, gain_vector, shift_vector):
    average = lax.optimization_barrier(jnp.mean(values, axis=-1, keepdims=True))
    centered = values - average
    variance = lax.optimization_barrier(jnp.mean(centered * centered, axis=-1, keepdims=True))
    return centered * lax.rsqrt(variance + norm_epsilon) * gain_vector + shift_vector

def forward(inputs, params, buckets, valid):
    project_weight, project_bias, table_line, table_across, table_down, output_weight, output_bias, first_gain, first_shift, expand_weight, expand_bias, reduce_weight, reduce_bias, second_gain, second_shift = params
    bucket_line, bucket_across, bucket_down = buckets
    row_count = inputs.shape[0]
    head_width = D // HEADS
    projected = jnp.einsum('ld,kde->kle', inputs, project_weight, precision=highest)
    queries = low(low_back(projected[0] + project_bias[0]))
    key_rows = low(low_back(projected[1]))
    value_rows = low(low_back(projected[2] + project_bias[1]))
    query_heads = queries.reshape(row_count, HEADS, head_width)
    key_heads = key_rows.reshape(row_count, HEADS, head_width)
    value_heads = value_rows.reshape(row_count, HEADS, head_width)
    position_bias = jnp.take(table_line, bucket_line, axis=0) + jnp.take(table_across, bucket_across, axis=0) + jnp.take(table_down, bucket_down, axis=0)
    scores = jnp.einsum('ihd,jhd->hij', query_heads, key_heads, precision=highest) * 0.125
    scores = scores + jnp.transpose(position_bias, (2, 0, 1))
    scores = jnp.where(valid[None, None, :] > 0, scores, large_negative)
    scores = low_back(scores)
    topmost = lax.optimization_barrier(jnp.max(scores, axis=-1, keepdims=True))
    exponent = jnp.exp(scores - topmost)
    attention = low(exponent / lax.optimization_barrier(jnp.sum(exponent, axis=-1, keepdims=True)))
    context = jnp.einsum('hij,jhd->ihd', attention, value_heads, precision=highest).reshape(row_count, D)
    context = low(low_back(context))
    attended = low_back(jnp.dot(context, output_weight, precision=highest) + output_bias)
    first_norm = layer_norm(inputs + attended, first_gain, first_shift)
    before = low_back(jnp.dot(low(first_norm), expand_weight, precision=highest) + expand_bias)
    activated = low(jax.nn.gelu(before, approximate=False))
    reduced = low_back(jnp.dot(activated, reduce_weight, precision=highest) + reduce_bias)
    return layer_norm(first_norm + reduced, second_gain, second_shift) * valid[:, None]

def reference(tokens, cotangent, long_flag, token_mask, bucket_line, bucket_across, bucket_down, project_weight, project_bias, table_line, table_across, table_down, output_weight, output_bias, first_gain, first_shift, expand_weight, expand_bias, reduce_weight, reduce_bias, second_gain, second_shift):
    params = tuple((jnp.asarray(member, jnp.float32) for member in (project_weight, project_bias, table_line, table_across, table_down, output_weight, output_bias, first_gain, first_shift, expand_weight, expand_bias, reduce_weight, reduce_bias, second_gain, second_shift)))
    positions = jnp.arange(LONG, dtype=jnp.int32)
    limits = jnp.where(long_flag > 0, LONG, SHORT).astype(jnp.int32)
    valid_all = ((token_mask > 0) & (positions[None, :] < limits[:, None])).astype(jnp.float32)

    def one_item(running, member):
        inputs, upstream, valid, line_rows, across_rows, down_rows = member

        def apply(inputs_float, params_float):
            return forward(inputs_float, params_float, (line_rows, across_rows, down_rows), valid)
        output, backward = jax.vjp(apply, inputs.astype(jnp.float32), params)
        grad_inputs, grad_params = backward(upstream.astype(jnp.float32))
        running = jax.tree.map(jnp.add, running, grad_params)
        return (running, (output.astype(jnp.bfloat16), grad_inputs))
    zeros_start = jax.tree.map(jnp.zeros_like, params)
    sums, (layer_out, input_grad) = lax.scan(one_item, zeros_start, (tokens, cotangent, valid_all, bucket_line, bucket_across, bucket_down))
    project_weight_grad, project_bias_grad, table_line_grad, table_across_grad, table_down_grad, output_weight_grad, output_bias_grad, first_gain_grad, first_shift_grad, expand_weight_grad, expand_bias_grad, reduce_weight_grad, reduce_bias_grad, second_gain_grad, second_shift_grad = sums
    return (layer_out, input_grad, project_weight_grad, project_bias_grad, table_line_grad, table_across_grad, table_down_grad, output_weight_grad, output_bias_grad, first_gain_grad, first_shift_grad, expand_weight_grad, expand_bias_grad, reduce_weight_grad, reduce_bias_grad, second_gain_grad, second_shift_grad)
```

```python
from functools import partial

import jax
import jax.numpy as jnp
from jax import lax
from jax.experimental import pallas as pl
from jax.experimental.pallas import tpu as pltpu
from jax.sharding import PartitionSpec as P

LONG = 1089
SHORT = 709
HEAD = 64
LANES = 128
STRIP = 16
BLOCK_ROWS = 224

large_negative = -1000000000.0
norm_epsilon = 1e-05
vmem_limit = 56 * 2**20
bf16 = jnp.bfloat16
f32 = jnp.float32


def round_up(value, step):
    return (value + step - 1) // step * step


def whole_spec(array):
    zeros = (0,) * array.ndim
    return pl.BlockSpec(array.shape, lambda i: zeros)


def dot_f32(left, right):
    return jnp.dot(left, right, preferred_element_type=f32)


def gather_lanes(values, index):
    dims = lax.GatherDimensionNumbers(
        offset_dims=(),
        collapsed_slice_dims=(1,),
        start_index_map=(1,),
        operand_batching_dims=(0,),
        start_indices_batching_dims=(0,),
    )
    return lax.gather(
        values,
        index[..., None],
        dims,
        slice_sizes=(1, 1),
        mode=lax.GatherScatterMode.PROMISE_IN_BOUNDS,
    )


def attend_kernel(
    query_ref,
    key_ref,
    value_ref,
    line_ref,
    across_ref,
    down_ref,
    mask_ref,
    table_ref,
    exp_ref,
    context_ref,
    inverse_ref,
    score_ref,
    *,
    line_count,
    plane_count,
):
    heads, rows, keys = exp_ref.shape
    for h in range(heads):
        pair = slice(h // 2 * LANES, (h // 2 + 1) * LANES)
        score_ref[h] = dot_f32(query_ref[:, pair], key_ref[h])

    def strip(r, carry):
        at = pl.ds(pl.multiple_of(r * STRIP, STRIP), STRIP)
        tops = [None] * heads
        for c in range(keys // LANES):
            cols = slice(c * LANES, (c + 1) * LANES)
            line = line_ref[0, at, cols].astype(jnp.int16) & jnp.int16(line_count - 1)
            across = across_ref[0, at, cols].astype(jnp.int16) & jnp.int16(plane_count - 1)
            down = down_ref[0, at, cols].astype(jnp.int16) & jnp.int16(plane_count - 1)
            bias = [None] * heads
            for t, index in enumerate((line | mask_ref[:, cols], across, down)):
                for h in range(heads):
                    found = gather_lanes(table_ref[t * heads + h], index).astype(f32)
                    bias[h] = found if t == 0 else bias[h] + found
            for h in range(heads):
                score = score_ref[h, at, cols] + bias[h]
                score_ref[h, at, cols] = score
                tops[h] = score if c == 0 else jnp.maximum(tops[h], score)
        for h in range(heads):
            top = jnp.max(tops[h], axis=1, keepdims=True)
            for c in range(keys // LANES):
                cols = slice(c * LANES, (c + 1) * LANES)
                exp_ref[h, at, cols] = jnp.exp(score_ref[h, at, cols] - top).astype(bf16)
        return carry

    lax.fori_loop(0, rows // STRIP, strip, 0)
    first = lax.broadcasted_iota(jnp.int32, (rows, LANES), 1) < HEAD
    for p in range(heads // 2):
        cols = slice(p * LANES, (p + 1) * LANES)
        even = dot_f32(exp_ref[2 * p], value_ref[2 * p])
        odd = dot_f32(exp_ref[2 * p + 1], value_ref[2 * p + 1])
        sums = jnp.where(first, pltpu.roll(even, HEAD, 1), pltpu.roll(odd, HEAD, 1))
        inverse = 1.0 / sums
        inverse_ref[:, cols] = inverse
        context_ref[:, cols] = jnp.where(first, even, odd) * inverse


def attend(query, key_wide, value_wide, buckets, mask, tables, row_count, counts):
    heads, _, keys = key_wide.shape
    width = heads * HEAD
    bucket_spec = pl.BlockSpec((1, BLOCK_ROWS, keys), lambda i: (0, i, 0))
    row_spec = pl.BlockSpec((BLOCK_ROWS, width), lambda i: (i, 0))
    return pl.pallas_call(
        partial(attend_kernel, line_count=counts[0], plane_count=counts[1]),
        grid=(row_count // BLOCK_ROWS,),
        in_specs=[
            row_spec,
            whole_spec(key_wide),
            whole_spec(value_wide),
            bucket_spec,
            bucket_spec,
            bucket_spec,
            whole_spec(mask),
            whole_spec(tables),
        ],
        out_specs=[
            pl.BlockSpec((heads, BLOCK_ROWS, keys), lambda i: (0, i, 0)),
            row_spec,
            row_spec,
        ],
        out_shape=[
            jax.ShapeDtypeStruct((heads, row_count, keys), bf16),
            jax.ShapeDtypeStruct((row_count, width), f32),
            jax.ShapeDtypeStruct((row_count, width), f32),
        ],
        scratch_shapes=[pltpu.VMEM((heads, BLOCK_ROWS, keys), f32)],
        compiler_params=pltpu.CompilerParams(vmem_limit_bytes=vmem_limit),
        name="attend",
    )(query, key_wide, value_wide, *buckets, mask, tables)


def attend_back_kernel(
    exp_ref,
    grad_ref,
    context_ref,
    query_ref,
    value_ref,
    key_ref,
    grad_score_ref,
    grad_query_ref,
    grad_key_ref,
    grad_value_ref,
):
    heads, rows, _ = exp_ref.shape

    @pl.when(pl.program_id(0) == 0)
    def _():
        grad_key_ref[...] = jnp.zeros_like(grad_key_ref)
        grad_value_ref[...] = jnp.zeros_like(grad_value_ref)

    first = lax.broadcasted_iota(jnp.int32, (rows, LANES), 1) < HEAD
    for p in range(heads // 2):
        cols = slice(p * LANES, (p + 1) * LANES)
        grad = grad_ref[:, cols]
        product = grad.astype(f32) * context_ref[:, cols]
        query_turned = query_ref[:, cols].T
        grad_turned = grad.T
        grad_query = None
        for u in range(2):
            h = 2 * p + u
            half = slice(u * HEAD, (u + 1) * HEAD)
            own = first if u == 0 else ~first
            total = jnp.sum(jnp.where(own, product, 0.0), axis=1, keepdims=True)
            grad_exp = dot_f32(grad, value_ref[h])
            grad_score = (exp_ref[h].astype(f32) * (grad_exp - total)).astype(bf16)
            grad_score_ref[h] = grad_score
            part = dot_f32(grad_score, key_ref[h])
            grad_query = part if u == 0 else grad_query + part
            grad_key_ref[h] += dot_f32(query_turned[half], grad_score)
            grad_value_ref[h] += dot_f32(grad_turned[half], exp_ref[h])
        grad_query_ref[:, cols] = (grad_query * 0.125).astype(bf16)


def attend_back(exps, grad, context, query, value_turned, key_wide):
    heads, row_count, keys = exps.shape
    width = heads * HEAD
    row_spec = pl.BlockSpec((BLOCK_ROWS, width), lambda i: (i, 0))
    exp_spec = pl.BlockSpec((heads, BLOCK_ROWS, keys), lambda i: (0, i, 0))
    sum_spec = pl.BlockSpec((heads, HEAD, keys), lambda i: (0, 0, 0))
    return pl.pallas_call(
        attend_back_kernel,
        grid=(row_count // BLOCK_ROWS,),
        in_specs=[
            exp_spec,
            row_spec,
            row_spec,
            row_spec,
            whole_spec(value_turned),
            whole_spec(key_wide),
        ],
        out_specs=[exp_spec, row_spec, sum_spec, sum_spec],
        out_shape=[
            jax.ShapeDtypeStruct((heads, row_count, keys), bf16),
            jax.ShapeDtypeStruct((row_count, width), bf16),
            jax.ShapeDtypeStruct((heads, HEAD, keys), f32),
            jax.ShapeDtypeStruct((heads, HEAD, keys), f32),
        ],
        compiler_params=pltpu.CompilerParams(vmem_limit_bytes=vmem_limit),
        name="attend_back",
    )(exps, grad, context, query, value_turned, key_wide)


def table_kernel(
    grad_score_ref, line_ref, across_ref, down_ref, out_ref, high_ref, low_ref, sum_ref, *, high_counts
):
    heads, rows, keys = grad_score_ref.shape
    step = pl.program_id(0)

    @pl.when(step == 0)
    def _():
        sum_ref[...] = jnp.zeros_like(sum_ref)

    def strip(r, carry):
        at = pl.ds(pl.multiple_of(r * STRIP, STRIP), STRIP)
        base = 0
        for t, ref in enumerate((line_ref, across_ref, down_ref)):
            for c in range(keys // LANES):
                cols = slice(c * LANES, (c + 1) * LANES)
                index = ref[0, at, cols].astype(jnp.int16)
                low = index & jnp.int16(15)
                high = index >> jnp.int16(4)
                for x in range(16):
                    low_ref[t, x * STRIP : (x + 1) * STRIP, cols] = jnp.where(
                        low == jnp.int16(x), bf16(1), bf16(0)
                    )
                for x in range(high_counts[t]):
                    mask = high == jnp.int16(x)
                    for h in range(heads):
                        start = base + (x * heads + h) * STRIP
                        high_ref[start : start + STRIP, cols] = jnp.where(
                            mask, grad_score_ref[h, at, cols], bf16(0)
                        )
            span = slice(base, base + high_counts[t] * heads * STRIP)
            sum_ref[span, :] += lax.dot_general(
                high_ref[span, :], low_ref[t], (((1,), (1,)), ((), ())), preferred_element_type=f32
            )
            base = span.stop
        return carry

    lax.fori_loop(0, rows // STRIP, strip, 0)

    @pl.when(step == pl.num_programs(0) - 1)
    def _():
        across_rows = lax.broadcasted_iota(jnp.int32, (STRIP, 16 * STRIP), 1) % STRIP
        same = across_rows == lax.broadcasted_iota(jnp.int32, (STRIP, 16 * STRIP), 0)
        for o in range(out_ref.shape[0]):
            block = sum_ref[o * STRIP : (o + 1) * STRIP, :]
            out_ref[o : o + 1, :] = jnp.sum(jnp.where(same, block, 0.0), axis=0, keepdims=True)


def table_sums(grad_scores, buckets, counts):
    heads, row_count, keys = grad_scores.shape
    high_counts = (counts[0] // 16, counts[1] // 16, counts[1] // 16)
    high_rows = sum(high_counts) * heads
    bucket_spec = pl.BlockSpec((1, BLOCK_ROWS, keys), lambda i: (0, i, 0))
    out = pl.pallas_call(
        partial(table_kernel, high_counts=high_counts),
        grid=(row_count // BLOCK_ROWS,),
        in_specs=[
            pl.BlockSpec((heads, BLOCK_ROWS, keys), lambda i: (0, i, 0)),
            bucket_spec,
            bucket_spec,
            bucket_spec,
        ],
        out_specs=pl.BlockSpec((high_rows, 16 * STRIP), lambda i: (0, 0)),
        out_shape=jax.ShapeDtypeStruct((high_rows, 16 * STRIP), f32),
        scratch_shapes=[
            pltpu.VMEM((high_rows * STRIP, keys), bf16),
            pltpu.VMEM((3, 16 * STRIP, keys), bf16),
            pltpu.VMEM((high_rows * STRIP, 16 * STRIP), f32),
        ],
        compiler_params=pltpu.CompilerParams(vmem_limit_bytes=vmem_limit),
        name="table_sums",
    )(grad_scores, *buckets)
    summed = jnp.sum(out.reshape(sum(high_counts), heads, 16, STRIP), axis=-1)
    return summed.transpose(0, 2, 1).reshape(-1, heads)


def swap(array):
    return lax.ppermute(array, "mp", [(0, 1), (1, 0)])


def both_shares(array, axis):
    other = swap(array)
    lead = lax.axis_index("mp") == 0
    return jnp.concatenate(
        [jnp.where(lead, array, other), jnp.where(lead, other, array)], axis=axis
    )


def partner(array, count, bit):
    return lax.ppermute(array, "dp", [(i, i ^ bit) for i in range(count)])


def sum_rows_over_dp(array, count):
    place = lax.axis_index("dp")
    bits = []
    bit = 1
    while bit < count:
        mine = (place // bit) % 2
        halves = array.reshape((2, array.shape[0] // 2) + array.shape[1:])
        sent = lax.dynamic_index_in_dim(halves, 1 - mine, 0, keepdims=False)
        kept = lax.dynamic_index_in_dim(halves, mine, 0, keepdims=False)
        array = kept + partner(sent, count, bit)
        bits.append(bit)
        bit *= 2
    for bit in reversed(bits):
        lead = (place // bit) % 2 == 0
        other = partner(array, count, bit)
        array = jnp.concatenate(
            [jnp.where(lead, array, other), jnp.where(lead, other, array)], axis=0
        )
    return array


def sum_small_over_dp(arrays, count):
    sizes = [a.size for a in arrays]
    total = sum(sizes)
    flat = jnp.concatenate([a.reshape(-1) for a in arrays])
    flat = jnp.pad(flat, (0, round_up(total, 1024) - total)).reshape(-1, LANES)
    bit = 1
    while bit < count:
        flat = flat + partner(flat, count, bit)
        bit *= 2
    flat = flat.reshape(-1)
    outs = []
    start = 0
    for array, size in zip(arrays, sizes):
        outs.append(flat[start : start + size].reshape(array.shape))
        start += size
    return outs


def norm_parts(values, gain_vector, shift_vector):
    average = jnp.mean(values, axis=-1, keepdims=True)
    centered = values - average
    variance = jnp.mean(centered * centered, axis=-1, keepdims=True)
    inverse = lax.rsqrt(variance + norm_epsilon)
    normal_hat = centered * inverse
    return (normal_hat * gain_vector + shift_vector, normal_hat, inverse)


def norm_back(grad_hat, normal_hat, inverse):
    first_mean = jnp.mean(grad_hat, axis=-1, keepdims=True)
    cross_mean = jnp.mean(grad_hat * normal_hat, axis=-1, keepdims=True)
    return inverse * (grad_hat - first_mean - normal_hat * cross_mean)


def widen(heads_rows, other):
    fill = jnp.full(heads_rows[:, 0].shape, other, bf16)
    wide = []
    for h in range(heads_rows.shape[1]):
        parts = [heads_rows[:, h], fill]
        wide.append(jnp.concatenate(parts if h % 2 == 0 else parts[::-1], axis=1))
    return jnp.stack(wide)


def per_device(
    dp_count,
    tokens,
    cotangent,
    long_flag,
    token_mask,
    bucket_line,
    bucket_across,
    bucket_down,
    project_weight,
    project_bias,
    table_line,
    table_across,
    table_down,
    output_weight,
    output_bias,
    first_gain,
    first_shift,
    expand_weight,
    expand_bias,
    reduce_weight,
    reduce_bias,
    second_gain,
    second_shift,
):
    length = tokens.shape[1]
    width = project_weight.shape[2]
    heads = table_line.shape[1]
    counts = (table_line.shape[0], table_across.shape[0])
    rows = round_up(length, BLOCK_ROWS)
    keys = round_up(length, LANES)
    buckets = (bucket_line, bucket_across, bucket_down)
    mp_index = lax.axis_index("mp")

    positions = jnp.arange(length, dtype=jnp.int32)
    limit = jnp.where(long_flag[0] > 0, LONG, SHORT).astype(jnp.int32)
    valid = ((token_mask[0] > 0) & (positions < limit)).astype(f32)
    valid_rows = jnp.pad(valid, (0, rows - length))[:, None]
    valid_keys = jnp.pad(valid, (0, keys - length))
    mask = jnp.broadcast_to(
        jnp.where(valid_keys > 0, 0, counts[0]).astype(jnp.int16), (STRIP, keys)
    )
    tables = []
    for table in (table_line, table_across, table_down):
        lanes = jnp.pad(
            table.T, ((0, 0), (0, LANES - table.shape[0])), constant_values=large_negative
        )
        tables.append(jnp.broadcast_to(lanes[:, None, :], (heads, STRIP, LANES)))
    tables = jnp.concatenate(tables).astype(bf16)

    output_full = both_shares(output_weight, 0)
    padded = jnp.pad(tokens[0], ((0, keys - length), (0, 0)))
    token_rows = padded[:rows]
    projected = jnp.einsum("ld,kde->kle", padded, project_weight, preferred_element_type=f32)
    query = (projected[0] + project_bias[0].astype(f32)).astype(bf16) * bf16(0.125)
    key_heads = projected[1].astype(bf16).reshape(keys, heads, HEAD)
    value_heads = (projected[2] + project_bias[1].astype(f32)).astype(bf16)
    value_heads = value_heads.reshape(keys, heads, HEAD)
    key_wide = widen(key_heads, 0)
    value_ones = widen(value_heads, 1)
    value_wide = widen(value_heads, 0)

    exps, context, inverse = attend(
        query,
        key_wide.transpose(0, 2, 1),
        value_ones,
        buckets,
        mask,
        tables,
        rows,
        counts,
    )
    context_low = context.astype(bf16)
    context_full = both_shares(context_low, 1)
    attended = dot_f32(context_full, output_full) + output_bias.astype(f32)
    first_norm, first_hat, first_inverse = norm_parts(
        token_rows.astype(f32) + attended, first_gain, first_shift
    )
    expand_input = first_norm.astype(bf16)
    before = dot_f32(expand_input, expand_weight) + expand_bias.astype(f32)
    activated, gelu_back = jax.vjp(partial(jax.nn.gelu, approximate=False), before)
    activated_low = activated.astype(bf16)
    reduced_part = dot_f32(activated_low, reduce_weight).astype(bf16)
    reduced = reduced_part.astype(f32) + swap(reduced_part).astype(f32)
    reduced = reduced + reduce_bias.astype(f32)
    second_norm, second_hat, second_inverse = norm_parts(
        first_norm + reduced, second_gain, second_shift
    )
    layer_out = (second_norm * valid_rows).astype(bf16)[None, :length]
    grad_out = jnp.pad(cotangent[0], ((0, rows - length), (0, 0))).astype(f32) * valid_rows
    second_gain_grad = jnp.sum(grad_out * second_hat, axis=0)
    second_shift_grad = jnp.sum(grad_out, axis=0)
    grad_mixed = norm_back(grad_out * second_gain, second_hat, second_inverse)
    grad_reduced = grad_mixed.astype(bf16)
    reduce_bias_grad = jnp.sum(grad_reduced, axis=0, dtype=f32)
    reduce_weight_grad = jnp.einsum(
        "lf,ld->fd", activated_low, grad_reduced, preferred_element_type=f32
    )
    grad_active = jnp.einsum("ld,fd->lf", grad_reduced, reduce_weight, preferred_element_type=f32)
    grad_before = gelu_back(grad_active)[0].astype(bf16)
    expand_bias_grad = jnp.sum(grad_before, axis=0, dtype=f32)
    expand_weight_grad = jnp.einsum(
        "ld,lf->df", expand_input, grad_before, preferred_element_type=f32
    )
    reduce_weight_grad = sum_rows_over_dp(reduce_weight_grad.astype(bf16), dp_count)
    expand_weight_grad = sum_rows_over_dp(expand_weight_grad.astype(bf16), dp_count)

    hidden_part = jnp.einsum(
        "lf,df->ld", grad_before, expand_weight, preferred_element_type=f32
    ).astype(bf16)
    hidden = hidden_part.astype(f32) + swap(hidden_part).astype(f32)
    grad_first = grad_mixed + hidden
    first_gain_grad = jnp.sum(grad_first * first_hat, axis=0)
    first_shift_grad = jnp.sum(grad_first, axis=0)
    grad_inner = norm_back(grad_first * first_gain, first_hat, first_inverse)
    grad_attended = grad_inner.astype(bf16)
    output_bias_grad = jnp.sum(grad_attended, axis=0, dtype=f32)
    output_weight_grad = jnp.einsum(
        "le,lf->ef", context_low, grad_attended, preferred_element_type=f32
    )
    output_weight_grad = sum_rows_over_dp(output_weight_grad.astype(bf16), dp_count)
    grad_context = jnp.einsum(
        "lf,ef->le", grad_attended, output_weight, preferred_element_type=f32
    )
    grad_scaled = (grad_context * inverse).astype(bf16)

    grad_scores, grad_query, grad_key, grad_value = attend_back(
        exps, grad_scaled, context, query, value_wide.transpose(0, 2, 1), key_wide
    )
    grad_key = grad_key.reshape(width, keys)[:, :rows].astype(bf16)
    grad_value = grad_value.reshape(width, keys)[:, :rows].astype(bf16)
    project_weight_grad = jnp.stack(
        [
            jnp.einsum("ld,le->de", token_rows, grad_query, preferred_element_type=f32),
            jnp.einsum("ld,el->de", token_rows, grad_key, preferred_element_type=f32),
            jnp.einsum("ld,el->de", token_rows, grad_value, preferred_element_type=f32),
        ]
    ).astype(bf16)
    project_weight_grad = sum_rows_over_dp(
        project_weight_grad.reshape(-1, width), dp_count
    ).reshape(project_weight.shape)
    project_bias_grad = jnp.stack(
        [jnp.sum(grad_query, axis=0, dtype=f32), jnp.sum(grad_value, axis=1, dtype=f32)]
    )
    input_part = (
        jnp.einsum("le,de->ld", grad_query, project_weight[0], preferred_element_type=f32)
        + jnp.einsum("el,de->ld", grad_key, project_weight[1], preferred_element_type=f32)
        + jnp.einsum("el,de->ld", grad_value, project_weight[2], preferred_element_type=f32)
    )
    lead = mp_index == 0
    sent = jnp.where(lead, input_part[:, width:], input_part[:, :width]).astype(bf16)
    own = jnp.where(
        lead,
        input_part[:, :width] + grad_inner[:, :width],
        input_part[:, width:] + grad_inner[:, width:],
    )
    input_grad = (own + swap(sent).astype(f32))[None, :length]

    table_grads = table_sums(grad_scores, buckets, counts)
    (
        second_gain_grad,
        second_shift_grad,
        reduce_bias_grad,
        expand_bias_grad,
        first_gain_grad,
        first_shift_grad,
        output_bias_grad,
    ) = sum_small_over_dp(
        [
            second_gain_grad,
            second_shift_grad,
            reduce_bias_grad,
            expand_bias_grad,
            first_gain_grad,
            first_shift_grad,
            output_bias_grad,
        ],
        dp_count,
    )
    table_grads, project_bias_grad = sum_small_over_dp([table_grads, project_bias_grad], dp_count)
    mine = mp_index * width
    return (
        layer_out,
        input_grad,
        project_weight_grad.astype(f32),
        project_bias_grad,
        table_grads[: counts[0]],
        table_grads[counts[0] : counts[0] + counts[1]],
        table_grads[counts[0] + counts[1] :],
        output_weight_grad.astype(f32),
        output_bias_grad,
        lax.dynamic_slice_in_dim(first_gain_grad, mine, width, 0),
        lax.dynamic_slice_in_dim(first_shift_grad, mine, width, 0),
        expand_weight_grad.astype(f32),
        expand_bias_grad,
        reduce_weight_grad.astype(f32),
        reduce_bias_grad,
        second_gain_grad,
        second_shift_grad,
    )


def solution(mesh):
    placed = (
        P("dp", None, None),
        P("dp", None, None),
        P("dp"),
        P("dp", None),
        P("dp", None, None),
        P("dp", None, None),
        P("dp", None, None),
        P(None, None, "mp"),
        P(None, "mp"),
        P(None, "mp"),
        P(None, "mp"),
        P(None, "mp"),
        P("mp", None),
        P(),
        P(),
        P(),
        P(None, "mp"),
        P("mp"),
        P("mp", None),
        P(),
        P(),
        P(),
    )
    return jax.shard_map(
        partial(per_device, mesh.shape["dp"]),
        mesh=mesh,
        in_specs=placed,
        out_specs=(
            P("dp", None, None),
            P("dp", None, "mp"),
            P(None, None, "mp"),
            P(None, "mp"),
            P(None, "mp"),
            P(None, "mp"),
            P(None, "mp"),
            P("mp", None),
            P(),
            P("mp"),
            P("mp"),
            P(None, "mp"),
            P("mp"),
            P("mp", None),
            P(),
            P(),
            P(),
        ),
        check_vma=False,
    )
```

```python
from functools import partial

import jax
import jax.numpy as jnp
from jax import lax
from jax.experimental import pallas as pl
from jax.experimental.pallas import tpu as pltpu
from jax.sharding import PartitionSpec as P

LONG = 1089
SHORT = 709
HEAD = 64
LANES = 128
STRIP = 16
BLOCK_ROWS = 224

large_negative = -1000000000.0
norm_epsilon = 1e-05
vmem_limit = 56 * 2**20
bf16 = jnp.bfloat16
f32 = jnp.float32


def round_up(value, step):
    return (value + step - 1) // step * step


def whole_spec(array):
    zeros = (0,) * array.ndim
    return pl.BlockSpec(array.shape, lambda i: zeros)


def dot_f32(left, right):
    return jnp.dot(left, right, preferred_element_type=f32)


def gather_lanes(values, index):
    dims = lax.GatherDimensionNumbers(
        offset_dims=(),
        collapsed_slice_dims=(1,),
        start_index_map=(1,),
        operand_batching_dims=(0,),
        start_indices_batching_dims=(0,),
    )
    return lax.gather(
        values,
        index[..., None],
        dims,
        slice_sizes=(1, 1),
        mode=lax.GatherScatterMode.PROMISE_IN_BOUNDS,
    )


def project_kernel(
    token_ref, weight_ref, bias_ref, query_ref, key_ref, key_turned_ref, value_ref, value_turned_ref, *, length
):
    rows = token_ref.shape[0]
    place = pl.program_id(0) * rows + lax.broadcasted_iota(jnp.int32, token_ref.shape, 0)
    token = jnp.where(place < length, token_ref[...].astype(f32), 0.0).astype(bf16)
    query = (dot_f32(token, weight_ref[0]) + bias_ref[0:1, :]).astype(bf16)
    query_ref[...] = (query.astype(f32) * 0.125).astype(bf16)
    key = dot_f32(token, weight_ref[1])
    value = dot_f32(token, weight_ref[2]) + bias_ref[1:2, :]
    lane_first = lax.broadcasted_iota(jnp.int32, (rows, LANES), 1) < HEAD
    row_first = lax.broadcasted_iota(jnp.int32, (LANES, rows), 0) < HEAD
    for p in range(key.shape[1] // LANES):
        cols = slice(p * LANES, (p + 1) * LANES)
        key_pair, value_pair = key[:, cols], value[:, cols]
        key_turned, value_turned = key_pair.T, value_pair.T
        for u in range(2):
            h = 2 * p + u
            lane_own = lane_first if u == 0 else ~lane_first
            row_own = row_first if u == 0 else ~row_first
            key_ref[h] = jnp.where(lane_own, key_pair, 0.0).astype(bf16)
            value_ref[h] = jnp.where(lane_own, value_pair, 1.0).astype(bf16)
            key_turned_ref[h] = jnp.where(row_own, key_turned, 0.0).astype(bf16)
            value_turned_ref[h] = jnp.where(row_own, value_turned, 0.0).astype(bf16)


def project(tokens, weight, bias, keys):
    length, depth = tokens.shape
    width = weight.shape[2]
    heads = width // HEAD
    block = 3 * LANES
    wide = pl.BlockSpec((heads, block, LANES), lambda i: (0, i, 0))
    turned = pl.BlockSpec((heads, LANES, block), lambda i: (0, 0, i))
    wide_shape = jax.ShapeDtypeStruct((heads, keys, LANES), bf16)
    turned_shape = jax.ShapeDtypeStruct((heads, LANES, keys), bf16)
    return pl.pallas_call(
        partial(project_kernel, length=length),
        grid=(keys // block,),
        in_specs=[
            pl.BlockSpec((block, depth), lambda i: (i, 0)),
            whole_spec(weight),
            whole_spec(bias),
        ],
        out_specs=[pl.BlockSpec((block, width), lambda i: (i, 0)), wide, turned, wide, turned],
        out_shape=[
            jax.ShapeDtypeStruct((keys, width), bf16),
            wide_shape,
            turned_shape,
            wide_shape,
            turned_shape,
        ],
        compiler_params=pltpu.CompilerParams(vmem_limit_bytes=vmem_limit),
        name="project",
    )(tokens, weight, bias)


def attend_kernel(
    query_ref,
    key_ref,
    value_ref,
    plane_ref,
    down_ref,
    table_ref,
    exp_ref,
    context_ref,
    inverse_ref,
    score_ref,
):
    heads, rows, keys = exp_ref.shape
    for h in range(heads):
        pair = slice(h // 2 * LANES, (h // 2 + 1) * LANES)
        score_ref[h] = dot_f32(query_ref[:, pair], key_ref[h])

    def strip(r, carry):
        at = pl.ds(pl.multiple_of(r * STRIP, STRIP), STRIP)
        tops = [None] * heads
        for c in range(keys // LANES):
            cols = slice(c * LANES, (c + 1) * LANES)
            packed = plane_ref[at, cols]
            bias = [None] * heads
            for t, index in enumerate(
                (packed & jnp.int16(255), packed >> jnp.int16(8), down_ref[at, cols])
            ):
                for h in range(heads):
                    found = gather_lanes(table_ref[t * heads + h], index).astype(f32)
                    bias[h] = found if t == 0 else bias[h] + found
            for h in range(heads):
                score = score_ref[h, at, cols] + bias[h]
                score_ref[h, at, cols] = score
                tops[h] = score if c == 0 else jnp.maximum(tops[h], score)
        for h in range(heads):
            top = jnp.max(tops[h], axis=1, keepdims=True)
            for c in range(keys // LANES):
                cols = slice(c * LANES, (c + 1) * LANES)
                exp_ref[h, at, cols] = jnp.exp(score_ref[h, at, cols] - top).astype(bf16)
        return carry

    lax.fori_loop(0, rows // STRIP, strip, 0)
    first = lax.broadcasted_iota(jnp.int32, (rows, LANES), 1) < HEAD
    for p in range(heads // 2):
        cols = slice(p * LANES, (p + 1) * LANES)
        even = dot_f32(exp_ref[2 * p], value_ref[2 * p])
        odd = dot_f32(exp_ref[2 * p + 1], value_ref[2 * p + 1])
        sums = jnp.where(first, pltpu.roll(even, HEAD, 1), pltpu.roll(odd, HEAD, 1))
        inverse = 1.0 / sums
        inverse_ref[:, cols] = inverse
        context_ref[:, cols] = (jnp.where(first, even, odd) * inverse).astype(bf16)


def attend(query, key_turned, value_ones, plane, down, tables):
    heads, _, keys = key_turned.shape
    row_count = plane.shape[0]
    width = heads * HEAD
    index_spec = pl.BlockSpec((BLOCK_ROWS, keys), lambda i: (i, 0))
    row_spec = pl.BlockSpec((BLOCK_ROWS, width), lambda i: (i, 0))
    return pl.pallas_call(
        attend_kernel,
        grid=(row_count // BLOCK_ROWS,),
        in_specs=[
            row_spec,
            whole_spec(key_turned),
            whole_spec(value_ones),
            index_spec,
            index_spec,
            whole_spec(tables),
        ],
        out_specs=[
            pl.BlockSpec((heads, BLOCK_ROWS, keys), lambda i: (0, i, 0)),
            row_spec,
            row_spec,
        ],
        out_shape=[
            jax.ShapeDtypeStruct((heads, row_count, keys), bf16),
            jax.ShapeDtypeStruct((row_count, width), bf16),
            jax.ShapeDtypeStruct((row_count, width), f32),
        ],
        scratch_shapes=[pltpu.VMEM((heads, BLOCK_ROWS, keys), f32)],
        compiler_params=pltpu.CompilerParams(vmem_limit_bytes=vmem_limit),
        name="attend",
    )(query, key_turned, value_ones, plane, down, tables)


def attend_back_kernel(
    exp_ref,
    grad_ref,
    context_ref,
    query_ref,
    value_ref,
    key_ref,
    grad_score_ref,
    grad_query_ref,
    grad_key_ref,
    grad_value_ref,
):
    heads, rows, _ = exp_ref.shape

    @pl.when(pl.program_id(0) == 0)
    def _():
        grad_key_ref[...] = jnp.zeros_like(grad_key_ref)
        grad_value_ref[...] = jnp.zeros_like(grad_value_ref)

    first = lax.broadcasted_iota(jnp.int32, (rows, LANES), 1) < HEAD
    for p in range(heads // 2):
        cols = slice(p * LANES, (p + 1) * LANES)
        grad = grad_ref[:, cols]
        product = grad.astype(f32) * context_ref[:, cols].astype(f32)
        query_turned = query_ref[:, cols].T
        grad_turned = grad.T
        grad_query = None
        for u in range(2):
            h = 2 * p + u
            half = slice(u * HEAD, (u + 1) * HEAD)
            own = first if u == 0 else ~first
            total = jnp.sum(jnp.where(own, product, 0.0), axis=1, keepdims=True)
            grad_exp = dot_f32(grad, value_ref[h])
            grad_score = (exp_ref[h].astype(f32) * (grad_exp - total)).astype(bf16)
            grad_score_ref[h] = grad_score
            part = dot_f32(grad_score, key_ref[h])
            grad_query = part if u == 0 else grad_query + part
            grad_key_ref[h] += dot_f32(query_turned[half], grad_score)
            grad_value_ref[h] += dot_f32(grad_turned[half], exp_ref[h])
        grad_query_ref[:, cols] = (grad_query * 0.125).astype(bf16)


def attend_back(exps, grad, context, query, value_turned, key_wide):
    heads, row_count, keys = exps.shape
    width = heads * HEAD
    row_spec = pl.BlockSpec((BLOCK_ROWS, width), lambda i: (i, 0))
    exp_spec = pl.BlockSpec((heads, BLOCK_ROWS, keys), lambda i: (0, i, 0))
    sum_spec = pl.BlockSpec((heads, HEAD, keys), lambda i: (0, 0, 0))
    return pl.pallas_call(
        attend_back_kernel,
        grid=(row_count // BLOCK_ROWS,),
        in_specs=[
            exp_spec,
            row_spec,
            row_spec,
            row_spec,
            whole_spec(value_turned),
            whole_spec(key_wide),
        ],
        out_specs=[exp_spec, row_spec, sum_spec, sum_spec],
        out_shape=[
            jax.ShapeDtypeStruct((heads, row_count, keys), bf16),
            jax.ShapeDtypeStruct((row_count, width), bf16),
            jax.ShapeDtypeStruct((heads, HEAD, keys), f32),
            jax.ShapeDtypeStruct((heads, HEAD, keys), f32),
        ],
        compiler_params=pltpu.CompilerParams(vmem_limit_bytes=vmem_limit),
        name="attend_back",
    )(exps, grad, context, query, value_turned, key_wide)


def table_strip(grad_of, plane_of, down_of, high_ref, low_ref, sum_ref, heads, keys, high_counts):
    base = 0
    for t in range(3):
        for c in range(keys // LANES):
            cols = slice(c * LANES, (c + 1) * LANES)
            if t == 2:
                index = down_of(cols)
            elif t == 1:
                index = plane_of(cols) >> jnp.int16(8)
            else:
                index = plane_of(cols) & jnp.int16(255)
            low = index & jnp.int16(15)
            high = index >> jnp.int16(4)
            for x in range(16):
                low_ref[t, x * STRIP : (x + 1) * STRIP, cols] = jnp.where(
                    low == jnp.int16(x), bf16(1), bf16(0)
                )
            for x in range(high_counts[t]):
                mask = high == jnp.int16(x)
                for h in range(heads):
                    start = base + (x * heads + h) * STRIP
                    high_ref[start : start + STRIP, cols] = jnp.where(mask, grad_of(h, cols), bf16(0))
        span = slice(base, base + high_counts[t] * heads * STRIP)
        sum_ref[span, :] += lax.dot_general(
            high_ref[span, :], low_ref[t], (((1,), (1,)), ((), ())), preferred_element_type=f32
        )
        base = span.stop


def table_finish(sum_ref, out_ref):
    row_of_lane = lax.broadcasted_iota(jnp.int32, (STRIP, 16 * STRIP), 1) % STRIP
    same = row_of_lane == lax.broadcasted_iota(jnp.int32, (STRIP, 16 * STRIP), 0)
    for o in range(out_ref.shape[0]):
        block = sum_ref[o * STRIP : (o + 1) * STRIP, :]
        out_ref[o : o + 1, :] = jnp.sum(jnp.where(same, block, 0.0), axis=0, keepdims=True)


def table_scratch(high_rows, keys):
    return [
        pltpu.VMEM((high_rows * STRIP, keys), bf16),
        pltpu.VMEM((3, 16 * STRIP, keys), bf16),
        pltpu.VMEM((high_rows * STRIP, 16 * STRIP), f32),
    ]


def table_result(out, high_counts, heads):
    summed = jnp.sum(out.reshape(sum(high_counts), heads, 16, STRIP), axis=-1)
    return summed.transpose(0, 2, 1).reshape(-1, heads)


def table_kernel(grad_score_ref, plane_ref, down_ref, out_ref, high_ref, low_ref, sum_ref, *, high_counts):
    heads, rows, keys = grad_score_ref.shape
    step = pl.program_id(0)

    @pl.when(step == 0)
    def _():
        sum_ref[...] = jnp.zeros_like(sum_ref)

    def strip(r, carry):
        at = pl.ds(pl.multiple_of(r * STRIP, STRIP), STRIP)
        table_strip(
            lambda h, cols: grad_score_ref[h, at, cols],
            lambda cols: plane_ref[at, cols],
            lambda cols: down_ref[at, cols],
            high_ref,
            low_ref,
            sum_ref,
            heads,
            keys,
            high_counts,
        )
        return carry

    lax.fori_loop(0, rows // STRIP, strip, 0)

    @pl.when(step == pl.num_programs(0) - 1)
    def _():
        table_finish(sum_ref, out_ref)


def table_sums(grad_scores, plane, down, counts):
    heads, row_count, keys = grad_scores.shape
    high_counts = (counts[0] // 16, counts[1] // 16, counts[1] // 16)
    high_rows = sum(high_counts) * heads
    index_spec = pl.BlockSpec((BLOCK_ROWS, keys), lambda i: (i, 0))
    out = pl.pallas_call(
        partial(table_kernel, high_counts=high_counts),
        grid=(row_count // BLOCK_ROWS,),
        in_specs=[
            pl.BlockSpec((heads, BLOCK_ROWS, keys), lambda i: (0, i, 0)),
            index_spec,
            index_spec,
        ],
        out_specs=pl.BlockSpec((high_rows, 16 * STRIP), lambda i: (0, 0)),
        out_shape=jax.ShapeDtypeStruct((high_rows, 16 * STRIP), f32),
        scratch_shapes=table_scratch(high_rows, keys),
        compiler_params=pltpu.CompilerParams(vmem_limit_bytes=vmem_limit),
        name="table_sums",
    )(grad_scores, plane, down)
    return table_result(out, high_counts, heads)


CHUNK = 768
CHUNKS = 6
AWAY = 4
PARTS = (CHUNK // 2, CHUNK // 4, CHUNK // 8, CHUNK // 16)


def exchange_schedule(strips):
    plan = []
    for k in range(CHUNKS):
        plan.append((0, 0, k))
        plan.append((1 + k, 1, k))
    for k in range(CHUNKS):
        if k < CHUNKS - AWAY:
            start = 9 + 5 * k
        else:
            arrival = 15 + 11 * (k - CHUNKS + AWAY)
            plan.append((arrival, 2, k))
            start = arrival + 7
        for event, delay in ((3, 0), (4, 4), (5, 8), (6, 12), (7, 16), (8, 23), (9, 27)):
            plan.append((start + delay, event, k))
    slots = [[] for _ in range(strips + 1)]
    for at, event, k in sorted(plan):
        slots[min(at, strips)].append((event, k))
    return slots


def table_exchange_kernel(
    grad_score_ref,
    plane_ref,
    down_ref,
    project_ref,
    output_ref,
    expand_ref,
    expand_away_ref,
    reduce_ref,
    reduce_away_ref,
    table_ref,
    total_ref,
    high_ref,
    low_ref,
    sum_ref,
    grad_buf,
    plane_buf,
    down_buf,
    own_buf,
    away_buf,
    core_buf,
    core_away_buf,
    y_buf,
    x_buf,
    near_buf,
    far_buf,
    block_sem,
    load_sem,
    local_sem,
    send_sem,
    recv_sem,
    *,
    high_counts,
):
    heads, row_count, keys = grad_score_ref.shape
    block_rows = grad_buf.shape[2]
    per_block = block_rows // STRIP
    blocks = row_count // block_rows
    strips = row_count // STRIP
    place = lax.axis_index("dp")
    sides = [(place // bit) % 2 for bit in (1, 2, 4, 8)]
    partners = [
        {"dp": place + bit * (1 - 2 * side)} for bit, side in zip((1, 2, 4, 8), sides)
    ]
    across_mp = {"mp": 1 - lax.axis_index("mp")}

    barrier = pltpu.get_barrier_semaphore()
    for device in (*partners, across_mp):
        pl.semaphore_signal(barrier, inc=1, device_id=device, device_id_type=pl.DeviceIdType.MESH)
    pl.semaphore_wait(barrier, 5)

    def block_copies(block, slot):
        rows = pl.ds(pl.multiple_of(block * block_rows, STRIP), block_rows)
        return (
            pltpu.make_async_copy(
                grad_score_ref.at[:, rows, :], grad_buf.at[slot], block_sem.at[slot, 0]
            ),
            pltpu.make_async_copy(plane_ref.at[rows, :], plane_buf.at[slot], block_sem.at[slot, 1]),
            pltpu.make_async_copy(down_ref.at[rows, :], down_buf.at[slot], block_sem.at[slot, 2]),
        )

    half = CHUNK // 2
    loads = [
        [
            (project_ref.at[0:CHUNK, :], own_buf.at[0, :, 0:half]),
            (project_ref.at[1152 : 1152 + CHUNK, :], own_buf.at[0, :, half:CHUNK]),
        ],
        [
            (project_ref.at[CHUNK:1152, :], own_buf.at[1, 0:half, 0:half]),
            (project_ref.at[1152 + CHUNK : 2304, :], own_buf.at[1, 0:half, half:CHUNK]),
            (output_ref, own_buf.at[1, half:CHUNK, :]),
        ],
    ]
    for ref, away_ref, wide in (
        (expand_ref, expand_away_ref, True),
        (reduce_ref, reduce_away_ref, False),
    ):
        for k in range(2):
            piece = slice(k * CHUNK, (k + 1) * CHUNK)
            index = (slice(None), piece) if wide else (piece, slice(None))
            chunk = len(loads)
            loads.append(
                [
                    (ref.at[index], own_buf.at[chunk]),
                    (away_ref.at[index], away_buf.at[chunk - CHUNKS + AWAY]),
                ]
            )
    copies = [
        [pltpu.make_async_copy(src, dst, load_sem.at[k, n]) for n, (src, dst) in enumerate(group)]
        for k, group in enumerate(loads)
    ]

    keeps, leaves = [], []
    base = 0
    for size, side in zip(PARTS, sides):
        keeps.append(base + side * size)
        leaves.append(base + (1 - side) * size)
        base = base + side * size

    def rows_at(start, size):
        return pl.ds(pl.multiple_of(start, STRIP), size)

    def remote(src, dst, chunk, stage, device):
        return pltpu.make_async_remote_copy(
            src_ref=src,
            dst_ref=dst,
            send_sem=send_sem.at[chunk, stage],
            recv_sem=recv_sem.at[chunk, stage],
            device_id=device,
            device_id_type=pl.DeviceIdType.MESH,
        )

    def is_away(chunk):
        return chunk >= CHUNKS - AWAY

    def away_at(chunk):
        return chunk - CHUNKS + AWAY

    arrivals = (core_buf, x_buf, near_buf, far_buf)

    def scatter(chunk, level):
        return remote(
            own_buf.at[chunk, rows_at(leaves[level], PARTS[level]), :],
            arrivals[level].at[chunk],
            chunk,
            level,
            partners[level],
        )

    def scatter_away(chunk):
        return remote(
            away_buf.at[away_at(chunk), rows_at(leaves[0], PARTS[0]), :],
            core_away_buf.at[away_at(chunk)],
            chunk,
            4,
            partners[0],
        )

    def hand_over(chunk):
        return remote(
            away_buf.at[away_at(chunk), rows_at(keeps[0], PARTS[0]), :],
            y_buf.at[away_at(chunk)],
            chunk,
            5,
            across_mp,
        )

    def total_rows(chunk, start, size):
        return total_ref.at[rows_at(chunk * CHUNK + start, size), :]

    def gather(chunk, level):
        if level == 3:
            src = own_buf.at[chunk, rows_at(keeps[3], PARTS[3]), :]
        else:
            src = total_rows(chunk, keeps[level], PARTS[level])
        return remote(
            src, total_rows(chunk, keeps[level], PARTS[level]), chunk, 6 + level, partners[level]
        )

    def gathered(chunk, level):
        place_of = total_rows(chunk, leaves[level], PARTS[level])
        return remote(place_of, place_of, chunk, 6 + level, partners[level])

    def store_own(chunk):
        return pltpu.make_async_copy(
            own_buf.at[chunk, rows_at(keeps[3], PARTS[3]), :],
            total_rows(chunk, keeps[3], PARTS[3]),
            local_sem.at[chunk],
        )

    def add(buf, chunk, start, size, arrived):
        piece = PARTS[3]

        def step(n, carry):
            here = rows_at(start + n * piece, piece)
            there = rows_at(n * piece, piece)
            buf[chunk, here, :] = buf[chunk, here, :] + arrived[there, :]
            return carry

        lax.fori_loop(0, size // piece, step, 0)

    def run(event, chunk):
        if event == 0:
            for copy in copies[chunk]:
                copy.wait()
            scatter(chunk, 0).start()
            if is_away(chunk):
                scatter_away(chunk).start()
        elif event == 1:
            if is_away(chunk):
                scatter_away(chunk).wait_recv()
                add(away_buf, away_at(chunk), keeps[0], PARTS[0], core_away_buf.at[away_at(chunk)])
                hand_over(chunk).start()
            scatter(chunk, 0).wait_recv()
            add(own_buf, chunk, keeps[0], PARTS[0], core_buf.at[chunk])
            if not is_away(chunk):
                scatter(chunk, 1).start()
        elif event == 2:
            hand_over(chunk).wait_recv()
            add(own_buf, chunk, keeps[0], PARTS[0], y_buf.at[away_at(chunk)])
            scatter(chunk, 1).start()
        elif event in (3, 4, 5):
            level = event - 2
            scatter(chunk, level).wait_recv()
            add(own_buf, chunk, keeps[level], PARTS[level], arrivals[level].at[chunk])
            if level < 3:
                scatter(chunk, level + 1).start()
            else:
                store_own(chunk).start()
                gather(chunk, 3).start()
        else:
            level = 9 - event
            if level == 3:
                store_own(chunk).wait()
            gathered(chunk, level).wait_recv()
            if level > 0:
                gather(chunk, level - 1).start()

    for group in copies[:2]:
        for copy in group:
            copy.start()
    for copy in block_copies(0, 0):
        copy.start()
    for group in copies[2:]:
        for copy in group:
            copy.start()
    sum_ref[...] = jnp.zeros_like(sum_ref)
    slots = exchange_schedule(strips)

    def dispatch(s, low, high):
        if not any(slots[low:high]):
            return
        if high - low == 1:
            for event, chunk in slots[low]:
                run(event, chunk)
            return
        middle = (low + high) // 2
        if any(slots[low:middle]):
            pl.when(s < middle)(lambda: dispatch(s, low, middle))
        if any(slots[middle:high]):
            pl.when(s >= middle)(lambda: dispatch(s, middle, high))

    def strip(s, carry):
        block = s // per_block
        slot = block % 2

        @pl.when(s % per_block == 0)
        def _():
            for copy in block_copies(block, slot):
                copy.wait()

            @pl.when(block + 1 < blocks)
            def _():
                for copy in block_copies(block + 1, 1 - slot):
                    copy.start()

        dispatch(s, 0, strips)
        at = rows_at((s % per_block) * STRIP, STRIP)
        table_strip(
            lambda h, cols: grad_buf[slot, h, at, cols],
            lambda cols: plane_buf[slot, at, cols],
            lambda cols: down_buf[slot, at, cols],
            high_ref,
            low_ref,
            sum_ref,
            heads,
            keys,
            high_counts,
        )
        return carry

    lax.fori_loop(0, strips, strip, 0)
    for event, chunk in slots[strips]:
        run(event, chunk)
    table_finish(sum_ref, table_ref)
    for chunk in range(CHUNKS):
        for level in range(4):
            scatter(chunk, level).wait_send()
            gather(chunk, level).wait_send()
        if is_away(chunk):
            scatter_away(chunk).wait_send()
            hand_over(chunk).wait_send()


def table_exchange(grad_scores, plane, down, counts, project, output, expand, reduce):
    heads, row_count, keys = grad_scores.shape
    high_counts = (counts[0] // 16, counts[1] // 16, counts[1] // 16)
    high_rows = sum(high_counts) * heads
    anywhere = pl.BlockSpec(memory_space=pl.ANY)
    out, total = pl.pallas_call(
        partial(table_exchange_kernel, high_counts=high_counts),
        in_specs=[anywhere] * 9,
        out_specs=[pl.BlockSpec(memory_space=pltpu.VMEM), anywhere],
        out_shape=[
            jax.ShapeDtypeStruct((high_rows, 16 * STRIP), f32),
            jax.ShapeDtypeStruct((CHUNKS * CHUNK, CHUNK), bf16),
        ],
        scratch_shapes=[
            *table_scratch(high_rows, keys),
            pltpu.VMEM((2, heads, BLOCK_ROWS, keys), bf16),
            pltpu.VMEM((2, BLOCK_ROWS, keys), jnp.int16),
            pltpu.VMEM((2, BLOCK_ROWS, keys), jnp.int16),
            pltpu.VMEM((CHUNKS, CHUNK, CHUNK), bf16),
            pltpu.VMEM((AWAY, CHUNK, CHUNK), bf16),
            pltpu.VMEM((CHUNKS, PARTS[0], CHUNK), bf16),
            pltpu.VMEM((AWAY, PARTS[0], CHUNK), bf16),
            pltpu.VMEM((AWAY, PARTS[0], CHUNK), bf16),
            pltpu.VMEM((CHUNKS, PARTS[1], CHUNK), bf16),
            pltpu.VMEM((CHUNKS, PARTS[2], CHUNK), bf16),
            pltpu.VMEM((CHUNKS, PARTS[3], CHUNK), bf16),
            pltpu.SemaphoreType.DMA((2, 3)),
            pltpu.SemaphoreType.DMA((CHUNKS, 3)),
            pltpu.SemaphoreType.DMA((CHUNKS,)),
            pltpu.SemaphoreType.DMA((CHUNKS, 10)),
            pltpu.SemaphoreType.DMA((CHUNKS, 10)),
        ],
        compiler_params=pltpu.CompilerParams(
            vmem_limit_bytes=vmem_limit, collective_id=0, has_side_effects=True
        ),
        name="table_exchange",
    )(grad_scores, plane, down, project, output, *expand, *reduce)
    half = CHUNK // 2
    project_total = jnp.concatenate([total[:1152, :half], total[:1152, half:]])
    output_total = total[1152 : 2 * CHUNK]
    expand_total = jnp.concatenate(
        [total[2 * CHUNK : 3 * CHUNK], total[3 * CHUNK : 4 * CHUNK]], axis=1
    )
    reduce_total = total[4 * CHUNK :]
    return table_result(out, high_counts, heads), project_total, output_total, expand_total, reduce_total


def swap(array):
    return lax.ppermute(array, "mp", [(0, 1), (1, 0)])


def partner(array, count, bit):
    return lax.ppermute(array, "dp", [(i, i ^ bit) for i in range(count)])


def other_share(array, count):
    core = lax.axis_index("dp") % 2
    half = array.shape[0] // 2
    fetched = swap(lax.dynamic_slice_in_dim(array, core * half, half, 0))
    handed = partner(fetched, count, 1)
    even = core == 0
    return jnp.concatenate(
        [jnp.where(even, fetched, handed), jnp.where(even, handed, fetched)], axis=0
    )


def sum_rows_over_dp(array, count):
    place = lax.axis_index("dp")
    bits = []
    bit = 1
    while bit < count:
        mine = (place // bit) % 2
        halves = array.reshape((2, array.shape[0] // 2) + array.shape[1:])
        sent = lax.dynamic_index_in_dim(halves, 1 - mine, 0, keepdims=False)
        kept = lax.dynamic_index_in_dim(halves, mine, 0, keepdims=False)
        array = kept + partner(sent, count, bit)
        bits.append(bit)
        bit *= 2
    for bit in reversed(bits):
        lead = (place // bit) % 2 == 0
        other = partner(array, count, bit)
        array = jnp.concatenate(
            [jnp.where(lead, array, other), jnp.where(lead, other, array)], axis=0
        )
    return array


def sum_small(arrays, count, over_mp):
    sizes = [a.size for a in arrays]
    total = sum(sizes)
    flat = jnp.concatenate([a.reshape(-1) for a in arrays])
    flat = jnp.pad(flat, (0, round_up(total, 1024) - total)).reshape(-1, LANES)
    if over_mp:
        flat = flat + swap(flat)
    bit = 1
    while bit < count:
        flat = flat + partner(flat, count, bit)
        bit *= 2
    flat = flat.reshape(-1)
    outs = []
    start = 0
    for array, size in zip(arrays, sizes):
        outs.append(flat[start : start + size].reshape(array.shape))
        start += size
    return outs


def norm_parts(values, gain_vector, shift_vector):
    average = jnp.mean(values, axis=-1, keepdims=True)
    centered = values - average
    variance = jnp.mean(centered * centered, axis=-1, keepdims=True)
    inverse = lax.rsqrt(variance + norm_epsilon)
    normal_hat = centered * inverse
    return (normal_hat * gain_vector + shift_vector, normal_hat, inverse)


def norm_back(grad_hat, normal_hat, inverse):
    first_mean = jnp.mean(grad_hat, axis=-1, keepdims=True)
    cross_mean = jnp.mean(grad_hat * normal_hat, axis=-1, keepdims=True)
    return inverse * (grad_hat - first_mean - normal_hat * cross_mean)


def per_device(
    dp_count,
    tokens,
    cotangent,
    long_flag,
    token_mask,
    bucket_line,
    bucket_across,
    bucket_down,
    project_weight,
    project_bias,
    table_line,
    table_across,
    table_down,
    output_weight,
    output_bias,
    first_gain,
    first_shift,
    expand_weight,
    expand_bias,
    reduce_weight,
    reduce_bias,
    second_gain,
    second_shift,
):
    length = tokens.shape[1]
    width = project_weight.shape[2]
    heads = table_line.shape[1]
    counts = (table_line.shape[0], table_across.shape[0])
    rows = round_up(length, BLOCK_ROWS)
    half_rows = rows // 2
    keys = round_up(length, 3 * LANES)
    mp_index = lax.axis_index("mp")
    lead = mp_index == 0

    def own_rows(array):
        return lax.dynamic_slice_in_dim(array, mp_index * half_rows, half_rows, 0)

    def other_rows(array):
        return lax.dynamic_slice_in_dim(array, (1 - mp_index) * half_rows, half_rows, 0)

    def in_order(mine, other):
        return jnp.where(lead, mine, other), jnp.where(lead, other, mine)

    output_other = other_share(output_weight, dp_count)
    expand_other = other_share(expand_weight, dp_count)
    reduce_other = other_share(reduce_weight, dp_count)
    expand_bias_other = swap(expand_bias)

    positions = jnp.arange(length, dtype=jnp.int32)
    limit = jnp.where(long_flag[0] > 0, LONG, SHORT).astype(jnp.int32)
    valid = (token_mask[0] > 0) & (positions < limit)
    valid_rows = own_rows(jnp.pad(valid.astype(f32), (0, rows - length)))[:, None]
    grow = ((0, rows - length), (0, keys - length))
    line = jnp.where(valid[None, :], bucket_line[0], bucket_line[0] + counts[0])
    plane = jnp.pad(
        (line | (bucket_across[0] << 8)).astype(jnp.int16), grow, constant_values=counts[0]
    )
    down = jnp.pad(bucket_down[0].astype(jnp.int16), grow)
    tables = []
    for table in (table_line, table_across, table_down):
        lanes = jnp.pad(
            table.T, ((0, 0), (0, LANES - table.shape[0])), constant_values=large_negative
        )
        tables.append(jnp.broadcast_to(lanes[:, None, :], (heads, STRIP, LANES)))
    tables = jnp.concatenate(tables).astype(bf16)

    query, key_wide, key_turned, value_ones, value_turned = project(
        tokens[0], project_weight, project_bias.astype(f32), keys
    )
    exps, context, inverse = attend(query, key_turned, value_ones, plane, down, tables)

    context_other = swap(other_rows(context))
    attended = (
        dot_f32(own_rows(context), output_weight)
        + dot_f32(context_other, output_other)
        + output_bias.astype(f32)
    )
    padded = jnp.pad(tokens[0], ((0, rows - length), (0, 0)))
    first_norm, first_hat, first_inverse = norm_parts(
        own_rows(padded).astype(f32) + attended, first_gain, first_shift
    )
    expand_input = first_norm.astype(bf16)
    reduced = reduce_bias.astype(f32)
    kept = []
    for weight, bias, back in (
        (expand_weight, expand_bias, reduce_weight),
        (expand_other, expand_bias_other, reduce_other),
    ):
        before = dot_f32(expand_input, weight) + bias.astype(f32)
        activated, gelu_back = jax.vjp(partial(jax.nn.gelu, approximate=False), before)
        activated_low = activated.astype(bf16)
        reduced = reduced + dot_f32(activated_low, back)
        kept.append((weight, back, activated_low, gelu_back))
    second_norm, second_hat, second_inverse = norm_parts(
        first_norm + reduced, second_gain, second_shift
    )
    layer_mine = (second_norm * valid_rows).astype(bf16)
    layer_out = jnp.concatenate(in_order(layer_mine, swap(layer_mine)))[None, :length]
    grad_out = own_rows(jnp.pad(cotangent[0], ((0, rows - length), (0, 0)))).astype(f32)
    grad_out = grad_out * valid_rows
    second_gain_grad = jnp.sum(grad_out * second_hat, axis=0)
    second_shift_grad = jnp.sum(grad_out, axis=0)
    grad_mixed = norm_back(grad_out * second_gain, second_hat, second_inverse)
    grad_reduced = grad_mixed.astype(bf16)
    reduce_bias_grad = jnp.sum(grad_reduced, axis=0, dtype=f32)
    grad_first = grad_mixed
    reduce_grads, expand_grads, expand_bias_grads = [], [], []
    for weight, back, activated_low, gelu_back in kept:
        grad_active = jnp.einsum("ld,fd->lf", grad_reduced, back, preferred_element_type=f32)
        grad_before = gelu_back(grad_active)[0].astype(bf16)
        expand_bias_grads.append(jnp.sum(grad_before, axis=0, dtype=f32))
        grad_first = grad_first + jnp.einsum(
            "lf,df->ld", grad_before, weight, preferred_element_type=f32
        )
        reduce_grads.append(
            jnp.einsum("lf,ld->fd", activated_low, grad_reduced, preferred_element_type=f32)
        )
        expand_grads.append(
            jnp.einsum("ld,lf->df", expand_input, grad_before, preferred_element_type=f32)
        )
    first_gain_grad = jnp.sum(grad_first * first_hat, axis=0)
    first_shift_grad = jnp.sum(grad_first, axis=0)
    grad_inner = norm_back(grad_first * first_gain, first_hat, first_inverse)
    grad_mine = grad_inner.astype(bf16)
    grad_attended = jnp.concatenate(in_order(grad_mine, swap(grad_mine)))
    output_bias_grad = jnp.sum(grad_mine, axis=0, dtype=f32)
    output_weight_grad = jnp.einsum(
        "le,lf->ef", context, grad_attended, preferred_element_type=f32
    ).astype(bf16)
    grad_context = jnp.einsum(
        "lf,ef->le", grad_attended, output_weight, preferred_element_type=f32
    )
    grad_scaled = (grad_context * inverse).astype(bf16)

    grad_scores, grad_query, grad_key, grad_value = attend_back(
        exps, grad_scaled, context, query, value_turned, key_wide
    )
    grad_key = grad_key.reshape(width, keys).astype(bf16)
    grad_value = grad_value.reshape(width, keys).astype(bf16)
    cut_key, cut_value = grad_key[:, :rows], grad_value[:, :rows]
    project_weight_grad = jnp.concatenate(
        [
            jnp.einsum("ld,le->de", padded, grad_query, preferred_element_type=f32),
            jnp.einsum("ld,el->de", padded, cut_key, preferred_element_type=f32),
            jnp.einsum("ld,el->de", padded, cut_value, preferred_element_type=f32),
        ]
    ).astype(bf16)
    project_bias_grad = jnp.stack(
        [jnp.sum(grad_query, axis=0, dtype=f32), jnp.sum(cut_value, axis=1, dtype=f32)]
    )
    input_part = (
        jnp.einsum("le,de->ld", grad_query, project_weight[0], preferred_element_type=f32)
        + jnp.einsum("el,de->ld", cut_key, project_weight[1], preferred_element_type=f32)
        + jnp.einsum("el,de->ld", cut_value, project_weight[2], preferred_element_type=f32)
    )
    input_part = lax.dynamic_update_slice_in_dim(
        input_part, own_rows(input_part) + grad_inner, mp_index * half_rows, 0
    )
    sent = jnp.where(lead, input_part[:, width:], input_part[:, :width]).astype(bf16)
    own = jnp.where(lead, input_part[:, :width], input_part[:, width:])
    input_grad = (own + swap(sent).astype(f32))[None, :length]

    reduce_own, reduce_sent = (g.astype(bf16) for g in reduce_grads)
    expand_own, expand_sent = (g.astype(bf16) for g in expand_grads)
    if dp_count == 16 and expand_own.shape == (CHUNK, 2 * CHUNK):
        (
            table_grads,
            project_weight_grad,
            output_weight_grad,
            expand_weight_grad,
            reduce_weight_grad,
        ) = table_exchange(
            grad_scores,
            plane,
            down,
            counts,
            project_weight_grad,
            output_weight_grad,
            (expand_own, expand_sent),
            (reduce_own, reduce_sent),
        )
    else:
        table_grads = table_sums(grad_scores, plane, down, counts)
        reduce_weight_grad = sum_rows_over_dp(reduce_own + swap(reduce_sent), dp_count)
        expand_weight_grad = sum_rows_over_dp(expand_own + swap(expand_sent), dp_count)
        output_weight_grad = sum_rows_over_dp(output_weight_grad, dp_count)
        project_weight_grad = sum_rows_over_dp(project_weight_grad, dp_count)
    project_weight_grad = project_weight_grad.reshape(project_weight.shape)

    (
        second_gain_grad,
        second_shift_grad,
        reduce_bias_grad,
        expand_bias_grad,
        expand_bias_sent,
        first_gain_grad,
        first_shift_grad,
        output_bias_grad,
    ) = sum_small(
        [
            second_gain_grad,
            second_shift_grad,
            reduce_bias_grad,
            *in_order(*expand_bias_grads),
            first_gain_grad,
            first_shift_grad,
            output_bias_grad,
        ],
        dp_count,
        True,
    )
    expand_bias_grad = jnp.where(lead, expand_bias_grad, expand_bias_sent)
    table_grads, project_bias_grad = sum_small([table_grads, project_bias_grad], dp_count, False)
    mine = mp_index * width
    return (
        layer_out,
        input_grad,
        project_weight_grad.astype(f32),
        project_bias_grad,
        table_grads[: counts[0]],
        table_grads[counts[0] : counts[0] + counts[1]],
        table_grads[counts[0] + counts[1] :],
        output_weight_grad.astype(f32),
        output_bias_grad,
        lax.dynamic_slice_in_dim(first_gain_grad, mine, width, 0),
        lax.dynamic_slice_in_dim(first_shift_grad, mine, width, 0),
        expand_weight_grad.astype(f32),
        expand_bias_grad,
        reduce_weight_grad.astype(f32),
        reduce_bias_grad,
        second_gain_grad,
        second_shift_grad,
    )


def solution(mesh):
    placed = (
        P("dp", None, None),
        P("dp", None, None),
        P("dp"),
        P("dp", None),
        P("dp", None, None),
        P("dp", None, None),
        P("dp", None, None),
        P(None, None, "mp"),
        P(None, "mp"),
        P(None, "mp"),
        P(None, "mp"),
        P(None, "mp"),
        P("mp", None),
        P(),
        P(),
        P(),
        P(None, "mp"),
        P("mp"),
        P("mp", None),
        P(),
        P(),
        P(),
    )
    return jax.shard_map(
        partial(per_device, mesh.shape["dp"]),
        mesh=mesh,
        in_specs=placed,
        out_specs=(
            P("dp", None, None),
            P("dp", None, "mp"),
            P(None, None, "mp"),
            P(None, "mp"),
            P(None, "mp"),
            P(None, "mp"),
            P(None, "mp"),
            P("mp", None),
            P(),
            P("mp"),
            P("mp"),
            P(None, "mp"),
            P("mp"),
            P("mp", None),
            P(),
            P(),
            P(),
        ),
        check_vma=False,
    )
```

```python
from functools import partial

import jax
import jax.numpy as jnp
from jax import lax
from jax.experimental import pallas as pl
from jax.experimental.pallas import tpu as pltpu
from jax.sharding import PartitionSpec as P

LONG = 1089
SHORT = 709
HEAD = 64
LANES = 128
STRIP = 16
BLOCK_ROWS = 224
FEED_PIECE = 768
FEED_STRIP = 112
TABLE_STRIPS = 2
ATTEND_STRIPS = 7

large_negative = -1000000000.0
norm_epsilon = 1e-05
vmem_limit = 56 * 2**20
bf16 = jnp.bfloat16
f32 = jnp.float32


def round_up(value, step):
    return (value + step - 1) // step * step


def whole_spec(array):
    zeros = (0,) * array.ndim
    return pl.BlockSpec(array.shape, lambda i: zeros)


def dot_f32(left, right):
    return jnp.dot(left, right, preferred_element_type=f32)


def gather_lanes(values, index):
    dims = lax.GatherDimensionNumbers(
        offset_dims=(),
        collapsed_slice_dims=(1,),
        start_index_map=(1,),
        operand_batching_dims=(0,),
        start_indices_batching_dims=(0,),
    )
    return lax.gather(
        values,
        index[..., None],
        dims,
        slice_sizes=(1, 1),
        mode=lax.GatherScatterMode.PROMISE_IN_BOUNDS,
    )


def project_kernel(
    token_ref, weight_ref, bias_ref, query_ref, key_ref, key_turned_ref, value_ref, value_turned_ref, *, length
):
    rows = token_ref.shape[0]
    place = pl.program_id(0) * rows + lax.broadcasted_iota(jnp.int32, token_ref.shape, 0)
    token = jnp.where(place < length, token_ref[...].astype(f32), 0.0).astype(bf16)
    query = (dot_f32(token, weight_ref[0]) + bias_ref[0:1, :]).astype(bf16)
    query_ref[...] = (query.astype(f32) * 0.125).astype(bf16)
    key = dot_f32(token, weight_ref[1])
    value = dot_f32(token, weight_ref[2]) + bias_ref[1:2, :]
    lane_first = lax.broadcasted_iota(jnp.int32, (rows, LANES), 1) < HEAD
    row_first = lax.broadcasted_iota(jnp.int32, (LANES, rows), 0) < HEAD
    for p in range(key.shape[1] // LANES):
        cols = slice(p * LANES, (p + 1) * LANES)
        key_pair, value_pair = key[:, cols], value[:, cols]
        key_turned, value_turned = key_pair.T, value_pair.T
        for u in range(2):
            h = 2 * p + u
            lane_own = lane_first if u == 0 else ~lane_first
            row_own = row_first if u == 0 else ~row_first
            key_ref[h] = jnp.where(lane_own, key_pair, 0.0).astype(bf16)
            value_ref[h] = jnp.where(lane_own, value_pair, 1.0).astype(bf16)
            key_turned_ref[h] = jnp.where(row_own, key_turned, 0.0).astype(bf16)
            value_turned_ref[h] = jnp.where(row_own, value_turned, 0.0).astype(bf16)


def project(tokens, weight, bias, keys):
    length, depth = tokens.shape
    width = weight.shape[2]
    heads = width // HEAD
    block = 3 * LANES
    wide = pl.BlockSpec((heads, block, LANES), lambda i: (0, i, 0))
    turned = pl.BlockSpec((heads, LANES, block), lambda i: (0, 0, i))
    wide_shape = jax.ShapeDtypeStruct((heads, keys, LANES), bf16)
    turned_shape = jax.ShapeDtypeStruct((heads, LANES, keys), bf16)
    return pl.pallas_call(
        partial(project_kernel, length=length),
        grid=(keys // block,),
        in_specs=[
            pl.BlockSpec((block, depth), lambda i: (i, 0)),
            whole_spec(weight),
            whole_spec(bias),
        ],
        out_specs=[pl.BlockSpec((block, width), lambda i: (i, 0)), wide, turned, wide, turned],
        out_shape=[
            jax.ShapeDtypeStruct((keys, width), bf16),
            wide_shape,
            turned_shape,
            wide_shape,
            turned_shape,
        ],
        compiler_params=pltpu.CompilerParams(vmem_limit_bytes=vmem_limit),
        name="project",
    )(tokens, weight, bias)


def attend_kernel(
    query_ref,
    key_ref,
    value_ref,
    plane_ref,
    down_ref,
    table_ref,
    exp_ref,
    context_ref,
    inverse_ref,
    score_ref,
):
    heads, rows, keys = exp_ref.shape
    for h in range(heads):
        pair = slice(h // 2 * LANES, (h // 2 + 1) * LANES)
        score_ref[h] = dot_f32(query_ref[:, pair], key_ref[h])

    lanes = [slice(c * LANES, (c + 1) * LANES) for c in range(keys // LANES)]

    def scores_of(at):
        scores = [[] for _ in range(heads)]
        for cols in lanes:
            packed = plane_ref[at, cols]
            bias = [None] * heads
            for t, index in enumerate(
                (packed & jnp.int16(255), packed >> jnp.int16(8), down_ref[at, cols])
            ):
                for h in range(heads):
                    found = gather_lanes(table_ref[t * heads + h], index).astype(f32)
                    bias[h] = found if t == 0 else bias[h] + found
            for h in range(heads):
                scores[h].append(score_ref[h, at, cols] + bias[h])
        return scores

    def exps_of(scores):
        exps = []
        for parts in scores:
            top = parts[0]
            for part in parts[1:]:
                top = jnp.maximum(top, part)
            top = jnp.max(top, axis=1, keepdims=True)
            exps.append([jnp.exp(part - top).astype(bf16) for part in parts])
        return exps

    def strips(n, carry):
        start = pl.multiple_of(n * ATTEND_STRIPS * STRIP, STRIP)
        places = [pl.ds(start + k * STRIP, STRIP) for k in range(ATTEND_STRIPS)]
        scores = [scores_of(at) for at in places]
        exps = [exps_of(part) for part in scores]
        for at, part in zip(places, exps):
            for h in range(heads):
                for c, cols in enumerate(lanes):
                    exp_ref[h, at, cols] = part[h][c]
        return carry

    lax.fori_loop(0, rows // (ATTEND_STRIPS * STRIP), strips, 0)
    first = lax.broadcasted_iota(jnp.int32, (rows, LANES), 1) < HEAD
    for p in range(heads // 2):
        cols = slice(p * LANES, (p + 1) * LANES)
        even = dot_f32(exp_ref[2 * p], value_ref[2 * p])
        odd = dot_f32(exp_ref[2 * p + 1], value_ref[2 * p + 1])
        sums = jnp.where(first, pltpu.roll(even, HEAD, 1), pltpu.roll(odd, HEAD, 1))
        inverse = 1.0 / sums
        inverse_ref[:, cols] = inverse
        context_ref[:, cols] = (jnp.where(first, even, odd) * inverse).astype(bf16)


def attend(query, key_turned, value_ones, plane, down, tables):
    heads, _, keys = key_turned.shape
    row_count = plane.shape[0]
    width = heads * HEAD
    index_spec = pl.BlockSpec((BLOCK_ROWS, keys), lambda i: (i, 0))
    row_spec = pl.BlockSpec((BLOCK_ROWS, width), lambda i: (i, 0))
    return pl.pallas_call(
        attend_kernel,
        grid=(row_count // BLOCK_ROWS,),
        in_specs=[
            row_spec,
            whole_spec(key_turned),
            whole_spec(value_ones),
            index_spec,
            index_spec,
            whole_spec(tables),
        ],
        out_specs=[
            pl.BlockSpec((heads, BLOCK_ROWS, keys), lambda i: (0, i, 0)),
            row_spec,
            row_spec,
        ],
        out_shape=[
            jax.ShapeDtypeStruct((heads, row_count, keys), bf16),
            jax.ShapeDtypeStruct((row_count, width), bf16),
            jax.ShapeDtypeStruct((row_count, width), f32),
        ],
        scratch_shapes=[pltpu.VMEM((heads, BLOCK_ROWS, keys), f32)],
        compiler_params=pltpu.CompilerParams(vmem_limit_bytes=vmem_limit),
        name="attend",
    )(query, key_turned, value_ones, plane, down, tables)


def attend_back_kernel(
    exp_ref,
    grad_ref,
    context_ref,
    query_ref,
    value_ref,
    key_ref,
    grad_score_ref,
    grad_query_ref,
    grad_key_ref,
    grad_value_ref,
):
    heads, rows, _ = exp_ref.shape

    @pl.when(pl.program_id(0) == 0)
    def _():
        grad_key_ref[...] = jnp.zeros_like(grad_key_ref)
        grad_value_ref[...] = jnp.zeros_like(grad_value_ref)

    first = lax.broadcasted_iota(jnp.int32, (rows, LANES), 1) < HEAD
    for p in range(heads // 2):
        cols = slice(p * LANES, (p + 1) * LANES)
        grad = grad_ref[:, cols]
        product = grad.astype(f32) * context_ref[:, cols].astype(f32)
        query_turned = query_ref[:, cols].T
        grad_turned = grad.T
        grad_query = None
        for u in range(2):
            h = 2 * p + u
            half = slice(u * HEAD, (u + 1) * HEAD)
            own = first if u == 0 else ~first
            total = jnp.sum(jnp.where(own, product, 0.0), axis=1, keepdims=True)
            grad_exp = dot_f32(grad, value_ref[h])
            grad_score = (exp_ref[h].astype(f32) * (grad_exp - total)).astype(bf16)
            grad_score_ref[h] = grad_score
            part = dot_f32(grad_score, key_ref[h])
            grad_query = part if u == 0 else grad_query + part
            grad_key_ref[h] += dot_f32(query_turned[half], grad_score)
            grad_value_ref[h] += dot_f32(grad_turned[half], exp_ref[h])
        grad_query_ref[:, cols] = (grad_query * 0.125).astype(bf16)


def attend_back(exps, grad, context, query, value_turned, key_wide):
    heads, row_count, keys = exps.shape
    width = heads * HEAD
    row_spec = pl.BlockSpec((BLOCK_ROWS, width), lambda i: (i, 0))
    exp_spec = pl.BlockSpec((heads, BLOCK_ROWS, keys), lambda i: (0, i, 0))
    sum_spec = pl.BlockSpec((heads, HEAD, keys), lambda i: (0, 0, 0))
    return pl.pallas_call(
        attend_back_kernel,
        grid=(row_count // BLOCK_ROWS,),
        in_specs=[
            exp_spec,
            row_spec,
            row_spec,
            row_spec,
            whole_spec(value_turned),
            whole_spec(key_wide),
        ],
        out_specs=[exp_spec, row_spec, sum_spec, sum_spec],
        out_shape=[
            jax.ShapeDtypeStruct((heads, row_count, keys), bf16),
            jax.ShapeDtypeStruct((row_count, width), bf16),
            jax.ShapeDtypeStruct((heads, HEAD, keys), f32),
            jax.ShapeDtypeStruct((heads, HEAD, keys), f32),
        ],
        compiler_params=pltpu.CompilerParams(vmem_limit_bytes=vmem_limit),
        name="attend_back",
    )(exps, grad, context, query, value_turned, key_wide)


def table_strips(strips, sum_ref, heads, keys, high_counts):
    base = 0
    for t in range(3):
        shift = 8 if t == 1 else 0
        highs, lows = [], []
        for grad_of, plane_of, down_of in strips:
            for c in range(keys // LANES):
                cols = slice(c * LANES, (c + 1) * LANES)
                index = down_of(cols) if t == 2 else plane_of(cols)
                low = index & jnp.int16(15 << shift)
                high = index & jnp.int16(48 << shift)
                lows.append(
                    jnp.concatenate(
                        [
                            jnp.where(low == jnp.int16(x << shift), bf16(1), bf16(0))
                            for x in range(16)
                        ]
                    )
                )
                parts = []
                for x in range(high_counts[t]):
                    mask = high == jnp.int16(x << (4 + shift))
                    parts += [jnp.where(mask, grad_of(h, cols), bf16(0)) for h in range(heads)]
                highs.append(jnp.concatenate(parts))
        span = slice(base, base + high_counts[t] * heads * STRIP)
        sum_ref[span, :] += lax.dot_general(
            jnp.concatenate(highs, axis=1),
            jnp.concatenate(lows, axis=1),
            (((1,), (1,)), ((), ())),
            preferred_element_type=f32,
        )
        base = span.stop


def table_finish(sum_ref, out_ref):
    row_of_lane = lax.broadcasted_iota(jnp.int32, (STRIP, 16 * STRIP), 1) % STRIP
    same = row_of_lane == lax.broadcasted_iota(jnp.int32, (STRIP, 16 * STRIP), 0)
    for o in range(out_ref.shape[0]):
        block = sum_ref[o * STRIP : (o + 1) * STRIP, :]
        out_ref[o : o + 1, :] = jnp.sum(jnp.where(same, block, 0.0), axis=0, keepdims=True)


def table_result(out, high_counts, heads):
    summed = jnp.sum(out.reshape(sum(high_counts), heads, 16, STRIP), axis=-1)
    return summed.transpose(0, 2, 1).reshape(-1, heads)


def table_kernel(grad_score_ref, plane_ref, down_ref, out_ref, sum_ref, *, high_counts):
    heads, rows, keys = grad_score_ref.shape
    step = pl.program_id(0)

    @pl.when(step == 0)
    def _():
        sum_ref[...] = jnp.zeros_like(sum_ref)

    def refs_at(start):
        at = pl.ds(pl.multiple_of(start, STRIP), STRIP)
        return (
            lambda h, cols: grad_score_ref[h, at, cols],
            lambda cols: plane_ref[at, cols],
            lambda cols: down_ref[at, cols],
        )

    def strips(r, carry):
        start = r * (TABLE_STRIPS * STRIP)
        table_strips(
            [refs_at(start + k * STRIP) for k in range(TABLE_STRIPS)],
            sum_ref,
            heads,
            keys,
            high_counts,
        )
        return carry

    lax.fori_loop(0, rows // (TABLE_STRIPS * STRIP), strips, 0)

    @pl.when(step == pl.num_programs(0) - 1)
    def _():
        table_finish(sum_ref, out_ref)


def table_sums(grad_scores, plane, down, counts):
    heads, row_count, keys = grad_scores.shape
    high_counts = (counts[0] // 16, counts[1] // 16, counts[1] // 16)
    high_rows = sum(high_counts) * heads
    index_spec = pl.BlockSpec((BLOCK_ROWS, keys), lambda i: (i, 0))
    out = pl.pallas_call(
        partial(table_kernel, high_counts=high_counts),
        grid=(row_count // BLOCK_ROWS,),
        in_specs=[
            pl.BlockSpec((heads, BLOCK_ROWS, keys), lambda i: (0, i, 0)),
            index_spec,
            index_spec,
        ],
        out_specs=pl.BlockSpec((high_rows, 16 * STRIP), lambda i: (0, 0)),
        out_shape=jax.ShapeDtypeStruct((high_rows, 16 * STRIP), f32),
        scratch_shapes=[pltpu.VMEM((high_rows * STRIP, 16 * STRIP), f32)],
        compiler_params=pltpu.CompilerParams(vmem_limit_bytes=vmem_limit),
        name="table_sums",
    )(grad_scores, plane, down)
    return table_result(out, high_counts, heads)


CHUNK = 768
CHUNKS = 6
AWAY = 4
PARTS = (CHUNK // 2, CHUNK // 4, CHUNK // 8, CHUNK // 16)


def exchange_schedule(turns):
    plan = []
    for k in range(CHUNKS):
        plan.append((0, 0, k))
        plan.append((1 + 1.5 * k, 1, k))
    for k in range(CHUNKS):
        if k < CHUNKS - AWAY:
            start = 11 + 7 * k
        else:
            arrival = 19 + 13.5 * (k - CHUNKS + AWAY)
            plan.append((arrival, 2, k))
            start = arrival + 8
        for event, delay in ((3, 0), (4, 4.5), (5, 9), (6, 13.5), (7, 18), (8, 26), (9, 29)):
            plan.append((start + delay, event, k))
    slots = [[] for _ in range(turns + 1)]
    for at, event, k in sorted(plan):
        slots[min(int(at / 1.6), turns)].append((event, k))
    return slots


def table_exchange_kernel(
    grad_score_ref,
    plane_ref,
    down_ref,
    project_ref,
    output_ref,
    expand_ref,
    expand_away_ref,
    reduce_ref,
    reduce_away_ref,
    table_ref,
    total_ref,
    sum_ref,
    grad_buf,
    plane_buf,
    down_buf,
    own_buf,
    away_buf,
    core_buf,
    core_away_buf,
    y_buf,
    x_buf,
    near_buf,
    far_buf,
    block_sem,
    load_sem,
    local_sem,
    send_sem,
    recv_sem,
    *,
    high_counts,
):
    heads, row_count, keys = grad_score_ref.shape
    block_rows = grad_buf.shape[2]
    turn_rows = TABLE_STRIPS * STRIP
    per_block = block_rows // turn_rows
    blocks = row_count // block_rows
    turns = row_count // turn_rows
    place = lax.axis_index("dp")
    sides = [(place // bit) % 2 for bit in (1, 2, 4, 8)]
    partners = [
        {"dp": place + bit * (1 - 2 * side)} for bit, side in zip((1, 2, 4, 8), sides)
    ]
    across_mp = {"mp": 1 - lax.axis_index("mp")}

    barrier = pltpu.get_barrier_semaphore()
    for device in (*partners, across_mp):
        pl.semaphore_signal(barrier, inc=1, device_id=device, device_id_type=pl.DeviceIdType.MESH)
    pl.semaphore_wait(barrier, 5)

    def block_copies(block, slot):
        rows = pl.ds(pl.multiple_of(block * block_rows, STRIP), block_rows)
        return (
            pltpu.make_async_copy(
                grad_score_ref.at[:, rows, :], grad_buf.at[slot], block_sem.at[slot, 0]
            ),
            pltpu.make_async_copy(plane_ref.at[rows, :], plane_buf.at[slot], block_sem.at[slot, 1]),
            pltpu.make_async_copy(down_ref.at[rows, :], down_buf.at[slot], block_sem.at[slot, 2]),
        )

    half = CHUNK // 2
    loads = [
        [
            (project_ref.at[0:CHUNK, :], own_buf.at[0, :, 0:half]),
            (project_ref.at[1152 : 1152 + CHUNK, :], own_buf.at[0, :, half:CHUNK]),
        ],
        [
            (project_ref.at[CHUNK:1152, :], own_buf.at[1, 0:half, 0:half]),
            (project_ref.at[1152 + CHUNK : 2304, :], own_buf.at[1, 0:half, half:CHUNK]),
            (output_ref, own_buf.at[1, half:CHUNK, :]),
        ],
    ]
    for ref, away_ref, wide in (
        (expand_ref, expand_away_ref, True),
        (reduce_ref, reduce_away_ref, False),
    ):
        for k in range(2):
            piece = slice(k * CHUNK, (k + 1) * CHUNK)
            index = (slice(None), piece) if wide else (piece, slice(None))
            chunk = len(loads)
            loads.append(
                [
                    (ref.at[index], own_buf.at[chunk]),
                    (away_ref.at[index], away_buf.at[chunk - CHUNKS + AWAY]),
                ]
            )
    copies = [
        [pltpu.make_async_copy(src, dst, load_sem.at[k, n]) for n, (src, dst) in enumerate(group)]
        for k, group in enumerate(loads)
    ]

    keeps, leaves = [], []
    base = 0
    for size, side in zip(PARTS, sides):
        keeps.append(base + side * size)
        leaves.append(base + (1 - side) * size)
        base = base + side * size

    def rows_at(start, size):
        return pl.ds(pl.multiple_of(start, STRIP), size)

    def remote(src, dst, chunk, stage, device):
        return pltpu.make_async_remote_copy(
            src_ref=src,
            dst_ref=dst,
            send_sem=send_sem.at[chunk, stage],
            recv_sem=recv_sem.at[chunk, stage],
            device_id=device,
            device_id_type=pl.DeviceIdType.MESH,
        )

    def is_away(chunk):
        return chunk >= CHUNKS - AWAY

    def away_at(chunk):
        return chunk - CHUNKS + AWAY

    arrivals = (core_buf, x_buf, near_buf, far_buf)

    def scatter(chunk, level):
        return remote(
            own_buf.at[chunk, rows_at(leaves[level], PARTS[level]), :],
            arrivals[level].at[chunk],
            chunk,
            level,
            partners[level],
        )

    def scatter_away(chunk):
        return remote(
            away_buf.at[away_at(chunk), rows_at(leaves[0], PARTS[0]), :],
            core_away_buf.at[away_at(chunk)],
            chunk,
            4,
            partners[0],
        )

    def hand_over(chunk):
        return remote(
            away_buf.at[away_at(chunk), rows_at(keeps[0], PARTS[0]), :],
            y_buf.at[away_at(chunk)],
            chunk,
            5,
            across_mp,
        )

    def total_rows(chunk, start, size):
        return total_ref.at[rows_at(chunk * CHUNK + start, size), :]

    def gather(chunk, level):
        if level == 3:
            src = own_buf.at[chunk, rows_at(keeps[3], PARTS[3]), :]
        else:
            src = total_rows(chunk, keeps[level], PARTS[level])
        return remote(
            src, total_rows(chunk, keeps[level], PARTS[level]), chunk, 6 + level, partners[level]
        )

    def gathered(chunk, level):
        place_of = total_rows(chunk, leaves[level], PARTS[level])
        return remote(place_of, place_of, chunk, 6 + level, partners[level])

    def store_own(chunk):
        return pltpu.make_async_copy(
            own_buf.at[chunk, rows_at(keeps[3], PARTS[3]), :],
            total_rows(chunk, keeps[3], PARTS[3]),
            local_sem.at[chunk],
        )

    def add(buf, chunk, start, size, arrived):
        piece = PARTS[3]

        def step(n, carry):
            here = rows_at(start + n * piece, piece)
            there = rows_at(n * piece, piece)
            buf[chunk, here, :] = buf[chunk, here, :] + arrived[there, :]
            return carry

        lax.fori_loop(0, size // piece, step, 0)

    def run(event, chunk):
        if event == 0:
            for copy in copies[chunk]:
                copy.wait()
            scatter(chunk, 0).start()
            if is_away(chunk):
                scatter_away(chunk).start()
        elif event == 1:
            if is_away(chunk):
                scatter_away(chunk).wait_recv()
                add(away_buf, away_at(chunk), keeps[0], PARTS[0], core_away_buf.at[away_at(chunk)])
                hand_over(chunk).start()
            scatter(chunk, 0).wait_recv()
            add(own_buf, chunk, keeps[0], PARTS[0], core_buf.at[chunk])
            if not is_away(chunk):
                scatter(chunk, 1).start()
        elif event == 2:
            hand_over(chunk).wait_recv()
            add(own_buf, chunk, keeps[0], PARTS[0], y_buf.at[away_at(chunk)])
            scatter(chunk, 1).start()
        elif event in (3, 4, 5):
            level = event - 2
            scatter(chunk, level).wait_recv()
            add(own_buf, chunk, keeps[level], PARTS[level], arrivals[level].at[chunk])
            if level < 3:
                scatter(chunk, level + 1).start()
            else:
                store_own(chunk).start()
                gather(chunk, 3).start()
        else:
            level = 9 - event
            if level == 3:
                store_own(chunk).wait()
            gathered(chunk, level).wait_recv()
            if level > 0:
                gather(chunk, level - 1).start()

    for group in copies[:2]:
        for copy in group:
            copy.start()
    for copy in block_copies(0, 0):
        copy.start()
    for group in copies[2:]:
        for copy in group:
            copy.start()
    sum_ref[...] = jnp.zeros_like(sum_ref)
    slots = exchange_schedule(turns)

    def dispatch(s, low, high):
        if not any(slots[low:high]):
            return
        if high - low == 1:
            for event, chunk in slots[low]:
                run(event, chunk)
            return
        middle = (low + high) // 2
        if any(slots[low:middle]):
            pl.when(s < middle)(lambda: dispatch(s, low, middle))
        if any(slots[middle:high]):
            pl.when(s >= middle)(lambda: dispatch(s, middle, high))

    def turn(s, carry):
        block = s // per_block
        slot = block % 2

        @pl.when(s % per_block == 0)
        def _():
            for copy in block_copies(block, slot):
                copy.wait()

            @pl.when(block + 1 < blocks)
            def _():
                for copy in block_copies(block + 1, 1 - slot):
                    copy.start()

        dispatch(s, 0, turns)

        def refs_at(start):
            at = rows_at(start, STRIP)
            return (
                lambda h, cols: grad_buf[slot, h, at, cols],
                lambda cols: plane_buf[slot, at, cols],
                lambda cols: down_buf[slot, at, cols],
            )

        start = (s % per_block) * turn_rows
        table_strips(
            [refs_at(start + k * STRIP) for k in range(TABLE_STRIPS)],
            sum_ref,
            heads,
            keys,
            high_counts,
        )
        return carry

    lax.fori_loop(0, turns, turn, 0)
    for event, chunk in slots[turns]:
        run(event, chunk)
    table_finish(sum_ref, table_ref)
    for chunk in range(CHUNKS):
        for level in range(4):
            scatter(chunk, level).wait_send()
            gather(chunk, level).wait_send()
        if is_away(chunk):
            scatter_away(chunk).wait_send()
            hand_over(chunk).wait_send()


def table_exchange(grad_scores, plane, down, counts, project, output, expand, reduce):
    heads, row_count, keys = grad_scores.shape
    high_counts = (counts[0] // 16, counts[1] // 16, counts[1] // 16)
    high_rows = sum(high_counts) * heads
    anywhere = pl.BlockSpec(memory_space=pl.ANY)
    out, total = pl.pallas_call(
        partial(table_exchange_kernel, high_counts=high_counts),
        in_specs=[anywhere] * 9,
        out_specs=[pl.BlockSpec(memory_space=pltpu.VMEM), anywhere],
        out_shape=[
            jax.ShapeDtypeStruct((high_rows, 16 * STRIP), f32),
            jax.ShapeDtypeStruct((CHUNKS * CHUNK, CHUNK), bf16),
        ],
        scratch_shapes=[
            pltpu.VMEM((high_rows * STRIP, 16 * STRIP), f32),
            pltpu.VMEM((2, heads, BLOCK_ROWS, keys), bf16),
            pltpu.VMEM((2, BLOCK_ROWS, keys), jnp.int16),
            pltpu.VMEM((2, BLOCK_ROWS, keys), jnp.int16),
            pltpu.VMEM((CHUNKS, CHUNK, CHUNK), bf16),
            pltpu.VMEM((AWAY, CHUNK, CHUNK), bf16),
            pltpu.VMEM((CHUNKS, PARTS[0], CHUNK), bf16),
            pltpu.VMEM((AWAY, PARTS[0], CHUNK), bf16),
            pltpu.VMEM((AWAY, PARTS[0], CHUNK), bf16),
            pltpu.VMEM((CHUNKS, PARTS[1], CHUNK), bf16),
            pltpu.VMEM((CHUNKS, PARTS[2], CHUNK), bf16),
            pltpu.VMEM((CHUNKS, PARTS[3], CHUNK), bf16),
            pltpu.SemaphoreType.DMA((2, 3)),
            pltpu.SemaphoreType.DMA((CHUNKS, 3)),
            pltpu.SemaphoreType.DMA((CHUNKS,)),
            pltpu.SemaphoreType.DMA((CHUNKS, 10)),
            pltpu.SemaphoreType.DMA((CHUNKS, 10)),
        ],
        compiler_params=pltpu.CompilerParams(
            vmem_limit_bytes=vmem_limit, collective_id=0, has_side_effects=True
        ),
        name="table_exchange",
    )(grad_scores, plane, down, project, output, *expand, *reduce)
    half = CHUNK // 2
    project_total = jnp.concatenate([total[:1152, :half], total[:1152, half:]])
    output_total = total[1152 : 2 * CHUNK]
    expand_total = jnp.concatenate(
        [total[2 * CHUNK : 3 * CHUNK], total[3 * CHUNK : 4 * CHUNK]], axis=1
    )
    reduce_total = total[4 * CHUNK :]
    return table_result(out, high_counts, heads), project_total, output_total, expand_total, reduce_total


def feed_kernel(
    context_ref,
    context_away_ref,
    token_ref,
    cotangent_ref,
    valid_ref,
    output_ref,
    output_away_ref,
    expand_ref,
    expand_away_ref,
    reduce_ref,
    reduce_away_ref,
    expand_bias_ref,
    vector_ref,
    layer_ref,
    grad_ref,
    inner_ref,
    expand_grad_ref,
    expand_grad_away_ref,
    reduce_grad_ref,
    reduce_grad_away_ref,
    vector_grad_ref,
    expand_bias_grad_ref,
    input_buf,
    norm_buf,
    hat_buf,
    inverse_buf,
    total_buf,
    reduced_buf,
    active_buf,
    slope_buf,
    before_buf,
    *,
    pieces,
    tiles,
):
    rows, width = token_ref.shape
    step = pl.program_id(0)
    piece = step % (2 * pieces)
    strip_rows = FEED_STRIP
    strips = rows // strip_rows

    def vector(n):
        return vector_ref[n : n + 1, :]

    def for_strips(body, sums):
        def run(n, carry):
            at = pl.ds(pl.multiple_of(n * strip_rows, STRIP), strip_rows)
            return tuple(
                old + jnp.sum(new.reshape(strip_rows // 8, 8, width), axis=0)
                for old, new in zip(carry, body(at))
            )

        start = tuple(jnp.zeros((8, width), f32) for _ in range(sums))
        done = lax.fori_loop(0, strips, run, start)
        return [jnp.sum(part, axis=0, keepdims=True) for part in done]

    def mean(values):
        return jnp.sum(values, axis=-1, keepdims=True) * (1.0 / width)

    @pl.when(step == 0)
    def _():
        vector_grad_ref[...] = jnp.zeros_like(vector_grad_ref)
        total_buf[...] = dot_f32(context_ref[...], output_ref[...]) + dot_f32(
            context_away_ref[...], output_away_ref[...]
        )

        def body(at):
            values = token_ref[at, :].astype(f32) + (total_buf[at, :] + vector(0))
            centered = values - mean(values)
            inverse = lax.rsqrt(mean(centered * centered) + norm_epsilon)
            hat = centered * inverse
            norm = hat * vector(1) + vector(2)
            hat_buf[at, :] = hat
            inverse_buf[at, :] = jnp.broadcast_to(inverse, (strip_rows, LANES))
            norm_buf[at, :] = norm
            input_buf[at, :] = norm.astype(bf16)
            total_buf[at, :] = norm + vector(3)
            return ()

        for_strips(body, 0)

    def forward(expand, reduce):
        for start, size in tiles:
            at = slice(start, start + size)
            before = dot_f32(input_buf[at, :], expand[...]) + expand_bias_ref[0]
            phi = 0.5 * lax.erf(before * 0.7071067811865476) + 0.5
            slope_buf[piece, at, :] = phi + before * (
                0.3989422804014327 * jnp.exp(-0.5 * (before * before))
            )
            active = (before * phi).astype(bf16)
            active_buf[piece, at, :] = active
            total_buf[at, :] += dot_f32(active, reduce[...])

    pl.when(step < pieces)(lambda: forward(expand_ref, reduce_ref))
    pl.when((step >= pieces) & (step < 2 * pieces))(
        lambda: forward(expand_away_ref, reduce_away_ref)
    )

    @pl.when(step == 2 * pieces)
    def _():
        def body(at):
            values = total_buf[at, :]
            valid = valid_ref[at, :]
            centered = values - mean(values)
            inverse = lax.rsqrt(mean(centered * centered) + norm_epsilon)
            hat = centered * inverse
            layer_ref[at, :] = (valid * (hat * vector(4) + vector(5))).astype(bf16)
            grad_out = cotangent_ref[at, :].astype(f32) * valid
            grad_hat = grad_out * vector(4)
            mixed = inverse * (grad_hat - mean(grad_hat) - hat * mean(grad_hat * hat))
            low = mixed.astype(bf16)
            reduced_buf[at, :] = low
            total_buf[at, :] = mixed
            return grad_out * hat, grad_out, low.astype(f32)

        for n, part in enumerate(for_strips(body, 3)):
            vector_grad_ref[n : n + 1, :] = part

    def backward(expand, reduce):
        sums = None
        for start, size in tiles:
            at = slice(start, start + size)
            grad_active = lax.dot_general(
                reduced_buf[at, :], reduce[...], (((1,), (1,)), ((), ())), preferred_element_type=f32
            )
            before = (grad_active * slope_buf[piece, at, :]).astype(bf16)
            before_buf[piece, at, :] = before
            part = jnp.sum(before.astype(f32), axis=0, keepdims=True)
            sums = part if sums is None else sums + part
            total_buf[at, :] += lax.dot_general(
                before, expand[...], (((1,), (1,)), ((), ())), preferred_element_type=f32
            )
        expand_bias_grad_ref[0] = sums

    pl.when((step >= 2 * pieces) & (step < 3 * pieces))(lambda: backward(expand_ref, reduce_ref))
    pl.when((step >= 3 * pieces) & (step < 4 * pieces))(
        lambda: backward(expand_away_ref, reduce_away_ref)
    )

    @pl.when(step == 4 * pieces)
    def _():
        def body(at):
            grad_first = total_buf[at, :]
            hat = hat_buf[at, :]
            grad_hat = grad_first * vector(1)
            inverse = inverse_buf[at, 0:1]
            inner = inverse * (grad_hat - mean(grad_hat) - hat * mean(grad_hat * hat))
            low = inner.astype(bf16)
            inner_ref[at, :] = inner
            grad_ref[at, :] = low
            return grad_first * hat, grad_first, low.astype(f32)

        for n, part in enumerate(for_strips(body, 3)):
            vector_grad_ref[n + 3 : n + 4, :] = part

    def weights(expand_grad, reduce_grad):
        reduce_grad[...] = lax.dot_general(
            active_buf[piece], reduced_buf[...], (((0,), (0,)), ((), ())), preferred_element_type=f32
        ).astype(bf16)
        expand_grad[...] = lax.dot_general(
            input_buf[...], before_buf[piece], (((0,), (0,)), ((), ())), preferred_element_type=f32
        ).astype(bf16)

    pl.when((step >= 4 * pieces) & (step < 5 * pieces))(
        lambda: weights(expand_grad_ref, reduce_grad_ref)
    )
    pl.when(step >= 5 * pieces)(lambda: weights(expand_grad_away_ref, reduce_grad_away_ref))


def feed(
    context,
    context_away,
    tokens,
    cotangent,
    valid,
    output,
    output_away,
    expand,
    expand_away,
    reduce,
    reduce_away,
    expand_biases,
    vectors,
):
    rows, width = tokens.shape
    hidden = expand.shape[1]
    size = FEED_PIECE
    pieces = hidden // size
    split = round_up(rows // 2, STRIP)
    tiles = ((0, split), (split, rows - split))

    def once(array):
        zeros = (0,) * array.ndim
        return pl.BlockSpec(array.shape, lambda i: zeros, pipeline_mode=pl.Buffered(1))

    def place(first, i):
        at = lax.rem(i, 2 * pieces) - first
        at = jnp.clip(at, 0, pieces - 1)
        return jnp.where(i < 4 * pieces, at, pieces - 1)

    def grad_place(first, i):
        return jnp.clip(i - 4 * pieces - first, 0, pieces - 1)

    wide = lambda first: pl.BlockSpec((width, size), lambda i: (0, place(first, i)))
    tall = lambda first: pl.BlockSpec((size, width), lambda i: (place(first, i), 0))
    wide_grad = lambda first: pl.BlockSpec((width, size), lambda i: (0, grad_place(first, i)))
    tall_grad = lambda first: pl.BlockSpec((size, width), lambda i: (grad_place(first, i), 0))
    bias_rows = expand_biases.reshape(2 * pieces, 1, size)
    whole = lambda shape: pl.BlockSpec(
        shape, lambda i: (0,) * len(shape), pipeline_mode=pl.Buffered(1)
    )
    full = jax.ShapeDtypeStruct((rows, width), bf16)
    return pl.pallas_call(
        partial(feed_kernel, pieces=pieces, tiles=tiles),
        grid=(6 * pieces,),
        in_specs=[
            once(context),
            once(context_away),
            once(tokens),
            once(cotangent),
            once(valid),
            once(output),
            once(output_away),
            wide(0),
            wide(pieces),
            tall(0),
            tall(pieces),
            pl.BlockSpec((1, 1, size), lambda i: (lax.rem(i, 2 * pieces), 0, 0)),
            once(vectors),
        ],
        out_specs=[
            whole((rows, width)),
            whole((rows, width)),
            whole((rows, width)),
            wide_grad(0),
            wide_grad(pieces),
            tall_grad(0),
            tall_grad(pieces),
            whole((8, width)),
            pl.BlockSpec((1, 1, size), lambda i: (jnp.clip(i - 2 * pieces, 0, 2 * pieces - 1), 0, 0)),
        ],
        out_shape=[
            full,
            full,
            jax.ShapeDtypeStruct((rows, width), f32),
            jax.ShapeDtypeStruct((width, hidden), bf16),
            jax.ShapeDtypeStruct((width, hidden), bf16),
            jax.ShapeDtypeStruct((hidden, width), bf16),
            jax.ShapeDtypeStruct((hidden, width), bf16),
            jax.ShapeDtypeStruct((8, width), f32),
            jax.ShapeDtypeStruct((2 * pieces, 1, size), f32),
        ],
        scratch_shapes=[
            pltpu.VMEM((rows, width), bf16),
            pltpu.VMEM((rows, width), f32),
            pltpu.VMEM((rows, width), f32),
            pltpu.VMEM((rows, LANES), f32),
            pltpu.VMEM((rows, width), f32),
            pltpu.VMEM((rows, width), bf16),
            pltpu.VMEM((2 * pieces, rows, size), bf16),
            pltpu.VMEM((2 * pieces, rows, size), f32),
            pltpu.VMEM((2 * pieces, rows, size), bf16),
        ],
        compiler_params=pltpu.CompilerParams(vmem_limit_bytes=vmem_limit),
        name="feed",
    )(
        context,
        context_away,
        tokens,
        cotangent,
        valid,
        output,
        output_away,
        expand,
        expand_away,
        reduce,
        reduce_away,
        bias_rows,
        vectors,
    )


def swap(array):
    return lax.ppermute(array, "mp", [(0, 1), (1, 0)])


def partner(array, count, bit):
    return lax.ppermute(array, "dp", [(i, i ^ bit) for i in range(count)])


def other_share(array, count):
    core = lax.axis_index("dp") % 2
    half = array.shape[0] // 2
    fetched = swap(lax.dynamic_slice_in_dim(array, core * half, half, 0))
    handed = partner(fetched, count, 1)
    even = core == 0
    return jnp.concatenate(
        [jnp.where(even, fetched, handed), jnp.where(even, handed, fetched)], axis=0
    )


def sum_rows_over_dp(array, count):
    place = lax.axis_index("dp")
    bits = []
    bit = 1
    while bit < count:
        mine = (place // bit) % 2
        halves = array.reshape((2, array.shape[0] // 2) + array.shape[1:])
        sent = lax.dynamic_index_in_dim(halves, 1 - mine, 0, keepdims=False)
        kept = lax.dynamic_index_in_dim(halves, mine, 0, keepdims=False)
        array = kept + partner(sent, count, bit)
        bits.append(bit)
        bit *= 2
    for bit in reversed(bits):
        lead = (place // bit) % 2 == 0
        other = partner(array, count, bit)
        array = jnp.concatenate(
            [jnp.where(lead, array, other), jnp.where(lead, other, array)], axis=0
        )
    return array


def sum_small(arrays, count, over_mp):
    sizes = [a.size for a in arrays]
    total = sum(sizes)
    flat = jnp.concatenate([a.reshape(-1) for a in arrays])
    flat = jnp.pad(flat, (0, round_up(total, 1024) - total)).reshape(-1, LANES)
    if over_mp:
        flat = flat + swap(flat)
    bit = 1
    while bit < count:
        flat = flat + partner(flat, count, bit)
        bit *= 2
    flat = flat.reshape(-1)
    outs = []
    start = 0
    for array, size in zip(arrays, sizes):
        outs.append(flat[start : start + size].reshape(array.shape))
        start += size
    return outs


def per_device(
    dp_count,
    tokens,
    cotangent,
    long_flag,
    token_mask,
    bucket_line,
    bucket_across,
    bucket_down,
    project_weight,
    project_bias,
    table_line,
    table_across,
    table_down,
    output_weight,
    output_bias,
    first_gain,
    first_shift,
    expand_weight,
    expand_bias,
    reduce_weight,
    reduce_bias,
    second_gain,
    second_shift,
):
    length = tokens.shape[1]
    width = project_weight.shape[2]
    heads = table_line.shape[1]
    counts = (table_line.shape[0], table_across.shape[0])
    rows = round_up(length, BLOCK_ROWS)
    half_rows = rows // 2
    keys = round_up(length, 3 * LANES)
    mp_index = lax.axis_index("mp")
    lead = mp_index == 0

    def own_rows(array):
        return lax.dynamic_slice_in_dim(array, mp_index * half_rows, half_rows, 0)

    def other_rows(array):
        return lax.dynamic_slice_in_dim(array, (1 - mp_index) * half_rows, half_rows, 0)

    def in_order(mine, other):
        return jnp.where(lead, mine, other), jnp.where(lead, other, mine)

    output_other = other_share(output_weight, dp_count)
    expand_other = other_share(expand_weight, dp_count)
    reduce_other = other_share(reduce_weight, dp_count)
    expand_bias_other = swap(expand_bias)

    positions = jnp.arange(length, dtype=jnp.int32)
    limit = jnp.where(long_flag[0] > 0, LONG, SHORT).astype(jnp.int32)
    valid = (token_mask[0] > 0) & (positions < limit)
    valid_rows = own_rows(jnp.pad(valid.astype(f32), (0, rows - length)))[:, None]
    grow = ((0, rows - length), (0, keys - length))
    line = jnp.where(valid[None, :], bucket_line[0], bucket_line[0] + counts[0])
    plane = jnp.pad(
        (line | (bucket_across[0] << 8)).astype(jnp.int16), grow, constant_values=counts[0]
    )
    down = jnp.pad(bucket_down[0].astype(jnp.int16), grow)
    tables = []
    for table in (table_line, table_across, table_down):
        lanes = jnp.pad(
            table.T, ((0, 0), (0, LANES - table.shape[0])), constant_values=large_negative
        )
        tables.append(jnp.broadcast_to(lanes[:, None, :], (heads, STRIP, LANES)))
    tables = jnp.concatenate(tables).astype(bf16)

    query, key_wide, key_turned, value_ones, value_turned = project(
        tokens[0], project_weight, project_bias.astype(f32), keys
    )
    exps, context, inverse = attend(query, key_turned, value_ones, plane, down, tables)

    context_other = swap(other_rows(context))
    padded = jnp.pad(tokens[0], ((0, rows - length), (0, 0)))
    vectors = jnp.stack(
        [
            output_bias.astype(f32),
            first_gain,
            first_shift,
            reduce_bias.astype(f32),
            second_gain,
            second_shift,
            second_shift,
            second_shift,
        ]
    )
    expand_biases = jnp.concatenate([expand_bias, expand_bias_other]).astype(f32)
    (
        layer_mine,
        grad_mine,
        grad_inner,
        expand_own,
        expand_sent,
        reduce_own,
        reduce_sent,
        vector_grads,
        expand_bias_grads,
    ) = feed(
        own_rows(context),
        context_other,
        own_rows(padded),
        own_rows(jnp.pad(cotangent[0], ((0, rows - length), (0, 0)))),
        valid_rows,
        output_weight,
        output_other,
        expand_weight,
        expand_other,
        reduce_weight,
        reduce_other,
        expand_biases,
        vectors,
    )
    layer_out = jnp.concatenate(in_order(layer_mine, swap(layer_mine)))[None, :length]
    expand_bias_grads = expand_bias_grads.reshape(2, -1)
    grad_attended = jnp.concatenate(in_order(grad_mine, swap(grad_mine)))
    output_weight_grad = jnp.einsum(
        "le,lf->ef", context, grad_attended, preferred_element_type=f32
    ).astype(bf16)
    grad_context = jnp.einsum(
        "lf,ef->le", grad_attended, output_weight, preferred_element_type=f32
    )
    grad_scaled = (grad_context * inverse).astype(bf16)

    grad_scores, grad_query, grad_key, grad_value = attend_back(
        exps, grad_scaled, context, query, value_turned, key_wide
    )
    grad_key = grad_key.reshape(width, keys).astype(bf16)
    grad_value = grad_value.reshape(width, keys).astype(bf16)
    cut_key, cut_value = grad_key[:, :rows], grad_value[:, :rows]
    project_weight_grad = jnp.concatenate(
        [
            jnp.einsum("ld,le->de", padded, grad_query, preferred_element_type=f32),
            jnp.einsum("ld,el->de", padded, cut_key, preferred_element_type=f32),
            jnp.einsum("ld,el->de", padded, cut_value, preferred_element_type=f32),
        ]
    ).astype(bf16)
    project_bias_grad = jnp.stack(
        [jnp.sum(grad_query, axis=0, dtype=f32), jnp.sum(cut_value, axis=1, dtype=f32)]
    )
    input_part = (
        jnp.einsum("le,de->ld", grad_query, project_weight[0], preferred_element_type=f32)
        + jnp.einsum("el,de->ld", cut_key, project_weight[1], preferred_element_type=f32)
        + jnp.einsum("el,de->ld", cut_value, project_weight[2], preferred_element_type=f32)
    )
    input_part = lax.dynamic_update_slice_in_dim(
        input_part, own_rows(input_part) + grad_inner, mp_index * half_rows, 0
    )
    sent = jnp.where(lead, input_part[:, width:], input_part[:, :width]).astype(bf16)
    own = jnp.where(lead, input_part[:, :width], input_part[:, width:])
    input_grad = (own + swap(sent).astype(f32))[None, :length]

    if dp_count == 16 and expand_own.shape == (CHUNK, 2 * CHUNK):
        (
            table_grads,
            project_weight_grad,
            output_weight_grad,
            expand_weight_grad,
            reduce_weight_grad,
        ) = table_exchange(
            grad_scores,
            plane,
            down,
            counts,
            project_weight_grad,
            output_weight_grad,
            (expand_own, expand_sent),
            (reduce_own, reduce_sent),
        )
    else:
        table_grads = table_sums(grad_scores, plane, down, counts)
        reduce_weight_grad = sum_rows_over_dp(reduce_own + swap(reduce_sent), dp_count)
        expand_weight_grad = sum_rows_over_dp(expand_own + swap(expand_sent), dp_count)
        output_weight_grad = sum_rows_over_dp(output_weight_grad, dp_count)
        project_weight_grad = sum_rows_over_dp(project_weight_grad, dp_count)
    project_weight_grad = project_weight_grad.reshape(project_weight.shape)

    vector_grads, expand_bias_grad, expand_bias_sent = sum_small(
        [vector_grads, *in_order(expand_bias_grads[0], expand_bias_grads[1])], dp_count, True
    )
    (
        second_gain_grad,
        second_shift_grad,
        reduce_bias_grad,
        first_gain_grad,
        first_shift_grad,
        output_bias_grad,
    ) = (vector_grads[n] for n in range(6))
    expand_bias_grad = jnp.where(lead, expand_bias_grad, expand_bias_sent)
    table_grads, project_bias_grad = sum_small([table_grads, project_bias_grad], dp_count, False)
    mine = mp_index * width
    return (
        layer_out,
        input_grad,
        project_weight_grad.astype(f32),
        project_bias_grad,
        table_grads[: counts[0]],
        table_grads[counts[0] : counts[0] + counts[1]],
        table_grads[counts[0] + counts[1] :],
        output_weight_grad.astype(f32),
        output_bias_grad,
        lax.dynamic_slice_in_dim(first_gain_grad, mine, width, 0),
        lax.dynamic_slice_in_dim(first_shift_grad, mine, width, 0),
        expand_weight_grad.astype(f32),
        expand_bias_grad,
        reduce_weight_grad.astype(f32),
        reduce_bias_grad,
        second_gain_grad,
        second_shift_grad,
    )


def solution(mesh):
    placed = (
        P("dp", None, None),
        P("dp", None, None),
        P("dp"),
        P("dp", None),
        P("dp", None, None),
        P("dp", None, None),
        P("dp", None, None),
        P(None, None, "mp"),
        P(None, "mp"),
        P(None, "mp"),
        P(None, "mp"),
        P(None, "mp"),
        P("mp", None),
        P(),
        P(),
        P(),
        P(None, "mp"),
        P("mp"),
        P("mp", None),
        P(),
        P(),
        P(),
    )
    return jax.shard_map(
        partial(per_device, mesh.shape["dp"]),
        mesh=mesh,
        in_specs=placed,
        out_specs=(
            P("dp", None, None),
            P("dp", None, "mp"),
            P(None, None, "mp"),
            P(None, "mp"),
            P(None, "mp"),
            P(None, "mp"),
            P(None, "mp"),
            P("mp", None),
            P(),
            P("mp"),
            P("mp"),
            P(None, "mp"),
            P("mp"),
            P("mp", None),
            P(),
            P(),
            P(),
        ),
        check_vma=False,
    )
```

```python
from functools import partial

import jax
import jax.numpy as jnp
from jax import lax
from jax.experimental import pallas as pl
from jax.experimental.pallas import tpu as pltpu
from jax.sharding import PartitionSpec as P

LONG = 1089
SHORT = 709
HEAD = 64
LANES = 128
STRIP = 16
BLOCK_ROWS = 224
FEED_PIECE = 768
FEED_STRIP = 112
TABLE_STRIPS = 2
ATTEND_STRIPS = 7

large_negative = -1000000000.0
norm_epsilon = 1e-05
vmem_limit = 56 * 2**20
FINISH_VMEM = 62 * 2**20
bf16 = jnp.bfloat16
f32 = jnp.float32


def round_up(value, step):
    return (value + step - 1) // step * step


def whole_spec(array):
    zeros = (0,) * array.ndim
    return pl.BlockSpec(array.shape, lambda i: zeros)


def dot_f32(left, right):
    return jnp.dot(left, right, preferred_element_type=f32)


def gather_lanes(values, index):
    dims = lax.GatherDimensionNumbers(
        offset_dims=(),
        collapsed_slice_dims=(1,),
        start_index_map=(1,),
        operand_batching_dims=(0,),
        start_indices_batching_dims=(0,),
    )
    return lax.gather(
        values,
        index[..., None],
        dims,
        slice_sizes=(1, 1),
        mode=lax.GatherScatterMode.PROMISE_IN_BOUNDS,
    )


def project_kernel(
    token_ref, weight_ref, bias_ref, query_ref, key_ref, key_turned_ref, value_ref, value_turned_ref, *, length
):
    rows = token_ref.shape[0]
    place = pl.program_id(0) * rows + lax.broadcasted_iota(jnp.int32, token_ref.shape, 0)
    token = jnp.where(place < length, token_ref[...].astype(f32), 0.0).astype(bf16)
    query = (dot_f32(token, weight_ref[0]) + bias_ref[0:1, :]).astype(bf16)
    query_ref[...] = (query.astype(f32) * 0.125).astype(bf16)
    key = dot_f32(token, weight_ref[1])
    value = dot_f32(token, weight_ref[2]) + bias_ref[1:2, :]
    lane_first = lax.broadcasted_iota(jnp.int32, (rows, LANES), 1) < HEAD
    row_first = lax.broadcasted_iota(jnp.int32, (LANES, rows), 0) < HEAD
    for p in range(key.shape[1] // LANES):
        cols = slice(p * LANES, (p + 1) * LANES)
        key_pair, value_pair = key[:, cols], value[:, cols]
        key_turned, value_turned = key_pair.T, value_pair.T
        for u in range(2):
            h = 2 * p + u
            lane_own = lane_first if u == 0 else ~lane_first
            row_own = row_first if u == 0 else ~row_first
            key_ref[h] = jnp.where(lane_own, key_pair, 0.0).astype(bf16)
            value_ref[h] = jnp.where(lane_own, value_pair, 1.0).astype(bf16)
            key_turned_ref[h] = jnp.where(row_own, key_turned, 0.0).astype(bf16)
            value_turned_ref[h] = jnp.where(row_own, value_turned, 0.0).astype(bf16)


def project(tokens, weight, bias, keys):
    length, depth = tokens.shape
    width = weight.shape[2]
    heads = width // HEAD
    block = 3 * LANES
    wide = pl.BlockSpec((heads, block, LANES), lambda i: (0, i, 0))
    turned = pl.BlockSpec((heads, LANES, block), lambda i: (0, 0, i))
    wide_shape = jax.ShapeDtypeStruct((heads, keys, LANES), bf16)
    turned_shape = jax.ShapeDtypeStruct((heads, LANES, keys), bf16)
    return pl.pallas_call(
        partial(project_kernel, length=length),
        grid=(keys // block,),
        in_specs=[
            pl.BlockSpec((block, depth), lambda i: (i, 0)),
            whole_spec(weight),
            whole_spec(bias),
        ],
        out_specs=[pl.BlockSpec((block, width), lambda i: (i, 0)), wide, turned, wide, turned],
        out_shape=[
            jax.ShapeDtypeStruct((keys, width), bf16),
            wide_shape,
            turned_shape,
            wide_shape,
            turned_shape,
        ],
        compiler_params=pltpu.CompilerParams(vmem_limit_bytes=vmem_limit),
        name="project",
    )(tokens, weight, bias)


def attend_kernel(
    query_ref,
    key_ref,
    value_ref,
    plane_ref,
    down_ref,
    table_ref,
    exp_ref,
    context_ref,
    inverse_ref,
    score_ref,
):
    heads, rows, keys = exp_ref.shape
    for h in range(heads):
        pair = slice(h // 2 * LANES, (h // 2 + 1) * LANES)
        score_ref[h] = dot_f32(query_ref[:, pair], key_ref[h])

    lanes = [slice(c * LANES, (c + 1) * LANES) for c in range(keys // LANES)]

    def scores_of(at):
        scores = [[] for _ in range(heads)]
        for cols in lanes:
            packed = plane_ref[at, cols]
            bias = [None] * heads
            for t, index in enumerate(
                (packed & jnp.int16(255), packed >> jnp.int16(8), down_ref[at, cols])
            ):
                for h in range(heads):
                    found = gather_lanes(table_ref[t * heads + h], index).astype(f32)
                    bias[h] = found if t == 0 else bias[h] + found
            for h in range(heads):
                scores[h].append(score_ref[h, at, cols] + bias[h])
        return scores

    def exps_of(scores):
        exps = []
        for parts in scores:
            top = parts[0]
            for part in parts[1:]:
                top = jnp.maximum(top, part)
            top = jnp.max(top, axis=1, keepdims=True)
            exps.append([jnp.exp(part - top).astype(bf16) for part in parts])
        return exps

    def strips(n, carry):
        start = pl.multiple_of(n * ATTEND_STRIPS * STRIP, STRIP)
        places = [pl.ds(start + k * STRIP, STRIP) for k in range(ATTEND_STRIPS)]
        scores = [scores_of(at) for at in places]
        exps = [exps_of(part) for part in scores]
        for at, part in zip(places, exps):
            for h in range(heads):
                for c, cols in enumerate(lanes):
                    exp_ref[h, at, cols] = part[h][c]
        return carry

    lax.fori_loop(0, rows // (ATTEND_STRIPS * STRIP), strips, 0)
    first = lax.broadcasted_iota(jnp.int32, (rows, LANES), 1) < HEAD
    for p in range(heads // 2):
        cols = slice(p * LANES, (p + 1) * LANES)
        even = dot_f32(exp_ref[2 * p], value_ref[2 * p])
        odd = dot_f32(exp_ref[2 * p + 1], value_ref[2 * p + 1])
        sums = jnp.where(first, pltpu.roll(even, HEAD, 1), pltpu.roll(odd, HEAD, 1))
        inverse = 1.0 / sums
        inverse_ref[:, cols] = inverse
        context_ref[:, cols] = (jnp.where(first, even, odd) * inverse).astype(bf16)


def attend(query, key_turned, value_ones, plane, down, tables):
    heads, _, keys = key_turned.shape
    row_count = plane.shape[0]
    width = heads * HEAD
    index_spec = pl.BlockSpec((BLOCK_ROWS, keys), lambda i: (i, 0))
    row_spec = pl.BlockSpec((BLOCK_ROWS, width), lambda i: (i, 0))
    return pl.pallas_call(
        attend_kernel,
        grid=(row_count // BLOCK_ROWS,),
        in_specs=[
            row_spec,
            whole_spec(key_turned),
            whole_spec(value_ones),
            index_spec,
            index_spec,
            whole_spec(tables),
        ],
        out_specs=[
            pl.BlockSpec((heads, BLOCK_ROWS, keys), lambda i: (0, i, 0)),
            row_spec,
            row_spec,
        ],
        out_shape=[
            jax.ShapeDtypeStruct((heads, row_count, keys), bf16),
            jax.ShapeDtypeStruct((row_count, width), bf16),
            jax.ShapeDtypeStruct((row_count, width), f32),
        ],
        scratch_shapes=[pltpu.VMEM((heads, BLOCK_ROWS, keys), f32)],
        compiler_params=pltpu.CompilerParams(vmem_limit_bytes=vmem_limit),
        name="attend",
    )(query, key_turned, value_ones, plane, down, tables)


def attend_back_kernel(
    exp_ref,
    grad_ref,
    context_ref,
    query_ref,
    value_ref,
    key_ref,
    grad_score_ref,
    grad_query_ref,
    grad_key_ref,
    grad_value_ref,
):
    heads, rows, _ = exp_ref.shape

    @pl.when(pl.program_id(0) == 0)
    def _():
        grad_key_ref[...] = jnp.zeros_like(grad_key_ref)
        grad_value_ref[...] = jnp.zeros_like(grad_value_ref)

    first = lax.broadcasted_iota(jnp.int32, (rows, LANES), 1) < HEAD
    for p in range(heads // 2):
        cols = slice(p * LANES, (p + 1) * LANES)
        grad = grad_ref[:, cols]
        product = grad.astype(f32) * context_ref[:, cols].astype(f32)
        query_turned = query_ref[:, cols].T
        grad_turned = grad.T
        grad_query = None
        for u in range(2):
            h = 2 * p + u
            half = slice(u * HEAD, (u + 1) * HEAD)
            own = first if u == 0 else ~first
            total = jnp.sum(jnp.where(own, product, 0.0), axis=1, keepdims=True)
            grad_exp = dot_f32(grad, value_ref[h])
            grad_score = (exp_ref[h].astype(f32) * (grad_exp - total)).astype(bf16)
            grad_score_ref[h] = grad_score
            part = dot_f32(grad_score, key_ref[h])
            grad_query = part if u == 0 else grad_query + part
            grad_key_ref[h] += dot_f32(query_turned[half], grad_score)
            grad_value_ref[h] += dot_f32(grad_turned[half], exp_ref[h])
        grad_query_ref[:, cols] = (grad_query * 0.125).astype(bf16)


def attend_back(exps, grad, context, query, value_turned, key_wide):
    heads, row_count, keys = exps.shape
    width = heads * HEAD
    row_spec = pl.BlockSpec((BLOCK_ROWS, width), lambda i: (i, 0))
    exp_spec = pl.BlockSpec((heads, BLOCK_ROWS, keys), lambda i: (0, i, 0))
    sum_spec = pl.BlockSpec((heads, HEAD, keys), lambda i: (0, 0, 0))
    return pl.pallas_call(
        attend_back_kernel,
        grid=(row_count // BLOCK_ROWS,),
        in_specs=[
            exp_spec,
            row_spec,
            row_spec,
            row_spec,
            whole_spec(value_turned),
            whole_spec(key_wide),
        ],
        out_specs=[exp_spec, row_spec, sum_spec, sum_spec],
        out_shape=[
            jax.ShapeDtypeStruct((heads, row_count, keys), bf16),
            jax.ShapeDtypeStruct((row_count, width), bf16),
            jax.ShapeDtypeStruct((heads, HEAD, keys), f32),
            jax.ShapeDtypeStruct((heads, HEAD, keys), f32),
        ],
        compiler_params=pltpu.CompilerParams(vmem_limit_bytes=vmem_limit),
        name="attend_back",
    )(exps, grad, context, query, value_turned, key_wide)


def table_strips(strips, sum_ref, heads, keys, high_counts):
    base = 0
    for t in range(3):
        shift = 8 if t == 1 else 0
        highs, lows = [], []
        for grad_of, plane_of, down_of in strips:
            for c in range(keys // LANES):
                cols = slice(c * LANES, (c + 1) * LANES)
                index = down_of(cols) if t == 2 else plane_of(cols)
                low = index & jnp.int16(15 << shift)
                high = index & jnp.int16(48 << shift)
                lows.append(
                    jnp.concatenate(
                        [
                            jnp.where(low == jnp.int16(x << shift), bf16(1), bf16(0))
                            for x in range(16)
                        ]
                    )
                )
                parts = []
                for x in range(high_counts[t]):
                    mask = high == jnp.int16(x << (4 + shift))
                    parts += [jnp.where(mask, grad_of(h, cols), bf16(0)) for h in range(heads)]
                highs.append(jnp.concatenate(parts))
        span = slice(base, base + high_counts[t] * heads * STRIP)
        sum_ref[span, :] += lax.dot_general(
            jnp.concatenate(highs, axis=1),
            jnp.concatenate(lows, axis=1),
            (((1,), (1,)), ((), ())),
            preferred_element_type=f32,
        )
        base = span.stop


def table_finish(sum_ref, out_ref, count):
    row_of_lane = lax.broadcasted_iota(jnp.int32, (STRIP, 16 * STRIP), 1) % STRIP
    same = row_of_lane == lax.broadcasted_iota(jnp.int32, (STRIP, 16 * STRIP), 0)
    for o in range(count):
        block = sum_ref[o * STRIP : (o + 1) * STRIP, :]
        out_ref[o : o + 1, :] = jnp.sum(jnp.where(same, block, 0.0), axis=0, keepdims=True)


def table_result(out, high_counts, heads):
    summed = jnp.sum(out.reshape(sum(high_counts), heads, 16, STRIP), axis=-1)
    return summed.transpose(0, 2, 1).reshape(-1, heads)


def table_kernel(grad_score_ref, plane_ref, down_ref, out_ref, sum_ref, *, high_counts):
    heads, rows, keys = grad_score_ref.shape
    step = pl.program_id(0)

    @pl.when(step == 0)
    def _():
        sum_ref[...] = jnp.zeros_like(sum_ref)

    def refs_at(start):
        at = pl.ds(pl.multiple_of(start, STRIP), STRIP)
        return (
            lambda h, cols: grad_score_ref[h, at, cols],
            lambda cols: plane_ref[at, cols],
            lambda cols: down_ref[at, cols],
        )

    def strips(r, carry):
        start = r * (TABLE_STRIPS * STRIP)
        table_strips(
            [refs_at(start + k * STRIP) for k in range(TABLE_STRIPS)],
            sum_ref,
            heads,
            keys,
            high_counts,
        )
        return carry

    lax.fori_loop(0, rows // (TABLE_STRIPS * STRIP), strips, 0)

    @pl.when(step == pl.num_programs(0) - 1)
    def _():
        table_finish(sum_ref, out_ref, out_ref.shape[0])


def table_sums(grad_scores, plane, down, counts):
    heads, row_count, keys = grad_scores.shape
    high_counts = (counts[0] // 16, counts[1] // 16, counts[1] // 16)
    high_rows = sum(high_counts) * heads
    index_spec = pl.BlockSpec((BLOCK_ROWS, keys), lambda i: (i, 0))
    out = pl.pallas_call(
        partial(table_kernel, high_counts=high_counts),
        grid=(row_count // BLOCK_ROWS,),
        in_specs=[
            pl.BlockSpec((heads, BLOCK_ROWS, keys), lambda i: (0, i, 0)),
            index_spec,
            index_spec,
        ],
        out_specs=pl.BlockSpec((high_rows, 16 * STRIP), lambda i: (0, 0)),
        out_shape=jax.ShapeDtypeStruct((high_rows, 16 * STRIP), f32),
        scratch_shapes=[pltpu.VMEM((high_rows * STRIP, 16 * STRIP), f32)],
        compiler_params=pltpu.CompilerParams(vmem_limit_bytes=vmem_limit),
        name="table_sums",
    )(grad_scores, plane, down)
    return table_result(out, high_counts, heads)


CHUNK = 768
CHUNKS = 6
LOCAL_CHUNKS = 2
PARTS = (CHUNK // 2, CHUNK // 4, CHUNK // 8, CHUNK // 16)
BITS = ((1, 2, 4, 8), (1, 4, 2, 8), (1, 2, 4, 8), (1, 2, 4, 8), (1, 4, 2, 8), (1, 4, 2, 8))
BACK_ROWS = 112
BACK_TIME = 2.8
TURN_START = 36.0
TURN_TIME = 1.65
EXCHANGE = (
    (0, 0, 2), (0.5, 0, 3), (1.0, 0, 4), (1.5, 0, 5), (4.9, 1, 2), (7.2, 1, 3), (9.6, 1, 4),
    (11.9, 1, 5), (21.8, 2, 2), (26.5, 2, 4), (32.0, 3, 2), (36.0, 2, 3), (38.7, 3, 4), (39.2, 1, 0),
    (39.9, 1, 1), (40.4, 2, 5), (43.2, 4, 2), (45.5, 4, 4), (50.1, 2, 1), (50.6, 5, 2), (52.2, 2, 0),
    (53.9, 5, 4), (56.9, 3, 1), (57.9, 6, 2), (59.1, 3, 0), (61.3, 6, 4), (64.6, 4, 1), (65.1, 7, 2),
    (65.6, 3, 3), (68.0, 4, 0), (68.5, 7, 4), (72.0, 3, 5), (72.5, 5, 1), (73.0, 4, 3), (75.3, 5, 0),
    (75.8, 8, 2), (78.8, 4, 5), (79.3, 8, 4), (79.8, 9, 2), (80.3, 5, 3), (82.2, 6, 1), (82.7, 6, 0),
    (83.2, 9, 4), (86.2, 5, 5), (89.5, 6, 3), (92.4, 7, 1), (92.9, 7, 0), (93.5, 6, 5), (96.0, 8, 1),
    (96.5, 7, 3), (97.2, 8, 0), (100.4, 7, 5), (107.1, 8, 3), (110.6, 8, 5), (111.1, 9, 3),
    (114.2, 9, 5),
)
SMALL_TIMES = (38.0, 46.0, 52.0, 60.0, 68.0, 76.0)
LAYER_TIME = 56.0
INPUT_TIME = 84.0


def plan_slots(blocks, turns):
    block_slots = [[] for _ in range(blocks)]
    turn_slots = [[] for _ in range(turns + 1)]
    steps = list(EXCHANGE)
    steps += [(at, "small", n) for n, at in enumerate(SMALL_TIMES)]
    steps += [(LAYER_TIME, "layer", 0), (INPUT_TIME, "input", 0)]
    for at, event, which in sorted(steps, key=lambda step: step[0]):
        block = int(at / BACK_TIME)
        if block < blocks and event != "small":
            block_slots[block].append((event, which))
        else:
            turn = max(0, int((at - TURN_START) / TURN_TIME))
            turn_slots[min(turn, turns)].append((event, which))
    return block_slots, turn_slots


def finish_kernel(
    exp_ref,
    inverse_ref,
    plane_ref,
    down_ref,
    context_ref,
    query_ref,
    token_ref,
    grad_ref,
    layer_ref,
    value_ref,
    key_ref,
    project_ref,
    output_ref,
    expand_ref,
    expand_away_ref,
    reduce_ref,
    reduce_away_ref,
    small_ref,
    total_ref,
    layer_out_ref,
    input_ref,
    small_out_ref,
    table_ref,
    score_ref,
    output_buf,
    grad_buf,
    value_buf,
    key_buf,
    context_buf,
    query_buf,
    token_buf,
    project_buf,
    ring_buf,
    inverse_buf,
    grad_key_buf,
    grad_value_buf,
    triple_buf,
    input_send_buf,
    input_recv_buf,
    input_buf,
    plane_buf,
    down_buf,
    sum_ref,
    own_buf,
    away_buf,
    core_buf,
    core_away_buf,
    first_buf,
    first_away_buf,
    y_buf,
    second_buf,
    third_buf,
    small_buf,
    small_recv_buf,
    table_buf,
    table_recv_buf,
    resident_sem,
    block_sem,
    ring_sem,
    load_sem,
    local_sem,
    out_sem,
    send_sem,
    recv_sem,
    wide_send_sem,
    wide_recv_sem,
    small_send_sem,
    small_recv_sem,
    table_send_sem,
    table_recv_sem,
    *,
    high_counts,
):
    heads, row_count, keys = exp_ref.shape
    width = heads * HEAD
    half_rows = row_count // 2
    rows = BACK_ROWS
    blocks = row_count // rows
    block_strips = rows // STRIP
    turns = row_count // (TABLE_STRIPS * STRIP)
    place = lax.axis_index("dp")
    mp_index = lax.axis_index("mp")
    side_of = {bit: (place // bit) % 2 for bit in (1, 2, 4, 8)}
    partner_of = {bit: {"dp": place + bit * (1 - 2 * side_of[bit])} for bit in (1, 2, 4, 8)}
    across_mp = {"mp": 1 - mp_index}

    barrier = pltpu.get_barrier_semaphore()
    for device in (*partner_of.values(), across_mp):
        pl.semaphore_signal(barrier, inc=1, device_id=device, device_id_type=pl.DeviceIdType.MESH)
    pl.semaphore_wait(barrier, 5)

    def rows_at(start, size):
        return pl.ds(pl.multiple_of(start, STRIP), size)

    def remote(src, dst, send, recv, device):
        return pltpu.make_async_remote_copy(
            src_ref=src,
            dst_ref=dst,
            send_sem=send,
            recv_sem=recv,
            device_id=device,
            device_id_type=pl.DeviceIdType.MESH,
        )

    mine = rows_at(mp_index * half_rows, half_rows)
    others = rows_at((1 - mp_index) * half_rows, half_rows)
    grad_swap = remote(
        grad_ref, grad_buf.at[1], wide_send_sem.at[0], wide_recv_sem.at[0], across_mp
    )
    input_swap = remote(
        input_send_buf, input_recv_buf, wide_send_sem.at[1], wide_recv_sem.at[1], across_mp
    )
    layer_swap = remote(
        layer_ref, layer_out_ref.at[mine, :], wide_send_sem.at[2], wide_recv_sem.at[2], across_mp
    )
    layer_arrival = remote(
        layer_out_ref.at[others, :],
        layer_out_ref.at[others, :],
        wide_send_sem.at[2],
        wide_recv_sem.at[2],
        across_mp,
    )
    layer_keep = pltpu.make_async_copy(layer_ref, layer_out_ref.at[mine, :], out_sem.at[2])
    grad_swap.start()

    residents = [
        pltpu.make_async_copy(src, dst, resident_sem.at[n])
        for n, (src, dst) in enumerate(
            (
                (grad_ref, grad_buf.at[0]),
                (output_ref, output_buf),
                (context_ref, context_buf),
                (query_ref, query_buf),
                (value_ref, value_buf),
                (key_ref, key_buf),
                (small_ref, small_buf.at[0]),
                (token_ref, token_buf),
                (project_ref, project_buf),
            )
        )
    ]

    def block_rows(block):
        start = (mp_index * (blocks // 2) + block) % blocks
        return rows_at(start * rows, rows)

    def block_copies(block, slot):
        at = block_rows(block)
        return (
            pltpu.make_async_copy(exp_ref.at[:, at, :], ring_buf.at[slot], block_sem.at[slot, 0]),
            pltpu.make_async_copy(inverse_ref.at[at, :], inverse_buf.at[slot], block_sem.at[slot, 1]),
        )

    def score_copy(block, slot):
        return pltpu.make_async_copy(
            ring_buf.at[2 + slot], score_ref.at[:, block_rows(block), :], out_sem.at[slot]
        )

    def ring_copies(block):
        slot = block % 4
        at = rows_at(block * rows, rows)
        return (
            pltpu.make_async_copy(score_ref.at[:, at, :], ring_buf.at[slot], ring_sem.at[slot, 0]),
            pltpu.make_async_copy(plane_ref.at[at, :], plane_buf.at[slot], ring_sem.at[slot, 1]),
            pltpu.make_async_copy(down_ref.at[at, :], down_buf.at[slot], ring_sem.at[slot, 2]),
        )

    def is_away(chunk):
        return chunk >= LOCAL_CHUNKS

    loads = {}
    for ref, away_ref, wide in (
        (expand_ref, expand_away_ref, True),
        (reduce_ref, reduce_away_ref, False),
    ):
        for k in range(2):
            piece = slice(k * CHUNK, (k + 1) * CHUNK)
            index = (slice(None), piece) if wide else (piece, slice(None))
            chunk = LOCAL_CHUNKS + len(loads)
            loads[chunk] = (
                pltpu.make_async_copy(ref.at[index], own_buf.at[chunk], load_sem.at[chunk, 0]),
                pltpu.make_async_copy(
                    away_ref.at[index], away_buf.at[chunk - LOCAL_CHUNKS], load_sem.at[chunk, 1]
                ),
            )

    for copy in residents[:2]:
        copy.start()
    for copy in block_copies(0, 0):
        copy.start()
    for copy in residents[2:7]:
        copy.start()
    for pair in loads.values():
        for copy in pair:
            copy.start()
    for copy in residents[7:]:
        copy.start()

    keeps, leaves = [], []
    for bits in BITS:
        kept, left, base = [], [], 0
        for size, bit in zip(PARTS, bits):
            kept.append(base + side_of[bit] * size)
            left.append(base + (1 - side_of[bit]) * size)
            base = base + side_of[bit] * size
        keeps.append(kept)
        leaves.append(left)
    arrivals = (core_buf, first_buf, second_buf, third_buf)
    away_arrivals = (core_away_buf, first_away_buf)

    def staged(src, dst, chunk, stage, device):
        return remote(src, dst, send_sem.at[chunk, stage], recv_sem.at[chunk, stage], device)

    def scatter(chunk, level):
        return staged(
            own_buf.at[chunk, rows_at(leaves[chunk][level], PARTS[level]), :],
            arrivals[level].at[chunk],
            chunk,
            level,
            partner_of[BITS[chunk][level]],
        )

    def scatter_away(chunk, level):
        return staged(
            away_buf.at[chunk - LOCAL_CHUNKS, rows_at(leaves[chunk][level], PARTS[level]), :],
            away_arrivals[level].at[chunk - LOCAL_CHUNKS],
            chunk,
            4 + level,
            partner_of[BITS[chunk][level]],
        )

    def hand_over(chunk):
        return staged(
            away_buf.at[chunk - LOCAL_CHUNKS, rows_at(keeps[chunk][1], PARTS[1]), :],
            y_buf.at[chunk - LOCAL_CHUNKS],
            chunk,
            6,
            across_mp,
        )

    def total_rows(chunk, start, size):
        return total_ref.at[rows_at(chunk * CHUNK + start, size), :]

    def gather(chunk, level):
        kept, size = keeps[chunk][level], PARTS[level]
        if level == 3:
            src = own_buf.at[chunk, rows_at(kept, size), :]
        else:
            src = total_rows(chunk, kept, size)
        return staged(
            src, total_rows(chunk, kept, size), chunk, 7 + level, partner_of[BITS[chunk][level]]
        )

    def gathered(chunk, level):
        region = total_rows(chunk, leaves[chunk][level], PARTS[level])
        return staged(region, region, chunk, 7 + level, partner_of[BITS[chunk][level]])

    def store_own(chunk):
        return pltpu.make_async_copy(
            own_buf.at[chunk, rows_at(keeps[chunk][3], PARTS[3]), :],
            total_rows(chunk, keeps[chunk][3], PARTS[3]),
            local_sem.at[chunk],
        )

    def add(buf, chunk, start, size, arrived):
        piece = PARTS[3]

        def step(n, carry):
            here = rows_at(start + n * piece, piece)
            there = rows_at(n * piece, piece)
            buf[chunk, here, :] = buf[chunk, here, :] + arrived[there, :]
            return carry

        lax.fori_loop(0, size // piece, step, 0)

    def add_level(chunk, level):
        scatter(chunk, level).wait_recv()
        add(own_buf, chunk, keeps[chunk][level], PARTS[level], arrivals[level].at[chunk])

    def add_level_away(chunk, level):
        at = chunk - LOCAL_CHUNKS
        scatter_away(chunk, level).wait_recv()
        add(away_buf, at, keeps[chunk][level], PARTS[level], away_arrivals[level].at[at])

    def exchange(event, chunk):
        away = is_away(chunk)
        if event == 0:
            if away:
                for copy in loads[chunk]:
                    copy.wait()
                scatter_away(chunk, 0).start()
            scatter(chunk, 0).start()
            return
        if event == 1:
            if away:
                add_level_away(chunk, 0)
                scatter_away(chunk, 1).start()
            add_level(chunk, 0)
            scatter(chunk, 1).start()
            return
        if away and event == 2:
            add_level_away(chunk, 1)
            hand_over(chunk).start()
            add_level(chunk, 1)
            return
        if away:
            event -= 1
            if event == 2:
                hand_over(chunk).wait_recv()
                add(own_buf, chunk, keeps[chunk][1], PARTS[1], y_buf.at[chunk - LOCAL_CHUNKS])
        elif event == 2:
            add_level(chunk, 1)
        if event == 2:
            scatter(chunk, 2).start()
        elif event == 3:
            add_level(chunk, 2)
            scatter(chunk, 3).start()
        elif event == 4:
            add_level(chunk, 3)
            store_own(chunk).start()
            gather(chunk, 3).start()
        else:
            level = 8 - event
            if level == 3:
                store_own(chunk).wait()
            gathered(chunk, level).wait_recv()
            if level > 0:
                gather(chunk, level - 1).start()

    small_devices = (across_mp, *partner_of.values())

    def small_hop(n):
        return remote(
            small_buf.at[n],
            small_recv_buf.at[n],
            small_send_sem.at[n],
            small_recv_sem.at[n],
            small_devices[n],
        )

    def small_step(n):
        if n == 0:
            residents[6].wait()
        else:
            small_hop(n - 1).wait_recv()
            small_buf[n] = small_buf[n - 1] + small_recv_buf[n - 1]
        if n < 5:
            small_hop(n).start()
        else:
            small_out_ref[...] = small_buf[n]

    def input_rows(side):
        return mine if side == 0 else others

    def input_product(side, target):
        at = input_rows(side)
        part = None
        for k in range(3):
            product = lax.dot_general(
                triple_buf[k, at, :],
                project_buf[k, rows_at(target * width, width), :],
                (((1,), (1,)), ((), ())),
                preferred_element_type=f32,
            )
            part = product if part is None else part + product
        if side == 0:
            cols = pl.ds(pl.multiple_of(target * width, LANES), width)
            part = part + grad_buf[0, :, cols].astype(f32)
        return part

    def input_store(side):
        return pltpu.make_async_copy(
            input_buf.at[side], input_ref.at[input_rows(side), :], out_sem.at[3 + side]
        )

    def run(event, which):
        if event == "small":
            small_step(which)
        elif event == "layer":
            layer_swap.start()
            layer_keep.start()
        elif event == "input":
            input_swap.wait_recv()
            for side in range(2):
                part = input_product(side, mp_index)
                input_buf[side] = part + input_recv_buf[input_rows(side), :].astype(f32)
                input_store(side).start()
        else:
            exchange(event, which)

    block_slots, turn_slots = plan_slots(blocks, turns)

    def dispatch(slots, n, low, high):
        if not any(slots[low:high]):
            return
        if high - low == 1:
            for event, which in slots[low]:
                run(event, which)
            return
        middle = (low + high) // 2
        if any(slots[low:middle]):
            pl.when(n < middle)(lambda: dispatch(slots, n, low, middle))
        if any(slots[middle:high]):
            pl.when(n >= middle)(lambda: dispatch(slots, n, middle, high))

    grad_key_buf[...] = jnp.zeros_like(grad_key_buf)
    grad_value_buf[...] = jnp.zeros_like(grad_value_buf)
    sum_ref[...] = jnp.zeros_like(sum_ref)
    for copy in residents[:6]:
        copy.wait()
    first = lax.broadcasted_iota(jnp.int32, (rows, LANES), 1) < HEAD

    def back(block, carry):
        slot = block % 2
        at = block_rows(block)
        for copy in block_copies(block, slot):
            copy.wait()

        @pl.when(block + 1 < blocks)
        def _():
            for copy in block_copies(block + 1, 1 - slot):
                copy.start()

        pl.when(block == blocks // 2)(grad_swap.wait_recv)
        pl.when(block >= 2)(lambda: score_copy(block - 2, slot).wait())
        dispatch(block_slots, block, 0, blocks)
        side = block // (blocks // 2)
        local = rows_at((block % (blocks // 2)) * rows, rows)
        grad_context = lax.dot_general(
            grad_buf[side, local, :],
            output_buf[...],
            (((1,), (1,)), ((), ())),
            preferred_element_type=f32,
        )
        scaled = (grad_context * inverse_buf[slot]).astype(bf16)
        for p in range(heads // 2):
            cols = slice(p * LANES, (p + 1) * LANES)
            grad = scaled[:, cols]
            product = grad.astype(f32) * context_buf[at, cols].astype(f32)
            query_turned = query_buf[at, cols].T
            grad_turned = grad.T
            grad_query = None
            for u in range(2):
                h = 2 * p + u
                half = slice(u * HEAD, (u + 1) * HEAD)
                own = first if u == 0 else ~first
                total = jnp.sum(jnp.where(own, product, 0.0), axis=1, keepdims=True)
                exps = ring_buf[slot, h]
                grad_exp = dot_f32(grad, value_buf[h])
                grad_score = (exps.astype(f32) * (grad_exp - total)).astype(bf16)
                ring_buf[2 + slot, h] = grad_score
                part = dot_f32(grad_score, key_buf[h])
                grad_query = part if u == 0 else grad_query + part
                grad_key_buf[h] += dot_f32(query_turned[half], grad_score)
                grad_value_buf[h] += dot_f32(grad_turned[half], exps)
            triple_buf[0, at, cols] = (grad_query * 0.125).astype(bf16)
        score_copy(block, slot).start()
        return carry

    lax.fori_loop(0, blocks, back, 0)

    score_copy(blocks - 2, blocks % 2).wait()
    score_copy(blocks - 1, (blocks - 1) % 2).wait()
    for block in range(2):
        for copy in ring_copies(block):
            copy.start()
    triple_buf[0, row_count:keys, :] = jnp.zeros((keys - row_count, width), bf16)
    for k, ref in ((1, grad_key_buf), (2, grad_value_buf)):
        for h in range(0, heads, 2):
            pair = ref[h : h + 2].reshape(LANES, keys)
            triple_buf[k, :, h * HEAD : (h + 2) * HEAD] = pair.T.astype(bf16)
    for copy in residents[7:]:
        copy.wait()
    tokens_in = (((0,), (0,)), ((), ()))
    places = ((0, 0), (0, width), (1, 0))
    for k, (chunk, start) in enumerate(places):
        own_buf[chunk, start : start + width, :] = lax.dot_general(
            triple_buf[k], token_buf[...], tokens_in, preferred_element_type=f32
        ).astype(bf16)
    own_buf[1, width : 2 * width, :] = (
        lax.dot_general(
            context_buf[mine, :], grad_buf[0], tokens_in, preferred_element_type=f32
        )
        + lax.dot_general(
            context_buf[others, :], grad_buf[1], tokens_in, preferred_element_type=f32
        )
    ).astype(bf16)
    exchange(0, 0)
    exchange(0, 1)
    for side in range(2):
        input_send_buf[input_rows(side), :] = input_product(side, 1 - mp_index).astype(bf16)
    input_swap.start()
    biases = jnp.concatenate(
        [
            jnp.sum(triple_buf[0].astype(f32), axis=0, keepdims=True),
            jnp.sum(triple_buf[2].astype(f32), axis=0, keepdims=True),
        ],
        axis=1,
    )

    def turn(n, carry):
        last = n * TABLE_STRIPS + TABLE_STRIPS - 1
        block = last // block_strips

        @pl.when(last % block_strips < TABLE_STRIPS)
        def _():
            for copy in ring_copies(block):
                copy.wait()

            @pl.when(block + 2 < blocks)
            def _():
                for copy in ring_copies(block + 2):
                    copy.start()

        dispatch(turn_slots, n, 0, turns)

        def refs_at(strip):
            slot = (strip // block_strips) % 4
            at = rows_at((strip % block_strips) * STRIP, STRIP)
            return (
                lambda h, cols: ring_buf[slot, h, at, cols],
                lambda cols: plane_buf[slot, at, cols],
                lambda cols: down_buf[slot, at, cols],
            )

        table_strips(
            [refs_at(n * TABLE_STRIPS + k) for k in range(TABLE_STRIPS)],
            sum_ref,
            heads,
            keys,
            high_counts,
        )
        return carry

    lax.fori_loop(0, turns, turn, 0)

    table_rows = sum(high_counts) * heads
    table_finish(sum_ref, table_buf.at[0], table_rows)
    lanes = table_buf.shape[2]
    pieces = 2 * width // lanes
    for n in range(pieces):
        table_buf[0, table_rows + n : table_rows + n + 1, :] = biases[:, n * lanes : (n + 1) * lanes]
    spare = table_buf.shape[1] - table_rows - pieces
    table_buf[0, table_rows + pieces :, :] = jnp.zeros((spare, lanes), f32)
    table_devices = tuple(partner_of.values())

    def table_hop(n):
        return remote(
            table_buf.at[n],
            table_recv_buf.at[n],
            table_send_sem.at[n],
            table_recv_sem.at[n],
            table_devices[n],
        )

    def table_step(n):
        if n > 0:
            table_hop(n - 1).wait_recv()
            table_buf[n] = table_buf[n - 1] + table_recv_buf[n - 1]
        if n < 4:
            table_hop(n).start()

    table_step(0)
    rest = turn_slots[turns]
    for n, (event, which) in enumerate(rest):
        if n % 3 == 2 and n // 3 < 4:
            table_step(n // 3 + 1)
        run(event, which)
    for n in range(min(len(rest) // 3, 4), 4):
        table_step(n + 1)
    table_ref[...] = table_buf[4]

    layer_arrival.wait_recv()
    layer_keep.wait()
    grad_swap.wait_send()
    input_swap.wait_send()
    layer_swap.wait_send()
    for side in range(2):
        input_store(side).wait()
    for n in range(5):
        small_hop(n).wait_send()
    for n in range(4):
        table_hop(n).wait_send()
    for chunk in range(CHUNKS):
        for level in range(4):
            scatter(chunk, level).wait_send()
            gather(chunk, level).wait_send()
        if is_away(chunk):
            scatter_away(chunk, 0).wait_send()
            scatter_away(chunk, 1).wait_send()
            hand_over(chunk).wait_send()


def finish(
    exps,
    inverse,
    plane,
    down,
    context,
    query,
    tokens,
    grad,
    layer,
    value_turned,
    key_wide,
    project_weight,
    output_weight,
    expand,
    reduce,
    small,
    counts,
):
    heads, row_count, keys = exps.shape
    width = heads * HEAD
    depth = tokens.shape[1]
    half_rows = row_count // 2
    high_counts = (counts[0] // 16, counts[1] // 16, counts[1] // 16)
    high_rows = sum(high_counts) * heads
    low_lanes = 16 * STRIP
    table_shape = (round_up(high_rows + 2 * width // low_lanes, 8), low_lanes)
    away = CHUNKS - LOCAL_CHUNKS
    anywhere = pl.BlockSpec(memory_space=pl.ANY)
    in_vmem = pl.BlockSpec(memory_space=pltpu.VMEM)
    dma = pltpu.SemaphoreType.DMA
    total, layer_full, input_full, small_sum, table_sum, _ = pl.pallas_call(
        partial(finish_kernel, high_counts=high_counts),
        in_specs=[anywhere] * 18,
        out_specs=[anywhere, anywhere, anywhere, in_vmem, in_vmem, anywhere],
        out_shape=[
            jax.ShapeDtypeStruct((CHUNKS * CHUNK, CHUNK), bf16),
            jax.ShapeDtypeStruct((row_count, depth), bf16),
            jax.ShapeDtypeStruct((row_count, width), f32),
            jax.ShapeDtypeStruct(small.shape, f32),
            jax.ShapeDtypeStruct(table_shape, f32),
            jax.ShapeDtypeStruct(exps.shape, bf16),
        ],
        scratch_shapes=[
            pltpu.VMEM(output_weight.shape, bf16),
            pltpu.VMEM((2, half_rows, depth), bf16),
            pltpu.VMEM(value_turned.shape, bf16),
            pltpu.VMEM(key_wide.shape, bf16),
            pltpu.VMEM(context.shape, bf16),
            pltpu.VMEM(query.shape, bf16),
            pltpu.VMEM(tokens.shape, bf16),
            pltpu.VMEM(project_weight.shape, bf16),
            pltpu.VMEM((4, heads, BACK_ROWS, keys), bf16),
            pltpu.VMEM((2, BACK_ROWS, width), f32),
            pltpu.VMEM((heads, HEAD, keys), f32),
            pltpu.VMEM((heads, HEAD, keys), f32),
            pltpu.VMEM((3, keys, width), bf16),
            pltpu.VMEM((row_count, width), bf16),
            pltpu.VMEM((row_count, width), bf16),
            pltpu.VMEM((2, half_rows, width), f32),
            pltpu.VMEM((4, BACK_ROWS, keys), jnp.int16),
            pltpu.VMEM((4, BACK_ROWS, keys), jnp.int16),
            pltpu.VMEM((high_rows * STRIP, low_lanes), f32),
            pltpu.VMEM((CHUNKS, CHUNK, CHUNK), bf16),
            pltpu.VMEM((away, CHUNK, CHUNK), bf16),
            pltpu.VMEM((CHUNKS, PARTS[0], CHUNK), bf16),
            pltpu.VMEM((away, PARTS[0], CHUNK), bf16),
            pltpu.VMEM((CHUNKS, PARTS[1], CHUNK), bf16),
            pltpu.VMEM((away, PARTS[1], CHUNK), bf16),
            pltpu.VMEM((away, PARTS[1], CHUNK), bf16),
            pltpu.VMEM((CHUNKS, PARTS[2], CHUNK), bf16),
            pltpu.VMEM((CHUNKS, PARTS[3], CHUNK), bf16),
            pltpu.VMEM((6, *small.shape), f32),
            pltpu.VMEM((5, *small.shape), f32),
            pltpu.VMEM((5, *table_shape), f32),
            pltpu.VMEM((4, *table_shape), f32),
            dma((9,)),
            dma((2, 2)),
            dma((4, 3)),
            dma((CHUNKS, 2)),
            dma((CHUNKS,)),
            dma((5,)),
            dma((CHUNKS, 11)),
            dma((CHUNKS, 11)),
            dma((3,)),
            dma((3,)),
            dma((5,)),
            dma((5,)),
            dma((4,)),
            dma((4,)),
        ],
        compiler_params=pltpu.CompilerParams(
            vmem_limit_bytes=FINISH_VMEM, collective_id=0, has_side_effects=True
        ),
        name="finish",
    )(
        exps,
        inverse,
        plane,
        down,
        context,
        query,
        tokens,
        grad,
        layer,
        value_turned,
        key_wide,
        project_weight,
        output_weight,
        *expand,
        *reduce,
        small,
    )
    projects = total[: 3 * width].reshape(3, width, depth).transpose(0, 2, 1)
    outputs = total[3 * width : 2 * CHUNK]
    expands = jnp.concatenate([total[2 * CHUNK : 3 * CHUNK], total[3 * CHUNK : 4 * CHUNK]], axis=1)
    reduces = total[4 * CHUNK :]
    tables = table_result(table_sum[:high_rows], high_counts, heads)
    biases = table_sum[high_rows : high_rows + 2 * width // low_lanes].reshape(2, width)
    return layer_full, input_full, projects, outputs, expands, reduces, tables, biases, small_sum


def feed_kernel(
    context_ref,
    context_away_ref,
    token_ref,
    cotangent_ref,
    valid_ref,
    output_ref,
    output_away_ref,
    expand_ref,
    expand_away_ref,
    reduce_ref,
    reduce_away_ref,
    expand_bias_ref,
    vector_ref,
    layer_ref,
    grad_ref,
    expand_grad_ref,
    expand_grad_away_ref,
    reduce_grad_ref,
    reduce_grad_away_ref,
    vector_grad_ref,
    expand_bias_grad_ref,
    input_buf,
    norm_buf,
    hat_buf,
    inverse_buf,
    total_buf,
    reduced_buf,
    active_buf,
    slope_buf,
    before_buf,
    *,
    pieces,
    tiles,
):
    rows, width = token_ref.shape
    step = pl.program_id(0)
    piece = step % (2 * pieces)
    strip_rows = FEED_STRIP
    strips = rows // strip_rows

    def vector(n):
        return vector_ref[n : n + 1, :]

    def for_strips(body, sums):
        def run(n, carry):
            at = pl.ds(pl.multiple_of(n * strip_rows, STRIP), strip_rows)
            return tuple(
                old + jnp.sum(new.reshape(strip_rows // 8, 8, width), axis=0)
                for old, new in zip(carry, body(at))
            )

        start = tuple(jnp.zeros((8, width), f32) for _ in range(sums))
        done = lax.fori_loop(0, strips, run, start)
        return [jnp.sum(part, axis=0, keepdims=True) for part in done]

    def mean(values):
        return jnp.sum(values, axis=-1, keepdims=True) * (1.0 / width)

    @pl.when(step == 0)
    def _():
        vector_grad_ref[...] = jnp.zeros_like(vector_grad_ref)
        total_buf[...] = dot_f32(context_ref[...], output_ref[...]) + dot_f32(
            context_away_ref[...], output_away_ref[...]
        )

        def body(at):
            values = token_ref[at, :].astype(f32) + (total_buf[at, :] + vector(0))
            centered = values - mean(values)
            inverse = lax.rsqrt(mean(centered * centered) + norm_epsilon)
            hat = centered * inverse
            norm = hat * vector(1) + vector(2)
            hat_buf[at, :] = hat
            inverse_buf[at, :] = jnp.broadcast_to(inverse, (strip_rows, LANES))
            norm_buf[at, :] = norm
            input_buf[at, :] = norm.astype(bf16)
            total_buf[at, :] = norm + vector(3)
            return ()

        for_strips(body, 0)

    def forward(expand, reduce):
        for start, size in tiles:
            at = slice(start, start + size)
            before = dot_f32(input_buf[at, :], expand[...]) + expand_bias_ref[0]
            phi = 0.5 * lax.erf(before * 0.7071067811865476) + 0.5
            slope_buf[piece, at, :] = phi + before * (
                0.3989422804014327 * jnp.exp(-0.5 * (before * before))
            )
            active = (before * phi).astype(bf16)
            active_buf[piece, at, :] = active
            total_buf[at, :] += dot_f32(active, reduce[...])

    pl.when(step < pieces)(lambda: forward(expand_ref, reduce_ref))
    pl.when((step >= pieces) & (step < 2 * pieces))(
        lambda: forward(expand_away_ref, reduce_away_ref)
    )

    @pl.when(step == 2 * pieces)
    def _():
        def body(at):
            values = total_buf[at, :]
            valid = valid_ref[at, :]
            centered = values - mean(values)
            inverse = lax.rsqrt(mean(centered * centered) + norm_epsilon)
            hat = centered * inverse
            layer_ref[at, :] = (valid * (hat * vector(4) + vector(5))).astype(bf16)
            grad_out = cotangent_ref[at, :].astype(f32) * valid
            grad_hat = grad_out * vector(4)
            mixed = inverse * (grad_hat - mean(grad_hat) - hat * mean(grad_hat * hat))
            low = mixed.astype(bf16)
            reduced_buf[at, :] = low
            total_buf[at, :] = mixed
            return grad_out * hat, grad_out, low.astype(f32)

        for n, part in enumerate(for_strips(body, 3)):
            vector_grad_ref[n : n + 1, :] = part

    def backward(expand, reduce):
        sums = None
        for start, size in tiles:
            at = slice(start, start + size)
            grad_active = lax.dot_general(
                reduced_buf[at, :], reduce[...], (((1,), (1,)), ((), ())), preferred_element_type=f32
            )
            before = (grad_active * slope_buf[piece, at, :]).astype(bf16)
            before_buf[piece, at, :] = before
            part = jnp.sum(before.astype(f32), axis=0, keepdims=True)
            sums = part if sums is None else sums + part
            total_buf[at, :] += lax.dot_general(
                before, expand[...], (((1,), (1,)), ((), ())), preferred_element_type=f32
            )
        expand_bias_grad_ref[0] = sums

    pl.when((step >= 2 * pieces) & (step < 3 * pieces))(lambda: backward(expand_ref, reduce_ref))
    pl.when((step >= 3 * pieces) & (step < 4 * pieces))(
        lambda: backward(expand_away_ref, reduce_away_ref)
    )

    @pl.when(step == 4 * pieces)
    def _():
        def body(at):
            grad_first = total_buf[at, :]
            hat = hat_buf[at, :]
            grad_hat = grad_first * vector(1)
            inverse = inverse_buf[at, 0:1]
            inner = inverse * (grad_hat - mean(grad_hat) - hat * mean(grad_hat * hat))
            low = inner.astype(bf16)
            grad_ref[at, :] = low
            return grad_first * hat, grad_first, low.astype(f32)

        for n, part in enumerate(for_strips(body, 3)):
            vector_grad_ref[n + 3 : n + 4, :] = part

    def weights(expand_grad, reduce_grad):
        reduce_grad[...] = lax.dot_general(
            active_buf[piece], reduced_buf[...], (((0,), (0,)), ((), ())), preferred_element_type=f32
        ).astype(bf16)
        expand_grad[...] = lax.dot_general(
            input_buf[...], before_buf[piece], (((0,), (0,)), ((), ())), preferred_element_type=f32
        ).astype(bf16)

    pl.when((step >= 4 * pieces) & (step < 5 * pieces))(
        lambda: weights(expand_grad_ref, reduce_grad_ref)
    )
    pl.when(step >= 5 * pieces)(lambda: weights(expand_grad_away_ref, reduce_grad_away_ref))


def feed(
    context,
    context_away,
    tokens,
    cotangent,
    valid,
    output,
    output_away,
    expand,
    expand_away,
    reduce,
    reduce_away,
    expand_biases,
    vectors,
):
    rows, width = tokens.shape
    hidden = expand.shape[1]
    size = FEED_PIECE
    pieces = hidden // size
    split = round_up(rows // 2, STRIP)
    tiles = ((0, split), (split, rows - split))

    def once(array):
        zeros = (0,) * array.ndim
        return pl.BlockSpec(array.shape, lambda i: zeros, pipeline_mode=pl.Buffered(1))

    def place(first, i):
        at = lax.rem(i, 2 * pieces) - first
        at = jnp.clip(at, 0, pieces - 1)
        return jnp.where(i < 4 * pieces, at, pieces - 1)

    def grad_place(first, i):
        return jnp.clip(i - 4 * pieces - first, 0, pieces - 1)

    wide = lambda first: pl.BlockSpec((width, size), lambda i: (0, place(first, i)))
    tall = lambda first: pl.BlockSpec((size, width), lambda i: (place(first, i), 0))
    wide_grad = lambda first: pl.BlockSpec((width, size), lambda i: (0, grad_place(first, i)))
    tall_grad = lambda first: pl.BlockSpec((size, width), lambda i: (grad_place(first, i), 0))
    bias_rows = expand_biases.reshape(2 * pieces, 1, size)
    whole = lambda shape: pl.BlockSpec(
        shape, lambda i: (0,) * len(shape), pipeline_mode=pl.Buffered(1)
    )
    full = jax.ShapeDtypeStruct((rows, width), bf16)
    return pl.pallas_call(
        partial(feed_kernel, pieces=pieces, tiles=tiles),
        grid=(6 * pieces,),
        in_specs=[
            once(context),
            once(context_away),
            once(tokens),
            once(cotangent),
            once(valid),
            once(output),
            once(output_away),
            wide(0),
            wide(pieces),
            tall(0),
            tall(pieces),
            pl.BlockSpec((1, 1, size), lambda i: (lax.rem(i, 2 * pieces), 0, 0)),
            once(vectors),
        ],
        out_specs=[
            whole((rows, width)),
            whole((rows, width)),
            wide_grad(0),
            wide_grad(pieces),
            tall_grad(0),
            tall_grad(pieces),
            whole((8, width)),
            pl.BlockSpec((1, 1, size), lambda i: (jnp.clip(i - 2 * pieces, 0, 2 * pieces - 1), 0, 0)),
        ],
        out_shape=[
            full,
            full,
            jax.ShapeDtypeStruct((width, hidden), bf16),
            jax.ShapeDtypeStruct((width, hidden), bf16),
            jax.ShapeDtypeStruct((hidden, width), bf16),
            jax.ShapeDtypeStruct((hidden, width), bf16),
            jax.ShapeDtypeStruct((8, width), f32),
            jax.ShapeDtypeStruct((2 * pieces, 1, size), f32),
        ],
        scratch_shapes=[
            pltpu.VMEM((rows, width), bf16),
            pltpu.VMEM((rows, width), f32),
            pltpu.VMEM((rows, width), f32),
            pltpu.VMEM((rows, LANES), f32),
            pltpu.VMEM((rows, width), f32),
            pltpu.VMEM((rows, width), bf16),
            pltpu.VMEM((2 * pieces, rows, size), bf16),
            pltpu.VMEM((2 * pieces, rows, size), f32),
            pltpu.VMEM((2 * pieces, rows, size), bf16),
        ],
        compiler_params=pltpu.CompilerParams(vmem_limit_bytes=vmem_limit),
        name="feed",
    )(
        context,
        context_away,
        tokens,
        cotangent,
        valid,
        output,
        output_away,
        expand,
        expand_away,
        reduce,
        reduce_away,
        bias_rows,
        vectors,
    )


def swap(array):
    return lax.ppermute(array, "mp", [(0, 1), (1, 0)])


def partner(array, count, bit):
    return lax.ppermute(array, "dp", [(i, i ^ bit) for i in range(count)])


def other_share(array, count):
    core = lax.axis_index("dp") % 2
    half = array.shape[0] // 2
    fetched = swap(lax.dynamic_slice_in_dim(array, core * half, half, 0))
    handed = partner(fetched, count, 1)
    even = core == 0
    return jnp.concatenate(
        [jnp.where(even, fetched, handed), jnp.where(even, handed, fetched)], axis=0
    )


def sum_rows_over_dp(array, count):
    place = lax.axis_index("dp")
    bits = []
    bit = 1
    while bit < count:
        mine = (place // bit) % 2
        halves = array.reshape((2, array.shape[0] // 2) + array.shape[1:])
        sent = lax.dynamic_index_in_dim(halves, 1 - mine, 0, keepdims=False)
        kept = lax.dynamic_index_in_dim(halves, mine, 0, keepdims=False)
        array = kept + partner(sent, count, bit)
        bits.append(bit)
        bit *= 2
    for bit in reversed(bits):
        lead = (place // bit) % 2 == 0
        other = partner(array, count, bit)
        array = jnp.concatenate(
            [jnp.where(lead, array, other), jnp.where(lead, other, array)], axis=0
        )
    return array


def sum_small(arrays, count, over_mp):
    sizes = [a.size for a in arrays]
    total = sum(sizes)
    flat = jnp.concatenate([a.reshape(-1) for a in arrays])
    flat = jnp.pad(flat, (0, round_up(total, 1024) - total)).reshape(-1, LANES)
    if over_mp:
        flat = flat + swap(flat)
    bit = 1
    while bit < count:
        flat = flat + partner(flat, count, bit)
        bit *= 2
    flat = flat.reshape(-1)
    outs = []
    start = 0
    for array, size in zip(arrays, sizes):
        outs.append(flat[start : start + size].reshape(array.shape))
        start += size
    return outs


def per_device(
    dp_count,
    tokens,
    cotangent,
    long_flag,
    token_mask,
    bucket_line,
    bucket_across,
    bucket_down,
    project_weight,
    project_bias,
    table_line,
    table_across,
    table_down,
    output_weight,
    output_bias,
    first_gain,
    first_shift,
    expand_weight,
    expand_bias,
    reduce_weight,
    reduce_bias,
    second_gain,
    second_shift,
):
    length = tokens.shape[1]
    width = project_weight.shape[2]
    heads = table_line.shape[1]
    counts = (table_line.shape[0], table_across.shape[0])
    rows = round_up(length, BLOCK_ROWS)
    half_rows = rows // 2
    keys = round_up(length, 3 * LANES)
    mp_index = lax.axis_index("mp")
    lead = mp_index == 0

    def own_rows(array):
        return lax.dynamic_slice_in_dim(array, mp_index * half_rows, half_rows, 0)

    def other_rows(array):
        return lax.dynamic_slice_in_dim(array, (1 - mp_index) * half_rows, half_rows, 0)

    def in_order(mine, other):
        return jnp.where(lead, mine, other), jnp.where(lead, other, mine)

    output_other = other_share(output_weight, dp_count)
    expand_other = other_share(expand_weight, dp_count)
    reduce_other = other_share(reduce_weight, dp_count)
    expand_bias_other = swap(expand_bias)

    positions = jnp.arange(length, dtype=jnp.int32)
    limit = jnp.where(long_flag[0] > 0, LONG, SHORT).astype(jnp.int32)
    valid = (token_mask[0] > 0) & (positions < limit)
    valid_rows = own_rows(jnp.pad(valid.astype(f32), (0, rows - length)))[:, None]
    grow = ((0, rows - length), (0, keys - length))
    line = jnp.where(valid[None, :], bucket_line[0], bucket_line[0] + counts[0])
    plane = jnp.pad(
        (line | (bucket_across[0] << 8)).astype(jnp.int16), grow, constant_values=counts[0]
    )
    down = jnp.pad(bucket_down[0].astype(jnp.int16), grow)
    tables = []
    for table in (table_line, table_across, table_down):
        lanes = jnp.pad(
            table.T, ((0, 0), (0, LANES - table.shape[0])), constant_values=large_negative
        )
        tables.append(jnp.broadcast_to(lanes[:, None, :], (heads, STRIP, LANES)))
    tables = jnp.concatenate(tables).astype(bf16)

    query, key_wide, key_turned, value_ones, value_turned = project(
        tokens[0], project_weight, project_bias.astype(f32), keys
    )
    exps, context, inverse = attend(query, key_turned, value_ones, plane, down, tables)

    context_other = swap(other_rows(context))
    padded = jnp.pad(tokens[0], ((0, keys - length), (0, 0)))
    vectors = jnp.stack(
        [
            output_bias.astype(f32),
            first_gain,
            first_shift,
            reduce_bias.astype(f32),
            second_gain,
            second_shift,
            second_shift,
            second_shift,
        ]
    )
    expand_biases = jnp.concatenate([expand_bias, expand_bias_other]).astype(f32)
    (
        layer_mine,
        grad_mine,
        expand_own,
        expand_sent,
        reduce_own,
        reduce_sent,
        vector_grads,
        expand_bias_grads,
    ) = feed(
        own_rows(context),
        context_other,
        own_rows(padded),
        own_rows(jnp.pad(cotangent[0], ((0, rows - length), (0, 0)))),
        valid_rows,
        output_weight,
        output_other,
        expand_weight,
        expand_other,
        reduce_weight,
        reduce_other,
        expand_biases,
        vectors,
    )
    expand_bias_grads = expand_bias_grads.reshape(2, -1)
    ordered_biases = in_order(expand_bias_grads[0], expand_bias_grads[1])
    if dp_count == 16 and expand_own.shape == (CHUNK, 2 * CHUNK):
        bias_rows = jnp.concatenate(ordered_biases).reshape(-1, tokens.shape[2])
        small = jnp.concatenate([vector_grads, jnp.pad(bias_rows, ((0, 4), (0, 0)))])
        (
            layer_full,
            input_full,
            project_weight_grad,
            output_weight_grad,
            expand_weight_grad,
            reduce_weight_grad,
            table_grads,
            project_bias_grad,
            small,
        ) = finish(
            exps,
            inverse,
            plane,
            down,
            context,
            query,
            padded,
            grad_mine,
            layer_mine,
            value_turned,
            key_wide,
            project_weight,
            output_weight,
            (expand_own, expand_sent),
            (reduce_own, reduce_sent),
            small,
            counts,
        )
        layer_out = layer_full[None, :length]
        input_grad = input_full[None, :length]
        vector_grads = small[:8]
        expand_bias_grad = jnp.where(lead, small[8:10], small[10:12]).reshape(-1)
    else:
        layer_out = jnp.concatenate(in_order(layer_mine, swap(layer_mine)))[None, :length]
        grad_attended = jnp.concatenate(in_order(grad_mine, swap(grad_mine)))
        output_weight_grad = jnp.einsum(
            "le,lf->ef", context, grad_attended, preferred_element_type=f32
        ).astype(bf16)
        grad_context = jnp.einsum(
            "lf,ef->le", grad_attended, output_weight, preferred_element_type=f32
        )
        grad_scaled = (grad_context * inverse).astype(bf16)
        grad_scores, grad_query, grad_key, grad_value = attend_back(
            exps, grad_scaled, context, query, value_turned, key_wide
        )
        grad_key = grad_key.reshape(width, keys)[:, :rows].T.astype(bf16)
        grad_value = grad_value.reshape(width, keys)[:, :rows].T.astype(bf16)
        triple = jnp.stack([grad_query, grad_key, grad_value])
        project_weight_grad = jnp.einsum(
            "ld,kle->kde", padded[:rows], triple, preferred_element_type=f32
        ).astype(bf16)
        project_bias_grad = jnp.stack(
            [jnp.sum(grad_query, axis=0, dtype=f32), jnp.sum(grad_value, axis=0, dtype=f32)]
        )
        input_part = jnp.einsum("kle,kde->ld", triple, project_weight, preferred_element_type=f32)
        input_part = lax.dynamic_update_slice_in_dim(
            input_part,
            own_rows(input_part) + grad_mine.astype(f32),
            mp_index * half_rows,
            0,
        )
        sent = jnp.where(lead, input_part[:, width:], input_part[:, :width]).astype(bf16)
        own = jnp.where(lead, input_part[:, :width], input_part[:, width:])
        input_grad = (own + swap(sent).astype(f32))[None, :length]
        table_grads = table_sums(grad_scores, plane, down, counts)
        reduce_weight_grad = sum_rows_over_dp(reduce_own + swap(reduce_sent), dp_count)
        expand_weight_grad = sum_rows_over_dp(expand_own + swap(expand_sent), dp_count)
        output_weight_grad = sum_rows_over_dp(output_weight_grad, dp_count)
        project_weight_grad = sum_rows_over_dp(
            project_weight_grad.reshape(-1, width), dp_count
        ).reshape(project_weight.shape)
        vector_grads, even_biases, odd_biases = sum_small(
            [vector_grads, *ordered_biases], dp_count, True
        )
        expand_bias_grad = jnp.where(lead, even_biases, odd_biases)
        table_grads, project_bias_grad = sum_small(
            [table_grads, project_bias_grad], dp_count, False
        )
    (
        second_gain_grad,
        second_shift_grad,
        reduce_bias_grad,
        first_gain_grad,
        first_shift_grad,
        output_bias_grad,
    ) = (vector_grads[n] for n in range(6))
    mine = mp_index * width
    return (
        layer_out,
        input_grad,
        project_weight_grad.astype(f32),
        project_bias_grad,
        table_grads[: counts[0]],
        table_grads[counts[0] : counts[0] + counts[1]],
        table_grads[counts[0] + counts[1] :],
        output_weight_grad.astype(f32),
        output_bias_grad,
        lax.dynamic_slice_in_dim(first_gain_grad, mine, width, 0),
        lax.dynamic_slice_in_dim(first_shift_grad, mine, width, 0),
        expand_weight_grad.astype(f32),
        expand_bias_grad,
        reduce_weight_grad.astype(f32),
        reduce_bias_grad,
        second_gain_grad,
        second_shift_grad,
    )


def solution(mesh):
    placed = (
        P("dp", None, None),
        P("dp", None, None),
        P("dp"),
        P("dp", None),
        P("dp", None, None),
        P("dp", None, None),
        P("dp", None, None),
        P(None, None, "mp"),
        P(None, "mp"),
        P(None, "mp"),
        P(None, "mp"),
        P(None, "mp"),
        P("mp", None),
        P(),
        P(),
        P(),
        P(None, "mp"),
        P("mp"),
        P("mp", None),
        P(),
        P(),
        P(),
    )
    return jax.shard_map(
        partial(per_device, mesh.shape["dp"]),
        mesh=mesh,
        in_specs=placed,
        out_specs=(
            P("dp", None, None),
            P("dp", None, "mp"),
            P(None, None, "mp"),
            P(None, "mp"),
            P(None, "mp"),
            P(None, "mp"),
            P(None, "mp"),
            P("mp", None),
            P(),
            P("mp"),
            P("mp"),
            P(None, "mp"),
            P("mp"),
            P("mp", None),
            P(),
            P(),
            P(),
        ),
        check_vma=False,
    )
```

```python
from functools import partial

import jax
import jax.numpy as jnp
from jax import lax
from jax.experimental import pallas as pl
from jax.experimental.pallas import tpu as pltpu
from jax.sharding import PartitionSpec as P

LONG = 1089
SHORT = 709
HEAD = 64
LANES = 128
STRIP = 16
BLOCK_ROWS = 224
FEED_PIECE = 768
FEED_STRIP = 112
TABLE_STRIPS = 2
ATTEND_STRIPS = 7

large_negative = -1000000000.0
norm_epsilon = 1e-05
vmem_limit = 56 * 2**20
FINISH_VMEM = 62 * 2**20
bf16 = jnp.bfloat16
f32 = jnp.float32


def round_up(value, step):
    return (value + step - 1) // step * step


def whole_spec(array):
    zeros = (0,) * array.ndim
    return pl.BlockSpec(array.shape, lambda i: zeros)


def dot_f32(left, right):
    return jnp.dot(left, right, preferred_element_type=f32)


def gather_lanes(values, index):
    dims = lax.GatherDimensionNumbers(
        offset_dims=(),
        collapsed_slice_dims=(1,),
        start_index_map=(1,),
        operand_batching_dims=(0,),
        start_indices_batching_dims=(0,),
    )
    return lax.gather(
        values,
        index[..., None],
        dims,
        slice_sizes=(1, 1),
        mode=lax.GatherScatterMode.PROMISE_IN_BOUNDS,
    )


def project_kernel(
    token_ref, weight_ref, bias_ref, query_ref, key_ref, key_turned_ref, value_ref, value_turned_ref, *, length
):
    rows = token_ref.shape[0]
    place = pl.program_id(0) * rows + lax.broadcasted_iota(jnp.int32, token_ref.shape, 0)
    token = jnp.where(place < length, token_ref[...].astype(f32), 0.0).astype(bf16)
    query = (dot_f32(token, weight_ref[0]) + bias_ref[0:1, :]).astype(bf16)
    query_ref[...] = (query.astype(f32) * 0.125).astype(bf16)
    key = dot_f32(token, weight_ref[1])
    value = dot_f32(token, weight_ref[2]) + bias_ref[1:2, :]
    lane_first = lax.broadcasted_iota(jnp.int32, (rows, LANES), 1) < HEAD
    row_first = lax.broadcasted_iota(jnp.int32, (LANES, rows), 0) < HEAD
    for p in range(key.shape[1] // LANES):
        cols = slice(p * LANES, (p + 1) * LANES)
        key_pair, value_pair = key[:, cols], value[:, cols]
        key_turned, value_turned = key_pair.T, value_pair.T
        for u in range(2):
            h = 2 * p + u
            lane_own = lane_first if u == 0 else ~lane_first
            row_own = row_first if u == 0 else ~row_first
            key_ref[h] = jnp.where(lane_own, key_pair, 0.0).astype(bf16)
            value_ref[h] = jnp.where(lane_own, value_pair, 1.0).astype(bf16)
            key_turned_ref[h] = jnp.where(row_own, key_turned, 0.0).astype(bf16)
            value_turned_ref[h] = jnp.where(row_own, value_turned, 0.0).astype(bf16)


def project(tokens, weight, bias, keys):
    length, depth = tokens.shape
    width = weight.shape[2]
    heads = width // HEAD
    block = 3 * LANES
    wide = pl.BlockSpec((heads, block, LANES), lambda i: (0, i, 0))
    turned = pl.BlockSpec((heads, LANES, block), lambda i: (0, 0, i))
    wide_shape = jax.ShapeDtypeStruct((heads, keys, LANES), bf16)
    turned_shape = jax.ShapeDtypeStruct((heads, LANES, keys), bf16)
    return pl.pallas_call(
        partial(project_kernel, length=length),
        grid=(keys // block,),
        in_specs=[
            pl.BlockSpec((block, depth), lambda i: (i, 0)),
            whole_spec(weight),
            whole_spec(bias),
        ],
        out_specs=[pl.BlockSpec((block, width), lambda i: (i, 0)), wide, turned, wide, turned],
        out_shape=[
            jax.ShapeDtypeStruct((keys, width), bf16),
            wide_shape,
            turned_shape,
            wide_shape,
            turned_shape,
        ],
        compiler_params=pltpu.CompilerParams(vmem_limit_bytes=vmem_limit),
        name="project",
    )(tokens, weight, bias)


def attend_kernel(
    query_ref,
    key_ref,
    value_ref,
    plane_ref,
    down_ref,
    table_ref,
    exp_ref,
    context_ref,
    inverse_ref,
    context_away_ref,
    score_ref,
    send_ref,
    send_sem,
    recv_sem,
):
    heads, rows, keys = exp_ref.shape
    step = pl.program_id(0)
    across_mp = {"mp": 1 - lax.axis_index("mp")}

    @pl.when(step == 0)
    def _():
        barrier = pltpu.get_barrier_semaphore()
        pl.semaphore_signal(
            barrier, inc=1, device_id=across_mp, device_id_type=pl.DeviceIdType.MESH
        )
        pl.semaphore_wait(barrier, 1)

    context_swap = pltpu.make_async_remote_copy(
        src_ref=send_ref,
        dst_ref=context_away_ref,
        send_sem=send_sem,
        recv_sem=recv_sem,
        device_id=across_mp,
        device_id_type=pl.DeviceIdType.MESH,
    )
    for h in range(heads):
        pair = slice(h // 2 * LANES, (h // 2 + 1) * LANES)
        score_ref[h] = dot_f32(query_ref[:, pair], key_ref[h])

    lanes = [slice(c * LANES, (c + 1) * LANES) for c in range(keys // LANES)]

    def scores_of(at):
        scores = [[] for _ in range(heads)]
        for cols in lanes:
            packed = plane_ref[at, cols]
            bias = [None] * heads
            for t, index in enumerate(
                (packed & jnp.int16(255), packed >> jnp.int16(8), down_ref[at, cols])
            ):
                for h in range(heads):
                    found = gather_lanes(table_ref[t * heads + h], index).astype(f32)
                    bias[h] = found if t == 0 else bias[h] + found
            for h in range(heads):
                scores[h].append(score_ref[h, at, cols] + bias[h])
        return scores

    def exps_of(scores):
        exps = []
        for parts in scores:
            top = parts[0]
            for part in parts[1:]:
                top = jnp.maximum(top, part)
            top = jnp.max(top, axis=1, keepdims=True)
            exps.append([jnp.exp(part - top).astype(bf16) for part in parts])
        return exps

    def strips(n, carry):
        start = pl.multiple_of(n * ATTEND_STRIPS * STRIP, STRIP)
        places = [pl.ds(start + k * STRIP, STRIP) for k in range(ATTEND_STRIPS)]
        scores = [scores_of(at) for at in places]
        exps = [exps_of(part) for part in scores]
        for at, part in zip(places, exps):
            for h in range(heads):
                for c, cols in enumerate(lanes):
                    exp_ref[h, at, cols] = part[h][c]
        return carry

    lax.fori_loop(0, rows // (ATTEND_STRIPS * STRIP), strips, 0)
    first = lax.broadcasted_iota(jnp.int32, (rows, LANES), 1) < HEAD
    for p in range(heads // 2):
        cols = slice(p * LANES, (p + 1) * LANES)
        even = dot_f32(exp_ref[2 * p], value_ref[2 * p])
        odd = dot_f32(exp_ref[2 * p + 1], value_ref[2 * p + 1])
        sums = jnp.where(first, pltpu.roll(even, HEAD, 1), pltpu.roll(odd, HEAD, 1))
        inverse = 1.0 / sums
        inverse_ref[:, cols] = inverse
        context = (jnp.where(first, even, odd) * inverse).astype(bf16)
        context_ref[:, cols] = context

        @pl.when(step == 0)
        def _():
            send_ref[:, cols] = context

    pl.when(step == 0)(context_swap.start)
    pl.when(step == 1)(context_swap.wait)


def attend(query, key_turned, value_ones, plane, down, tables):
    heads, _, keys = key_turned.shape
    row_count = plane.shape[0]
    width = heads * HEAD
    half_rows = row_count // 2

    def half(i):
        return lax.rem(i + 1 - lax.axis_index("mp"), 2)

    index_spec = pl.BlockSpec((half_rows, keys), lambda i: (half(i), 0))
    row_spec = pl.BlockSpec((half_rows, width), lambda i: (half(i), 0))
    return pl.pallas_call(
        attend_kernel,
        grid=(2,),
        in_specs=[
            row_spec,
            whole_spec(key_turned),
            whole_spec(value_ones),
            index_spec,
            index_spec,
            whole_spec(tables),
        ],
        out_specs=[
            pl.BlockSpec((heads, half_rows, keys), lambda i: (0, half(i), 0)),
            row_spec,
            row_spec,
            pl.BlockSpec(memory_space=pl.ANY),
        ],
        out_shape=[
            jax.ShapeDtypeStruct((heads, row_count, keys), bf16),
            jax.ShapeDtypeStruct((row_count, width), bf16),
            jax.ShapeDtypeStruct((row_count, width), f32),
            jax.ShapeDtypeStruct((half_rows, width), bf16),
        ],
        scratch_shapes=[
            pltpu.VMEM((heads, half_rows, keys), f32),
            pltpu.VMEM((half_rows, width), bf16),
            pltpu.SemaphoreType.DMA,
            pltpu.SemaphoreType.DMA,
        ],
        compiler_params=pltpu.CompilerParams(
            vmem_limit_bytes=vmem_limit, collective_id=1, has_side_effects=True
        ),
        name="attend",
    )(query, key_turned, value_ones, plane, down, tables)


def attend_back_kernel(
    exp_ref,
    grad_ref,
    context_ref,
    query_ref,
    value_ref,
    key_ref,
    grad_score_ref,
    grad_query_ref,
    grad_key_ref,
    grad_value_ref,
):
    heads, rows, _ = exp_ref.shape

    @pl.when(pl.program_id(0) == 0)
    def _():
        grad_key_ref[...] = jnp.zeros_like(grad_key_ref)
        grad_value_ref[...] = jnp.zeros_like(grad_value_ref)

    first = lax.broadcasted_iota(jnp.int32, (rows, LANES), 1) < HEAD
    for p in range(heads // 2):
        cols = slice(p * LANES, (p + 1) * LANES)
        grad = grad_ref[:, cols]
        product = grad.astype(f32) * context_ref[:, cols].astype(f32)
        query_turned = query_ref[:, cols].T
        grad_turned = grad.T
        grad_query = None
        for u in range(2):
            h = 2 * p + u
            half = slice(u * HEAD, (u + 1) * HEAD)
            own = first if u == 0 else ~first
            total = jnp.sum(jnp.where(own, product, 0.0), axis=1, keepdims=True)
            grad_exp = dot_f32(grad, value_ref[h])
            grad_score = (exp_ref[h].astype(f32) * (grad_exp - total)).astype(bf16)
            grad_score_ref[h] = grad_score
            part = dot_f32(grad_score, key_ref[h])
            grad_query = part if u == 0 else grad_query + part
            grad_key_ref[h] += dot_f32(query_turned[half], grad_score)
            grad_value_ref[h] += dot_f32(grad_turned[half], exp_ref[h])
        grad_query_ref[:, cols] = (grad_query * 0.125).astype(bf16)


def attend_back(exps, grad, context, query, value_turned, key_wide):
    heads, row_count, keys = exps.shape
    width = heads * HEAD
    row_spec = pl.BlockSpec((BLOCK_ROWS, width), lambda i: (i, 0))
    exp_spec = pl.BlockSpec((heads, BLOCK_ROWS, keys), lambda i: (0, i, 0))
    sum_spec = pl.BlockSpec((heads, HEAD, keys), lambda i: (0, 0, 0))
    return pl.pallas_call(
        attend_back_kernel,
        grid=(row_count // BLOCK_ROWS,),
        in_specs=[
            exp_spec,
            row_spec,
            row_spec,
            row_spec,
            whole_spec(value_turned),
            whole_spec(key_wide),
        ],
        out_specs=[exp_spec, row_spec, sum_spec, sum_spec],
        out_shape=[
            jax.ShapeDtypeStruct((heads, row_count, keys), bf16),
            jax.ShapeDtypeStruct((row_count, width), bf16),
            jax.ShapeDtypeStruct((heads, HEAD, keys), f32),
            jax.ShapeDtypeStruct((heads, HEAD, keys), f32),
        ],
        compiler_params=pltpu.CompilerParams(vmem_limit_bytes=vmem_limit),
        name="attend_back",
    )(exps, grad, context, query, value_turned, key_wide)


def table_strips(strips, sum_ref, heads, keys, high_counts):
    base = 0
    for t in range(3):
        shift = 8 if t == 1 else 0
        highs, lows = [], []
        for grad_of, plane_of, down_of in strips:
            for c in range(keys // LANES):
                cols = slice(c * LANES, (c + 1) * LANES)
                index = down_of(cols) if t == 2 else plane_of(cols)
                low = index & jnp.int16(15 << shift)
                high = index & jnp.int16(48 << shift)
                lows.append(
                    jnp.concatenate(
                        [
                            jnp.where(low == jnp.int16(x << shift), bf16(1), bf16(0))
                            for x in range(16)
                        ]
                    )
                )
                parts = []
                for x in range(high_counts[t]):
                    mask = high == jnp.int16(x << (4 + shift))
                    parts += [jnp.where(mask, grad_of(h, cols), bf16(0)) for h in range(heads)]
                highs.append(jnp.concatenate(parts))
        span = slice(base, base + high_counts[t] * heads * STRIP)
        sum_ref[span, :] += lax.dot_general(
            jnp.concatenate(highs, axis=1),
            jnp.concatenate(lows, axis=1),
            (((1,), (1,)), ((), ())),
            preferred_element_type=f32,
        )
        base = span.stop


def table_finish(sum_ref, out_ref, count):
    row_of_lane = lax.broadcasted_iota(jnp.int32, (STRIP, 16 * STRIP), 1) % STRIP
    same = row_of_lane == lax.broadcasted_iota(jnp.int32, (STRIP, 16 * STRIP), 0)
    for o in range(count):
        block = sum_ref[o * STRIP : (o + 1) * STRIP, :]
        out_ref[o : o + 1, :] = jnp.sum(jnp.where(same, block, 0.0), axis=0, keepdims=True)


def table_result(out, high_counts, heads):
    summed = jnp.sum(out.reshape(sum(high_counts), heads, 16, STRIP), axis=-1)
    return summed.transpose(0, 2, 1).reshape(-1, heads)


def table_kernel(grad_score_ref, plane_ref, down_ref, out_ref, sum_ref, *, high_counts):
    heads, rows, keys = grad_score_ref.shape
    step = pl.program_id(0)

    @pl.when(step == 0)
    def _():
        sum_ref[...] = jnp.zeros_like(sum_ref)

    def refs_at(start):
        at = pl.ds(pl.multiple_of(start, STRIP), STRIP)
        return (
            lambda h, cols: grad_score_ref[h, at, cols],
            lambda cols: plane_ref[at, cols],
            lambda cols: down_ref[at, cols],
        )

    def strips(r, carry):
        start = r * (TABLE_STRIPS * STRIP)
        table_strips(
            [refs_at(start + k * STRIP) for k in range(TABLE_STRIPS)],
            sum_ref,
            heads,
            keys,
            high_counts,
        )
        return carry

    lax.fori_loop(0, rows // (TABLE_STRIPS * STRIP), strips, 0)

    @pl.when(step == pl.num_programs(0) - 1)
    def _():
        table_finish(sum_ref, out_ref, out_ref.shape[0])


def table_sums(grad_scores, plane, down, counts):
    heads, row_count, keys = grad_scores.shape
    high_counts = (counts[0] // 16, counts[1] // 16, counts[1] // 16)
    high_rows = sum(high_counts) * heads
    index_spec = pl.BlockSpec((BLOCK_ROWS, keys), lambda i: (i, 0))
    out = pl.pallas_call(
        partial(table_kernel, high_counts=high_counts),
        grid=(row_count // BLOCK_ROWS,),
        in_specs=[
            pl.BlockSpec((heads, BLOCK_ROWS, keys), lambda i: (0, i, 0)),
            index_spec,
            index_spec,
        ],
        out_specs=pl.BlockSpec((high_rows, 16 * STRIP), lambda i: (0, 0)),
        out_shape=jax.ShapeDtypeStruct((high_rows, 16 * STRIP), f32),
        scratch_shapes=[pltpu.VMEM((high_rows * STRIP, 16 * STRIP), f32)],
        compiler_params=pltpu.CompilerParams(vmem_limit_bytes=vmem_limit),
        name="table_sums",
    )(grad_scores, plane, down)
    return table_result(out, high_counts, heads)


CHUNK = 768
CHUNKS = 6
LOCAL_CHUNKS = 2
PARTS = (CHUNK // 2, CHUNK // 4, CHUNK // 8, CHUNK // 16)
BITS = ((1, 2, 4, 8), (1, 4, 2, 8), (1, 2, 4, 8), (1, 4, 2, 8), (1, 2, 4, 8), (1, 4, 2, 8))
BACK_ROWS = 112
EXCHANGE = (
    ("b", 0, 0, 2), ("b", 0, 0, 3), ("b", 0, 0, 4), ("b", 1, 0, 5), ("b", 4, 1, 2), ("b", 6, 1, 3),
    ("b", 8, 1, 4), ("b", 9, 1, 5), ("b", 20, 2, 2), ("b", 22, 2, 3), ("p", 0, 3, 2), ("p", 2, 2, 4),
    ("p", 3, 2, 5), ("p", 3, 3, 3), ("p", 3, 0, 0), ("p", 3, 0, 1), ("t", 0, 4, 2), ("t", 1, 1, 0),
    ("t", 1, 1, 1), ("t", 2, 4, 3), ("t", 2, "small", 0), ("t", 3, 3, 4), ("t", 4, 5, 2),
    ("t", 5, "send", 0), ("t", 6, 3, 5), ("t", 6, 2, 0), ("t", 6, 2, 1), ("t", 6, "small", 1),
    ("t", 8, 5, 3), ("t", 9, 4, 4), ("t", 10, 4, 5), ("t", 11, 6, 2), ("t", 11, "small", 2),
    ("t", 12, 3, 1), ("t", 12, 3, 0), ("t", 13, 6, 3), ("t", 15, 5, 4), ("t", 16, "layer", 0),
    ("t", 16, "small", 3), ("t", 17, 5, 5), ("t", 17, 7, 3), ("t", 18, 7, 2), ("t", 18, "input", 0),
    ("t", 19, 4, 1), ("t", 19, 4, 0), ("t", 20, "small", 4), ("t", 21, 6, 4), ("t", 22, 8, 2),
    ("t", 23, 6, 5), ("t", 24, 9, 2), ("t", 25, "small", 5), ("t", 26, 8, 3), ("t", 27, 5, 1),
    ("t", 27, 7, 5), ("t", 28, 9, 3), ("t", 29, 5, 0), ("t", 29, 7, 4), ("t", 31, 6, 1),
    ("t", 33, 8, 5), ("e", 0, 9, 5), ("e", 0, 8, 4), ("e", 0, 6, 0), ("e", 0, 9, 4), ("e", 0, 7, 1),
    ("e", 0, 8, 1), ("e", 0, 7, 0), ("e", 0, 8, 0),
)


def plan_slots(phase, count):
    slots = [[] for _ in range(count)]
    for name, at, event, which in EXCHANGE:
        if name == phase:
            slots[at].append((event, which))
    return slots


def finish_kernel(
    exp_ref,
    inverse_ref,
    plane_ref,
    down_ref,
    context_ref,
    query_ref,
    token_ref,
    grad_ref,
    layer_ref,
    value_ref,
    key_ref,
    project_ref,
    output_ref,
    expand_ref,
    expand_away_ref,
    reduce_ref,
    reduce_away_ref,
    small_ref,
    total_ref,
    layer_out_ref,
    input_ref,
    small_out_ref,
    table_ref,
    score_ref,
    output_buf,
    grad_buf,
    value_buf,
    key_buf,
    context_buf,
    query_buf,
    token_buf,
    project_buf,
    ring_buf,
    inverse_buf,
    grad_key_buf,
    grad_value_buf,
    triple_buf,
    input_send_buf,
    input_recv_buf,
    input_buf,
    plane_buf,
    down_buf,
    sum_ref,
    own_buf,
    away_buf,
    core_buf,
    core_away_buf,
    first_buf,
    first_away_buf,
    y_buf,
    second_buf,
    third_buf,
    small_buf,
    small_recv_buf,
    table_buf,
    table_recv_buf,
    resident_sem,
    block_sem,
    ring_sem,
    load_sem,
    local_sem,
    out_sem,
    send_sem,
    recv_sem,
    wide_send_sem,
    wide_recv_sem,
    small_send_sem,
    small_recv_sem,
    table_send_sem,
    table_recv_sem,
    *,
    high_counts,
):
    heads, row_count, keys = exp_ref.shape
    width = heads * HEAD
    half_rows = row_count // 2
    rows = BACK_ROWS
    blocks = row_count // rows
    block_strips = rows // STRIP
    turns = row_count // (TABLE_STRIPS * STRIP)
    place = lax.axis_index("dp")
    mp_index = lax.axis_index("mp")
    side_of = {bit: (place // bit) % 2 for bit in (1, 2, 4, 8)}
    partner_of = {bit: {"dp": place + bit * (1 - 2 * side_of[bit])} for bit in (1, 2, 4, 8)}
    across_mp = {"mp": 1 - mp_index}

    barrier = pltpu.get_barrier_semaphore()
    for device in (*partner_of.values(), across_mp):
        pl.semaphore_signal(barrier, inc=1, device_id=device, device_id_type=pl.DeviceIdType.MESH)
    pl.semaphore_wait(barrier, 5)

    def rows_at(start, size):
        return pl.ds(pl.multiple_of(start, STRIP), size)

    def remote(src, dst, send, recv, device):
        return pltpu.make_async_remote_copy(
            src_ref=src,
            dst_ref=dst,
            send_sem=send,
            recv_sem=recv,
            device_id=device,
            device_id_type=pl.DeviceIdType.MESH,
        )

    mine = rows_at(mp_index * half_rows, half_rows)
    others = rows_at((1 - mp_index) * half_rows, half_rows)
    grad_swap = remote(
        grad_ref, grad_buf.at[1], wide_send_sem.at[0], wide_recv_sem.at[0], across_mp
    )
    input_swap = remote(
        input_send_buf, input_recv_buf, wide_send_sem.at[1], wide_recv_sem.at[1], across_mp
    )
    layer_swap = remote(
        layer_ref, layer_out_ref.at[mine, :], wide_send_sem.at[2], wide_recv_sem.at[2], across_mp
    )
    layer_arrival = remote(
        layer_out_ref.at[others, :],
        layer_out_ref.at[others, :],
        wide_send_sem.at[2],
        wide_recv_sem.at[2],
        across_mp,
    )
    layer_keep = pltpu.make_async_copy(layer_ref, layer_out_ref.at[mine, :], out_sem.at[2])
    grad_swap.start()

    residents = [
        pltpu.make_async_copy(src, dst, resident_sem.at[n])
        for n, (src, dst) in enumerate(
            (
                (grad_ref, grad_buf.at[0]),
                (output_ref, output_buf),
                (context_ref, context_buf),
                (query_ref, query_buf),
                (value_ref, value_buf),
                (key_ref, key_buf),
                (small_ref, small_buf.at[0]),
                (token_ref, token_buf),
                (project_ref, project_buf),
            )
        )
    ]

    def block_rows(block):
        start = (mp_index * (blocks // 2) + block) % blocks
        return rows_at(start * rows, rows)

    def block_copies(block, slot):
        at = block_rows(block)
        return (
            pltpu.make_async_copy(exp_ref.at[:, at, :], ring_buf.at[slot], block_sem.at[slot, 0]),
            pltpu.make_async_copy(inverse_ref.at[at, :], inverse_buf.at[slot], block_sem.at[slot, 1]),
        )

    def score_copy(block, slot):
        return pltpu.make_async_copy(
            ring_buf.at[2 + slot], score_ref.at[:, block_rows(block), :], out_sem.at[slot]
        )

    def ring_copies(block):
        slot = block % 4
        at = rows_at(block * rows, rows)
        return (
            pltpu.make_async_copy(score_ref.at[:, at, :], ring_buf.at[slot], ring_sem.at[slot, 0]),
            pltpu.make_async_copy(plane_ref.at[at, :], plane_buf.at[slot], ring_sem.at[slot, 1]),
            pltpu.make_async_copy(down_ref.at[at, :], down_buf.at[slot], ring_sem.at[slot, 2]),
        )

    def is_away(chunk):
        return chunk >= LOCAL_CHUNKS

    loads = {}
    for ref, away_ref, wide in (
        (expand_ref, expand_away_ref, True),
        (reduce_ref, reduce_away_ref, False),
    ):
        for k in range(2):
            piece = slice(k * CHUNK, (k + 1) * CHUNK)
            index = (slice(None), piece) if wide else (piece, slice(None))
            chunk = LOCAL_CHUNKS + len(loads)
            loads[chunk] = (
                pltpu.make_async_copy(ref.at[index], own_buf.at[chunk], load_sem.at[chunk, 0]),
                pltpu.make_async_copy(
                    away_ref.at[index], away_buf.at[chunk - LOCAL_CHUNKS], load_sem.at[chunk, 1]
                ),
            )

    for copy in loads[LOCAL_CHUNKS]:
        copy.start()
    for copy in residents[:2]:
        copy.start()
    for copy in block_copies(0, 0):
        copy.start()
    for copy in residents[2:6]:
        copy.start()
    for chunk in range(LOCAL_CHUNKS + 1, CHUNKS):
        for copy in loads[chunk]:
            copy.start()
    residents[6].start()
    for copy in residents[7:]:
        copy.start()

    keeps, leaves = [], []
    for bits in BITS:
        kept, left, base = [], [], 0
        for size, bit in zip(PARTS, bits):
            kept.append(base + side_of[bit] * size)
            left.append(base + (1 - side_of[bit]) * size)
            base = base + side_of[bit] * size
        keeps.append(kept)
        leaves.append(left)
    arrivals = (core_buf, first_buf, second_buf, third_buf)
    away_arrivals = (core_away_buf, first_away_buf)

    def staged(src, dst, chunk, stage, device):
        return remote(src, dst, send_sem.at[chunk, stage], recv_sem.at[chunk, stage], device)

    def scatter(chunk, level):
        return staged(
            own_buf.at[chunk, rows_at(leaves[chunk][level], PARTS[level]), :],
            arrivals[level].at[chunk],
            chunk,
            level,
            partner_of[BITS[chunk][level]],
        )

    def scatter_away(chunk, level):
        return staged(
            away_buf.at[chunk - LOCAL_CHUNKS, rows_at(leaves[chunk][level], PARTS[level]), :],
            away_arrivals[level].at[chunk - LOCAL_CHUNKS],
            chunk,
            4 + level,
            partner_of[BITS[chunk][level]],
        )

    def hand_over(chunk):
        return staged(
            away_buf.at[chunk - LOCAL_CHUNKS, rows_at(keeps[chunk][1], PARTS[1]), :],
            y_buf.at[chunk - LOCAL_CHUNKS],
            chunk,
            6,
            across_mp,
        )

    def total_rows(chunk, start, size):
        return total_ref.at[rows_at(chunk * CHUNK + start, size), :]

    def gather(chunk, level):
        kept, size = keeps[chunk][level], PARTS[level]
        if level == 3:
            src = own_buf.at[chunk, rows_at(kept, size), :]
        else:
            src = total_rows(chunk, kept, size)
        return staged(
            src, total_rows(chunk, kept, size), chunk, 7 + level, partner_of[BITS[chunk][level]]
        )

    def gathered(chunk, level):
        region = total_rows(chunk, leaves[chunk][level], PARTS[level])
        return staged(region, region, chunk, 7 + level, partner_of[BITS[chunk][level]])

    def store_own(chunk):
        return pltpu.make_async_copy(
            own_buf.at[chunk, rows_at(keeps[chunk][3], PARTS[3]), :],
            total_rows(chunk, keeps[chunk][3], PARTS[3]),
            local_sem.at[chunk],
        )

    def add(buf, chunk, start, size, arrived):
        piece = PARTS[3]

        def step(n, carry):
            here = rows_at(start + n * piece, piece)
            there = rows_at(n * piece, piece)
            buf[chunk, here, :] = buf[chunk, here, :] + arrived[there, :]
            return carry

        lax.fori_loop(0, size // piece, step, 0)

    def add_level(chunk, level):
        scatter(chunk, level).wait_recv()
        add(own_buf, chunk, keeps[chunk][level], PARTS[level], arrivals[level].at[chunk])

    def add_level_away(chunk, level):
        at = chunk - LOCAL_CHUNKS
        scatter_away(chunk, level).wait_recv()
        add(away_buf, at, keeps[chunk][level], PARTS[level], away_arrivals[level].at[at])

    def exchange(event, chunk):
        away = is_away(chunk)
        if event == 0:
            if away:
                for copy in loads[chunk]:
                    copy.wait()
                scatter_away(chunk, 0).start()
            scatter(chunk, 0).start()
            return
        if event == 1:
            if away:
                add_level_away(chunk, 0)
                scatter_away(chunk, 1).start()
            add_level(chunk, 0)
            scatter(chunk, 1).start()
            return
        if away and event == 2:
            add_level_away(chunk, 1)
            hand_over(chunk).start()
            add_level(chunk, 1)
            return
        if away:
            event -= 1
            if event == 2:
                hand_over(chunk).wait_recv()
                add(own_buf, chunk, keeps[chunk][1], PARTS[1], y_buf.at[chunk - LOCAL_CHUNKS])
        elif event == 2:
            add_level(chunk, 1)
        if event == 2:
            scatter(chunk, 2).start()
        elif event == 3:
            add_level(chunk, 2)
            scatter(chunk, 3).start()
        elif event == 4:
            add_level(chunk, 3)
            store_own(chunk).start()
            gather(chunk, 3).start()
        else:
            level = 8 - event
            if level == 3:
                store_own(chunk).wait()
            gathered(chunk, level).wait_recv()
            if level > 0:
                gather(chunk, level - 1).start()

    small_devices = (across_mp, *partner_of.values())

    def small_hop(n):
        return remote(
            small_buf.at[n],
            small_recv_buf.at[n],
            small_send_sem.at[n],
            small_recv_sem.at[n],
            small_devices[n],
        )

    def small_step(n):
        if n == 0:
            residents[6].wait()
        else:
            small_hop(n - 1).wait_recv()
            small_buf[n] = small_buf[n - 1] + small_recv_buf[n - 1]
        if n < 5:
            small_hop(n).start()
        else:
            small_out_ref[...] = small_buf[n]

    def input_rows(side):
        return mine if side == 0 else others

    def input_product(side, target):
        at = input_rows(side)
        part = None
        for k in range(3):
            product = lax.dot_general(
                triple_buf[k, at, :],
                project_buf[k, rows_at(target * width, width), :],
                (((1,), (1,)), ((), ())),
                preferred_element_type=f32,
            )
            part = product if part is None else part + product
        if side == 0:
            cols = pl.ds(pl.multiple_of(target * width, LANES), width)
            part = part + grad_buf[0, :, cols].astype(f32)
        return part

    def input_store(side):
        return pltpu.make_async_copy(
            input_buf.at[side], input_ref.at[input_rows(side), :], out_sem.at[3 + side]
        )

    def run(event, which):
        if event == "small":
            small_step(which)
        elif event == "send":
            input_swap.start()
        elif event == "layer":
            layer_swap.start()
            layer_keep.start()
        elif event == "input":
            input_swap.wait_recv()
            for side in range(2):
                part = input_product(side, mp_index)
                input_buf[side] = part + input_recv_buf[input_rows(side), :].astype(f32)
                input_store(side).start()
        else:
            exchange(event, which)

    pairs = heads // 2
    block_slots = plan_slots("b", blocks * pairs)
    part_slots = plan_slots("p", 4)
    turn_slots = plan_slots("t", turns)
    rest = plan_slots("e", 1)[0]

    def run_all(steps):
        for event, which in steps:
            run(event, which)

    def dispatch(slots, n, low, high):
        if not any(slots[low:high]):
            return
        if high - low == 1:
            for event, which in slots[low]:
                run(event, which)
            return
        middle = (low + high) // 2
        if any(slots[low:middle]):
            pl.when(n < middle)(lambda: dispatch(slots, n, low, middle))
        if any(slots[middle:high]):
            pl.when(n >= middle)(lambda: dispatch(slots, n, middle, high))

    grad_key_buf[...] = jnp.zeros_like(grad_key_buf)
    grad_value_buf[...] = jnp.zeros_like(grad_value_buf)
    sum_ref[...] = jnp.zeros_like(sum_ref)
    for copy in residents[:6]:
        copy.wait()
    first = lax.broadcasted_iota(jnp.int32, (rows, LANES), 1) < HEAD

    def back(block, carry):
        slot = block % 2
        at = block_rows(block)
        for copy in block_copies(block, slot):
            copy.wait()

        @pl.when(block + 1 < blocks)
        def _():
            for copy in block_copies(block + 1, 1 - slot):
                copy.start()

        pl.when(block == blocks // 2)(grad_swap.wait_recv)
        pl.when(block >= 2)(lambda: score_copy(block - 2, slot).wait())
        side = block // (blocks // 2)
        local = rows_at((block % (blocks // 2)) * rows, rows)
        grad_context = lax.dot_general(
            grad_buf[side, local, :],
            output_buf[...],
            (((1,), (1,)), ((), ())),
            preferred_element_type=f32,
        )
        scaled = (grad_context * inverse_buf[slot]).astype(bf16)
        for p in range(pairs):
            dispatch(block_slots, block * pairs + p, 0, blocks * pairs)
            cols = slice(p * LANES, (p + 1) * LANES)
            grad = scaled[:, cols]
            product = grad.astype(f32) * context_buf[at, cols].astype(f32)
            query_turned = query_buf[at, cols].T
            grad_turned = grad.T
            grad_query = None
            for u in range(2):
                h = 2 * p + u
                half = slice(u * HEAD, (u + 1) * HEAD)
                own = first if u == 0 else ~first
                total = jnp.sum(jnp.where(own, product, 0.0), axis=1, keepdims=True)
                exps = ring_buf[slot, h]
                grad_exp = dot_f32(grad, value_buf[h])
                grad_score = (exps.astype(f32) * (grad_exp - total)).astype(bf16)
                ring_buf[2 + slot, h] = grad_score
                part = dot_f32(grad_score, key_buf[h])
                grad_query = part if u == 0 else grad_query + part
                grad_key_buf[h] += dot_f32(query_turned[half], grad_score)
                grad_value_buf[h] += dot_f32(grad_turned[half], exps)
            triple_buf[0, at, cols] = (grad_query * 0.125).astype(bf16)
        score_copy(block, slot).start()
        return carry

    lax.fori_loop(0, blocks, back, 0)

    score_copy(blocks - 2, blocks % 2).wait()
    score_copy(blocks - 1, (blocks - 1) % 2).wait()
    for block in range(2):
        for copy in ring_copies(block):
            copy.start()
    run_all(part_slots[0])
    triple_buf[0, row_count:keys, :] = jnp.zeros((keys - row_count, width), bf16)
    for k, ref in ((1, grad_key_buf), (2, grad_value_buf)):
        for h in range(0, heads, 2):
            pair = ref[h : h + 2].reshape(LANES, keys)
            triple_buf[k, :, h * HEAD : (h + 2) * HEAD] = pair.T.astype(bf16)
    run_all(part_slots[1])
    for copy in residents[7:]:
        copy.wait()
    tokens_in = (((0,), (0,)), ((), ()))
    places = ((0, 0), (0, width), (1, 0))
    for k, (chunk, start) in enumerate(places):
        own_buf[chunk, start : start + width, :] = lax.dot_general(
            triple_buf[k], token_buf[...], tokens_in, preferred_element_type=f32
        ).astype(bf16)
    run_all(part_slots[2])
    own_buf[1, width : 2 * width, :] = (
        lax.dot_general(
            context_buf[mine, :], grad_buf[0], tokens_in, preferred_element_type=f32
        )
        + lax.dot_general(
            context_buf[others, :], grad_buf[1], tokens_in, preferred_element_type=f32
        )
    ).astype(bf16)
    run_all(part_slots[3])
    for side in range(2):
        input_send_buf[input_rows(side), :] = input_product(side, 1 - mp_index).astype(bf16)
    biases = jnp.concatenate(
        [
            jnp.sum(triple_buf[0].astype(f32), axis=0, keepdims=True),
            jnp.sum(triple_buf[2].astype(f32), axis=0, keepdims=True),
        ],
        axis=1,
    )

    def turn(n, carry):
        last = n * TABLE_STRIPS + TABLE_STRIPS - 1
        block = last // block_strips

        @pl.when(last % block_strips < TABLE_STRIPS)
        def _():
            for copy in ring_copies(block):
                copy.wait()

            @pl.when(block + 2 < blocks)
            def _():
                for copy in ring_copies(block + 2):
                    copy.start()

        dispatch(turn_slots, n, 0, turns)

        def refs_at(strip):
            slot = (strip // block_strips) % 4
            at = rows_at((strip % block_strips) * STRIP, STRIP)
            return (
                lambda h, cols: ring_buf[slot, h, at, cols],
                lambda cols: plane_buf[slot, at, cols],
                lambda cols: down_buf[slot, at, cols],
            )

        table_strips(
            [refs_at(n * TABLE_STRIPS + k) for k in range(TABLE_STRIPS)],
            sum_ref,
            heads,
            keys,
            high_counts,
        )
        return carry

    lax.fori_loop(0, turns, turn, 0)

    table_rows = sum(high_counts) * heads
    table_finish(sum_ref, table_buf.at[0], table_rows)
    lanes = table_buf.shape[2]
    pieces = 2 * width // lanes
    for n in range(pieces):
        table_buf[0, table_rows + n : table_rows + n + 1, :] = biases[:, n * lanes : (n + 1) * lanes]
    spare = table_buf.shape[1] - table_rows - pieces
    table_buf[0, table_rows + pieces :, :] = jnp.zeros((spare, lanes), f32)
    table_devices = tuple(partner_of.values())

    def table_hop(n):
        return remote(
            table_buf.at[n],
            table_recv_buf.at[n],
            table_send_sem.at[n],
            table_recv_sem.at[n],
            table_devices[n],
        )

    def table_step(n):
        if n > 0:
            table_hop(n - 1).wait_recv()
            table_buf[n] = table_buf[n - 1] + table_recv_buf[n - 1]
        if n < 4:
            table_hop(n).start()

    table_step(0)
    for n, (event, which) in enumerate(rest):
        if n % 3 == 2 and n // 3 < 4:
            table_step(n // 3 + 1)
        run(event, which)
    for n in range(min(len(rest) // 3, 4), 4):
        table_step(n + 1)
    table_ref[...] = table_buf[4]

    layer_arrival.wait_recv()
    layer_keep.wait()
    grad_swap.wait_send()
    input_swap.wait_send()
    layer_swap.wait_send()
    for side in range(2):
        input_store(side).wait()
    for n in range(5):
        small_hop(n).wait_send()
    for n in range(4):
        table_hop(n).wait_send()
    for chunk in range(CHUNKS):
        for level in range(4):
            scatter(chunk, level).wait_send()
            gather(chunk, level).wait_send()
        if is_away(chunk):
            scatter_away(chunk, 0).wait_send()
            scatter_away(chunk, 1).wait_send()
            hand_over(chunk).wait_send()


def finish(
    exps,
    inverse,
    plane,
    down,
    context,
    query,
    tokens,
    grad,
    layer,
    value_turned,
    key_wide,
    project_weight,
    output_weight,
    expand,
    reduce,
    small,
    counts,
):
    heads, row_count, keys = exps.shape
    width = heads * HEAD
    depth = tokens.shape[1]
    half_rows = row_count // 2
    high_counts = (counts[0] // 16, counts[1] // 16, counts[1] // 16)
    high_rows = sum(high_counts) * heads
    low_lanes = 16 * STRIP
    table_shape = (round_up(high_rows + 2 * width // low_lanes, 8), low_lanes)
    away = CHUNKS - LOCAL_CHUNKS
    anywhere = pl.BlockSpec(memory_space=pl.ANY)
    in_vmem = pl.BlockSpec(memory_space=pltpu.VMEM)
    dma = pltpu.SemaphoreType.DMA
    total, layer_full, input_full, small_sum, table_sum, _ = pl.pallas_call(
        partial(finish_kernel, high_counts=high_counts),
        in_specs=[anywhere] * 18,
        out_specs=[anywhere, anywhere, anywhere, in_vmem, in_vmem, anywhere],
        out_shape=[
            jax.ShapeDtypeStruct((CHUNKS * CHUNK, CHUNK), bf16),
            jax.ShapeDtypeStruct((row_count, depth), bf16),
            jax.ShapeDtypeStruct((row_count, width), f32),
            jax.ShapeDtypeStruct(small.shape, f32),
            jax.ShapeDtypeStruct(table_shape, f32),
            jax.ShapeDtypeStruct(exps.shape, bf16),
        ],
        scratch_shapes=[
            pltpu.VMEM(output_weight.shape, bf16),
            pltpu.VMEM((2, half_rows, depth), bf16),
            pltpu.VMEM(value_turned.shape, bf16),
            pltpu.VMEM(key_wide.shape, bf16),
            pltpu.VMEM(context.shape, bf16),
            pltpu.VMEM(query.shape, bf16),
            pltpu.VMEM(tokens.shape, bf16),
            pltpu.VMEM(project_weight.shape, bf16),
            pltpu.VMEM((4, heads, BACK_ROWS, keys), bf16),
            pltpu.VMEM((2, BACK_ROWS, width), f32),
            pltpu.VMEM((heads, HEAD, keys), f32),
            pltpu.VMEM((heads, HEAD, keys), f32),
            pltpu.VMEM((3, keys, width), bf16),
            pltpu.VMEM((row_count, width), bf16),
            pltpu.VMEM((row_count, width), bf16),
            pltpu.VMEM((2, half_rows, width), f32),
            pltpu.VMEM((4, BACK_ROWS, keys), jnp.int16),
            pltpu.VMEM((4, BACK_ROWS, keys), jnp.int16),
            pltpu.VMEM((high_rows * STRIP, low_lanes), f32),
            pltpu.VMEM((CHUNKS, CHUNK, CHUNK), bf16),
            pltpu.VMEM((away, CHUNK, CHUNK), bf16),
            pltpu.VMEM((CHUNKS, PARTS[0], CHUNK), bf16),
            pltpu.VMEM((away, PARTS[0], CHUNK), bf16),
            pltpu.VMEM((CHUNKS, PARTS[1], CHUNK), bf16),
            pltpu.VMEM((away, PARTS[1], CHUNK), bf16),
            pltpu.VMEM((away, PARTS[1], CHUNK), bf16),
            pltpu.VMEM((CHUNKS, PARTS[2], CHUNK), bf16),
            pltpu.VMEM((CHUNKS, PARTS[3], CHUNK), bf16),
            pltpu.VMEM((6, *small.shape), f32),
            pltpu.VMEM((5, *small.shape), f32),
            pltpu.VMEM((5, *table_shape), f32),
            pltpu.VMEM((4, *table_shape), f32),
            dma((9,)),
            dma((2, 2)),
            dma((4, 3)),
            dma((CHUNKS, 2)),
            dma((CHUNKS,)),
            dma((5,)),
            dma((CHUNKS, 11)),
            dma((CHUNKS, 11)),
            dma((3,)),
            dma((3,)),
            dma((5,)),
            dma((5,)),
            dma((4,)),
            dma((4,)),
        ],
        compiler_params=pltpu.CompilerParams(
            vmem_limit_bytes=FINISH_VMEM, collective_id=0, has_side_effects=True
        ),
        name="finish",
    )(
        exps,
        inverse,
        plane,
        down,
        context,
        query,
        tokens,
        grad,
        layer,
        value_turned,
        key_wide,
        project_weight,
        output_weight,
        *expand,
        *reduce,
        small,
    )
    projects = total[: 3 * width].reshape(3, width, depth).transpose(0, 2, 1)
    outputs = total[3 * width : 2 * CHUNK]
    expands = jnp.concatenate([total[2 * CHUNK : 3 * CHUNK], total[3 * CHUNK : 4 * CHUNK]], axis=1)
    reduces = total[4 * CHUNK :]
    tables = table_result(table_sum[:high_rows], high_counts, heads)
    biases = table_sum[high_rows : high_rows + 2 * width // low_lanes].reshape(2, width)
    return layer_full, input_full, projects, outputs, expands, reduces, tables, biases, small_sum


def piece_of(step, pieces):
    return lax.rem(step, 2 * pieces) - pieces


def feed_kernel(
    context_ref,
    context_away_ref,
    token_ref,
    cotangent_ref,
    valid_ref,
    output_ref,
    output_away_ref,
    expand_ref,
    expand_half_ref,
    reduce_ref,
    reduce_half_ref,
    expand_bias_ref,
    vector_ref,
    layer_ref,
    grad_ref,
    expand_grad_ref,
    expand_grad_away_ref,
    reduce_grad_ref,
    reduce_grad_away_ref,
    vector_grad_ref,
    expand_bias_grad_ref,
    input_buf,
    norm_buf,
    hat_buf,
    inverse_buf,
    total_buf,
    reduced_buf,
    active_buf,
    slope_buf,
    before_buf,
    expand_buf,
    reduce_buf,
    local_sem,
    send_sem,
    recv_sem,
    *,
    pieces,
    tiles,
):
    rows, width = token_ref.shape
    size = expand_ref.shape[1]
    step = pl.program_id(0)
    place = lax.axis_index("dp")
    core = place % 2
    other_core = {"dp": place + 1 - 2 * core}

    keeps, hands = [], []
    for n, (half_ref, buf) in enumerate(((expand_half_ref, expand_buf), (reduce_half_ref, reduce_buf))):
        count = half_ref.shape[0]
        at = pl.ds(pl.multiple_of(core * count, STRIP), count)
        keeps.append(pltpu.make_async_copy(half_ref, buf.at[at, :], local_sem.at[n]))
        hands.append(
            pltpu.make_async_remote_copy(
                src_ref=half_ref,
                dst_ref=buf.at[at, :],
                send_sem=send_sem.at[n],
                recv_sem=recv_sem.at[n],
                device_id=other_core,
                device_id_type=pl.DeviceIdType.MESH,
            )
        )

    @pl.when(step == 0)
    def _():
        barrier = pltpu.get_barrier_semaphore()
        pl.semaphore_signal(
            barrier, inc=1, device_id=other_core, device_id_type=pl.DeviceIdType.MESH
        )
        pl.semaphore_wait(barrier, 1)
        for copy in (*hands, *keeps):
            copy.start()

    @pl.when(step == pieces)
    def _():
        for n, (half_ref, buf) in enumerate(
            ((expand_half_ref, expand_buf), (reduce_half_ref, reduce_buf))
        ):
            count = half_ref.shape[0]
            there = pl.ds(pl.multiple_of((1 - core) * count, STRIP), count)
            keeps[n].wait()
            pltpu.make_async_remote_copy(
                src_ref=half_ref,
                dst_ref=buf.at[there, :],
                send_sem=send_sem.at[n],
                recv_sem=recv_sem.at[n],
                device_id=other_core,
                device_id_type=pl.DeviceIdType.MESH,
            ).wait_recv()

    @pl.when(step == 6 * pieces - 1)
    def _():
        for copy in hands:
            copy.wait_send()

    away_cols = pl.ds(pl.multiple_of(jnp.clip(piece_of(step, pieces), 0, pieces - 1) * size, LANES), size)
    expand_away = expand_buf.at[:, away_cols]
    reduce_away = reduce_buf.at[away_cols, :]
    piece = step % (2 * pieces)
    strip_rows = FEED_STRIP
    strips = rows // strip_rows

    def vector(n):
        return vector_ref[n : n + 1, :]

    def for_strips(body, sums):
        def run(n, carry):
            at = pl.ds(pl.multiple_of(n * strip_rows, STRIP), strip_rows)
            return tuple(
                old + jnp.sum(new.reshape(strip_rows // 8, 8, width), axis=0)
                for old, new in zip(carry, body(at))
            )

        start = tuple(jnp.zeros((8, width), f32) for _ in range(sums))
        done = lax.fori_loop(0, strips, run, start)
        return [jnp.sum(part, axis=0, keepdims=True) for part in done]

    def mean(values):
        return jnp.sum(values, axis=-1, keepdims=True) * (1.0 / width)

    @pl.when(step == 0)
    def _():
        vector_grad_ref[...] = jnp.zeros_like(vector_grad_ref)
        total_buf[...] = dot_f32(context_ref[...], output_ref[...]) + dot_f32(
            context_away_ref[...], output_away_ref[...]
        )

        def body(at):
            values = token_ref[at, :].astype(f32) + (total_buf[at, :] + vector(0))
            centered = values - mean(values)
            inverse = lax.rsqrt(mean(centered * centered) + norm_epsilon)
            hat = centered * inverse
            norm = hat * vector(1) + vector(2)
            hat_buf[at, :] = hat
            inverse_buf[at, :] = jnp.broadcast_to(inverse, (strip_rows, LANES))
            norm_buf[at, :] = norm
            input_buf[at, :] = norm.astype(bf16)
            total_buf[at, :] = norm + vector(3)
            return ()

        for_strips(body, 0)

    def forward(expand, reduce):
        for start, size in tiles:
            at = slice(start, start + size)
            before = dot_f32(input_buf[at, :], expand[...]) + expand_bias_ref[0]
            phi = 0.5 * lax.erf(before * 0.7071067811865476) + 0.5
            slope_buf[piece, at, :] = phi + before * (
                0.3989422804014327 * jnp.exp(-0.5 * (before * before))
            )
            active = (before * phi).astype(bf16)
            active_buf[piece, at, :] = active
            total_buf[at, :] += dot_f32(active, reduce[...])

    pl.when(step < pieces)(lambda: forward(expand_ref, reduce_ref))
    pl.when((step >= pieces) & (step < 2 * pieces))(
        lambda: forward(expand_away, reduce_away)
    )

    @pl.when(step == 2 * pieces)
    def _():
        def body(at):
            values = total_buf[at, :]
            valid = valid_ref[at, :]
            centered = values - mean(values)
            inverse = lax.rsqrt(mean(centered * centered) + norm_epsilon)
            hat = centered * inverse
            layer_ref[at, :] = (valid * (hat * vector(4) + vector(5))).astype(bf16)
            grad_out = cotangent_ref[at, :].astype(f32) * valid
            grad_hat = grad_out * vector(4)
            mixed = inverse * (grad_hat - mean(grad_hat) - hat * mean(grad_hat * hat))
            low = mixed.astype(bf16)
            reduced_buf[at, :] = low
            total_buf[at, :] = mixed
            return grad_out * hat, grad_out, low.astype(f32)

        for n, part in enumerate(for_strips(body, 3)):
            vector_grad_ref[n : n + 1, :] = part

    def backward(expand, reduce):
        sums = None
        for start, size in tiles:
            at = slice(start, start + size)
            grad_active = lax.dot_general(
                reduced_buf[at, :], reduce[...], (((1,), (1,)), ((), ())), preferred_element_type=f32
            )
            before = (grad_active * slope_buf[piece, at, :]).astype(bf16)
            before_buf[piece, at, :] = before
            part = jnp.sum(before.astype(f32), axis=0, keepdims=True)
            sums = part if sums is None else sums + part
            total_buf[at, :] += lax.dot_general(
                before, expand[...], (((1,), (1,)), ((), ())), preferred_element_type=f32
            )
        expand_bias_grad_ref[0] = sums

    pl.when((step >= 2 * pieces) & (step < 3 * pieces))(lambda: backward(expand_ref, reduce_ref))
    pl.when((step >= 3 * pieces) & (step < 4 * pieces))(
        lambda: backward(expand_away, reduce_away)
    )

    @pl.when(step == 4 * pieces)
    def _():
        def body(at):
            grad_first = total_buf[at, :]
            hat = hat_buf[at, :]
            grad_hat = grad_first * vector(1)
            inverse = inverse_buf[at, 0:1]
            inner = inverse * (grad_hat - mean(grad_hat) - hat * mean(grad_hat * hat))
            low = inner.astype(bf16)
            grad_ref[at, :] = low
            return grad_first * hat, grad_first, low.astype(f32)

        for n, part in enumerate(for_strips(body, 3)):
            vector_grad_ref[n + 3 : n + 4, :] = part

    def weights(expand_grad, reduce_grad):
        reduce_grad[...] = lax.dot_general(
            active_buf[piece], reduced_buf[...], (((0,), (0,)), ((), ())), preferred_element_type=f32
        ).astype(bf16)
        expand_grad[...] = lax.dot_general(
            input_buf[...], before_buf[piece], (((0,), (0,)), ((), ())), preferred_element_type=f32
        ).astype(bf16)

    pl.when((step >= 4 * pieces) & (step < 5 * pieces))(
        lambda: weights(expand_grad_ref, reduce_grad_ref)
    )
    pl.when(step >= 5 * pieces)(lambda: weights(expand_grad_away_ref, reduce_grad_away_ref))


def feed(
    context,
    context_away,
    tokens,
    cotangent,
    valid,
    output,
    output_away,
    expand,
    expand_half,
    reduce,
    reduce_half,
    expand_biases,
    vectors,
):
    rows, width = context_away.shape[0], tokens.shape[1]
    hidden = expand.shape[1]
    size = FEED_PIECE
    pieces = hidden // size
    split = round_up(rows // 2, STRIP)
    tiles = ((0, split), (split, rows - split))

    def once(array):
        zeros = (0,) * array.ndim
        return pl.BlockSpec(array.shape, lambda i: zeros, pipeline_mode=pl.Buffered(1))

    def mine(array):
        return pl.BlockSpec(
            (rows, array.shape[1]),
            lambda i: (lax.axis_index("mp"), 0),
            pipeline_mode=pl.Buffered(1),
        )

    def place(first, i):
        at = lax.rem(i, 2 * pieces) - first
        at = jnp.clip(at, 0, pieces - 1)
        return jnp.where(i < 4 * pieces, at, pieces - 1)

    def grad_place(first, i):
        return jnp.clip(i - 4 * pieces - first, 0, pieces - 1)

    wide = lambda first: pl.BlockSpec((width, size), lambda i: (0, place(first, i)))
    tall = lambda first: pl.BlockSpec((size, width), lambda i: (place(first, i), 0))
    wide_grad = lambda first: pl.BlockSpec((width, size), lambda i: (0, grad_place(first, i)))
    tall_grad = lambda first: pl.BlockSpec((size, width), lambda i: (grad_place(first, i), 0))
    bias_rows = expand_biases.reshape(2 * pieces, 1, size)
    whole = lambda shape: pl.BlockSpec(
        shape, lambda i: (0,) * len(shape), pipeline_mode=pl.Buffered(1)
    )
    full = jax.ShapeDtypeStruct((rows, width), bf16)
    return pl.pallas_call(
        partial(feed_kernel, pieces=pieces, tiles=tiles),
        grid=(6 * pieces,),
        in_specs=[
            mine(context),
            once(context_away),
            mine(tokens),
            mine(cotangent),
            mine(valid),
            once(output),
            once(output_away),
            wide(0),
            pl.BlockSpec(memory_space=pl.ANY),
            tall(0),
            pl.BlockSpec(memory_space=pl.ANY),
            pl.BlockSpec((1, 1, size), lambda i: (lax.rem(i, 2 * pieces), 0, 0)),
            once(vectors),
        ],
        out_specs=[
            whole((rows, width)),
            whole((rows, width)),
            wide_grad(0),
            wide_grad(pieces),
            tall_grad(0),
            tall_grad(pieces),
            whole((8, width)),
            pl.BlockSpec((1, 1, size), lambda i: (jnp.clip(i - 2 * pieces, 0, 2 * pieces - 1), 0, 0)),
        ],
        out_shape=[
            full,
            full,
            jax.ShapeDtypeStruct((width, hidden), bf16),
            jax.ShapeDtypeStruct((width, hidden), bf16),
            jax.ShapeDtypeStruct((hidden, width), bf16),
            jax.ShapeDtypeStruct((hidden, width), bf16),
            jax.ShapeDtypeStruct((8, width), f32),
            jax.ShapeDtypeStruct((2 * pieces, 1, size), f32),
        ],
        scratch_shapes=[
            pltpu.VMEM((rows, width), bf16),
            pltpu.VMEM((rows, width), f32),
            pltpu.VMEM((rows, width), f32),
            pltpu.VMEM((rows, LANES), f32),
            pltpu.VMEM((rows, width), f32),
            pltpu.VMEM((rows, width), bf16),
            pltpu.VMEM((2 * pieces, rows, size), bf16),
            pltpu.VMEM((2 * pieces, rows, size), f32),
            pltpu.VMEM((2 * pieces, rows, size), bf16),
            pltpu.VMEM((width, hidden), bf16),
            pltpu.VMEM((hidden, width), bf16),
            pltpu.SemaphoreType.DMA((2,)),
            pltpu.SemaphoreType.DMA((2,)),
            pltpu.SemaphoreType.DMA((2,)),
        ],
        compiler_params=pltpu.CompilerParams(
            vmem_limit_bytes=vmem_limit, collective_id=2, has_side_effects=True
        ),
        name="feed",
    )(
        context,
        context_away,
        tokens,
        cotangent,
        valid,
        output,
        output_away,
        expand,
        expand_half,
        reduce,
        reduce_half,
        bias_rows,
        vectors,
    )


def swap(array):
    return lax.ppermute(array, "mp", [(0, 1), (1, 0)])


def partner(array, count, bit):
    return lax.ppermute(array, "dp", [(i, i ^ bit) for i in range(count)])


def fetched_half(array):
    half = array.shape[0] // 2
    core = lax.axis_index("dp") % 2
    return swap(lax.dynamic_slice_in_dim(array, core * half, half, 0))


def other_share(array, count):
    fetched = fetched_half(array)
    handed = partner(fetched, count, 1)
    even = lax.axis_index("dp") % 2 == 0
    return jnp.concatenate(
        [jnp.where(even, fetched, handed), jnp.where(even, handed, fetched)], axis=0
    )


def sum_rows_over_dp(array, count):
    place = lax.axis_index("dp")
    bits = []
    bit = 1
    while bit < count:
        mine = (place // bit) % 2
        halves = array.reshape((2, array.shape[0] // 2) + array.shape[1:])
        sent = lax.dynamic_index_in_dim(halves, 1 - mine, 0, keepdims=False)
        kept = lax.dynamic_index_in_dim(halves, mine, 0, keepdims=False)
        array = kept + partner(sent, count, bit)
        bits.append(bit)
        bit *= 2
    for bit in reversed(bits):
        lead = (place // bit) % 2 == 0
        other = partner(array, count, bit)
        array = jnp.concatenate(
            [jnp.where(lead, array, other), jnp.where(lead, other, array)], axis=0
        )
    return array


def sum_small(arrays, count, over_mp):
    sizes = [a.size for a in arrays]
    total = sum(sizes)
    flat = jnp.concatenate([a.reshape(-1) for a in arrays])
    flat = jnp.pad(flat, (0, round_up(total, 1024) - total)).reshape(-1, LANES)
    if over_mp:
        flat = flat + swap(flat)
    bit = 1
    while bit < count:
        flat = flat + partner(flat, count, bit)
        bit *= 2
    flat = flat.reshape(-1)
    outs = []
    start = 0
    for array, size in zip(arrays, sizes):
        outs.append(flat[start : start + size].reshape(array.shape))
        start += size
    return outs


def per_device(
    dp_count,
    tokens,
    cotangent,
    long_flag,
    token_mask,
    bucket_line,
    bucket_across,
    bucket_down,
    project_weight,
    project_bias,
    table_line,
    table_across,
    table_down,
    output_weight,
    output_bias,
    first_gain,
    first_shift,
    expand_weight,
    expand_bias,
    reduce_weight,
    reduce_bias,
    second_gain,
    second_shift,
):
    length = tokens.shape[1]
    width = project_weight.shape[2]
    heads = table_line.shape[1]
    counts = (table_line.shape[0], table_across.shape[0])
    rows = round_up(length, BLOCK_ROWS)
    half_rows = rows // 2
    keys = round_up(length, 3 * LANES)
    mp_index = lax.axis_index("mp")
    lead = mp_index == 0

    def own_rows(array):
        return lax.dynamic_slice_in_dim(array, mp_index * half_rows, half_rows, 0)

    def in_order(mine, other):
        return jnp.where(lead, mine, other), jnp.where(lead, other, mine)

    output_other = other_share(output_weight, dp_count)
    expand_half = fetched_half(expand_weight)
    reduce_half = fetched_half(reduce_weight)
    expand_bias_other = swap(expand_bias)

    positions = jnp.arange(length, dtype=jnp.int32)
    limit = jnp.where(long_flag[0] > 0, LONG, SHORT).astype(jnp.int32)
    valid = (token_mask[0] > 0) & (positions < limit)
    valid_rows = jnp.pad(valid.astype(f32), (0, rows - length))[:, None]
    grow = ((0, rows - length), (0, keys - length))
    line, across, down = (
        jnp.pad(array[0], grow) for array in (bucket_line, bucket_across, bucket_down)
    )
    away = jnp.where(jnp.pad(valid, (0, keys - length)), 0, counts[0])
    plane = (line | away[None, :] | (across << 8)).astype(jnp.int16)
    down = down.astype(jnp.int16)
    tables = []
    for table in (table_line, table_across, table_down):
        lanes = jnp.pad(
            table.T, ((0, 0), (0, LANES - table.shape[0])), constant_values=large_negative
        )
        tables.append(jnp.broadcast_to(lanes[:, None, :], (heads, STRIP, LANES)))
    tables = jnp.concatenate(tables).astype(bf16)

    query, key_wide, key_turned, value_ones, value_turned = project(
        tokens[0], project_weight, project_bias.astype(f32), keys
    )
    exps, context, inverse, context_away = attend(query, key_turned, value_ones, plane, down, tables)

    padded = jnp.pad(tokens[0], ((0, keys - length), (0, 0)))
    vectors = jnp.stack(
        [
            output_bias.astype(f32),
            first_gain,
            first_shift,
            reduce_bias.astype(f32),
            second_gain,
            second_shift,
            second_shift,
            second_shift,
        ]
    )
    expand_biases = jnp.concatenate([expand_bias, expand_bias_other]).astype(f32)
    (
        layer_mine,
        grad_mine,
        expand_own,
        expand_sent,
        reduce_own,
        reduce_sent,
        vector_grads,
        expand_bias_grads,
    ) = feed(
        context,
        context_away,
        padded,
        jnp.pad(cotangent[0], ((0, rows - length), (0, 0))),
        valid_rows,
        output_weight,
        output_other,
        expand_weight,
        expand_half,
        reduce_weight,
        reduce_half,
        expand_biases,
        vectors,
    )
    expand_bias_grads = expand_bias_grads.reshape(2, -1)
    ordered_biases = in_order(expand_bias_grads[0], expand_bias_grads[1])
    if dp_count == 16 and expand_own.shape == (CHUNK, 2 * CHUNK):
        bias_rows = jnp.concatenate(ordered_biases).reshape(-1, tokens.shape[2])
        small = jnp.concatenate([vector_grads, jnp.pad(bias_rows, ((0, 4), (0, 0)))])
        (
            layer_full,
            input_full,
            project_weight_grad,
            output_weight_grad,
            expand_weight_grad,
            reduce_weight_grad,
            table_grads,
            project_bias_grad,
            small,
        ) = finish(
            exps,
            inverse,
            plane,
            down,
            context,
            query,
            padded,
            grad_mine,
            layer_mine,
            value_turned,
            key_wide,
            project_weight,
            output_weight,
            (expand_own, expand_sent),
            (reduce_own, reduce_sent),
            small,
            counts,
        )
        layer_out = layer_full[None, :length]
        input_grad = input_full[None, :length]
        vector_grads = small[:8]
        expand_bias_grad = jnp.where(lead, small[8:10], small[10:12]).reshape(-1)
    else:
        layer_out = jnp.concatenate(in_order(layer_mine, swap(layer_mine)))[None, :length]
        grad_attended = jnp.concatenate(in_order(grad_mine, swap(grad_mine)))
        output_weight_grad = jnp.einsum(
            "le,lf->ef", context, grad_attended, preferred_element_type=f32
        ).astype(bf16)
        grad_context = jnp.einsum(
            "lf,ef->le", grad_attended, output_weight, preferred_element_type=f32
        )
        grad_scaled = (grad_context * inverse).astype(bf16)
        grad_scores, grad_query, grad_key, grad_value = attend_back(
            exps, grad_scaled, context, query, value_turned, key_wide
        )
        grad_key = grad_key.reshape(width, keys)[:, :rows].T.astype(bf16)
        grad_value = grad_value.reshape(width, keys)[:, :rows].T.astype(bf16)
        triple = jnp.stack([grad_query, grad_key, grad_value])
        project_weight_grad = jnp.einsum(
            "ld,kle->kde", padded[:rows], triple, preferred_element_type=f32
        ).astype(bf16)
        project_bias_grad = jnp.stack(
            [jnp.sum(grad_query, axis=0, dtype=f32), jnp.sum(grad_value, axis=0, dtype=f32)]
        )
        input_part = jnp.einsum("kle,kde->ld", triple, project_weight, preferred_element_type=f32)
        input_part = lax.dynamic_update_slice_in_dim(
            input_part,
            own_rows(input_part) + grad_mine.astype(f32),
            mp_index * half_rows,
            0,
        )
        sent = jnp.where(lead, input_part[:, width:], input_part[:, :width]).astype(bf16)
        own = jnp.where(lead, input_part[:, :width], input_part[:, width:])
        input_grad = (own + swap(sent).astype(f32))[None, :length]
        table_grads = table_sums(grad_scores, plane, down, counts)
        reduce_weight_grad = sum_rows_over_dp(reduce_own + swap(reduce_sent), dp_count)
        expand_weight_grad = sum_rows_over_dp(expand_own + swap(expand_sent), dp_count)
        output_weight_grad = sum_rows_over_dp(output_weight_grad, dp_count)
        project_weight_grad = sum_rows_over_dp(
            project_weight_grad.reshape(-1, width), dp_count
        ).reshape(project_weight.shape)
        vector_grads, even_biases, odd_biases = sum_small(
            [vector_grads, *ordered_biases], dp_count, True
        )
        expand_bias_grad = jnp.where(lead, even_biases, odd_biases)
        table_grads, project_bias_grad = sum_small(
            [table_grads, project_bias_grad], dp_count, False
        )
    (
        second_gain_grad,
        second_shift_grad,
        reduce_bias_grad,
        first_gain_grad,
        first_shift_grad,
        output_bias_grad,
    ) = (vector_grads[n] for n in range(6))
    mine = mp_index * width
    return (
        layer_out,
        input_grad,
        project_weight_grad.astype(f32),
        project_bias_grad,
        table_grads[: counts[0]],
        table_grads[counts[0] : counts[0] + counts[1]],
        table_grads[counts[0] + counts[1] :],
        output_weight_grad.astype(f32),
        output_bias_grad,
        lax.dynamic_slice_in_dim(first_gain_grad, mine, width, 0),
        lax.dynamic_slice_in_dim(first_shift_grad, mine, width, 0),
        expand_weight_grad.astype(f32),
        expand_bias_grad,
        reduce_weight_grad.astype(f32),
        reduce_bias_grad,
        second_gain_grad,
        second_shift_grad,
    )


def solution(mesh):
    placed = (
        P("dp", None, None),
        P("dp", None, None),
        P("dp"),
        P("dp", None),
        P("dp", None, None),
        P("dp", None, None),
        P("dp", None, None),
        P(None, None, "mp"),
        P(None, "mp"),
        P(None, "mp"),
        P(None, "mp"),
        P(None, "mp"),
        P("mp", None),
        P(),
        P(),
        P(),
        P(None, "mp"),
        P("mp"),
        P("mp", None),
        P(),
        P(),
        P(),
    )
    return jax.shard_map(
        partial(per_device, mesh.shape["dp"]),
        mesh=mesh,
        in_specs=placed,
        out_specs=(
            P("dp", None, None),
            P("dp", None, "mp"),
            P(None, None, "mp"),
            P(None, "mp"),
            P(None, "mp"),
            P(None, "mp"),
            P(None, "mp"),
            P("mp", None),
            P(),
            P("mp"),
            P("mp"),
            P(None, "mp"),
            P("mp"),
            P("mp", None),
            P(),
            P(),
            P(),
        ),
        check_vma=False,
    )
```

```python
from functools import partial

import jax
import jax.numpy as jnp
from jax import lax
from jax.experimental import pallas as pl
from jax.experimental.pallas import tpu as pltpu
from jax.sharding import PartitionSpec as P

LONG = 1089
SHORT = 709
HEAD = 64
LANES = 128
STRIP = 16
BLOCK_ROWS = 224
FEED_PIECE = 768
FEED_STRIP = 112
TABLE_STRIPS = 2
ATTEND_STRIPS = 7

large_negative = -1000000000.0
norm_epsilon = 1e-05
vmem_limit = 56 * 2**20
FINISH_VMEM = 62 * 2**20
bf16 = jnp.bfloat16
f32 = jnp.float32


def round_up(value, step):
    return (value + step - 1) // step * step


def whole_spec(array):
    zeros = (0,) * array.ndim
    return pl.BlockSpec(array.shape, lambda i: zeros)


def dot_f32(left, right):
    return jnp.dot(left, right, preferred_element_type=f32)


def gather_lanes(values, index):
    dims = lax.GatherDimensionNumbers(
        offset_dims=(),
        collapsed_slice_dims=(1,),
        start_index_map=(1,),
        operand_batching_dims=(0,),
        start_indices_batching_dims=(0,),
    )
    return lax.gather(
        values,
        index[..., None],
        dims,
        slice_sizes=(1, 1),
        mode=lax.GatherScatterMode.PROMISE_IN_BOUNDS,
    )


def quarter_rows(ref, quarter):
    count = ref.shape[0] // 4
    return pl.ds(pl.multiple_of(quarter * count, STRIP), count)


def prepare_kernel(
    token_ref,
    weight_ref,
    bias_ref,
    line_ref,
    across_ref,
    down_ref,
    flag_ref,
    mask_ref,
    expand_ref,
    query_ref,
    key_ref,
    key_turned_ref,
    value_ref,
    value_turned_ref,
    token_out_ref,
    plane_ref,
    down_out_ref,
    valid_ref,
    quarter_ref,
    row_ref,
    send_sem,
    recv_sem,
    *,
    length,
    line_count,
):
    step = pl.program_id(0)
    across_mp = {"mp": 1 - lax.axis_index("mp")}
    fetch = pltpu.make_async_remote_copy(
        src_ref=expand_ref.at[quarter_rows(expand_ref, lax.axis_index("dp") % 4), :],
        dst_ref=quarter_ref,
        send_sem=send_sem,
        recv_sem=recv_sem,
        device_id=across_mp,
        device_id_type=pl.DeviceIdType.MESH,
    )

    @pl.when(step == 0)
    def _():
        barrier = pltpu.get_barrier_semaphore()
        pl.semaphore_signal(
            barrier, inc=1, device_id=across_mp, device_id_type=pl.DeviceIdType.MESH
        )
        pl.semaphore_wait(barrier, 1)
        fetch.start()
        limit = jnp.where(flag_ref[0] > 0, LONG, SHORT)
        position = lax.broadcasted_iota(jnp.int32, (1, length), 1)
        row_ref[...] = jnp.zeros_like(row_ref)
        row_ref[0:1, :length] = jnp.where((mask_ref[...] > 0) & (position < limit), 1.0, 0.0)

    pl.when(step == pl.num_programs(0) - 1)(fetch.wait)
    rows = token_ref.shape[0]
    keys = plane_ref.shape[1]
    place = pl.program_id(0) * rows + lax.broadcasted_iota(jnp.int32, token_ref.shape, 0)
    token = jnp.where(place < length, token_ref[...].astype(f32), 0.0).astype(bf16)
    token_out_ref[...] = token
    bias = bias_ref[...].astype(f32)
    query = (dot_f32(token, weight_ref[0]) + bias[0:1, :]).astype(bf16)
    query_ref[...] = (query.astype(f32) * 0.125).astype(bf16)
    key = dot_f32(token, weight_ref[1])
    value = dot_f32(token, weight_ref[2]) + bias[1:2, :]
    away = jnp.where(row_ref[0:1, :] > 0, 0, line_count)
    inside = pl.program_id(0) * rows + lax.broadcasted_iota(jnp.int32, (rows, length), 0) < length
    line = line_ref[...].reshape(rows, length)
    across = across_ref[...].reshape(rows, length)
    down = down_ref[...].reshape(rows, length)
    plane = jnp.where(inside, line | (across << 8), 0) | away[:, :length]
    plane_ref[:, :length] = plane.astype(jnp.int16)
    plane_ref[:, length:] = jnp.full((rows, keys - length), line_count, jnp.int16)
    here = pl.ds(pl.multiple_of(step * rows, LANES), rows)
    valid_ref[...] = jnp.broadcast_to(row_ref[0:1, here], (LANES, rows)).T
    down_out_ref[:, :length] = jnp.where(inside, down, 0).astype(jnp.int16)
    down_out_ref[:, length:] = jnp.zeros((rows, keys - length), jnp.int16)
    lane_first = lax.broadcasted_iota(jnp.int32, (rows, LANES), 1) < HEAD
    row_first = lax.broadcasted_iota(jnp.int32, (LANES, rows), 0) < HEAD
    for p in range(key.shape[1] // LANES):
        cols = slice(p * LANES, (p + 1) * LANES)
        key_pair, value_pair = key[:, cols], value[:, cols]
        key_turned, value_turned = key_pair.T, value_pair.T
        for u in range(2):
            h = 2 * p + u
            lane_own = lane_first if u == 0 else ~lane_first
            row_own = row_first if u == 0 else ~row_first
            key_ref[h] = jnp.where(lane_own, key_pair, 0.0).astype(bf16)
            value_ref[h] = jnp.where(lane_own, value_pair, 1.0).astype(bf16)
            key_turned_ref[h] = jnp.where(row_own, key_turned, 0.0).astype(bf16)
            value_turned_ref[h] = jnp.where(row_own, value_turned, 0.0).astype(bf16)


def prepare(tokens, weight, bias, buckets, flag, token_mask, expand, row_count, keys, line_count):
    length, depth = tokens.shape
    width = weight.shape[2]
    heads = width // HEAD
    block = 3 * LANES
    row = pl.BlockSpec((block, width), lambda i: (i, 0))
    deep_row = pl.BlockSpec((block, depth), lambda i: (i, 0))
    wide = pl.BlockSpec((heads, block, LANES), lambda i: (0, i, 0))
    turned = pl.BlockSpec((heads, LANES, block), lambda i: (0, 0, i))
    bucket = pl.BlockSpec((block, 1, length), lambda i: (i, 0, 0))
    packed = pl.BlockSpec((block, keys), lambda i: (i, 0))
    wide_shape = jax.ShapeDtypeStruct((heads, keys, LANES), bf16)
    turned_shape = jax.ShapeDtypeStruct((heads, LANES, keys), bf16)
    packed_shape = jax.ShapeDtypeStruct((row_count, keys), jnp.int16)
    return pl.pallas_call(
        partial(prepare_kernel, length=length, line_count=line_count),
        grid=(keys // block,),
        in_specs=[
            deep_row,
            whole_spec(weight),
            whole_spec(bias),
            bucket,
            bucket,
            bucket,
            pl.BlockSpec(memory_space=pltpu.SMEM),
            whole_spec(token_mask),
            pl.BlockSpec(memory_space=pl.ANY),
        ],
        out_specs=[
            row,
            wide,
            turned,
            wide,
            turned,
            deep_row,
            packed,
            packed,
            pl.BlockSpec((block, LANES), lambda i: (i, 0)),
            pl.BlockSpec(memory_space=pl.ANY),
        ],
        out_shape=[
            jax.ShapeDtypeStruct((keys, width), bf16),
            wide_shape,
            turned_shape,
            wide_shape,
            turned_shape,
            jax.ShapeDtypeStruct((keys, depth), bf16),
            packed_shape,
            packed_shape,
            jax.ShapeDtypeStruct((keys, LANES), f32),
            jax.ShapeDtypeStruct((expand.shape[0] // 4, expand.shape[1]), bf16),
        ],
        scratch_shapes=[
            pltpu.VMEM((8, keys), f32),
            pltpu.SemaphoreType.DMA,
            pltpu.SemaphoreType.DMA,
        ],
        compiler_params=pltpu.CompilerParams(
            vmem_limit_bytes=vmem_limit, collective_id=2, has_side_effects=True
        ),
        name="prepare",
    )(
        tokens,
        weight,
        bias,
        *(index.reshape(length, 1, length) for index in buckets),
        flag,
        token_mask,
        expand,
    )


def attend_kernel(
    query_ref,
    key_ref,
    value_ref,
    plane_ref,
    down_ref,
    line_table_ref,
    across_table_ref,
    down_table_ref,
    expand_bias_ref,
    expand_quarter_ref,
    output_ref,
    reduce_ref,
    exp_ref,
    context_ref,
    inverse_ref,
    context_away_ref,
    expand_away_ref,
    output_away_ref,
    reduce_away_ref,
    bias_away_ref,
    score_ref,
    send_ref,
    table_ref,
    bias_ref,
    local_sem,
    send_sem,
    recv_sem,
):
    heads, rows, keys = exp_ref.shape
    step = pl.program_id(0)
    place = lax.axis_index("dp")
    across_mp = {"mp": 1 - lax.axis_index("mp")}
    across = {bit: {"dp": place + bit * (1 - 2 * ((place // bit) % 2))} for bit in (1, 2)}

    def remote(src, dst, n, device):
        return pltpu.make_async_remote_copy(
            src_ref=src,
            dst_ref=dst,
            send_sem=send_sem.at[n],
            recv_sem=recv_sem.at[n],
            device_id=device,
            device_id_type=pl.DeviceIdType.MESH,
        )

    arrays = (
        (expand_quarter_ref, expand_away_ref),
        (output_ref, output_away_ref),
        (reduce_ref, reduce_away_ref),
    )
    quarter = place % 4
    other_chip = (place + 2) % 4
    other_core = quarter + 1 - 2 * (quarter % 2)
    third = (other_core + 2) % 4

    def rows_of(n, which):
        away = arrays[n][1]
        return away.at[quarter_rows(away, which), :]

    def fetch(n):
        ref = arrays[n][0]
        return remote(ref.at[quarter_rows(ref, quarter), :], rows_of(n, quarter), n, across_mp)

    def pass_on(n, stage):
        source = expand_quarter_ref if n == 0 and stage < 2 else rows_of(n, quarter)
        if stage == 0:
            return remote(source, rows_of(n, quarter), 3 + n, across[2])
        if stage == 1:
            return remote(source, rows_of(n, quarter), 6 + n, across[1])
        return remote(rows_of(n, other_chip), rows_of(n, other_chip), 9 + n, across[1])

    def arrival(n, stage):
        region = rows_of(n, (other_chip, other_core, third)[stage])
        return remote(region, region, 3 + 3 * stage + n, across_mp)

    keep = pltpu.make_async_copy(expand_quarter_ref, rows_of(0, quarter), local_sem)
    context_swap = remote(send_ref, context_away_ref, 12, across_mp)
    bias_swap = remote(bias_ref, bias_away_ref, 13, across_mp)

    def event(n, stage):
        if stage == "fetched":
            fetch(n).wait_recv()
            pass_on(n, 0).start()
            pass_on(n, 1).start()
        else:
            arrival(n, 0).wait_recv()
            pass_on(n, 2).start()

    events = {
        (0, 2): ((1, "fetched"),),
        (1, 0): ((0, "passed"), (2, "fetched")),
        (1, 1): ((1, "passed"),),
    }

    @pl.when(step == 0)
    def _():
        barrier = pltpu.get_barrier_semaphore()
        for device in (across_mp, across[1], across[2]):
            pl.semaphore_signal(
                barrier, inc=1, device_id=device, device_id_type=pl.DeviceIdType.MESH
            )
        pl.semaphore_wait(barrier, 3)
        bias_ref[...] = jnp.broadcast_to(
            expand_bias_ref[...].astype(f32).reshape(1, -1), bias_ref.shape
        )
        bias_swap.start()
        for t, ref in enumerate((line_table_ref, across_table_ref, down_table_ref)):
            count = ref.shape[1]
            lanes = jnp.concatenate(
                [ref[...].astype(f32), jnp.full((heads, LANES - count), large_negative, f32)], axis=1
            )
            for h in range(heads):
                table_ref[t * heads + h] = jnp.broadcast_to(lanes[h : h + 1], (STRIP, LANES)).astype(
                    bf16
                )
        fetch(1).start()
        fetch(2).start()
        pass_on(0, 0).start()
        pass_on(0, 1).start()
        keep.start()

    for h in range(heads):
        pair = slice(h // 2 * LANES, (h // 2 + 1) * LANES)
        score_ref[h] = dot_f32(query_ref[:, pair], key_ref[h])

    lanes = [slice(c * LANES, (c + 1) * LANES) for c in range(keys // LANES)]

    def scores_of(at):
        scores = [[] for _ in range(heads)]
        for cols in lanes:
            packed = plane_ref[at, cols]
            bias = [None] * heads
            for t, index in enumerate(
                (packed & jnp.int16(255), packed >> jnp.int16(8), down_ref[at, cols])
            ):
                for h in range(heads):
                    found = gather_lanes(table_ref[t * heads + h], index).astype(f32)
                    bias[h] = found if t == 0 else bias[h] + found
            for h in range(heads):
                scores[h].append(score_ref[h, at, cols] + bias[h])
        return scores

    def exps_of(scores):
        exps = []
        for parts in scores:
            top = parts[0]
            for part in parts[1:]:
                top = jnp.maximum(top, part)
            top = jnp.max(top, axis=1, keepdims=True)
            exps.append([jnp.exp(part - top).astype(bf16) for part in parts])
        return exps

    def strips(n, carry):
        for (at_step, at_turn), pieces in events.items():

            @pl.when((step == at_step) & (n == at_turn))
            def _():
                for piece in pieces:
                    event(*piece)

        start = pl.multiple_of(n * ATTEND_STRIPS * STRIP, STRIP)
        places = [pl.ds(start + k * STRIP, STRIP) for k in range(ATTEND_STRIPS)]
        scores = [scores_of(at) for at in places]
        exps = [exps_of(part) for part in scores]
        for at, part in zip(places, exps):
            for h in range(heads):
                for c, cols in enumerate(lanes):
                    exp_ref[h, at, cols] = part[h][c]
        return carry

    lax.fori_loop(0, rows // (ATTEND_STRIPS * STRIP), strips, 0)
    first = lax.broadcasted_iota(jnp.int32, (rows, LANES), 1) < HEAD
    for p in range(heads // 2):
        cols = slice(p * LANES, (p + 1) * LANES)
        even = dot_f32(exp_ref[2 * p], value_ref[2 * p])
        odd = dot_f32(exp_ref[2 * p + 1], value_ref[2 * p + 1])
        sums = jnp.where(first, pltpu.roll(even, HEAD, 1), pltpu.roll(odd, HEAD, 1))
        inverse = 1.0 / sums
        inverse_ref[:, cols] = inverse
        context = (jnp.where(first, even, odd) * inverse).astype(bf16)
        context_ref[:, cols] = context

        @pl.when(step == 0)
        def _():
            send_ref[:, cols] = context

    pl.when(step == 0)(context_swap.start)

    @pl.when(step == 1)
    def _():
        event(2, "passed")
        keep.wait()
        context_swap.wait()
        bias_swap.wait()
        for n in range(3):
            arrival(n, 1).wait_recv()
            arrival(n, 2).wait_recv()
            for stage in range(3):
                pass_on(n, stage).wait_send()
        fetch(1).wait_send()
        fetch(2).wait_send()


def attend(
    query,
    key_turned,
    value_ones,
    plane,
    down,
    tables,
    expand_bias,
    expand_quarter,
    output,
    reduce,
):
    heads, _, keys = key_turned.shape
    row_count = plane.shape[0]
    width = heads * HEAD
    half_rows = row_count // 2

    def half(i):
        return lax.rem(i + 1 - lax.axis_index("mp"), 2)

    anywhere = pl.BlockSpec(memory_space=pl.ANY)
    index_spec = pl.BlockSpec((half_rows, keys), lambda i: (half(i), 0))
    row_spec = pl.BlockSpec((half_rows, width), lambda i: (half(i), 0))
    return pl.pallas_call(
        attend_kernel,
        grid=(2,),
        in_specs=[
            row_spec,
            whole_spec(key_turned),
            whole_spec(value_ones),
            index_spec,
            index_spec,
            *(whole_spec(table) for table in tables),
            whole_spec(expand_bias),
            anywhere,
            anywhere,
            anywhere,
        ],
        out_specs=[
            pl.BlockSpec((heads, half_rows, keys), lambda i: (0, half(i), 0)),
            row_spec,
            row_spec,
            anywhere,
            anywhere,
            anywhere,
            anywhere,
            anywhere,
        ],
        out_shape=[
            jax.ShapeDtypeStruct((heads, row_count, keys), bf16),
            jax.ShapeDtypeStruct((row_count, width), bf16),
            jax.ShapeDtypeStruct((row_count, width), f32),
            jax.ShapeDtypeStruct((half_rows, width), bf16),
            jax.ShapeDtypeStruct((4 * expand_quarter.shape[0], expand_quarter.shape[1]), bf16),
            jax.ShapeDtypeStruct(output.shape, bf16),
            jax.ShapeDtypeStruct(reduce.shape, bf16),
            jax.ShapeDtypeStruct((8, expand_bias.size), f32),
        ],
        scratch_shapes=[
            pltpu.VMEM((heads, half_rows, keys), f32),
            pltpu.VMEM((half_rows, width), bf16),
            pltpu.VMEM((3 * heads, STRIP, LANES), bf16),
            pltpu.VMEM((8, expand_bias.size), f32),
            pltpu.SemaphoreType.DMA,
            pltpu.SemaphoreType.DMA((14,)),
            pltpu.SemaphoreType.DMA((14,)),
        ],
        compiler_params=pltpu.CompilerParams(
            vmem_limit_bytes=vmem_limit, collective_id=1, has_side_effects=True
        ),
        name="attend",
    )(
        query,
        key_turned,
        value_ones,
        plane,
        down,
        *tables,
        expand_bias,
        expand_quarter,
        output,
        reduce,
    )


def attend_back_kernel(
    exp_ref,
    grad_ref,
    context_ref,
    query_ref,
    value_ref,
    key_ref,
    grad_score_ref,
    grad_query_ref,
    grad_key_ref,
    grad_value_ref,
):
    heads, rows, _ = exp_ref.shape

    @pl.when(pl.program_id(0) == 0)
    def _():
        grad_key_ref[...] = jnp.zeros_like(grad_key_ref)
        grad_value_ref[...] = jnp.zeros_like(grad_value_ref)

    first = lax.broadcasted_iota(jnp.int32, (rows, LANES), 1) < HEAD
    for p in range(heads // 2):
        cols = slice(p * LANES, (p + 1) * LANES)
        grad = grad_ref[:, cols]
        product = grad.astype(f32) * context_ref[:, cols].astype(f32)
        query_turned = query_ref[:, cols].T
        grad_turned = grad.T
        grad_query = None
        for u in range(2):
            h = 2 * p + u
            half = slice(u * HEAD, (u + 1) * HEAD)
            own = first if u == 0 else ~first
            total = jnp.sum(jnp.where(own, product, 0.0), axis=1, keepdims=True)
            grad_exp = dot_f32(grad, value_ref[h])
            grad_score = (exp_ref[h].astype(f32) * (grad_exp - total)).astype(bf16)
            grad_score_ref[h] = grad_score
            part = dot_f32(grad_score, key_ref[h])
            grad_query = part if u == 0 else grad_query + part
            grad_key_ref[h] += dot_f32(query_turned[half], grad_score)
            grad_value_ref[h] += dot_f32(grad_turned[half], exp_ref[h])
        grad_query_ref[:, cols] = (grad_query * 0.125).astype(bf16)


def attend_back(exps, grad, context, query, value_turned, key_wide):
    heads, row_count, keys = exps.shape
    width = heads * HEAD
    row_spec = pl.BlockSpec((BLOCK_ROWS, width), lambda i: (i, 0))
    exp_spec = pl.BlockSpec((heads, BLOCK_ROWS, keys), lambda i: (0, i, 0))
    sum_spec = pl.BlockSpec((heads, HEAD, keys), lambda i: (0, 0, 0))
    return pl.pallas_call(
        attend_back_kernel,
        grid=(row_count // BLOCK_ROWS,),
        in_specs=[
            exp_spec,
            row_spec,
            row_spec,
            row_spec,
            whole_spec(value_turned),
            whole_spec(key_wide),
        ],
        out_specs=[exp_spec, row_spec, sum_spec, sum_spec],
        out_shape=[
            jax.ShapeDtypeStruct((heads, row_count, keys), bf16),
            jax.ShapeDtypeStruct((row_count, width), bf16),
            jax.ShapeDtypeStruct((heads, HEAD, keys), f32),
            jax.ShapeDtypeStruct((heads, HEAD, keys), f32),
        ],
        compiler_params=pltpu.CompilerParams(vmem_limit_bytes=vmem_limit),
        name="attend_back",
    )(exps, grad, context, query, value_turned, key_wide)


def table_strips(strips, sum_ref, heads, keys, high_counts):
    base = 0
    for t in range(3):
        shift = 8 if t == 1 else 0
        highs, lows = [], []
        for grad_of, plane_of, down_of in strips:
            for c in range(keys // LANES):
                cols = slice(c * LANES, (c + 1) * LANES)
                index = down_of(cols) if t == 2 else plane_of(cols)
                low = index & jnp.int16(15 << shift)
                high = index & jnp.int16(48 << shift)
                lows.append(
                    jnp.concatenate(
                        [
                            jnp.where(low == jnp.int16(x << shift), bf16(1), bf16(0))
                            for x in range(16)
                        ]
                    )
                )
                parts = []
                for x in range(high_counts[t]):
                    mask = high == jnp.int16(x << (4 + shift))
                    parts += [jnp.where(mask, grad_of(h, cols), bf16(0)) for h in range(heads)]
                highs.append(jnp.concatenate(parts))
        span = slice(base, base + high_counts[t] * heads * STRIP)
        sum_ref[span, :] += lax.dot_general(
            jnp.concatenate(highs, axis=1),
            jnp.concatenate(lows, axis=1),
            (((1,), (1,)), ((), ())),
            preferred_element_type=f32,
        )
        base = span.stop


def table_finish(sum_ref, out_ref, count):
    row_of_lane = lax.broadcasted_iota(jnp.int32, (STRIP, 16 * STRIP), 1) % STRIP
    same = row_of_lane == lax.broadcasted_iota(jnp.int32, (STRIP, 16 * STRIP), 0)
    for o in range(count):
        block = sum_ref[o * STRIP : (o + 1) * STRIP, :]
        out_ref[o : o + 1, :] = jnp.sum(jnp.where(same, block, 0.0), axis=0, keepdims=True)


def table_result(out, high_counts, heads):
    summed = jnp.sum(out.reshape(sum(high_counts), heads, 16, STRIP), axis=-1)
    return summed.transpose(0, 2, 1).reshape(-1, heads)


def table_kernel(grad_score_ref, plane_ref, down_ref, out_ref, sum_ref, *, high_counts):
    heads, rows, keys = grad_score_ref.shape
    step = pl.program_id(0)

    @pl.when(step == 0)
    def _():
        sum_ref[...] = jnp.zeros_like(sum_ref)

    def refs_at(start):
        at = pl.ds(pl.multiple_of(start, STRIP), STRIP)
        return (
            lambda h, cols: grad_score_ref[h, at, cols],
            lambda cols: plane_ref[at, cols],
            lambda cols: down_ref[at, cols],
        )

    def strips(r, carry):
        start = r * (TABLE_STRIPS * STRIP)
        table_strips(
            [refs_at(start + k * STRIP) for k in range(TABLE_STRIPS)],
            sum_ref,
            heads,
            keys,
            high_counts,
        )
        return carry

    lax.fori_loop(0, rows // (TABLE_STRIPS * STRIP), strips, 0)

    @pl.when(step == pl.num_programs(0) - 1)
    def _():
        table_finish(sum_ref, out_ref, out_ref.shape[0])


def table_sums(grad_scores, plane, down, counts):
    heads, row_count, keys = grad_scores.shape
    high_counts = (counts[0] // 16, counts[1] // 16, counts[1] // 16)
    high_rows = sum(high_counts) * heads
    index_spec = pl.BlockSpec((BLOCK_ROWS, keys), lambda i: (i, 0))
    out = pl.pallas_call(
        partial(table_kernel, high_counts=high_counts),
        grid=(row_count // BLOCK_ROWS,),
        in_specs=[
            pl.BlockSpec((heads, BLOCK_ROWS, keys), lambda i: (0, i, 0)),
            index_spec,
            index_spec,
        ],
        out_specs=pl.BlockSpec((high_rows, 16 * STRIP), lambda i: (0, 0)),
        out_shape=jax.ShapeDtypeStruct((high_rows, 16 * STRIP), f32),
        scratch_shapes=[pltpu.VMEM((high_rows * STRIP, 16 * STRIP), f32)],
        compiler_params=pltpu.CompilerParams(vmem_limit_bytes=vmem_limit),
        name="table_sums",
    )(grad_scores, plane, down)
    return table_result(out, high_counts, heads)


CHUNK = 768
CHUNKS = 6
LOCAL_CHUNKS = 2
PARTS = (CHUNK // 2, CHUNK // 4, CHUNK // 8, CHUNK // 16)
BITS = ((1, 2, 4, 8), (1, 4, 2, 8), (1, 2, 4, 8), (1, 4, 2, 8), (1, 2, 4, 8), (1, 4, 2, 8))
BACK_ROWS = 112
EXCHANGE = (
    ("b", 0, 0, 2), ("b", 0, 0, 3), ("b", 0, 0, 4), ("b", 1, 0, 5), ("b", 4, 1, 2), ("b", 6, 1, 3),
    ("b", 8, 1, 4), ("b", 9, 1, 5), ("b", 20, 2, 2), ("b", 22, 2, 3), ("p", 0, 3, 2), ("p", 2, 2, 4),
    ("p", 3, 2, 5), ("p", 3, 3, 3), ("p", 3, 0, 0), ("p", 3, 0, 1), ("t", 0, 4, 2), ("t", 1, 1, 0),
    ("t", 1, 1, 1), ("t", 2, 4, 3), ("t", 2, "small", 0), ("t", 3, 3, 4), ("t", 4, 5, 2),
    ("t", 5, "send", 0), ("t", 6, 3, 5), ("t", 6, 2, 0), ("t", 6, 2, 1), ("t", 6, "small", 1),
    ("t", 8, 5, 3), ("t", 9, 4, 4), ("t", 10, 4, 5), ("t", 11, 6, 2), ("t", 11, "small", 2),
    ("t", 12, 3, 1), ("t", 12, 3, 0), ("t", 13, 6, 3), ("t", 15, 5, 4), ("t", 16, "layer", 0),
    ("t", 16, "small", 3), ("t", 17, 5, 5), ("t", 17, 7, 3), ("t", 18, 7, 2), ("t", 18, "input", 0),
    ("t", 19, 4, 1), ("t", 19, 4, 0), ("t", 20, "small", 4), ("t", 21, 6, 4), ("t", 22, 8, 2),
    ("t", 23, 6, 5), ("t", 24, 9, 2), ("t", 25, "small", 5), ("t", 26, 8, 3), ("t", 27, 5, 1),
    ("t", 27, 7, 5), ("t", 28, 9, 3), ("t", 29, 5, 0), ("t", 29, 7, 4), ("t", 31, 6, 1),
    ("t", 33, 8, 5), ("e", 0, 9, 5), ("e", 0, 8, 4), ("e", 0, 6, 0), ("e", 0, 9, 4), ("e", 0, 7, 1),
    ("e", 0, 8, 1), ("e", 0, 7, 0), ("e", 0, 8, 0),
)


def plan_slots(phase, count):
    slots = [[] for _ in range(count)]
    for name, at, event, which in EXCHANGE:
        if name == phase:
            slots[at].append((event, which))
    return slots


def finish_kernel(
    exp_ref,
    inverse_ref,
    plane_ref,
    down_ref,
    context_ref,
    query_ref,
    token_ref,
    grad_ref,
    layer_ref,
    value_ref,
    key_ref,
    project_ref,
    output_ref,
    expand_ref,
    expand_away_ref,
    reduce_ref,
    reduce_away_ref,
    small_ref,
    total_ref,
    layer_out_ref,
    input_ref,
    small_out_ref,
    table_ref,
    score_ref,
    output_buf,
    grad_buf,
    value_buf,
    key_buf,
    context_buf,
    query_buf,
    token_buf,
    project_buf,
    ring_buf,
    inverse_buf,
    grad_key_buf,
    grad_value_buf,
    triple_buf,
    input_send_buf,
    input_recv_buf,
    input_buf,
    plane_buf,
    down_buf,
    sum_ref,
    own_buf,
    away_buf,
    core_buf,
    core_away_buf,
    first_buf,
    first_away_buf,
    y_buf,
    second_buf,
    third_buf,
    small_buf,
    small_recv_buf,
    table_buf,
    table_recv_buf,
    resident_sem,
    block_sem,
    ring_sem,
    load_sem,
    local_sem,
    out_sem,
    send_sem,
    recv_sem,
    wide_send_sem,
    wide_recv_sem,
    small_send_sem,
    small_recv_sem,
    table_send_sem,
    table_recv_sem,
    *,
    high_counts,
):
    heads, row_count, keys = exp_ref.shape
    width = heads * HEAD
    half_rows = row_count // 2
    rows = BACK_ROWS
    blocks = row_count // rows
    block_strips = rows // STRIP
    turns = row_count // (TABLE_STRIPS * STRIP)
    place = lax.axis_index("dp")
    mp_index = lax.axis_index("mp")
    side_of = {bit: (place // bit) % 2 for bit in (1, 2, 4, 8)}
    partner_of = {bit: {"dp": place + bit * (1 - 2 * side_of[bit])} for bit in (1, 2, 4, 8)}
    across_mp = {"mp": 1 - mp_index}

    barrier = pltpu.get_barrier_semaphore()
    for device in (*partner_of.values(), across_mp):
        pl.semaphore_signal(barrier, inc=1, device_id=device, device_id_type=pl.DeviceIdType.MESH)
    pl.semaphore_wait(barrier, 5)

    def rows_at(start, size):
        return pl.ds(pl.multiple_of(start, STRIP), size)

    def remote(src, dst, send, recv, device):
        return pltpu.make_async_remote_copy(
            src_ref=src,
            dst_ref=dst,
            send_sem=send,
            recv_sem=recv,
            device_id=device,
            device_id_type=pl.DeviceIdType.MESH,
        )

    mine = rows_at(mp_index * half_rows, half_rows)
    others = rows_at((1 - mp_index) * half_rows, half_rows)
    grad_swap = remote(
        grad_ref, grad_buf.at[1], wide_send_sem.at[0], wide_recv_sem.at[0], across_mp
    )
    input_swap = remote(
        input_send_buf, input_recv_buf, wide_send_sem.at[1], wide_recv_sem.at[1], across_mp
    )
    layer_swap = remote(
        layer_ref, layer_out_ref.at[mine, :], wide_send_sem.at[2], wide_recv_sem.at[2], across_mp
    )
    layer_arrival = remote(
        layer_out_ref.at[others, :],
        layer_out_ref.at[others, :],
        wide_send_sem.at[2],
        wide_recv_sem.at[2],
        across_mp,
    )
    layer_keep = pltpu.make_async_copy(layer_ref, layer_out_ref.at[mine, :], out_sem.at[2])
    grad_swap.start()

    residents = [
        pltpu.make_async_copy(src, dst, resident_sem.at[n])
        for n, (src, dst) in enumerate(
            (
                (grad_ref, grad_buf.at[0]),
                (output_ref, output_buf),
                (context_ref, context_buf),
                (query_ref, query_buf),
                (value_ref, value_buf),
                (key_ref, key_buf),
                (small_ref, small_buf.at[0]),
                (token_ref, token_buf),
                (project_ref, project_buf),
            )
        )
    ]

    def block_rows(block):
        start = (mp_index * (blocks // 2) + block) % blocks
        return rows_at(start * rows, rows)

    def block_copies(block, slot):
        at = block_rows(block)
        return (
            pltpu.make_async_copy(exp_ref.at[:, at, :], ring_buf.at[slot], block_sem.at[slot, 0]),
            pltpu.make_async_copy(inverse_ref.at[at, :], inverse_buf.at[slot], block_sem.at[slot, 1]),
        )

    def score_copy(block, slot):
        return pltpu.make_async_copy(
            ring_buf.at[2 + slot], score_ref.at[:, block_rows(block), :], out_sem.at[slot]
        )

    def ring_copies(block):
        slot = block % 4
        at = rows_at(block * rows, rows)
        return (
            pltpu.make_async_copy(score_ref.at[:, at, :], ring_buf.at[slot], ring_sem.at[slot, 0]),
            pltpu.make_async_copy(plane_ref.at[at, :], plane_buf.at[slot], ring_sem.at[slot, 1]),
            pltpu.make_async_copy(down_ref.at[at, :], down_buf.at[slot], ring_sem.at[slot, 2]),
        )

    def is_away(chunk):
        return chunk >= LOCAL_CHUNKS

    loads = {}
    for ref, away_ref, wide in (
        (expand_ref, expand_away_ref, True),
        (reduce_ref, reduce_away_ref, False),
    ):
        for k in range(2):
            piece = slice(k * CHUNK, (k + 1) * CHUNK)
            index = (slice(None), piece) if wide else (piece, slice(None))
            chunk = LOCAL_CHUNKS + len(loads)
            loads[chunk] = (
                pltpu.make_async_copy(ref.at[index], own_buf.at[chunk], load_sem.at[chunk, 0]),
                pltpu.make_async_copy(
                    away_ref.at[index], away_buf.at[chunk - LOCAL_CHUNKS], load_sem.at[chunk, 1]
                ),
            )

    for copy in loads[LOCAL_CHUNKS]:
        copy.start()
    for copy in residents[:2]:
        copy.start()
    for copy in block_copies(0, 0):
        copy.start()
    for copy in residents[2:6]:
        copy.start()
    for chunk in range(LOCAL_CHUNKS + 1, CHUNKS):
        for copy in loads[chunk]:
            copy.start()
    residents[6].start()
    for copy in residents[7:]:
        copy.start()

    keeps, leaves = [], []
    for bits in BITS:
        kept, left, base = [], [], 0
        for size, bit in zip(PARTS, bits):
            kept.append(base + side_of[bit] * size)
            left.append(base + (1 - side_of[bit]) * size)
            base = base + side_of[bit] * size
        keeps.append(kept)
        leaves.append(left)
    arrivals = (core_buf, first_buf, second_buf, third_buf)
    away_arrivals = (core_away_buf, first_away_buf)

    def staged(src, dst, chunk, stage, device):
        return remote(src, dst, send_sem.at[chunk, stage], recv_sem.at[chunk, stage], device)

    def scatter(chunk, level):
        return staged(
            own_buf.at[chunk, rows_at(leaves[chunk][level], PARTS[level]), :],
            arrivals[level].at[chunk],
            chunk,
            level,
            partner_of[BITS[chunk][level]],
        )

    def scatter_away(chunk, level):
        return staged(
            away_buf.at[chunk - LOCAL_CHUNKS, rows_at(leaves[chunk][level], PARTS[level]), :],
            away_arrivals[level].at[chunk - LOCAL_CHUNKS],
            chunk,
            4 + level,
            partner_of[BITS[chunk][level]],
        )

    def hand_over(chunk):
        return staged(
            away_buf.at[chunk - LOCAL_CHUNKS, rows_at(keeps[chunk][1], PARTS[1]), :],
            y_buf.at[chunk - LOCAL_CHUNKS],
            chunk,
            6,
            across_mp,
        )

    def total_rows(chunk, start, size):
        return total_ref.at[rows_at(chunk * CHUNK + start, size), :]

    def gather(chunk, level):
        kept, size = keeps[chunk][level], PARTS[level]
        if level == 3:
            src = own_buf.at[chunk, rows_at(kept, size), :]
        else:
            src = total_rows(chunk, kept, size)
        return staged(
            src, total_rows(chunk, kept, size), chunk, 7 + level, partner_of[BITS[chunk][level]]
        )

    def gathered(chunk, level):
        region = total_rows(chunk, leaves[chunk][level], PARTS[level])
        return staged(region, region, chunk, 7 + level, partner_of[BITS[chunk][level]])

    def store_own(chunk):
        return pltpu.make_async_copy(
            own_buf.at[chunk, rows_at(keeps[chunk][3], PARTS[3]), :],
            total_rows(chunk, keeps[chunk][3], PARTS[3]),
            local_sem.at[chunk],
        )

    def add(buf, chunk, start, size, arrived):
        piece = PARTS[3]

        def step(n, carry):
            here = rows_at(start + n * piece, piece)
            there = rows_at(n * piece, piece)
            buf[chunk, here, :] = buf[chunk, here, :] + arrived[there, :]
            return carry

        lax.fori_loop(0, size // piece, step, 0)

    def add_level(chunk, level):
        scatter(chunk, level).wait_recv()
        add(own_buf, chunk, keeps[chunk][level], PARTS[level], arrivals[level].at[chunk])

    def add_level_away(chunk, level):
        at = chunk - LOCAL_CHUNKS
        scatter_away(chunk, level).wait_recv()
        add(away_buf, at, keeps[chunk][level], PARTS[level], away_arrivals[level].at[at])

    def exchange(event, chunk):
        away = is_away(chunk)
        if event == 0:
            if away:
                for copy in loads[chunk]:
                    copy.wait()
                scatter_away(chunk, 0).start()
            scatter(chunk, 0).start()
            return
        if event == 1:
            if away:
                add_level_away(chunk, 0)
                scatter_away(chunk, 1).start()
            add_level(chunk, 0)
            scatter(chunk, 1).start()
            return
        if away and event == 2:
            add_level_away(chunk, 1)
            hand_over(chunk).start()
            add_level(chunk, 1)
            return
        if away:
            event -= 1
            if event == 2:
                hand_over(chunk).wait_recv()
                add(own_buf, chunk, keeps[chunk][1], PARTS[1], y_buf.at[chunk - LOCAL_CHUNKS])
        elif event == 2:
            add_level(chunk, 1)
        if event == 2:
            scatter(chunk, 2).start()
        elif event == 3:
            add_level(chunk, 2)
            scatter(chunk, 3).start()
        elif event == 4:
            add_level(chunk, 3)
            store_own(chunk).start()
            gather(chunk, 3).start()
        else:
            level = 8 - event
            if level == 3:
                store_own(chunk).wait()
            gathered(chunk, level).wait_recv()
            if level > 0:
                gather(chunk, level - 1).start()

    small_devices = (across_mp, *partner_of.values())

    def small_hop(n):
        return remote(
            small_buf.at[n],
            small_recv_buf.at[n],
            small_send_sem.at[n],
            small_recv_sem.at[n],
            small_devices[n],
        )

    def small_step(n):
        if n == 0:
            residents[6].wait()
        else:
            small_hop(n - 1).wait_recv()
            small_buf[n] = small_buf[n - 1] + small_recv_buf[n - 1]
        if n < 5:
            small_hop(n).start()
        else:
            small_out_ref[...] = small_buf[n]

    def input_rows(side):
        return mine if side == 0 else others

    def input_product(side, target):
        at = input_rows(side)
        part = None
        for k in range(3):
            product = lax.dot_general(
                triple_buf[k, at, :],
                project_buf[k, rows_at(target * width, width), :],
                (((1,), (1,)), ((), ())),
                preferred_element_type=f32,
            )
            part = product if part is None else part + product
        if side == 0:
            cols = pl.ds(pl.multiple_of(target * width, LANES), width)
            part = part + grad_buf[0, :, cols].astype(f32)
        return part

    def input_store(side):
        return pltpu.make_async_copy(
            input_buf.at[side], input_ref.at[input_rows(side), :], out_sem.at[3 + side]
        )

    def run(event, which):
        if event == "small":
            small_step(which)
        elif event == "send":
            input_swap.start()
        elif event == "layer":
            layer_swap.start()
            layer_keep.start()
        elif event == "input":
            input_swap.wait_recv()
            for side in range(2):
                part = input_product(side, mp_index)
                input_buf[side] = part + input_recv_buf[input_rows(side), :].astype(f32)
                input_store(side).start()
        else:
            exchange(event, which)

    pairs = heads // 2
    block_slots = plan_slots("b", blocks * pairs)
    part_slots = plan_slots("p", 4)
    turn_slots = plan_slots("t", turns)
    rest = plan_slots("e", 1)[0]

    def run_all(steps):
        for event, which in steps:
            run(event, which)

    def dispatch(slots, n, low, high):
        if not any(slots[low:high]):
            return
        if high - low == 1:
            for event, which in slots[low]:
                run(event, which)
            return
        middle = (low + high) // 2
        if any(slots[low:middle]):
            pl.when(n < middle)(lambda: dispatch(slots, n, low, middle))
        if any(slots[middle:high]):
            pl.when(n >= middle)(lambda: dispatch(slots, n, middle, high))

    grad_key_buf[...] = jnp.zeros_like(grad_key_buf)
    grad_value_buf[...] = jnp.zeros_like(grad_value_buf)
    sum_ref[...] = jnp.zeros_like(sum_ref)
    for copy in residents[:6]:
        copy.wait()
    first = lax.broadcasted_iota(jnp.int32, (rows, LANES), 1) < HEAD

    def back(block, carry):
        slot = block % 2
        at = block_rows(block)
        for copy in block_copies(block, slot):
            copy.wait()

        @pl.when(block + 1 < blocks)
        def _():
            for copy in block_copies(block + 1, 1 - slot):
                copy.start()

        pl.when(block == blocks // 2)(grad_swap.wait_recv)
        pl.when(block >= 2)(lambda: score_copy(block - 2, slot).wait())
        side = block // (blocks // 2)
        local = rows_at((block % (blocks // 2)) * rows, rows)
        grad_context = lax.dot_general(
            grad_buf[side, local, :],
            output_buf[...],
            (((1,), (1,)), ((), ())),
            preferred_element_type=f32,
        )
        scaled = (grad_context * inverse_buf[slot]).astype(bf16)
        for p in range(pairs):
            dispatch(block_slots, block * pairs + p, 0, blocks * pairs)
            cols = slice(p * LANES, (p + 1) * LANES)
            grad = scaled[:, cols]
            product = grad.astype(f32) * context_buf[at, cols].astype(f32)
            query_turned = query_buf[at, cols].T
            grad_turned = grad.T
            grad_query = None
            for u in range(2):
                h = 2 * p + u
                half = slice(u * HEAD, (u + 1) * HEAD)
                own = first if u == 0 else ~first
                total = jnp.sum(jnp.where(own, product, 0.0), axis=1, keepdims=True)
                exps = ring_buf[slot, h]
                grad_exp = dot_f32(grad, value_buf[h])
                grad_score = (exps.astype(f32) * (grad_exp - total)).astype(bf16)
                ring_buf[2 + slot, h] = grad_score
                part = dot_f32(grad_score, key_buf[h])
                grad_query = part if u == 0 else grad_query + part
                grad_key_buf[h] += dot_f32(query_turned[half], grad_score)
                grad_value_buf[h] += dot_f32(grad_turned[half], exps)
            triple_buf[0, at, cols] = (grad_query * 0.125).astype(bf16)
        score_copy(block, slot).start()
        return carry

    lax.fori_loop(0, blocks, back, 0)

    score_copy(blocks - 2, blocks % 2).wait()
    score_copy(blocks - 1, (blocks - 1) % 2).wait()
    for block in range(2):
        for copy in ring_copies(block):
            copy.start()
    run_all(part_slots[0])
    triple_buf[0, row_count:keys, :] = jnp.zeros((keys - row_count, width), bf16)
    for k, ref in ((1, grad_key_buf), (2, grad_value_buf)):
        for h in range(0, heads, 2):
            pair = ref[h : h + 2].reshape(LANES, keys)
            triple_buf[k, :, h * HEAD : (h + 2) * HEAD] = pair.T.astype(bf16)
    run_all(part_slots[1])
    for copy in residents[7:]:
        copy.wait()
    tokens_in = (((0,), (0,)), ((), ()))
    places = ((0, 0), (0, width), (1, 0))
    for k, (chunk, start) in enumerate(places):
        own_buf[chunk, start : start + width, :] = lax.dot_general(
            triple_buf[k], token_buf[...], tokens_in, preferred_element_type=f32
        ).astype(bf16)
    run_all(part_slots[2])
    own_buf[1, width : 2 * width, :] = (
        lax.dot_general(
            context_buf[mine, :], grad_buf[0], tokens_in, preferred_element_type=f32
        )
        + lax.dot_general(
            context_buf[others, :], grad_buf[1], tokens_in, preferred_element_type=f32
        )
    ).astype(bf16)
    run_all(part_slots[3])
    for side in range(2):
        input_send_buf[input_rows(side), :] = input_product(side, 1 - mp_index).astype(bf16)
    biases = jnp.concatenate(
        [
            jnp.sum(triple_buf[0].astype(f32), axis=0, keepdims=True),
            jnp.sum(triple_buf[2].astype(f32), axis=0, keepdims=True),
        ],
        axis=1,
    )

    def turn(n, carry):
        last = n * TABLE_STRIPS + TABLE_STRIPS - 1
        block = last // block_strips

        @pl.when(last % block_strips < TABLE_STRIPS)
        def _():
            for copy in ring_copies(block):
                copy.wait()

            @pl.when(block + 2 < blocks)
            def _():
                for copy in ring_copies(block + 2):
                    copy.start()

        dispatch(turn_slots, n, 0, turns)

        def refs_at(strip):
            slot = (strip // block_strips) % 4
            at = rows_at((strip % block_strips) * STRIP, STRIP)
            return (
                lambda h, cols: ring_buf[slot, h, at, cols],
                lambda cols: plane_buf[slot, at, cols],
                lambda cols: down_buf[slot, at, cols],
            )

        table_strips(
            [refs_at(n * TABLE_STRIPS + k) for k in range(TABLE_STRIPS)],
            sum_ref,
            heads,
            keys,
            high_counts,
        )
        return carry

    lax.fori_loop(0, turns, turn, 0)

    table_rows = sum(high_counts) * heads
    table_finish(sum_ref, table_buf.at[0], table_rows)
    lanes = table_buf.shape[2]
    pieces = 2 * width // lanes
    for n in range(pieces):
        table_buf[0, table_rows + n : table_rows + n + 1, :] = biases[:, n * lanes : (n + 1) * lanes]
    spare = table_buf.shape[1] - table_rows - pieces
    table_buf[0, table_rows + pieces :, :] = jnp.zeros((spare, lanes), f32)
    table_devices = tuple(partner_of.values())

    def table_hop(n):
        return remote(
            table_buf.at[n],
            table_recv_buf.at[n],
            table_send_sem.at[n],
            table_recv_sem.at[n],
            table_devices[n],
        )

    def table_step(n):
        if n > 0:
            table_hop(n - 1).wait_recv()
            table_buf[n] = table_buf[n - 1] + table_recv_buf[n - 1]
        if n < 4:
            table_hop(n).start()

    table_step(0)
    for n, (event, which) in enumerate(rest):
        if n % 3 == 2 and n // 3 < 4:
            table_step(n // 3 + 1)
        run(event, which)
    for n in range(min(len(rest) // 3, 4), 4):
        table_step(n + 1)
    table_ref[...] = table_buf[4]

    layer_arrival.wait_recv()
    layer_keep.wait()
    grad_swap.wait_send()
    input_swap.wait_send()
    layer_swap.wait_send()
    for side in range(2):
        input_store(side).wait()
    for n in range(5):
        small_hop(n).wait_send()
    for n in range(4):
        table_hop(n).wait_send()
    for chunk in range(CHUNKS):
        for level in range(4):
            scatter(chunk, level).wait_send()
            gather(chunk, level).wait_send()
        if is_away(chunk):
            scatter_away(chunk, 0).wait_send()
            scatter_away(chunk, 1).wait_send()
            hand_over(chunk).wait_send()


def finish(
    exps,
    inverse,
    plane,
    down,
    context,
    query,
    tokens,
    grad,
    layer,
    value_turned,
    key_wide,
    project_weight,
    output_weight,
    expand,
    reduce,
    small,
    counts,
):
    heads, row_count, keys = exps.shape
    width = heads * HEAD
    depth = tokens.shape[1]
    half_rows = row_count // 2
    high_counts = (counts[0] // 16, counts[1] // 16, counts[1] // 16)
    high_rows = sum(high_counts) * heads
    low_lanes = 16 * STRIP
    table_shape = (round_up(high_rows + 2 * width // low_lanes, 8), low_lanes)
    away = CHUNKS - LOCAL_CHUNKS
    anywhere = pl.BlockSpec(memory_space=pl.ANY)
    in_vmem = pl.BlockSpec(memory_space=pltpu.VMEM)
    dma = pltpu.SemaphoreType.DMA
    total, layer_full, input_full, small_sum, table_sum, _ = pl.pallas_call(
        partial(finish_kernel, high_counts=high_counts),
        in_specs=[anywhere] * 18,
        out_specs=[anywhere, anywhere, anywhere, in_vmem, in_vmem, anywhere],
        out_shape=[
            jax.ShapeDtypeStruct((CHUNKS * CHUNK, CHUNK), bf16),
            jax.ShapeDtypeStruct((row_count, depth), bf16),
            jax.ShapeDtypeStruct((row_count, width), f32),
            jax.ShapeDtypeStruct(small.shape, f32),
            jax.ShapeDtypeStruct(table_shape, f32),
            jax.ShapeDtypeStruct(exps.shape, bf16),
        ],
        scratch_shapes=[
            pltpu.VMEM(output_weight.shape, bf16),
            pltpu.VMEM((2, half_rows, depth), bf16),
            pltpu.VMEM(value_turned.shape, bf16),
            pltpu.VMEM(key_wide.shape, bf16),
            pltpu.VMEM(context.shape, bf16),
            pltpu.VMEM(query.shape, bf16),
            pltpu.VMEM(tokens.shape, bf16),
            pltpu.VMEM(project_weight.shape, bf16),
            pltpu.VMEM((4, heads, BACK_ROWS, keys), bf16),
            pltpu.VMEM((2, BACK_ROWS, width), f32),
            pltpu.VMEM((heads, HEAD, keys), f32),
            pltpu.VMEM((heads, HEAD, keys), f32),
            pltpu.VMEM((3, keys, width), bf16),
            pltpu.VMEM((row_count, width), bf16),
            pltpu.VMEM((row_count, width), bf16),
            pltpu.VMEM((2, half_rows, width), f32),
            pltpu.VMEM((4, BACK_ROWS, keys), jnp.int16),
            pltpu.VMEM((4, BACK_ROWS, keys), jnp.int16),
            pltpu.VMEM((high_rows * STRIP, low_lanes), f32),
            pltpu.VMEM((CHUNKS, CHUNK, CHUNK), bf16),
            pltpu.VMEM((away, CHUNK, CHUNK), bf16),
            pltpu.VMEM((CHUNKS, PARTS[0], CHUNK), bf16),
            pltpu.VMEM((away, PARTS[0], CHUNK), bf16),
            pltpu.VMEM((CHUNKS, PARTS[1], CHUNK), bf16),
            pltpu.VMEM((away, PARTS[1], CHUNK), bf16),
            pltpu.VMEM((away, PARTS[1], CHUNK), bf16),
            pltpu.VMEM((CHUNKS, PARTS[2], CHUNK), bf16),
            pltpu.VMEM((CHUNKS, PARTS[3], CHUNK), bf16),
            pltpu.VMEM((6, *small.shape), f32),
            pltpu.VMEM((5, *small.shape), f32),
            pltpu.VMEM((5, *table_shape), f32),
            pltpu.VMEM((4, *table_shape), f32),
            dma((9,)),
            dma((2, 2)),
            dma((4, 3)),
            dma((CHUNKS, 2)),
            dma((CHUNKS,)),
            dma((5,)),
            dma((CHUNKS, 11)),
            dma((CHUNKS, 11)),
            dma((3,)),
            dma((3,)),
            dma((5,)),
            dma((5,)),
            dma((4,)),
            dma((4,)),
        ],
        compiler_params=pltpu.CompilerParams(
            vmem_limit_bytes=FINISH_VMEM, collective_id=0, has_side_effects=True
        ),
        name="finish",
    )(
        exps,
        inverse,
        plane,
        down,
        context,
        query,
        tokens,
        grad,
        layer,
        value_turned,
        key_wide,
        project_weight,
        output_weight,
        *expand,
        *reduce,
        small,
    )
    return total, layer_full, input_full, table_sum, small_sum


UNPACK_ROWS = 96


def unpack_kernel(
    total_ref,
    layer_in_ref,
    input_in_ref,
    sum_ref,
    small_ref,
    layer_ref,
    input_ref,
    project_ref,
    output_ref,
    expand_ref,
    reduce_ref,
    line_ref,
    across_ref,
    down_ref,
    bias_ref,
    second_gain_ref,
    second_shift_ref,
    reduce_bias_ref,
    first_gain_ref,
    first_shift_ref,
    output_bias_ref,
    expand_bias_ref,
    *,
    high_counts,
):
    step = pl.program_id(0)
    layer_ref[...] = layer_in_ref[...]
    input_ref[...] = input_in_ref[...].reshape(input_ref.shape)
    values = total_ref[...].astype(f32)

    @pl.when(step < 3)
    def _():
        project_ref[0] = values.T

    @pl.when(step == 3)
    def _():
        output_ref[...] = values

    @pl.when((step >= 4) & (step < 8))
    def _():
        expand_ref[...] = values

    @pl.when(step >= 8)
    def _():
        reduce_ref[...] = values

    @pl.when(step == 0)
    def _():
        lanes = sum_ref.shape[1]
        row = lax.broadcasted_iota(jnp.int32, (lanes, LANES), 0) // STRIP
        same = row == lax.broadcasted_iota(jnp.int32, (lanes, LANES), 1)
        folded = jnp.dot(
            sum_ref[...],
            jnp.where(same, 1.0, 0.0),
            precision=lax.Precision.HIGHEST,
            preferred_element_type=f32,
        )
        heads = line_ref.shape[0]
        start = 0
        for ref, count in zip((line_ref, across_ref, down_ref), high_counts):
            parts = []
            for _ in range(count):
                parts.append(folded[start : start + heads, : lanes // STRIP])
                start += heads
            ref[...] = jnp.concatenate(parts, axis=1)
        half = bias_ref.shape[1] - lanes
        middle = sum_ref[start + 1 : start + 2, :]
        bias_ref[0:1, :] = jnp.concatenate([sum_ref[start : start + 1, :], middle[:, :half]], axis=1)
        bias_ref[1:2, :] = jnp.concatenate([middle[:, half:], sum_ref[start + 2 : start + 3, :]], axis=1)
        lead = lax.axis_index("mp") == 0
        for n, ref in enumerate(
            (
                second_gain_ref,
                second_shift_ref,
                reduce_bias_ref,
                first_gain_ref,
                first_shift_ref,
                output_bias_ref,
            )
        ):
            row = small_ref[n : n + 1, :]
            if ref.shape[0] < row.shape[1]:
                cut = ref.shape[0]
                row = jnp.where(lead, row[:, :cut], row[:, cut:])
            ref[...] = row.reshape(ref.shape)
        pieces = expand_bias_ref.shape[0] // small_ref.shape[1]
        width = small_ref.shape[1]
        for k in range(pieces):
            even = small_ref[8 + k : 9 + k, :]
            odd = small_ref[8 + pieces + k : 9 + pieces + k, :]
            expand_bias_ref[k * width : (k + 1) * width] = jnp.where(lead, even, odd).reshape(width)


def unpack(total, layer, inputs, sums, small, length, heads, counts):
    width = inputs.shape[1]
    depth = layer.shape[1]
    high_counts = (counts[0] // 16, counts[1] // 16, counts[1] // 16)
    half = CHUNK // 2
    steps = CHUNKS * 2

    def whole(shape):
        return pl.BlockSpec(shape, lambda i: (0,) * len(shape))

    def rows(columns):
        return pl.BlockSpec((UNPACK_ROWS, columns), lambda i: (i, 0))

    shapes = [
        ((length, depth), bf16),
        ((length, 1, width), f32),
        ((3, depth, width), f32),
        ((width, depth), f32),
        ((CHUNK, 2 * CHUNK), f32),
        ((2 * CHUNK, CHUNK), f32),
        ((heads, counts[0]), f32),
        ((heads, counts[1]), f32),
        ((heads, counts[1]), f32),
        ((2, width), f32),
        ((depth,), f32),
        ((depth,), f32),
        ((depth,), f32),
        ((width,), f32),
        ((width,), f32),
        ((depth,), f32),
        ((2 * CHUNK,), f32),
    ]
    return pl.pallas_call(
        partial(unpack_kernel, high_counts=high_counts),
        grid=(steps,),
        in_specs=[
            pl.BlockSpec((half, CHUNK), lambda i: (i, 0)),
            rows(depth),
            rows(width),
            whole(sums.shape),
            whole(small.shape),
        ],
        out_specs=[
            rows(depth),
            pl.BlockSpec((UNPACK_ROWS, 1, width), lambda i: (i, 0, 0)),
            pl.BlockSpec((1, depth, width), lambda i: (jnp.clip(i, 0, 2), 0, 0)),
            whole((width, depth)),
            pl.BlockSpec(
                (half, CHUNK),
                lambda i: (lax.rem(jnp.clip(i - 4, 0, 3), 2), jnp.clip(i - 4, 0, 3) // 2),
            ),
            pl.BlockSpec((half, CHUNK), lambda i: (jnp.clip(i - 8, 0, 3), 0)),
            *(whole(shape) for shape, _ in shapes[6:]),
        ],
        out_shape=[jax.ShapeDtypeStruct(shape, kind) for shape, kind in shapes],
        compiler_params=pltpu.CompilerParams(vmem_limit_bytes=vmem_limit),
        name="unpack",
    )(total, layer, inputs, sums, small)


def feed_kernel(
    context_ref,
    context_away_ref,
    token_ref,
    cotangent_ref,
    valid_ref,
    output_ref,
    output_away_ref,
    expand_ref,
    expand_away_ref,
    reduce_ref,
    reduce_away_ref,
    expand_bias_ref,
    expand_bias_away_ref,
    output_bias_ref,
    first_gain_ref,
    first_shift_ref,
    reduce_bias_ref,
    second_gain_ref,
    second_shift_ref,
    layer_ref,
    grad_ref,
    expand_grad_ref,
    expand_grad_away_ref,
    reduce_grad_ref,
    reduce_grad_away_ref,
    small_ref,
    input_buf,
    norm_buf,
    hat_buf,
    inverse_buf,
    total_buf,
    reduced_buf,
    active_buf,
    slope_buf,
    before_buf,
    vector_ref,
    bias_buf,
    *,
    pieces,
    tiles,
):
    rows, width = token_ref.shape
    step = pl.program_id(0)
    piece = step % (2 * pieces)
    strip_rows = FEED_STRIP
    strips = rows // strip_rows

    def vector(n):
        return vector_ref[n : n + 1, :]

    def for_strips(body, sums):
        def run(n, carry):
            at = pl.ds(pl.multiple_of(n * strip_rows, STRIP), strip_rows)
            return tuple(
                old + jnp.sum(new.reshape(strip_rows // 8, 8, width), axis=0)
                for old, new in zip(carry, body(at))
            )

        start = tuple(jnp.zeros((8, width), f32) for _ in range(sums))
        done = lax.fori_loop(0, strips, run, start)
        return [jnp.sum(part, axis=0, keepdims=True) for part in done]

    def mean(values):
        return jnp.sum(values, axis=-1, keepdims=True) * (1.0 / width)

    @pl.when(step == 0)
    def _():
        small_ref[...] = jnp.zeros_like(small_ref)
        for n, ref in enumerate(
            (
                output_bias_ref,
                first_gain_ref,
                first_shift_ref,
                reduce_bias_ref,
                second_gain_ref,
                second_shift_ref,
            )
        ):
            vector_ref[n : n + 1, :] = ref[...].astype(f32).reshape(1, width)
        bias = expand_bias_ref[...].astype(f32).reshape(1, -1)
        for k in range(pieces):
            cols = slice(k * expand_ref.shape[1], (k + 1) * expand_ref.shape[1])
            bias_buf[k : k + 1, :] = bias[:, cols]
            bias_buf[pieces + k : pieces + k + 1, :] = expand_bias_away_ref[0:1, cols]
        total_buf[...] = dot_f32(context_ref[...], output_ref[...]) + dot_f32(
            context_away_ref[...], output_away_ref[...]
        )

        def body(at):
            values = token_ref[at, :].astype(f32) + (total_buf[at, :] + vector(0))
            centered = values - mean(values)
            inverse = lax.rsqrt(mean(centered * centered) + norm_epsilon)
            hat = centered * inverse
            norm = hat * vector(1) + vector(2)
            hat_buf[at, :] = hat
            inverse_buf[at, :] = jnp.broadcast_to(inverse, (strip_rows, LANES))
            norm_buf[at, :] = norm
            input_buf[at, :] = norm.astype(bf16)
            total_buf[at, :] = norm + vector(3)
            return ()

        for_strips(body, 0)

    def forward(expand, reduce):
        for start, size in tiles:
            at = slice(start, start + size)
            before = dot_f32(input_buf[at, :], expand[...]) + bias_buf[pl.ds(piece, 1), :]
            phi = 0.5 * lax.erf(before * 0.7071067811865476) + 0.5
            slope_buf[piece, at, :] = phi + before * (
                0.3989422804014327 * jnp.exp(-0.5 * (before * before))
            )
            active = (before * phi).astype(bf16)
            active_buf[piece, at, :] = active
            total_buf[at, :] += dot_f32(active, reduce[...])

    pl.when(step < pieces)(lambda: forward(expand_ref, reduce_ref))
    pl.when((step >= pieces) & (step < 2 * pieces))(
        lambda: forward(expand_away_ref, reduce_away_ref)
    )

    @pl.when(step == 2 * pieces)
    def _():
        def body(at):
            values = total_buf[at, :]
            valid = valid_ref[at, 0:1]
            centered = values - mean(values)
            inverse = lax.rsqrt(mean(centered * centered) + norm_epsilon)
            hat = centered * inverse
            layer_ref[at, :] = (valid * (hat * vector(4) + vector(5))).astype(bf16)
            grad_out = jnp.where(valid > 0, cotangent_ref[at, :].astype(f32), 0.0)
            grad_hat = grad_out * vector(4)
            mixed = inverse * (grad_hat - mean(grad_hat) - hat * mean(grad_hat * hat))
            low = mixed.astype(bf16)
            reduced_buf[at, :] = low
            total_buf[at, :] = mixed
            return grad_out * hat, grad_out, low.astype(f32)

        for n, part in enumerate(for_strips(body, 3)):
            small_ref[n : n + 1, :] = part

    def backward(expand, reduce):
        sums = None
        for start, size in tiles:
            at = slice(start, start + size)
            grad_active = lax.dot_general(
                reduced_buf[at, :], reduce[...], (((1,), (1,)), ((), ())), preferred_element_type=f32
            )
            before = (grad_active * slope_buf[piece, at, :]).astype(bf16)
            before_buf[piece, at, :] = before
            part = jnp.sum(before.astype(f32), axis=0, keepdims=True)
            sums = part if sums is None else sums + part
            total_buf[at, :] += lax.dot_general(
                before, expand[...], (((1,), (1,)), ((), ())), preferred_element_type=f32
            )
        mp_index = lax.axis_index("mp")
        side = jnp.where(piece < pieces, mp_index, 1 - mp_index)
        small_ref[pl.ds(8 + side * pieces + lax.rem(piece, pieces), 1), :] = sums

    pl.when((step >= 2 * pieces) & (step < 3 * pieces))(lambda: backward(expand_ref, reduce_ref))
    pl.when((step >= 3 * pieces) & (step < 4 * pieces))(
        lambda: backward(expand_away_ref, reduce_away_ref)
    )

    @pl.when(step == 4 * pieces)
    def _():
        def body(at):
            grad_first = total_buf[at, :]
            hat = hat_buf[at, :]
            grad_hat = grad_first * vector(1)
            inverse = inverse_buf[at, 0:1]
            inner = inverse * (grad_hat - mean(grad_hat) - hat * mean(grad_hat * hat))
            low = inner.astype(bf16)
            grad_ref[at, :] = low
            return grad_first * hat, grad_first, low.astype(f32)

        for n, part in enumerate(for_strips(body, 3)):
            small_ref[n + 3 : n + 4, :] = part

    def weights(expand_grad, reduce_grad):
        reduce_grad[...] = lax.dot_general(
            active_buf[piece], reduced_buf[...], (((0,), (0,)), ((), ())), preferred_element_type=f32
        ).astype(bf16)
        expand_grad[...] = lax.dot_general(
            input_buf[...], before_buf[piece], (((0,), (0,)), ((), ())), preferred_element_type=f32
        ).astype(bf16)

    pl.when((step >= 4 * pieces) & (step < 5 * pieces))(
        lambda: weights(expand_grad_ref, reduce_grad_ref)
    )
    pl.when(step >= 5 * pieces)(lambda: weights(expand_grad_away_ref, reduce_grad_away_ref))


def feed(
    context,
    context_away,
    tokens,
    cotangent,
    valid,
    output,
    output_away,
    expand,
    expand_away,
    reduce,
    reduce_away,
    expand_bias,
    expand_bias_away,
    vectors,
):
    rows, width = context_away.shape[0], tokens.shape[1]
    hidden = expand.shape[1]
    size = FEED_PIECE
    pieces = hidden // size
    split = round_up(rows // 2, STRIP)
    tiles = ((0, split), (split, rows - split))

    def once(array):
        zeros = (0,) * array.ndim
        return pl.BlockSpec(array.shape, lambda i: zeros, pipeline_mode=pl.Buffered(1))

    def mine(array):
        return pl.BlockSpec(
            (rows, array.shape[1]),
            lambda i: (lax.axis_index("mp"), 0),
            pipeline_mode=pl.Buffered(1),
        )

    def place(first, i):
        at = lax.rem(i, 2 * pieces) - first
        at = jnp.clip(at, 0, pieces - 1)
        return jnp.where(i < 4 * pieces, at, pieces - 1)

    def grad_place(first, i):
        return jnp.clip(i - 4 * pieces - first, 0, pieces - 1)

    wide = lambda first: pl.BlockSpec((width, size), lambda i: (0, place(first, i)))
    tall = lambda first: pl.BlockSpec((size, width), lambda i: (place(first, i), 0))
    wide_grad = lambda first: pl.BlockSpec((width, size), lambda i: (0, grad_place(first, i)))
    tall_grad = lambda first: pl.BlockSpec((size, width), lambda i: (grad_place(first, i), 0))
    whole = lambda shape: pl.BlockSpec(
        shape, lambda i: (0,) * len(shape), pipeline_mode=pl.Buffered(1)
    )
    full = jax.ShapeDtypeStruct((rows, width), bf16)
    return pl.pallas_call(
        partial(feed_kernel, pieces=pieces, tiles=tiles),
        grid=(6 * pieces,),
        in_specs=[
            mine(context),
            once(context_away),
            mine(tokens),
            mine(cotangent),
            mine(valid),
            once(output),
            once(output_away),
            wide(0),
            wide(pieces),
            tall(0),
            tall(pieces),
            once(expand_bias),
            once(expand_bias_away),
            *(once(vector) for vector in vectors),
        ],
        out_specs=[
            whole((rows, width)),
            whole((rows, width)),
            wide_grad(0),
            wide_grad(pieces),
            tall_grad(0),
            tall_grad(pieces),
            whole((16, width)),
        ],
        out_shape=[
            full,
            full,
            jax.ShapeDtypeStruct((width, hidden), bf16),
            jax.ShapeDtypeStruct((width, hidden), bf16),
            jax.ShapeDtypeStruct((hidden, width), bf16),
            jax.ShapeDtypeStruct((hidden, width), bf16),
            jax.ShapeDtypeStruct((16, width), f32),
        ],
        scratch_shapes=[
            pltpu.VMEM((rows, width), bf16),
            pltpu.VMEM((rows, width), f32),
            pltpu.VMEM((rows, width), f32),
            pltpu.VMEM((rows, LANES), f32),
            pltpu.VMEM((rows, width), f32),
            pltpu.VMEM((rows, width), bf16),
            pltpu.VMEM((2 * pieces, rows, size), bf16),
            pltpu.VMEM((2 * pieces, rows, size), f32),
            pltpu.VMEM((2 * pieces, rows, size), bf16),
            pltpu.VMEM((8, width), f32),
            pltpu.VMEM((2 * pieces, size), f32),
        ],
        compiler_params=pltpu.CompilerParams(vmem_limit_bytes=vmem_limit),
        name="feed",
    )(
        context,
        context_away,
        tokens,
        cotangent,
        valid,
        output,
        output_away,
        expand,
        expand_away,
        reduce,
        reduce_away,
        expand_bias,
        expand_bias_away,
        *vectors,
    )


def swap(array):
    return lax.ppermute(array, "mp", [(0, 1), (1, 0)])


def partner(array, count, bit):
    return lax.ppermute(array, "dp", [(i, i ^ bit) for i in range(count)])


def sum_rows_over_dp(array, count):
    place = lax.axis_index("dp")
    bits = []
    bit = 1
    while bit < count:
        mine = (place // bit) % 2
        halves = array.reshape((2, array.shape[0] // 2) + array.shape[1:])
        sent = lax.dynamic_index_in_dim(halves, 1 - mine, 0, keepdims=False)
        kept = lax.dynamic_index_in_dim(halves, mine, 0, keepdims=False)
        array = kept + partner(sent, count, bit)
        bits.append(bit)
        bit *= 2
    for bit in reversed(bits):
        lead = (place // bit) % 2 == 0
        other = partner(array, count, bit)
        array = jnp.concatenate(
            [jnp.where(lead, array, other), jnp.where(lead, other, array)], axis=0
        )
    return array


def sum_small(arrays, count, over_mp):
    sizes = [a.size for a in arrays]
    total = sum(sizes)
    flat = jnp.concatenate([a.reshape(-1) for a in arrays])
    flat = jnp.pad(flat, (0, round_up(total, 1024) - total)).reshape(-1, LANES)
    if over_mp:
        flat = flat + swap(flat)
    bit = 1
    while bit < count:
        flat = flat + partner(flat, count, bit)
        bit *= 2
    flat = flat.reshape(-1)
    outs = []
    start = 0
    for array, size in zip(arrays, sizes):
        outs.append(flat[start : start + size].reshape(array.shape))
        start += size
    return outs


def per_device(
    dp_count,
    tokens,
    cotangent,
    long_flag,
    token_mask,
    bucket_line,
    bucket_across,
    bucket_down,
    project_weight,
    project_bias,
    table_line,
    table_across,
    table_down,
    output_weight,
    output_bias,
    first_gain,
    first_shift,
    expand_weight,
    expand_bias,
    reduce_weight,
    reduce_bias,
    second_gain,
    second_shift,
):
    length = tokens.shape[1]
    width = project_weight.shape[2]
    heads = table_line.shape[1]
    counts = (table_line.shape[0], table_across.shape[0])
    rows = round_up(length, BLOCK_ROWS)
    half_rows = rows // 2
    keys = round_up(length, 3 * LANES)
    mp_index = lax.axis_index("mp")
    lead = mp_index == 0

    def own_rows(array):
        return lax.dynamic_slice_in_dim(array, mp_index * half_rows, half_rows, 0)

    def in_order(mine, other):
        return jnp.where(lead, mine, other), jnp.where(lead, other, mine)


    (
        query,
        key_wide,
        key_turned,
        value_ones,
        value_turned,
        padded,
        plane,
        down,
        valid_rows,
        expand_quarter,
    ) = prepare(
        tokens[0],
        project_weight,
        project_bias,
        (bucket_line, bucket_across, bucket_down),
        long_flag,
        token_mask,
        expand_weight,
        rows,
        keys,
        counts[0],
    )
    (
        exps,
        context,
        inverse,
        context_away,
        expand_away,
        output_away,
        reduce_away,
        expand_bias_away,
    ) = attend(
        query,
        key_turned,
        value_ones,
        plane,
        down,
        (table_line.T, table_across.T, table_down.T),
        expand_bias,
        expand_quarter,
        output_weight,
        reduce_weight,
    )

    (
        layer_mine,
        grad_mine,
        expand_own,
        expand_sent,
        reduce_own,
        reduce_sent,
        small,
    ) = feed(
        context,
        context_away,
        padded,
        cotangent[0],
        valid_rows,
        output_weight,
        output_away,
        expand_weight,
        expand_away,
        reduce_weight,
        reduce_away,
        expand_bias,
        expand_bias_away,
        (output_bias, first_gain, first_shift, reduce_bias, second_gain, second_shift),
    )
    if dp_count == 16 and expand_own.shape == (CHUNK, 2 * CHUNK):
        total, layer_full, input_full, sums, small = finish(
            exps,
            inverse,
            plane,
            down,
            context,
            query,
            padded,
            grad_mine,
            layer_mine,
            value_turned,
            key_wide,
            project_weight,
            output_weight,
            (expand_own, expand_sent),
            (reduce_own, reduce_sent),
            small,
            counts,
        )
        (
            layer_out,
            input_grad,
            project_weight_grad,
            output_weight_grad,
            expand_weight_grad,
            reduce_weight_grad,
            line_grad,
            across_grad,
            down_grad,
            project_bias_grad,
            second_gain_grad,
            second_shift_grad,
            reduce_bias_grad,
            first_gain_grad,
            first_shift_grad,
            output_bias_grad,
            expand_bias_grad,
        ) = unpack(total, layer_full, input_full, sums, small, length, heads, counts)
        layer_out = layer_out[None]
        input_grad = input_grad.reshape(1, length, width)
        table_grads = (line_grad.T, across_grad.T, down_grad.T)
    else:
        layer_out = jnp.concatenate(in_order(layer_mine, swap(layer_mine)))[None, :length]
        grad_attended = jnp.concatenate(in_order(grad_mine, swap(grad_mine)))
        output_weight_grad = jnp.einsum(
            "le,lf->ef", context, grad_attended, preferred_element_type=f32
        ).astype(bf16)
        grad_context = jnp.einsum(
            "lf,ef->le", grad_attended, output_weight, preferred_element_type=f32
        )
        grad_scaled = (grad_context * inverse).astype(bf16)
        grad_scores, grad_query, grad_key, grad_value = attend_back(
            exps, grad_scaled, context, query, value_turned, key_wide
        )
        grad_key = grad_key.reshape(width, keys)[:, :rows].T.astype(bf16)
        grad_value = grad_value.reshape(width, keys)[:, :rows].T.astype(bf16)
        triple = jnp.stack([grad_query, grad_key, grad_value])
        project_weight_grad = jnp.einsum(
            "ld,kle->kde", padded[:rows], triple, preferred_element_type=f32
        ).astype(bf16)
        project_bias_grad = jnp.stack(
            [jnp.sum(grad_query, axis=0, dtype=f32), jnp.sum(grad_value, axis=0, dtype=f32)]
        )
        input_part = jnp.einsum("kle,kde->ld", triple, project_weight, preferred_element_type=f32)
        input_part = lax.dynamic_update_slice_in_dim(
            input_part,
            own_rows(input_part) + grad_mine.astype(f32),
            mp_index * half_rows,
            0,
        )
        sent = jnp.where(lead, input_part[:, width:], input_part[:, :width]).astype(bf16)
        own = jnp.where(lead, input_part[:, :width], input_part[:, width:])
        input_grad = (own + swap(sent).astype(f32))[None, :length]
        table_grads = table_sums(grad_scores, plane, down, counts)
        reduce_weight_grad = sum_rows_over_dp(reduce_own + swap(reduce_sent), dp_count)
        expand_weight_grad = sum_rows_over_dp(expand_own + swap(expand_sent), dp_count)
        output_weight_grad = sum_rows_over_dp(output_weight_grad, dp_count)
        project_weight_grad = sum_rows_over_dp(
            project_weight_grad.reshape(-1, width), dp_count
        ).reshape(project_weight.shape)
        (small,) = sum_small([small], dp_count, True)
        bias_rows = expand_bias.size // small.shape[1]
        bias_rows = lax.dynamic_slice_in_dim(small, 8 + mp_index * bias_rows, bias_rows, 0)
        expand_bias_grad = bias_rows.reshape(-1)
        (
            second_gain_grad,
            second_shift_grad,
            reduce_bias_grad,
            first_gain_grad,
            first_shift_grad,
            output_bias_grad,
        ) = (small[n] for n in range(6))
        first_gain_grad = lax.dynamic_slice_in_dim(first_gain_grad, mp_index * width, width, 0)
        first_shift_grad = lax.dynamic_slice_in_dim(first_shift_grad, mp_index * width, width, 0)
        table_grads, project_bias_grad = sum_small(
            [table_grads, project_bias_grad], dp_count, False
        )
        cuts = (counts[0], counts[0] + counts[1])
        table_grads = (
            table_grads[: cuts[0]],
            table_grads[cuts[0] : cuts[1]],
            table_grads[cuts[1] :],
        )
    return (
        layer_out,
        input_grad,
        project_weight_grad.astype(f32),
        project_bias_grad,
        *table_grads,
        output_weight_grad.astype(f32),
        output_bias_grad,
        first_gain_grad,
        first_shift_grad,
        expand_weight_grad.astype(f32),
        expand_bias_grad,
        reduce_weight_grad.astype(f32),
        reduce_bias_grad,
        second_gain_grad,
        second_shift_grad,
    )


def solution(mesh):
    placed = (
        P("dp", None, None),
        P("dp", None, None),
        P("dp"),
        P("dp", None),
        P("dp", None, None),
        P("dp", None, None),
        P("dp", None, None),
        P(None, None, "mp"),
        P(None, "mp"),
        P(None, "mp"),
        P(None, "mp"),
        P(None, "mp"),
        P("mp", None),
        P(),
        P(),
        P(),
        P(None, "mp"),
        P("mp"),
        P("mp", None),
        P(),
        P(),
        P(),
    )
    return jax.shard_map(
        partial(per_device, mesh.shape["dp"]),
        mesh=mesh,
        in_specs=placed,
        out_specs=(
            P("dp", None, None),
            P("dp", None, "mp"),
            P(None, None, "mp"),
            P(None, "mp"),
            P(None, "mp"),
            P(None, "mp"),
            P(None, "mp"),
            P("mp", None),
            P(),
            P("mp"),
            P("mp"),
            P(None, "mp"),
            P("mp"),
            P("mp", None),
            P(),
            P(),
            P(),
        ),
        check_vma=False,
    )
```

```python
from functools import partial

import jax
import jax.numpy as jnp
from jax import lax
from jax.experimental import pallas as pl
from jax.experimental.pallas import tpu as pltpu
from jax.sharding import PartitionSpec as P

LONG = 1089
SHORT = 709
HEAD = 64
LANES = 128
STRIP = 16
BLOCK_ROWS = 224
FEED_PIECE = 768
FEED_STRIP = 112
TABLE_STRIPS = 2
ATTEND_STRIPS = 7

large_negative = -1000000000.0
norm_epsilon = 1e-05
vmem_limit = 56 * 2**20
FINISH_VMEM = 62 * 2**20
bf16 = jnp.bfloat16
f32 = jnp.float32


def round_up(value, step):
    return (value + step - 1) // step * step


def whole_spec(array):
    zeros = (0,) * array.ndim
    return pl.BlockSpec(array.shape, lambda i: zeros)


def dot_f32(left, right):
    return jnp.dot(left, right, preferred_element_type=f32)


def gather_lanes(values, index):
    dims = lax.GatherDimensionNumbers(
        offset_dims=(),
        collapsed_slice_dims=(1,),
        start_index_map=(1,),
        operand_batching_dims=(0,),
        start_indices_batching_dims=(0,),
    )
    return lax.gather(
        values,
        index[..., None],
        dims,
        slice_sizes=(1, 1),
        mode=lax.GatherScatterMode.PROMISE_IN_BOUNDS,
    )


def quarter_rows(ref, quarter):
    count = ref.shape[0] // 4
    return pl.ds(pl.multiple_of(quarter * count, STRIP), count)


def prepare_kernel(
    token_ref,
    weight_ref,
    bias_ref,
    line_ref,
    across_ref,
    down_ref,
    flag_ref,
    mask_ref,
    expand_ref,
    query_ref,
    key_ref,
    key_turned_ref,
    value_ref,
    value_turned_ref,
    token_out_ref,
    plane_ref,
    down_out_ref,
    valid_ref,
    quarter_ref,
    row_ref,
    send_sem,
    recv_sem,
    *,
    length,
    line_count,
):
    step = pl.program_id(0)
    across_mp = {"mp": 1 - lax.axis_index("mp")}
    fetch = pltpu.make_async_remote_copy(
        src_ref=expand_ref.at[quarter_rows(expand_ref, lax.axis_index("dp") % 4), :],
        dst_ref=quarter_ref,
        send_sem=send_sem,
        recv_sem=recv_sem,
        device_id=across_mp,
        device_id_type=pl.DeviceIdType.MESH,
    )

    @pl.when(step == 0)
    def _():
        barrier = pltpu.get_barrier_semaphore()
        pl.semaphore_signal(
            barrier, inc=1, device_id=across_mp, device_id_type=pl.DeviceIdType.MESH
        )
        pl.semaphore_wait(barrier, 1)
        fetch.start()
        limit = jnp.where(flag_ref[0] > 0, LONG, SHORT)
        position = lax.broadcasted_iota(jnp.int32, (1, length), 1)
        row_ref[...] = jnp.zeros_like(row_ref)
        row_ref[0:1, :length] = jnp.where((mask_ref[...] > 0) & (position < limit), 1.0, 0.0)

    rows = token_ref.shape[0]
    keys = plane_ref.shape[1]
    place = pl.program_id(0) * rows + lax.broadcasted_iota(jnp.int32, token_ref.shape, 0)
    token = jnp.where(place < length, token_ref[...].astype(f32), 0.0).astype(bf16)
    token_out_ref[...] = token
    bias = bias_ref[...].astype(f32)
    query = (dot_f32(token, weight_ref[0]) + bias[0:1, :]).astype(bf16)
    query_ref[...] = (query.astype(f32) * 0.125).astype(bf16)
    key = dot_f32(token, weight_ref[1])
    value = dot_f32(token, weight_ref[2]) + bias[1:2, :]
    away = jnp.where(row_ref[0:1, :] > 0, 0, line_count)
    inside = pl.program_id(0) * rows + lax.broadcasted_iota(jnp.int32, (rows, length), 0) < length
    line = line_ref[...].reshape(rows, length)
    across = across_ref[...].reshape(rows, length)
    down = down_ref[...].reshape(rows, length)
    plane = jnp.where(inside, line | (across << 8), 0) | away[:, :length]
    plane_ref[:, :length] = plane.astype(jnp.int16)
    plane_ref[:, length:] = jnp.full((rows, keys - length), line_count, jnp.int16)
    here = pl.ds(pl.multiple_of(step * rows, LANES), rows)
    valid_ref[...] = jnp.broadcast_to(row_ref[0:1, here], (LANES, rows)).T
    down_out_ref[:, :length] = jnp.where(inside, down, 0).astype(jnp.int16)
    down_out_ref[:, length:] = jnp.zeros((rows, keys - length), jnp.int16)
    lane_first = lax.broadcasted_iota(jnp.int32, (rows, LANES), 1) < HEAD
    row_first = lax.broadcasted_iota(jnp.int32, (LANES, rows), 0) < HEAD
    for p in range(key.shape[1] // LANES):
        cols = slice(p * LANES, (p + 1) * LANES)
        key_pair, value_pair = key[:, cols], value[:, cols]
        key_turned, value_turned = key_pair.T, value_pair.T
        for u in range(2):
            h = 2 * p + u
            lane_own = lane_first if u == 0 else ~lane_first
            row_own = row_first if u == 0 else ~row_first
            key_ref[h] = jnp.where(lane_own, key_pair, 0.0).astype(bf16)
            value_ref[h] = jnp.where(lane_own, value_pair, 1.0).astype(bf16)
            key_turned_ref[h] = jnp.where(row_own, key_turned, 0.0).astype(bf16)
            value_turned_ref[h] = jnp.where(row_own, value_turned, 0.0).astype(bf16)
    pl.when(step == pl.num_programs(0) - 1)(fetch.wait)


def prepare(tokens, weight, bias, buckets, flag, token_mask, expand, row_count, keys, line_count):
    length, depth = tokens.shape
    width = weight.shape[2]
    heads = width // HEAD
    block = 3 * LANES
    row = pl.BlockSpec((block, width), lambda i: (i, 0))
    deep_row = pl.BlockSpec((block, depth), lambda i: (i, 0))
    wide = pl.BlockSpec((heads, block, LANES), lambda i: (0, i, 0))
    turned = pl.BlockSpec((heads, LANES, block), lambda i: (0, 0, i))
    bucket = pl.BlockSpec((block, 1, length), lambda i: (i, 0, 0))
    packed = pl.BlockSpec((block, keys), lambda i: (i, 0))
    wide_shape = jax.ShapeDtypeStruct((heads, keys, LANES), bf16)
    turned_shape = jax.ShapeDtypeStruct((heads, LANES, keys), bf16)
    packed_shape = jax.ShapeDtypeStruct((row_count, keys), jnp.int16)
    return pl.pallas_call(
        partial(prepare_kernel, length=length, line_count=line_count),
        grid=(keys // block,),
        in_specs=[
            deep_row,
            whole_spec(weight),
            whole_spec(bias),
            bucket,
            bucket,
            bucket,
            pl.BlockSpec(memory_space=pltpu.SMEM),
            whole_spec(token_mask),
            pl.BlockSpec(memory_space=pl.ANY),
        ],
        out_specs=[
            row,
            wide,
            turned,
            wide,
            turned,
            deep_row,
            packed,
            packed,
            pl.BlockSpec((block, LANES), lambda i: (i, 0)),
            pl.BlockSpec(memory_space=pl.ANY),
        ],
        out_shape=[
            jax.ShapeDtypeStruct((keys, width), bf16),
            wide_shape,
            turned_shape,
            wide_shape,
            turned_shape,
            jax.ShapeDtypeStruct((keys, depth), bf16),
            packed_shape,
            packed_shape,
            jax.ShapeDtypeStruct((keys, LANES), f32),
            jax.ShapeDtypeStruct((expand.shape[0] // 4, expand.shape[1]), bf16),
        ],
        scratch_shapes=[
            pltpu.VMEM((8, keys), f32),
            pltpu.SemaphoreType.DMA,
            pltpu.SemaphoreType.DMA,
        ],
        compiler_params=pltpu.CompilerParams(
            vmem_limit_bytes=vmem_limit, collective_id=2, has_side_effects=True
        ),
        name="prepare",
    )(
        tokens,
        weight,
        bias,
        *(index.reshape(length, 1, length) for index in buckets),
        flag,
        token_mask,
        expand,
    )


def attend_kernel(
    query_ref,
    key_ref,
    value_ref,
    plane_ref,
    down_ref,
    line_table_ref,
    across_table_ref,
    down_table_ref,
    expand_bias_ref,
    expand_quarter_ref,
    output_ref,
    reduce_ref,
    exp_out_ref,
    context_ref,
    inverse_ref,
    context_away_ref,
    expand_away_ref,
    output_away_ref,
    reduce_away_ref,
    bias_away_ref,
    score_ref,
    exp_ref,
    send_ref,
    table_ref,
    bias_ref,
    exp_sem,
    local_sem,
    send_sem,
    recv_sem,
):
    _, heads, rows, keys = exp_ref.shape
    step = pl.program_id(0)
    turn_rows = ATTEND_STRIPS * STRIP
    turns = rows // turn_rows
    place = lax.axis_index("dp")
    across_mp = {"mp": 1 - lax.axis_index("mp")}
    across = {bit: {"dp": place + bit * (1 - 2 * ((place // bit) % 2))} for bit in (1, 2)}

    def remote(src, dst, n, device):
        return pltpu.make_async_remote_copy(
            src_ref=src,
            dst_ref=dst,
            send_sem=send_sem.at[n],
            recv_sem=recv_sem.at[n],
            device_id=device,
            device_id_type=pl.DeviceIdType.MESH,
        )

    arrays = (
        (expand_quarter_ref, expand_away_ref),
        (output_ref, output_away_ref),
        (reduce_ref, reduce_away_ref),
    )
    quarter = place % 4
    other_chip = (place + 2) % 4
    other_core = quarter + 1 - 2 * (quarter % 2)
    third = (other_core + 2) % 4

    def rows_of(n, which):
        away = arrays[n][1]
        return away.at[quarter_rows(away, which), :]

    def fetch(n):
        ref = arrays[n][0]
        return remote(ref.at[quarter_rows(ref, quarter), :], rows_of(n, quarter), n, across_mp)

    def pass_on(n, stage):
        source = expand_quarter_ref if n == 0 and stage < 2 else rows_of(n, quarter)
        if stage == 0:
            return remote(source, rows_of(n, quarter), 3 + n, across[2])
        if stage == 1:
            return remote(source, rows_of(n, quarter), 6 + n, across[1])
        return remote(rows_of(n, other_chip), rows_of(n, other_chip), 9 + n, across[1])

    def arrival(n, stage):
        region = rows_of(n, (other_chip, other_core, third)[stage])
        return remote(region, region, 3 + 3 * stage + n, across_mp)

    def exp_copy(which, turn):
        half = lax.rem(which + 1 - lax.axis_index("mp"), 2)
        here = pl.ds(pl.multiple_of(turn * turn_rows, STRIP), turn_rows)
        there = pl.ds(pl.multiple_of(half * rows + turn * turn_rows, STRIP), turn_rows)
        return pltpu.make_async_copy(
            exp_ref.at[which, :, here, :], exp_out_ref.at[:, there, :], exp_sem.at[which, turn]
        )

    keep = pltpu.make_async_copy(expand_quarter_ref, rows_of(0, quarter), local_sem)
    context_swap = remote(send_ref, context_away_ref, 12, across_mp)
    bias_swap = remote(bias_ref, bias_away_ref, 13, across_mp)

    def event(n, stage):
        if stage == "fetched":
            fetch(n).wait_recv()
            pass_on(n, 0).start()
            pass_on(n, 1).start()
        else:
            arrival(n, 0).wait_recv()
            pass_on(n, 2).start()

    events = {
        (0, 2): ((1, "fetched"),),
        (1, 0): ((0, "passed"), (2, "fetched")),
        (1, 1): ((1, "passed"),),
    }

    @pl.when(step == 0)
    def _():
        barrier = pltpu.get_barrier_semaphore()
        for device in (across_mp, across[1], across[2]):
            pl.semaphore_signal(
                barrier, inc=1, device_id=device, device_id_type=pl.DeviceIdType.MESH
            )
        pl.semaphore_wait(barrier, 3)
        bias_ref[...] = jnp.broadcast_to(
            expand_bias_ref[...].astype(f32).reshape(1, -1), bias_ref.shape
        )
        bias_swap.start()
        for t, ref in enumerate((line_table_ref, across_table_ref, down_table_ref)):
            count = ref.shape[1]
            lanes = jnp.concatenate(
                [ref[...].astype(f32), jnp.full((heads, LANES - count), large_negative, f32)], axis=1
            )
            for h in range(heads):
                table_ref[t * heads + h] = jnp.broadcast_to(lanes[h : h + 1], (STRIP, LANES)).astype(
                    bf16
                )
        fetch(1).start()
        fetch(2).start()
        pass_on(0, 0).start()
        pass_on(0, 1).start()
        keep.start()

    for h in range(heads):
        pair = slice(h // 2 * LANES, (h // 2 + 1) * LANES)
        score_ref[h] = dot_f32(query_ref[:, pair], key_ref[h])

    lanes = [slice(c * LANES, (c + 1) * LANES) for c in range(keys // LANES)]

    def scores_of(at):
        scores = [[] for _ in range(heads)]
        for cols in lanes:
            packed = plane_ref[at, cols]
            bias = [None] * heads
            for t, index in enumerate(
                (packed & jnp.int16(255), packed >> jnp.int16(8), down_ref[at, cols])
            ):
                for h in range(heads):
                    found = gather_lanes(table_ref[t * heads + h], index).astype(f32)
                    bias[h] = found if t == 0 else bias[h] + found
            for h in range(heads):
                scores[h].append(score_ref[h, at, cols] + bias[h])
        return scores

    def exps_of(scores):
        exps = []
        for parts in scores:
            top = parts[0]
            for part in parts[1:]:
                top = jnp.maximum(top, part)
            top = jnp.max(top, axis=1, keepdims=True)
            exps.append([jnp.exp(part - top).astype(bf16) for part in parts])
        return exps

    def strips(n, carry):
        for (at_step, at_turn), pieces in events.items():

            @pl.when((step == at_step) & (n == at_turn))
            def _():
                for piece in pieces:
                    event(*piece)

        start = pl.multiple_of(n * turn_rows, STRIP)
        places = [pl.ds(start + k * STRIP, STRIP) for k in range(ATTEND_STRIPS)]
        scores = [scores_of(at) for at in places]
        exps = [exps_of(part) for part in scores]
        for at, part in zip(places, exps):
            for h in range(heads):
                for c, cols in enumerate(lanes):
                    exp_ref[step, h, at, cols] = part[h][c]
        exp_copy(step, n).start()
        return carry

    lax.fori_loop(0, turns, strips, 0)
    first = lax.broadcasted_iota(jnp.int32, (rows, LANES), 1) < HEAD
    for p in range(heads // 2):
        cols = slice(p * LANES, (p + 1) * LANES)
        even = dot_f32(exp_ref[step, 2 * p], value_ref[2 * p])
        odd = dot_f32(exp_ref[step, 2 * p + 1], value_ref[2 * p + 1])
        sums = jnp.where(first, pltpu.roll(even, HEAD, 1), pltpu.roll(odd, HEAD, 1))
        inverse = 1.0 / sums
        inverse_ref[:, cols] = inverse
        context = (jnp.where(first, even, odd) * inverse).astype(bf16)
        context_ref[:, cols] = context

        @pl.when(step == 0)
        def _():
            send_ref[:, cols] = context

    pl.when(step == 0)(context_swap.start)

    @pl.when(step == 1)
    def _():
        event(2, "passed")
        for which in range(2):
            for n in range(turns):
                exp_copy(which, n).wait()
        keep.wait()
        context_swap.wait()
        bias_swap.wait()
        for n in range(3):
            arrival(n, 1).wait_recv()
            arrival(n, 2).wait_recv()
            for stage in range(3):
                pass_on(n, stage).wait_send()
        fetch(1).wait_send()
        fetch(2).wait_send()


def attend(
    query,
    key_turned,
    value_ones,
    plane,
    down,
    tables,
    expand_bias,
    expand_quarter,
    output,
    reduce,
):
    heads, _, keys = key_turned.shape
    row_count = plane.shape[0]
    width = heads * HEAD
    half_rows = row_count // 2

    def half(i):
        return lax.rem(i + 1 - lax.axis_index("mp"), 2)

    anywhere = pl.BlockSpec(memory_space=pl.ANY)
    index_spec = pl.BlockSpec((half_rows, keys), lambda i: (half(i), 0))
    row_spec = pl.BlockSpec((half_rows, width), lambda i: (half(i), 0))
    return pl.pallas_call(
        attend_kernel,
        grid=(2,),
        in_specs=[
            row_spec,
            whole_spec(key_turned),
            whole_spec(value_ones),
            index_spec,
            index_spec,
            *(whole_spec(table) for table in tables),
            whole_spec(expand_bias),
            anywhere,
            anywhere,
            anywhere,
        ],
        out_specs=[
            anywhere,
            row_spec,
            row_spec,
            anywhere,
            anywhere,
            anywhere,
            anywhere,
            anywhere,
        ],
        out_shape=[
            jax.ShapeDtypeStruct((heads, row_count, keys), bf16),
            jax.ShapeDtypeStruct((row_count, width), bf16),
            jax.ShapeDtypeStruct((row_count, width), f32),
            jax.ShapeDtypeStruct((half_rows, width), bf16),
            jax.ShapeDtypeStruct((4 * expand_quarter.shape[0], expand_quarter.shape[1]), bf16),
            jax.ShapeDtypeStruct(output.shape, bf16),
            jax.ShapeDtypeStruct(reduce.shape, bf16),
            jax.ShapeDtypeStruct((8, expand_bias.size), f32),
        ],
        scratch_shapes=[
            pltpu.VMEM((heads, half_rows, keys), f32),
            pltpu.VMEM((2, heads, half_rows, keys), bf16),
            pltpu.VMEM((half_rows, width), bf16),
            pltpu.VMEM((3 * heads, STRIP, LANES), bf16),
            pltpu.VMEM((8, expand_bias.size), f32),
            pltpu.SemaphoreType.DMA((2, half_rows // (ATTEND_STRIPS * STRIP))),
            pltpu.SemaphoreType.DMA,
            pltpu.SemaphoreType.DMA((14,)),
            pltpu.SemaphoreType.DMA((14,)),
        ],
        compiler_params=pltpu.CompilerParams(
            vmem_limit_bytes=vmem_limit, collective_id=1, has_side_effects=True
        ),
        name="attend",
    )(
        query,
        key_turned,
        value_ones,
        plane,
        down,
        *tables,
        expand_bias,
        expand_quarter,
        output,
        reduce,
    )


def attend_back_kernel(
    exp_ref,
    grad_ref,
    context_ref,
    query_ref,
    value_ref,
    key_ref,
    grad_score_ref,
    grad_query_ref,
    grad_key_ref,
    grad_value_ref,
):
    heads, rows, _ = exp_ref.shape

    @pl.when(pl.program_id(0) == 0)
    def _():
        grad_key_ref[...] = jnp.zeros_like(grad_key_ref)
        grad_value_ref[...] = jnp.zeros_like(grad_value_ref)

    first = lax.broadcasted_iota(jnp.int32, (rows, LANES), 1) < HEAD
    for p in range(heads // 2):
        cols = slice(p * LANES, (p + 1) * LANES)
        grad = grad_ref[:, cols]
        product = grad.astype(f32) * context_ref[:, cols].astype(f32)
        query_turned = query_ref[:, cols].T
        grad_turned = grad.T
        grad_query = None
        for u in range(2):
            h = 2 * p + u
            half = slice(u * HEAD, (u + 1) * HEAD)
            own = first if u == 0 else ~first
            total = jnp.sum(jnp.where(own, product, 0.0), axis=1, keepdims=True)
            grad_exp = dot_f32(grad, value_ref[h])
            grad_score = (exp_ref[h].astype(f32) * (grad_exp - total)).astype(bf16)
            grad_score_ref[h] = grad_score
            part = dot_f32(grad_score, key_ref[h])
            grad_query = part if u == 0 else grad_query + part
            grad_key_ref[h] += dot_f32(query_turned[half], grad_score)
            grad_value_ref[h] += dot_f32(grad_turned[half], exp_ref[h])
        grad_query_ref[:, cols] = (grad_query * 0.125).astype(bf16)


def attend_back(exps, grad, context, query, value_turned, key_wide):
    heads, row_count, keys = exps.shape
    width = heads * HEAD
    row_spec = pl.BlockSpec((BLOCK_ROWS, width), lambda i: (i, 0))
    exp_spec = pl.BlockSpec((heads, BLOCK_ROWS, keys), lambda i: (0, i, 0))
    sum_spec = pl.BlockSpec((heads, HEAD, keys), lambda i: (0, 0, 0))
    return pl.pallas_call(
        attend_back_kernel,
        grid=(row_count // BLOCK_ROWS,),
        in_specs=[
            exp_spec,
            row_spec,
            row_spec,
            row_spec,
            whole_spec(value_turned),
            whole_spec(key_wide),
        ],
        out_specs=[exp_spec, row_spec, sum_spec, sum_spec],
        out_shape=[
            jax.ShapeDtypeStruct((heads, row_count, keys), bf16),
            jax.ShapeDtypeStruct((row_count, width), bf16),
            jax.ShapeDtypeStruct((heads, HEAD, keys), f32),
            jax.ShapeDtypeStruct((heads, HEAD, keys), f32),
        ],
        compiler_params=pltpu.CompilerParams(vmem_limit_bytes=vmem_limit),
        name="attend_back",
    )(exps, grad, context, query, value_turned, key_wide)


def table_strips(strips, sum_ref, heads, keys, high_counts):
    base = 0
    for t in range(3):
        shift = 8 if t == 1 else 0
        highs, lows = [], []
        for grad_of, plane_of, down_of in strips:
            for c in range(keys // LANES):
                cols = slice(c * LANES, (c + 1) * LANES)
                index = down_of(cols) if t == 2 else plane_of(cols)
                low = index & jnp.int16(15 << shift)
                high = index & jnp.int16(48 << shift)
                lows.append(
                    jnp.concatenate(
                        [
                            jnp.where(low == jnp.int16(x << shift), bf16(1), bf16(0))
                            for x in range(16)
                        ]
                    )
                )
                parts = []
                for x in range(high_counts[t]):
                    mask = high == jnp.int16(x << (4 + shift))
                    parts += [jnp.where(mask, grad_of(h, cols), bf16(0)) for h in range(heads)]
                highs.append(jnp.concatenate(parts))
        span = slice(base, base + high_counts[t] * heads * STRIP)
        sum_ref[span, :] += lax.dot_general(
            jnp.concatenate(highs, axis=1),
            jnp.concatenate(lows, axis=1),
            (((1,), (1,)), ((), ())),
            preferred_element_type=f32,
        )
        base = span.stop


def table_finish(sum_ref, out_ref, count):
    row_of_lane = lax.broadcasted_iota(jnp.int32, (STRIP, 16 * STRIP), 1) % STRIP
    same = row_of_lane == lax.broadcasted_iota(jnp.int32, (STRIP, 16 * STRIP), 0)
    for o in range(count):
        block = sum_ref[o * STRIP : (o + 1) * STRIP, :]
        out_ref[o : o + 1, :] = jnp.sum(jnp.where(same, block, 0.0), axis=0, keepdims=True)


def table_result(out, high_counts, heads):
    summed = jnp.sum(out.reshape(sum(high_counts), heads, 16, STRIP), axis=-1)
    return summed.transpose(0, 2, 1).reshape(-1, heads)


def table_kernel(grad_score_ref, plane_ref, down_ref, out_ref, sum_ref, *, high_counts):
    heads, rows, keys = grad_score_ref.shape
    step = pl.program_id(0)

    @pl.when(step == 0)
    def _():
        sum_ref[...] = jnp.zeros_like(sum_ref)

    def refs_at(start):
        at = pl.ds(pl.multiple_of(start, STRIP), STRIP)
        return (
            lambda h, cols: grad_score_ref[h, at, cols],
            lambda cols: plane_ref[at, cols],
            lambda cols: down_ref[at, cols],
        )

    def strips(r, carry):
        start = r * (TABLE_STRIPS * STRIP)
        table_strips(
            [refs_at(start + k * STRIP) for k in range(TABLE_STRIPS)],
            sum_ref,
            heads,
            keys,
            high_counts,
        )
        return carry

    lax.fori_loop(0, rows // (TABLE_STRIPS * STRIP), strips, 0)

    @pl.when(step == pl.num_programs(0) - 1)
    def _():
        table_finish(sum_ref, out_ref, out_ref.shape[0])


def table_sums(grad_scores, plane, down, counts):
    heads, row_count, keys = grad_scores.shape
    high_counts = (counts[0] // 16, counts[1] // 16, counts[1] // 16)
    high_rows = sum(high_counts) * heads
    index_spec = pl.BlockSpec((BLOCK_ROWS, keys), lambda i: (i, 0))
    out = pl.pallas_call(
        partial(table_kernel, high_counts=high_counts),
        grid=(row_count // BLOCK_ROWS,),
        in_specs=[
            pl.BlockSpec((heads, BLOCK_ROWS, keys), lambda i: (0, i, 0)),
            index_spec,
            index_spec,
        ],
        out_specs=pl.BlockSpec((high_rows, 16 * STRIP), lambda i: (0, 0)),
        out_shape=jax.ShapeDtypeStruct((high_rows, 16 * STRIP), f32),
        scratch_shapes=[pltpu.VMEM((high_rows * STRIP, 16 * STRIP), f32)],
        compiler_params=pltpu.CompilerParams(vmem_limit_bytes=vmem_limit),
        name="table_sums",
    )(grad_scores, plane, down)
    return table_result(out, high_counts, heads)


CHUNK = 768
CHUNKS = 6
LOCAL_CHUNKS = 2
PARTS = (CHUNK // 2, CHUNK // 4, CHUNK // 8, CHUNK // 16)
BITS = ((1, 2, 4, 8), (1, 4, 2, 8), (1, 2, 4, 8), (1, 4, 2, 8), (1, 2, 4, 8), (1, 4, 2, 8))
BACK_ROWS = 112
EXCHANGE = (
    ("b", 0, 0, 2), ("b", 0, 0, 3), ("b", 0, 0, 4), ("b", 1, 0, 5), ("b", 4, 1, 2), ("b", 6, 1, 3),
    ("b", 8, 1, 4), ("b", 9, 1, 5), ("b", 20, 2, 2), ("b", 22, 2, 3), ("p", 0, 3, 2), ("p", 2, 2, 4),
    ("p", 3, 2, 5), ("p", 3, 3, 3), ("p", 3, 0, 0), ("p", 3, 0, 1), ("t", 0, 4, 2), ("t", 1, 1, 0),
    ("t", 1, 1, 1), ("t", 2, 4, 3), ("t", 2, "small", 0), ("t", 3, 3, 4), ("t", 4, 5, 2),
    ("t", 6, 3, 5), ("t", 6, 2, 0), ("t", 6, 2, 1), ("t", 6, "small", 1), ("t", 8, 5, 3),
    ("t", 9, 4, 4), ("t", 10, 4, 5), ("t", 11, 6, 2), ("t", 11, "send", 0), ("t", 11, "small", 2),
    ("t", 12, 3, 1), ("t", 12, 3, 0), ("t", 13, 6, 3), ("t", 15, 5, 4), ("t", 16, "small", 3),
    ("t", 17, 5, 5), ("t", 17, 7, 3), ("t", 18, 7, 2), ("t", 19, 4, 1), ("t", 20, "small", 4),
    ("t", 21, 4, 0), ("t", 23, 6, 4), ("t", 24, 8, 2), ("t", 24, "input", 0), ("t", 25, 6, 5),
    ("t", 25, 9, 2), ("t", 25, "small", 5), ("t", 26, 8, 3), ("t", 26, "layer", 0), ("t", 27, 5, 1),
    ("t", 28, 9, 3), ("t", 29, 5, 0), ("t", 29, 7, 5), ("t", 29, 7, 4), ("t", 31, 6, 1),
    ("t", 33, 6, 0), ("e", 0, 8, 4), ("e", 0, 9, 4), ("e", 0, 8, 5), ("e", 0, 9, 5), ("e", 0, 7, 0),
    ("e", 0, 8, 0), ("e", 0, 7, 1), ("e", 0, 8, 1),
)


def plan_slots(phase, count):
    slots = [[] for _ in range(count)]
    for name, at, event, which in EXCHANGE:
        if name == phase:
            slots[at].append((event, which))
    return slots


def finish_kernel(
    exp_ref,
    inverse_ref,
    plane_ref,
    down_ref,
    context_ref,
    query_ref,
    token_ref,
    grad_ref,
    layer_ref,
    value_ref,
    key_ref,
    project_ref,
    output_ref,
    expand_ref,
    expand_away_ref,
    reduce_ref,
    reduce_away_ref,
    small_ref,
    total_ref,
    layer_out_ref,
    input_ref,
    small_out_ref,
    table_ref,
    score_ref,
    output_buf,
    grad_buf,
    value_buf,
    key_buf,
    context_buf,
    query_buf,
    token_buf,
    project_buf,
    ring_buf,
    inverse_buf,
    grad_key_buf,
    grad_value_buf,
    triple_buf,
    input_send_buf,
    input_recv_buf,
    input_buf,
    plane_buf,
    down_buf,
    sum_ref,
    own_buf,
    away_buf,
    core_buf,
    core_away_buf,
    first_buf,
    first_away_buf,
    y_buf,
    second_buf,
    third_buf,
    small_buf,
    small_recv_buf,
    table_buf,
    table_recv_buf,
    resident_sem,
    block_sem,
    ring_sem,
    load_sem,
    local_sem,
    out_sem,
    send_sem,
    recv_sem,
    wide_send_sem,
    wide_recv_sem,
    small_send_sem,
    small_recv_sem,
    table_send_sem,
    table_recv_sem,
    *,
    high_counts,
):
    heads, row_count, keys = exp_ref.shape
    width = heads * HEAD
    half_rows = row_count // 2
    rows = BACK_ROWS
    blocks = row_count // rows
    block_strips = rows // STRIP
    turns = row_count // (TABLE_STRIPS * STRIP)
    place = lax.axis_index("dp")
    mp_index = lax.axis_index("mp")
    side_of = {bit: (place // bit) % 2 for bit in (1, 2, 4, 8)}
    partner_of = {bit: {"dp": place + bit * (1 - 2 * side_of[bit])} for bit in (1, 2, 4, 8)}
    across_mp = {"mp": 1 - mp_index}

    barrier = pltpu.get_barrier_semaphore()
    for device in (*partner_of.values(), across_mp):
        pl.semaphore_signal(barrier, inc=1, device_id=device, device_id_type=pl.DeviceIdType.MESH)
    pl.semaphore_wait(barrier, 5)

    def rows_at(start, size):
        return pl.ds(pl.multiple_of(start, STRIP), size)

    def remote(src, dst, send, recv, device):
        return pltpu.make_async_remote_copy(
            src_ref=src,
            dst_ref=dst,
            send_sem=send,
            recv_sem=recv,
            device_id=device,
            device_id_type=pl.DeviceIdType.MESH,
        )

    mine = rows_at(mp_index * half_rows, half_rows)
    others = rows_at((1 - mp_index) * half_rows, half_rows)
    grad_swap = remote(
        grad_ref, grad_buf.at[1], wide_send_sem.at[0], wide_recv_sem.at[0], across_mp
    )
    input_swap = remote(
        input_send_buf, input_recv_buf, wide_send_sem.at[1], wide_recv_sem.at[1], across_mp
    )
    layer_swap = remote(
        layer_ref, layer_out_ref.at[mine, :], wide_send_sem.at[2], wide_recv_sem.at[2], across_mp
    )
    layer_arrival = remote(
        layer_out_ref.at[others, :],
        layer_out_ref.at[others, :],
        wide_send_sem.at[2],
        wide_recv_sem.at[2],
        across_mp,
    )
    layer_keep = pltpu.make_async_copy(layer_ref, layer_out_ref.at[mine, :], out_sem.at[2])
    grad_swap.start()

    residents = [
        pltpu.make_async_copy(src, dst, resident_sem.at[n])
        for n, (src, dst) in enumerate(
            (
                (grad_ref, grad_buf.at[0]),
                (output_ref, output_buf),
                (context_ref, context_buf),
                (query_ref, query_buf),
                (value_ref, value_buf),
                (key_ref, key_buf),
                (small_ref, small_buf.at[0]),
                (token_ref, token_buf),
                (project_ref, project_buf),
            )
        )
    ]

    def block_rows(block):
        start = (mp_index * (blocks // 2) + block) % blocks
        return rows_at(start * rows, rows)

    def block_copies(block, slot):
        at = block_rows(block)
        return (
            pltpu.make_async_copy(exp_ref.at[:, at, :], ring_buf.at[slot], block_sem.at[slot, 0]),
            pltpu.make_async_copy(inverse_ref.at[at, :], inverse_buf.at[slot], block_sem.at[slot, 1]),
        )

    def score_copy(block, slot):
        return pltpu.make_async_copy(
            ring_buf.at[2 + slot], score_ref.at[:, block_rows(block), :], out_sem.at[slot]
        )

    def ring_copies(block):
        slot = block % 4
        at = rows_at(block * rows, rows)
        return (
            pltpu.make_async_copy(score_ref.at[:, at, :], ring_buf.at[slot], ring_sem.at[slot, 0]),
            pltpu.make_async_copy(plane_ref.at[at, :], plane_buf.at[slot], ring_sem.at[slot, 1]),
            pltpu.make_async_copy(down_ref.at[at, :], down_buf.at[slot], ring_sem.at[slot, 2]),
        )

    def is_away(chunk):
        return chunk >= LOCAL_CHUNKS

    loads = {}
    for ref, away_ref, wide in (
        (expand_ref, expand_away_ref, True),
        (reduce_ref, reduce_away_ref, False),
    ):
        for k in range(2):
            piece = slice(k * CHUNK, (k + 1) * CHUNK)
            index = (slice(None), piece) if wide else (piece, slice(None))
            chunk = LOCAL_CHUNKS + len(loads)
            loads[chunk] = (
                pltpu.make_async_copy(ref.at[index], own_buf.at[chunk], load_sem.at[chunk, 0]),
                pltpu.make_async_copy(
                    away_ref.at[index], away_buf.at[chunk - LOCAL_CHUNKS], load_sem.at[chunk, 1]
                ),
            )

    for copy in loads[LOCAL_CHUNKS]:
        copy.start()
    for copy in residents[:2]:
        copy.start()
    for copy in block_copies(0, 0):
        copy.start()
    for copy in residents[2:6]:
        copy.start()
    for chunk in range(LOCAL_CHUNKS + 1, CHUNKS):
        for copy in loads[chunk]:
            copy.start()
    residents[6].start()
    for copy in residents[7:]:
        copy.start()

    keeps, leaves = [], []
    for bits in BITS:
        kept, left, base = [], [], 0
        for size, bit in zip(PARTS, bits):
            kept.append(base + side_of[bit] * size)
            left.append(base + (1 - side_of[bit]) * size)
            base = base + side_of[bit] * size
        keeps.append(kept)
        leaves.append(left)
    arrivals = (core_buf, first_buf, second_buf, third_buf)
    away_arrivals = (core_away_buf, first_away_buf)

    def staged(src, dst, chunk, stage, device):
        return remote(src, dst, send_sem.at[chunk, stage], recv_sem.at[chunk, stage], device)

    def scatter(chunk, level):
        return staged(
            own_buf.at[chunk, rows_at(leaves[chunk][level], PARTS[level]), :],
            arrivals[level].at[chunk],
            chunk,
            level,
            partner_of[BITS[chunk][level]],
        )

    def scatter_away(chunk, level):
        return staged(
            away_buf.at[chunk - LOCAL_CHUNKS, rows_at(leaves[chunk][level], PARTS[level]), :],
            away_arrivals[level].at[chunk - LOCAL_CHUNKS],
            chunk,
            4 + level,
            partner_of[BITS[chunk][level]],
        )

    def hand_over(chunk):
        return staged(
            away_buf.at[chunk - LOCAL_CHUNKS, rows_at(keeps[chunk][1], PARTS[1]), :],
            y_buf.at[chunk - LOCAL_CHUNKS],
            chunk,
            6,
            across_mp,
        )

    def total_rows(chunk, start, size):
        return total_ref.at[rows_at(chunk * CHUNK + start, size), :]

    def gather(chunk, level):
        kept, size = keeps[chunk][level], PARTS[level]
        if level == 3:
            src = own_buf.at[chunk, rows_at(kept, size), :]
        else:
            src = total_rows(chunk, kept, size)
        return staged(
            src, total_rows(chunk, kept, size), chunk, 7 + level, partner_of[BITS[chunk][level]]
        )

    def gathered(chunk, level):
        region = total_rows(chunk, leaves[chunk][level], PARTS[level])
        return staged(region, region, chunk, 7 + level, partner_of[BITS[chunk][level]])

    def store_own(chunk):
        return pltpu.make_async_copy(
            own_buf.at[chunk, rows_at(keeps[chunk][3], PARTS[3]), :],
            total_rows(chunk, keeps[chunk][3], PARTS[3]),
            local_sem.at[chunk],
        )

    def add(buf, chunk, start, size, arrived):
        piece = PARTS[3]

        def step(n, carry):
            here = rows_at(start + n * piece, piece)
            there = rows_at(n * piece, piece)
            buf[chunk, here, :] = buf[chunk, here, :] + arrived[there, :]
            return carry

        lax.fori_loop(0, size // piece, step, 0)

    def add_level(chunk, level):
        scatter(chunk, level).wait_recv()
        add(own_buf, chunk, keeps[chunk][level], PARTS[level], arrivals[level].at[chunk])

    def add_level_away(chunk, level):
        at = chunk - LOCAL_CHUNKS
        scatter_away(chunk, level).wait_recv()
        add(away_buf, at, keeps[chunk][level], PARTS[level], away_arrivals[level].at[at])

    def exchange(event, chunk):
        away = is_away(chunk)
        if event == 0:
            if away:
                for copy in loads[chunk]:
                    copy.wait()
                scatter_away(chunk, 0).start()
            scatter(chunk, 0).start()
            return
        if event == 1:
            if away:
                add_level_away(chunk, 0)
                scatter_away(chunk, 1).start()
            add_level(chunk, 0)
            scatter(chunk, 1).start()
            return
        if away and event == 2:
            add_level_away(chunk, 1)
            hand_over(chunk).start()
            add_level(chunk, 1)
            return
        if away:
            event -= 1
            if event == 2:
                hand_over(chunk).wait_recv()
                add(own_buf, chunk, keeps[chunk][1], PARTS[1], y_buf.at[chunk - LOCAL_CHUNKS])
        elif event == 2:
            add_level(chunk, 1)
        if event == 2:
            scatter(chunk, 2).start()
        elif event == 3:
            add_level(chunk, 2)
            scatter(chunk, 3).start()
        elif event == 4:
            add_level(chunk, 3)
            store_own(chunk).start()
            gather(chunk, 3).start()
        else:
            level = 8 - event
            if level == 3:
                store_own(chunk).wait()
            gathered(chunk, level).wait_recv()
            if level > 0:
                gather(chunk, level - 1).start()

    small_devices = (across_mp, *partner_of.values())

    def small_hop(n):
        return remote(
            small_buf.at[n],
            small_recv_buf.at[n],
            small_send_sem.at[n],
            small_recv_sem.at[n],
            small_devices[n],
        )

    def small_step(n):
        if n == 0:
            residents[6].wait()
        else:
            small_hop(n - 1).wait_recv()
            small_buf[n] = small_buf[n - 1] + small_recv_buf[n - 1]
        if n < 5:
            small_hop(n).start()
        else:
            small_out_ref[...] = small_buf[n]

    def input_rows(side):
        return mine if side == 0 else others

    def input_product(side, target):
        at = input_rows(side)
        part = None
        for k in range(3):
            product = lax.dot_general(
                triple_buf[k, at, :],
                project_buf[k, rows_at(target * width, width), :],
                (((1,), (1,)), ((), ())),
                preferred_element_type=f32,
            )
            part = product if part is None else part + product
        if side == 0:
            cols = pl.ds(pl.multiple_of(target * width, LANES), width)
            part = part + grad_buf[0, :, cols].astype(f32)
        return part

    def input_store(side):
        return pltpu.make_async_copy(
            input_buf.at[side], input_ref.at[input_rows(side), :], out_sem.at[3 + side]
        )

    def run(event, which):
        if event == "small":
            small_step(which)
        elif event == "send":
            input_swap.start()
        elif event == "layer":
            layer_swap.start()
            layer_keep.start()
        elif event == "input":
            input_swap.wait_recv()
            for side in range(2):
                part = input_product(side, mp_index)
                input_buf[side] = part + input_recv_buf[input_rows(side), :].astype(f32)
                input_store(side).start()
        else:
            exchange(event, which)

    pairs = heads // 2
    block_slots = plan_slots("b", blocks * pairs)
    part_slots = plan_slots("p", 4)
    turn_slots = plan_slots("t", turns)
    rest = plan_slots("e", 1)[0]

    def run_all(steps):
        for event, which in steps:
            run(event, which)

    def dispatch(slots, n, low, high):
        if not any(slots[low:high]):
            return
        if high - low == 1:
            for event, which in slots[low]:
                run(event, which)
            return
        middle = (low + high) // 2
        if any(slots[low:middle]):
            pl.when(n < middle)(lambda: dispatch(slots, n, low, middle))
        if any(slots[middle:high]):
            pl.when(n >= middle)(lambda: dispatch(slots, n, middle, high))

    grad_key_buf[...] = jnp.zeros_like(grad_key_buf)
    grad_value_buf[...] = jnp.zeros_like(grad_value_buf)
    sum_ref[...] = jnp.zeros_like(sum_ref)
    for copy in residents[:6]:
        copy.wait()
    first = lax.broadcasted_iota(jnp.int32, (rows, LANES), 1) < HEAD

    def back(block, carry):
        slot = block % 2
        at = block_rows(block)
        for copy in block_copies(block, slot):
            copy.wait()

        @pl.when(block + 1 < blocks)
        def _():
            for copy in block_copies(block + 1, 1 - slot):
                copy.start()

        pl.when(block == blocks // 2)(grad_swap.wait_recv)
        pl.when(block >= 2)(lambda: score_copy(block - 2, slot).wait())
        side = block // (blocks // 2)
        local = rows_at((block % (blocks // 2)) * rows, rows)
        grad_context = lax.dot_general(
            grad_buf[side, local, :],
            output_buf[...],
            (((1,), (1,)), ((), ())),
            preferred_element_type=f32,
        )
        scaled = (grad_context * inverse_buf[slot]).astype(bf16)
        for p in range(pairs):
            dispatch(block_slots, block * pairs + p, 0, blocks * pairs)
            cols = slice(p * LANES, (p + 1) * LANES)
            grad = scaled[:, cols]
            product = grad.astype(f32) * context_buf[at, cols].astype(f32)
            query_turned = query_buf[at, cols].T
            grad_turned = grad.T
            grad_query = None
            for u in range(2):
                h = 2 * p + u
                half = slice(u * HEAD, (u + 1) * HEAD)
                own = first if u == 0 else ~first
                total = jnp.sum(jnp.where(own, product, 0.0), axis=1, keepdims=True)
                exps = ring_buf[slot, h]
                grad_exp = dot_f32(grad, value_buf[h])
                grad_score = (exps.astype(f32) * (grad_exp - total)).astype(bf16)
                ring_buf[2 + slot, h] = grad_score
                part = dot_f32(grad_score, key_buf[h])
                grad_query = part if u == 0 else grad_query + part
                grad_key_buf[h] += dot_f32(query_turned[half], grad_score)
                grad_value_buf[h] += dot_f32(grad_turned[half], exps)
            triple_buf[0, at, cols] = (grad_query * 0.125).astype(bf16)
        score_copy(block, slot).start()
        return carry

    lax.fori_loop(0, blocks, back, 0)

    score_copy(blocks - 2, blocks % 2).wait()
    score_copy(blocks - 1, (blocks - 1) % 2).wait()
    for block in range(2):
        for copy in ring_copies(block):
            copy.start()
    run_all(part_slots[0])
    triple_buf[0, row_count:keys, :] = jnp.zeros((keys - row_count, width), bf16)
    for k, ref in ((1, grad_key_buf), (2, grad_value_buf)):
        for h in range(0, heads, 2):
            pair = ref[h : h + 2].reshape(LANES, keys)
            triple_buf[k, :, h * HEAD : (h + 2) * HEAD] = pair.T.astype(bf16)
    run_all(part_slots[1])
    for copy in residents[7:]:
        copy.wait()
    tokens_in = (((0,), (0,)), ((), ()))
    places = ((0, 0), (0, width), (1, 0))
    for k, (chunk, start) in enumerate(places):
        own_buf[chunk, start : start + width, :] = lax.dot_general(
            triple_buf[k], token_buf[...], tokens_in, preferred_element_type=f32
        ).astype(bf16)
    run_all(part_slots[2])
    own_buf[1, width : 2 * width, :] = (
        lax.dot_general(
            context_buf[mine, :], grad_buf[0], tokens_in, preferred_element_type=f32
        )
        + lax.dot_general(
            context_buf[others, :], grad_buf[1], tokens_in, preferred_element_type=f32
        )
    ).astype(bf16)
    run_all(part_slots[3])
    for side in range(2):
        input_send_buf[input_rows(side), :] = input_product(side, 1 - mp_index).astype(bf16)
    biases = jnp.concatenate(
        [
            jnp.sum(triple_buf[0].astype(f32), axis=0, keepdims=True),
            jnp.sum(triple_buf[2].astype(f32), axis=0, keepdims=True),
        ],
        axis=1,
    )

    def turn(n, carry):
        last = n * TABLE_STRIPS + TABLE_STRIPS - 1
        block = last // block_strips

        @pl.when(last % block_strips < TABLE_STRIPS)
        def _():
            for copy in ring_copies(block):
                copy.wait()

            @pl.when(block + 2 < blocks)
            def _():
                for copy in ring_copies(block + 2):
                    copy.start()

        dispatch(turn_slots, n, 0, turns)

        def refs_at(strip):
            slot = (strip // block_strips) % 4
            at = rows_at((strip % block_strips) * STRIP, STRIP)
            return (
                lambda h, cols: ring_buf[slot, h, at, cols],
                lambda cols: plane_buf[slot, at, cols],
                lambda cols: down_buf[slot, at, cols],
            )

        table_strips(
            [refs_at(n * TABLE_STRIPS + k) for k in range(TABLE_STRIPS)],
            sum_ref,
            heads,
            keys,
            high_counts,
        )
        return carry

    lax.fori_loop(0, turns, turn, 0)

    table_rows = sum(high_counts) * heads
    table_finish(sum_ref, table_buf.at[0], table_rows)
    lanes = table_buf.shape[2]
    pieces = 2 * width // lanes
    for n in range(pieces):
        table_buf[0, table_rows + n : table_rows + n + 1, :] = biases[:, n * lanes : (n + 1) * lanes]
    spare = table_buf.shape[1] - table_rows - pieces
    table_buf[0, table_rows + pieces :, :] = jnp.zeros((spare, lanes), f32)
    table_devices = tuple(partner_of.values())

    def table_hop(n):
        return remote(
            table_buf.at[n],
            table_recv_buf.at[n],
            table_send_sem.at[n],
            table_recv_sem.at[n],
            table_devices[n],
        )

    def table_step(n):
        if n > 0:
            table_hop(n - 1).wait_recv()
            table_buf[n] = table_buf[n - 1] + table_recv_buf[n - 1]
        if n < 4:
            table_hop(n).start()

    table_step(0)
    for n, (event, which) in enumerate(rest):
        if n % 3 == 2 and n // 3 < 4:
            table_step(n // 3 + 1)
        run(event, which)
    for n in range(min(len(rest) // 3, 4), 4):
        table_step(n + 1)
    table_ref[...] = table_buf[4]

    layer_arrival.wait_recv()
    layer_keep.wait()
    grad_swap.wait_send()
    input_swap.wait_send()
    layer_swap.wait_send()
    for side in range(2):
        input_store(side).wait()
    for n in range(5):
        small_hop(n).wait_send()
    for n in range(4):
        table_hop(n).wait_send()
    for chunk in range(CHUNKS):
        for level in range(4):
            scatter(chunk, level).wait_send()
            gather(chunk, level).wait_send()
        if is_away(chunk):
            scatter_away(chunk, 0).wait_send()
            scatter_away(chunk, 1).wait_send()
            hand_over(chunk).wait_send()


def finish(
    exps,
    inverse,
    plane,
    down,
    context,
    query,
    tokens,
    grad,
    layer,
    value_turned,
    key_wide,
    project_weight,
    output_weight,
    expand,
    reduce,
    small,
    counts,
):
    heads, row_count, keys = exps.shape
    width = heads * HEAD
    depth = tokens.shape[1]
    half_rows = row_count // 2
    high_counts = (counts[0] // 16, counts[1] // 16, counts[1] // 16)
    high_rows = sum(high_counts) * heads
    low_lanes = 16 * STRIP
    table_shape = (round_up(high_rows + 2 * width // low_lanes, 8), low_lanes)
    away = CHUNKS - LOCAL_CHUNKS
    anywhere = pl.BlockSpec(memory_space=pl.ANY)
    in_vmem = pl.BlockSpec(memory_space=pltpu.VMEM)
    dma = pltpu.SemaphoreType.DMA
    total, layer_full, input_full, small_sum, table_sum, _ = pl.pallas_call(
        partial(finish_kernel, high_counts=high_counts),
        in_specs=[anywhere] * 18,
        out_specs=[anywhere, anywhere, anywhere, in_vmem, in_vmem, anywhere],
        out_shape=[
            jax.ShapeDtypeStruct((CHUNKS * CHUNK, CHUNK), bf16),
            jax.ShapeDtypeStruct((row_count, depth), bf16),
            jax.ShapeDtypeStruct((row_count, width), f32),
            jax.ShapeDtypeStruct(small.shape, f32),
            jax.ShapeDtypeStruct(table_shape, f32),
            jax.ShapeDtypeStruct(exps.shape, bf16),
        ],
        scratch_shapes=[
            pltpu.VMEM(output_weight.shape, bf16),
            pltpu.VMEM((2, half_rows, depth), bf16),
            pltpu.VMEM(value_turned.shape, bf16),
            pltpu.VMEM(key_wide.shape, bf16),
            pltpu.VMEM(context.shape, bf16),
            pltpu.VMEM(query.shape, bf16),
            pltpu.VMEM(tokens.shape, bf16),
            pltpu.VMEM(project_weight.shape, bf16),
            pltpu.VMEM((4, heads, BACK_ROWS, keys), bf16),
            pltpu.VMEM((2, BACK_ROWS, width), f32),
            pltpu.VMEM((heads, HEAD, keys), f32),
            pltpu.VMEM((heads, HEAD, keys), f32),
            pltpu.VMEM((3, keys, width), bf16),
            pltpu.VMEM((row_count, width), bf16),
            pltpu.VMEM((row_count, width), bf16),
            pltpu.VMEM((2, half_rows, width), f32),
            pltpu.VMEM((4, BACK_ROWS, keys), jnp.int16),
            pltpu.VMEM((4, BACK_ROWS, keys), jnp.int16),
            pltpu.VMEM((high_rows * STRIP, low_lanes), f32),
            pltpu.VMEM((CHUNKS, CHUNK, CHUNK), bf16),
            pltpu.VMEM((away, CHUNK, CHUNK), bf16),
            pltpu.VMEM((CHUNKS, PARTS[0], CHUNK), bf16),
            pltpu.VMEM((away, PARTS[0], CHUNK), bf16),
            pltpu.VMEM((CHUNKS, PARTS[1], CHUNK), bf16),
            pltpu.VMEM((away, PARTS[1], CHUNK), bf16),
            pltpu.VMEM((away, PARTS[1], CHUNK), bf16),
            pltpu.VMEM((CHUNKS, PARTS[2], CHUNK), bf16),
            pltpu.VMEM((CHUNKS, PARTS[3], CHUNK), bf16),
            pltpu.VMEM((6, *small.shape), f32),
            pltpu.VMEM((5, *small.shape), f32),
            pltpu.VMEM((5, *table_shape), f32),
            pltpu.VMEM((4, *table_shape), f32),
            dma((9,)),
            dma((2, 2)),
            dma((4, 3)),
            dma((CHUNKS, 2)),
            dma((CHUNKS,)),
            dma((5,)),
            dma((CHUNKS, 11)),
            dma((CHUNKS, 11)),
            dma((3,)),
            dma((3,)),
            dma((5,)),
            dma((5,)),
            dma((4,)),
            dma((4,)),
        ],
        compiler_params=pltpu.CompilerParams(
            vmem_limit_bytes=FINISH_VMEM, collective_id=0, has_side_effects=True
        ),
        name="finish",
    )(
        exps,
        inverse,
        plane,
        down,
        context,
        query,
        tokens,
        grad,
        layer,
        value_turned,
        key_wide,
        project_weight,
        output_weight,
        *expand,
        *reduce,
        small,
    )
    return total, layer_full, input_full, table_sum, small_sum


UNPACK_ROWS = 192


def unpack_kernel(
    total_ref,
    layer_in_ref,
    input_in_ref,
    sum_ref,
    small_ref,
    layer_ref,
    input_ref,
    project_ref,
    output_ref,
    expand_ref,
    reduce_ref,
    line_ref,
    across_ref,
    down_ref,
    bias_ref,
    second_gain_ref,
    second_shift_ref,
    reduce_bias_ref,
    first_gain_ref,
    first_shift_ref,
    output_bias_ref,
    expand_bias_ref,
    *,
    high_counts,
):
    step = pl.program_id(0)
    layer_ref[...] = layer_in_ref[...]
    input_ref[...] = input_in_ref[...].reshape(input_ref.shape)
    values = total_ref[...].astype(f32)

    half = values.shape[0] // 2

    @pl.when(step < 2)
    def _():
        project_ref[0] = values[:half].T

    @pl.when(step == 0)
    def _():
        project_ref[1] = values[half:].T

    @pl.when(step == 1)
    def _():
        output_ref[...] = values[half:]

    @pl.when((step >= 2) & (step < 4))
    def _():
        expand_ref[...] = values

    @pl.when(step >= 4)
    def _():
        reduce_ref[...] = values

    @pl.when(step == 0)
    def _():
        lanes = sum_ref.shape[1]
        row = lax.broadcasted_iota(jnp.int32, (lanes, LANES), 0) // STRIP
        same = row == lax.broadcasted_iota(jnp.int32, (lanes, LANES), 1)
        folded = jnp.dot(
            sum_ref[...],
            jnp.where(same, 1.0, 0.0),
            precision=lax.Precision.HIGHEST,
            preferred_element_type=f32,
        )
        heads = line_ref.shape[0]
        start = 0
        for ref, count in zip((line_ref, across_ref, down_ref), high_counts):
            parts = []
            for _ in range(count):
                parts.append(folded[start : start + heads, : lanes // STRIP])
                start += heads
            ref[...] = jnp.concatenate(parts, axis=1)
        half = bias_ref.shape[1] - lanes
        middle = sum_ref[start + 1 : start + 2, :]
        bias_ref[0:1, :] = jnp.concatenate([sum_ref[start : start + 1, :], middle[:, :half]], axis=1)
        bias_ref[1:2, :] = jnp.concatenate([middle[:, half:], sum_ref[start + 2 : start + 3, :]], axis=1)
        lead = lax.axis_index("mp") == 0
        for n, ref in enumerate(
            (
                second_gain_ref,
                second_shift_ref,
                reduce_bias_ref,
                first_gain_ref,
                first_shift_ref,
                output_bias_ref,
            )
        ):
            row = small_ref[n : n + 1, :]
            if ref.shape[0] < row.shape[1]:
                cut = ref.shape[0]
                row = jnp.where(lead, row[:, :cut], row[:, cut:])
            ref[...] = row.reshape(ref.shape)
        pieces = expand_bias_ref.shape[0] // small_ref.shape[1]
        width = small_ref.shape[1]
        for k in range(pieces):
            even = small_ref[8 + k : 9 + k, :]
            odd = small_ref[8 + pieces + k : 9 + pieces + k, :]
            expand_bias_ref[k * width : (k + 1) * width] = jnp.where(lead, even, odd).reshape(width)


def unpack(total, layer, inputs, sums, small, length, heads, counts):
    width = inputs.shape[1]
    depth = layer.shape[1]
    high_counts = (counts[0] // 16, counts[1] // 16, counts[1] // 16)

    def whole(shape):
        return pl.BlockSpec(shape, lambda i: (0,) * len(shape))

    def rows(columns):
        return pl.BlockSpec((UNPACK_ROWS, columns), lambda i: (i, 0))

    shapes = [
        ((length, depth), bf16),
        ((length, 1, width), f32),
        ((3, depth, width), f32),
        ((width, depth), f32),
        ((CHUNK, 2 * CHUNK), f32),
        ((2 * CHUNK, CHUNK), f32),
        ((heads, counts[0]), f32),
        ((heads, counts[1]), f32),
        ((heads, counts[1]), f32),
        ((2, width), f32),
        ((depth,), f32),
        ((depth,), f32),
        ((depth,), f32),
        ((width,), f32),
        ((width,), f32),
        ((depth,), f32),
        ((2 * CHUNK,), f32),
    ]
    return pl.pallas_call(
        partial(unpack_kernel, high_counts=high_counts),
        grid=(CHUNKS,),
        in_specs=[
            pl.BlockSpec((CHUNK, CHUNK), lambda i: (i, 0)),
            rows(depth),
            rows(width),
            whole(sums.shape),
            whole(small.shape),
        ],
        out_specs=[
            rows(depth),
            pl.BlockSpec((UNPACK_ROWS, 1, width), lambda i: (i, 0, 0)),
            pl.BlockSpec((2, depth, width), lambda i: (jnp.minimum(i, 1), 0, 0)),
            whole((width, depth)),
            pl.BlockSpec((CHUNK, CHUNK), lambda i: (0, jnp.clip(i - 2, 0, 1))),
            pl.BlockSpec((CHUNK, CHUNK), lambda i: (jnp.clip(i - 4, 0, 1), 0)),
            *(whole(shape) for shape, _ in shapes[6:]),
        ],
        out_shape=[jax.ShapeDtypeStruct(shape, kind) for shape, kind in shapes],
        compiler_params=pltpu.CompilerParams(vmem_limit_bytes=vmem_limit),
        name="unpack",
    )(total, layer, inputs, sums, small)


def feed_kernel(
    context_ref,
    context_away_ref,
    token_ref,
    cotangent_ref,
    valid_ref,
    output_ref,
    output_away_ref,
    expand_ref,
    expand_away_ref,
    reduce_ref,
    reduce_away_ref,
    expand_bias_ref,
    expand_bias_away_ref,
    output_bias_ref,
    first_gain_ref,
    first_shift_ref,
    reduce_bias_ref,
    second_gain_ref,
    second_shift_ref,
    layer_ref,
    grad_ref,
    expand_grad_ref,
    expand_grad_away_ref,
    reduce_grad_ref,
    reduce_grad_away_ref,
    small_ref,
    input_buf,
    norm_buf,
    hat_buf,
    inverse_buf,
    total_buf,
    reduced_buf,
    active_buf,
    slope_buf,
    before_buf,
    vector_ref,
    bias_buf,
    *,
    pieces,
    tiles,
):
    rows, width = token_ref.shape
    step = pl.program_id(0)
    piece = step % (2 * pieces)
    strip_rows = FEED_STRIP
    strips = rows // strip_rows

    def vector(n):
        return vector_ref[n : n + 1, :]

    def for_strips(body, sums):
        def run(n, carry):
            at = pl.ds(pl.multiple_of(n * strip_rows, STRIP), strip_rows)
            return tuple(
                old + jnp.sum(new.reshape(strip_rows // 8, 8, width), axis=0)
                for old, new in zip(carry, body(at))
            )

        start = tuple(jnp.zeros((8, width), f32) for _ in range(sums))
        done = lax.fori_loop(0, strips, run, start)
        return [jnp.sum(part, axis=0, keepdims=True) for part in done]

    def mean(values):
        return jnp.sum(values, axis=-1, keepdims=True) * (1.0 / width)

    @pl.when(step == 0)
    def _():
        small_ref[...] = jnp.zeros_like(small_ref)
        for n, ref in enumerate(
            (
                output_bias_ref,
                first_gain_ref,
                first_shift_ref,
                reduce_bias_ref,
                second_gain_ref,
                second_shift_ref,
            )
        ):
            vector_ref[n : n + 1, :] = ref[...].astype(f32).reshape(1, width)
        bias = expand_bias_ref[...].astype(f32).reshape(1, -1)
        for k in range(pieces):
            cols = slice(k * expand_ref.shape[1], (k + 1) * expand_ref.shape[1])
            bias_buf[k : k + 1, :] = bias[:, cols]
            bias_buf[pieces + k : pieces + k + 1, :] = expand_bias_away_ref[0:1, cols]
        total_buf[...] = dot_f32(context_ref[...], output_ref[...]) + dot_f32(
            context_away_ref[...], output_away_ref[...]
        )

        def body(at):
            values = token_ref[at, :].astype(f32) + (total_buf[at, :] + vector(0))
            centered = values - mean(values)
            inverse = lax.rsqrt(mean(centered * centered) + norm_epsilon)
            hat = centered * inverse
            norm = hat * vector(1) + vector(2)
            hat_buf[at, :] = hat
            inverse_buf[at, :] = jnp.broadcast_to(inverse, (strip_rows, LANES))
            norm_buf[at, :] = norm
            input_buf[at, :] = norm.astype(bf16)
            total_buf[at, :] = norm + vector(3)
            return ()

        for_strips(body, 0)

    def forward(expand, reduce):
        for start, size in tiles:
            at = slice(start, start + size)
            before = dot_f32(input_buf[at, :], expand[...]) + bias_buf[pl.ds(piece, 1), :]
            phi = 0.5 * lax.erf(before * 0.7071067811865476) + 0.5
            slope_buf[piece, at, :] = phi + before * (
                0.3989422804014327 * jnp.exp(-0.5 * (before * before))
            )
            active = (before * phi).astype(bf16)
            active_buf[piece, at, :] = active
            total_buf[at, :] += dot_f32(active, reduce[...])

    pl.when(step < pieces)(lambda: forward(expand_ref, reduce_ref))
    pl.when((step >= pieces) & (step < 2 * pieces))(
        lambda: forward(expand_away_ref, reduce_away_ref)
    )

    @pl.when(step == 2 * pieces)
    def _():
        def body(at):
            values = total_buf[at, :]
            valid = valid_ref[at, 0:1]
            centered = values - mean(values)
            inverse = lax.rsqrt(mean(centered * centered) + norm_epsilon)
            hat = centered * inverse
            layer_ref[at, :] = (valid * (hat * vector(4) + vector(5))).astype(bf16)
            grad_out = jnp.where(valid > 0, cotangent_ref[at, :].astype(f32), 0.0)
            grad_hat = grad_out * vector(4)
            mixed = inverse * (grad_hat - mean(grad_hat) - hat * mean(grad_hat * hat))
            low = mixed.astype(bf16)
            reduced_buf[at, :] = low
            total_buf[at, :] = mixed
            return grad_out * hat, grad_out, low.astype(f32)

        for n, part in enumerate(for_strips(body, 3)):
            small_ref[n : n + 1, :] = part

    def backward(expand, reduce):
        sums = None
        for start, size in tiles:
            at = slice(start, start + size)
            grad_active = lax.dot_general(
                reduced_buf[at, :], reduce[...], (((1,), (1,)), ((), ())), preferred_element_type=f32
            )
            before = (grad_active * slope_buf[piece, at, :]).astype(bf16)
            before_buf[piece, at, :] = before
            part = jnp.sum(before.astype(f32), axis=0, keepdims=True)
            sums = part if sums is None else sums + part
            total_buf[at, :] += lax.dot_general(
                before, expand[...], (((1,), (1,)), ((), ())), preferred_element_type=f32
            )
        mp_index = lax.axis_index("mp")
        side = jnp.where(piece < pieces, mp_index, 1 - mp_index)
        small_ref[pl.ds(8 + side * pieces + lax.rem(piece, pieces), 1), :] = sums

    pl.when((step >= 2 * pieces) & (step < 3 * pieces))(lambda: backward(expand_ref, reduce_ref))
    pl.when((step >= 3 * pieces) & (step < 4 * pieces))(
        lambda: backward(expand_away_ref, reduce_away_ref)
    )

    @pl.when(step == 4 * pieces)
    def _():
        def body(at):
            grad_first = total_buf[at, :]
            hat = hat_buf[at, :]
            grad_hat = grad_first * vector(1)
            inverse = inverse_buf[at, 0:1]
            inner = inverse * (grad_hat - mean(grad_hat) - hat * mean(grad_hat * hat))
            low = inner.astype(bf16)
            grad_ref[at, :] = low
            return grad_first * hat, grad_first, low.astype(f32)

        for n, part in enumerate(for_strips(body, 3)):
            small_ref[n + 3 : n + 4, :] = part

    def weights(expand_grad, reduce_grad):
        reduce_grad[...] = lax.dot_general(
            active_buf[piece], reduced_buf[...], (((0,), (0,)), ((), ())), preferred_element_type=f32
        ).astype(bf16)
        expand_grad[...] = lax.dot_general(
            input_buf[...], before_buf[piece], (((0,), (0,)), ((), ())), preferred_element_type=f32
        ).astype(bf16)

    pl.when((step >= 4 * pieces) & (step < 5 * pieces))(
        lambda: weights(expand_grad_ref, reduce_grad_ref)
    )
    pl.when(step >= 5 * pieces)(lambda: weights(expand_grad_away_ref, reduce_grad_away_ref))


def feed(
    context,
    context_away,
    tokens,
    cotangent,
    valid,
    output,
    output_away,
    expand,
    expand_away,
    reduce,
    reduce_away,
    expand_bias,
    expand_bias_away,
    vectors,
):
    rows, width = context_away.shape[0], tokens.shape[1]
    hidden = expand.shape[1]
    size = FEED_PIECE
    pieces = hidden // size
    split = round_up(rows // 2, STRIP)
    tiles = ((0, split), (split, rows - split))

    def once(array):
        zeros = (0,) * array.ndim
        return pl.BlockSpec(array.shape, lambda i: zeros, pipeline_mode=pl.Buffered(1))

    def mine(array):
        return pl.BlockSpec(
            (rows, array.shape[1]),
            lambda i: (lax.axis_index("mp"), 0),
            pipeline_mode=pl.Buffered(1),
        )

    def place(first, i):
        at = lax.rem(i, 2 * pieces) - first
        at = jnp.clip(at, 0, pieces - 1)
        return jnp.where(i < 4 * pieces, at, pieces - 1)

    def grad_place(first, i):
        return jnp.clip(i - 4 * pieces - first, 0, pieces - 1)

    wide = lambda first: pl.BlockSpec((width, size), lambda i: (0, place(first, i)))
    tall = lambda first: pl.BlockSpec((size, width), lambda i: (place(first, i), 0))
    wide_grad = lambda first: pl.BlockSpec((width, size), lambda i: (0, grad_place(first, i)))
    tall_grad = lambda first: pl.BlockSpec((size, width), lambda i: (grad_place(first, i), 0))
    whole = lambda shape: pl.BlockSpec(
        shape, lambda i: (0,) * len(shape), pipeline_mode=pl.Buffered(1)
    )
    full = jax.ShapeDtypeStruct((rows, width), bf16)
    return pl.pallas_call(
        partial(feed_kernel, pieces=pieces, tiles=tiles),
        grid=(6 * pieces,),
        in_specs=[
            mine(context),
            once(context_away),
            mine(tokens),
            mine(cotangent),
            mine(valid),
            once(output),
            once(output_away),
            wide(0),
            wide(pieces),
            tall(0),
            tall(pieces),
            once(expand_bias),
            once(expand_bias_away),
            *(once(vector) for vector in vectors),
        ],
        out_specs=[
            whole((rows, width)),
            whole((rows, width)),
            wide_grad(0),
            wide_grad(pieces),
            tall_grad(0),
            tall_grad(pieces),
            whole((16, width)),
        ],
        out_shape=[
            full,
            full,
            jax.ShapeDtypeStruct((width, hidden), bf16),
            jax.ShapeDtypeStruct((width, hidden), bf16),
            jax.ShapeDtypeStruct((hidden, width), bf16),
            jax.ShapeDtypeStruct((hidden, width), bf16),
            jax.ShapeDtypeStruct((16, width), f32),
        ],
        scratch_shapes=[
            pltpu.VMEM((rows, width), bf16),
            pltpu.VMEM((rows, width), f32),
            pltpu.VMEM((rows, width), f32),
            pltpu.VMEM((rows, LANES), f32),
            pltpu.VMEM((rows, width), f32),
            pltpu.VMEM((rows, width), bf16),
            pltpu.VMEM((2 * pieces, rows, size), bf16),
            pltpu.VMEM((2 * pieces, rows, size), f32),
            pltpu.VMEM((2 * pieces, rows, size), bf16),
            pltpu.VMEM((8, width), f32),
            pltpu.VMEM((2 * pieces, size), f32),
        ],
        compiler_params=pltpu.CompilerParams(vmem_limit_bytes=vmem_limit),
        name="feed",
    )(
        context,
        context_away,
        tokens,
        cotangent,
        valid,
        output,
        output_away,
        expand,
        expand_away,
        reduce,
        reduce_away,
        expand_bias,
        expand_bias_away,
        *vectors,
    )


def swap(array):
    return lax.ppermute(array, "mp", [(0, 1), (1, 0)])


def partner(array, count, bit):
    return lax.ppermute(array, "dp", [(i, i ^ bit) for i in range(count)])


def sum_rows_over_dp(array, count):
    place = lax.axis_index("dp")
    bits = []
    bit = 1
    while bit < count:
        mine = (place // bit) % 2
        halves = array.reshape((2, array.shape[0] // 2) + array.shape[1:])
        sent = lax.dynamic_index_in_dim(halves, 1 - mine, 0, keepdims=False)
        kept = lax.dynamic_index_in_dim(halves, mine, 0, keepdims=False)
        array = kept + partner(sent, count, bit)
        bits.append(bit)
        bit *= 2
    for bit in reversed(bits):
        lead = (place // bit) % 2 == 0
        other = partner(array, count, bit)
        array = jnp.concatenate(
            [jnp.where(lead, array, other), jnp.where(lead, other, array)], axis=0
        )
    return array


def sum_small(arrays, count, over_mp):
    sizes = [a.size for a in arrays]
    total = sum(sizes)
    flat = jnp.concatenate([a.reshape(-1) for a in arrays])
    flat = jnp.pad(flat, (0, round_up(total, 1024) - total)).reshape(-1, LANES)
    if over_mp:
        flat = flat + swap(flat)
    bit = 1
    while bit < count:
        flat = flat + partner(flat, count, bit)
        bit *= 2
    flat = flat.reshape(-1)
    outs = []
    start = 0
    for array, size in zip(arrays, sizes):
        outs.append(flat[start : start + size].reshape(array.shape))
        start += size
    return outs


def per_device(
    dp_count,
    tokens,
    cotangent,
    long_flag,
    token_mask,
    bucket_line,
    bucket_across,
    bucket_down,
    project_weight,
    project_bias,
    table_line,
    table_across,
    table_down,
    output_weight,
    output_bias,
    first_gain,
    first_shift,
    expand_weight,
    expand_bias,
    reduce_weight,
    reduce_bias,
    second_gain,
    second_shift,
):
    length = tokens.shape[1]
    width = project_weight.shape[2]
    heads = table_line.shape[1]
    counts = (table_line.shape[0], table_across.shape[0])
    rows = round_up(length, BLOCK_ROWS)
    half_rows = rows // 2
    keys = round_up(length, 3 * LANES)
    mp_index = lax.axis_index("mp")
    lead = mp_index == 0

    def own_rows(array):
        return lax.dynamic_slice_in_dim(array, mp_index * half_rows, half_rows, 0)

    def in_order(mine, other):
        return jnp.where(lead, mine, other), jnp.where(lead, other, mine)


    (
        query,
        key_wide,
        key_turned,
        value_ones,
        value_turned,
        padded,
        plane,
        down,
        valid_rows,
        expand_quarter,
    ) = prepare(
        tokens[0],
        project_weight,
        project_bias,
        (bucket_line, bucket_across, bucket_down),
        long_flag,
        token_mask,
        expand_weight,
        rows,
        keys,
        counts[0],
    )
    (
        exps,
        context,
        inverse,
        context_away,
        expand_away,
        output_away,
        reduce_away,
        expand_bias_away,
    ) = attend(
        query,
        key_turned,
        value_ones,
        plane,
        down,
        (table_line.T, table_across.T, table_down.T),
        expand_bias,
        expand_quarter,
        output_weight,
        reduce_weight,
    )

    (
        layer_mine,
        grad_mine,
        expand_own,
        expand_sent,
        reduce_own,
        reduce_sent,
        small,
    ) = feed(
        context,
        context_away,
        padded,
        cotangent[0],
        valid_rows,
        output_weight,
        output_away,
        expand_weight,
        expand_away,
        reduce_weight,
        reduce_away,
        expand_bias,
        expand_bias_away,
        (output_bias, first_gain, first_shift, reduce_bias, second_gain, second_shift),
    )
    if dp_count == 16 and expand_own.shape == (CHUNK, 2 * CHUNK):
        total, layer_full, input_full, sums, small = finish(
            exps,
            inverse,
            plane,
            down,
            context,
            query,
            padded,
            grad_mine,
            layer_mine,
            value_turned,
            key_wide,
            project_weight,
            output_weight,
            (expand_own, expand_sent),
            (reduce_own, reduce_sent),
            small,
            counts,
        )
        (
            layer_out,
            input_grad,
            project_weight_grad,
            output_weight_grad,
            expand_weight_grad,
            reduce_weight_grad,
            line_grad,
            across_grad,
            down_grad,
            project_bias_grad,
            second_gain_grad,
            second_shift_grad,
            reduce_bias_grad,
            first_gain_grad,
            first_shift_grad,
            output_bias_grad,
            expand_bias_grad,
        ) = unpack(total, layer_full, input_full, sums, small, length, heads, counts)
        layer_out = layer_out[None]
        input_grad = input_grad.reshape(1, length, width)
        table_grads = (line_grad.T, across_grad.T, down_grad.T)
    else:
        layer_out = jnp.concatenate(in_order(layer_mine, swap(layer_mine)))[None, :length]
        grad_attended = jnp.concatenate(in_order(grad_mine, swap(grad_mine)))
        output_weight_grad = jnp.einsum(
            "le,lf->ef", context, grad_attended, preferred_element_type=f32
        ).astype(bf16)
        grad_context = jnp.einsum(
            "lf,ef->le", grad_attended, output_weight, preferred_element_type=f32
        )
        grad_scaled = (grad_context * inverse).astype(bf16)
        grad_scores, grad_query, grad_key, grad_value = attend_back(
            exps, grad_scaled, context, query, value_turned, key_wide
        )
        grad_key = grad_key.reshape(width, keys)[:, :rows].T.astype(bf16)
        grad_value = grad_value.reshape(width, keys)[:, :rows].T.astype(bf16)
        triple = jnp.stack([grad_query, grad_key, grad_value])
        project_weight_grad = jnp.einsum(
            "ld,kle->kde", padded[:rows], triple, preferred_element_type=f32
        ).astype(bf16)
        project_bias_grad = jnp.stack(
            [jnp.sum(grad_query, axis=0, dtype=f32), jnp.sum(grad_value, axis=0, dtype=f32)]
        )
        input_part = jnp.einsum("kle,kde->ld", triple, project_weight, preferred_element_type=f32)
        input_part = lax.dynamic_update_slice_in_dim(
            input_part,
            own_rows(input_part) + grad_mine.astype(f32),
            mp_index * half_rows,
            0,
        )
        sent = jnp.where(lead, input_part[:, width:], input_part[:, :width]).astype(bf16)
        own = jnp.where(lead, input_part[:, :width], input_part[:, width:])
        input_grad = (own + swap(sent).astype(f32))[None, :length]
        table_grads = table_sums(grad_scores, plane, down, counts)
        reduce_weight_grad = sum_rows_over_dp(reduce_own + swap(reduce_sent), dp_count)
        expand_weight_grad = sum_rows_over_dp(expand_own + swap(expand_sent), dp_count)
        output_weight_grad = sum_rows_over_dp(output_weight_grad, dp_count)
        project_weight_grad = sum_rows_over_dp(
            project_weight_grad.reshape(-1, width), dp_count
        ).reshape(project_weight.shape)
        (small,) = sum_small([small], dp_count, True)
        bias_rows = expand_bias.size // small.shape[1]
        bias_rows = lax.dynamic_slice_in_dim(small, 8 + mp_index * bias_rows, bias_rows, 0)
        expand_bias_grad = bias_rows.reshape(-1)
        (
            second_gain_grad,
            second_shift_grad,
            reduce_bias_grad,
            first_gain_grad,
            first_shift_grad,
            output_bias_grad,
        ) = (small[n] for n in range(6))
        first_gain_grad = lax.dynamic_slice_in_dim(first_gain_grad, mp_index * width, width, 0)
        first_shift_grad = lax.dynamic_slice_in_dim(first_shift_grad, mp_index * width, width, 0)
        table_grads, project_bias_grad = sum_small(
            [table_grads, project_bias_grad], dp_count, False
        )
        cuts = (counts[0], counts[0] + counts[1])
        table_grads = (
            table_grads[: cuts[0]],
            table_grads[cuts[0] : cuts[1]],
            table_grads[cuts[1] :],
        )
    return (
        layer_out,
        input_grad,
        project_weight_grad.astype(f32),
        project_bias_grad,
        *table_grads,
        output_weight_grad.astype(f32),
        output_bias_grad,
        first_gain_grad,
        first_shift_grad,
        expand_weight_grad.astype(f32),
        expand_bias_grad,
        reduce_weight_grad.astype(f32),
        reduce_bias_grad,
        second_gain_grad,
        second_shift_grad,
    )


def solution(mesh):
    placed = (
        P("dp", None, None),
        P("dp", None, None),
        P("dp"),
        P("dp", None),
        P("dp", None, None),
        P("dp", None, None),
        P("dp", None, None),
        P(None, None, "mp"),
        P(None, "mp"),
        P(None, "mp"),
        P(None, "mp"),
        P(None, "mp"),
        P("mp", None),
        P(),
        P(),
        P(),
        P(None, "mp"),
        P("mp"),
        P("mp", None),
        P(),
        P(),
        P(),
    )
    return jax.shard_map(
        partial(per_device, mesh.shape["dp"]),
        mesh=mesh,
        in_specs=placed,
        out_specs=(
            P("dp", None, None),
            P("dp", None, "mp"),
            P(None, None, "mp"),
            P(None, "mp"),
            P(None, "mp"),
            P(None, "mp"),
            P(None, "mp"),
            P("mp", None),
            P(),
            P("mp"),
            P("mp"),
            P(None, "mp"),
            P("mp"),
            P("mp", None),
            P(),
            P(),
            P(),
        ),
        check_vma=False,
    )
```

```python
from functools import partial

import jax
import jax.numpy as jnp
from jax import lax
from jax.experimental import pallas as pl
from jax.experimental.pallas import tpu as pltpu
from jax.sharding import PartitionSpec as P

LONG = 1089
SHORT = 709
HEAD = 64
LANES = 128
STRIP = 16
BLOCK_ROWS = 224
FEED_PIECE = 768
FEED_STRIP = 560
TABLE_STRIPS = 2
ATTEND_STRIPS = 7

large_negative = -1000000000.0
norm_epsilon = 1e-05
vmem_limit = 56 * 2**20
FINISH_VMEM = 62 * 2**20
bf16 = jnp.bfloat16
f32 = jnp.float32


def round_up(value, step):
    return (value + step - 1) // step * step


def whole_spec(array):
    zeros = (0,) * array.ndim
    return pl.BlockSpec(array.shape, lambda i: zeros)


def dot_f32(left, right):
    return jnp.dot(left, right, preferred_element_type=f32)


def gather_lanes(values, index):
    dims = lax.GatherDimensionNumbers(
        offset_dims=(),
        collapsed_slice_dims=(1,),
        start_index_map=(1,),
        operand_batching_dims=(0,),
        start_indices_batching_dims=(0,),
    )
    return lax.gather(
        values,
        index[..., None],
        dims,
        slice_sizes=(1, 1),
        mode=lax.GatherScatterMode.PROMISE_IN_BOUNDS,
    )


def quarter_rows(ref, quarter):
    count = ref.shape[0] // 4
    return pl.ds(pl.multiple_of(quarter * count, STRIP), count)


def prepare_kernel(
    token_ref,
    weight_ref,
    bias_ref,
    line_ref,
    across_ref,
    down_ref,
    flag_ref,
    mask_ref,
    expand_ref,
    query_ref,
    key_ref,
    key_turned_ref,
    value_ref,
    value_turned_ref,
    token_out_ref,
    plane_ref,
    down_out_ref,
    valid_ref,
    quarter_ref,
    row_ref,
    send_sem,
    recv_sem,
    *,
    length,
    line_count,
):
    step = pl.program_id(0)
    across_mp = {"mp": 1 - lax.axis_index("mp")}
    fetch = pltpu.make_async_remote_copy(
        src_ref=expand_ref.at[quarter_rows(expand_ref, lax.axis_index("dp") % 4), :],
        dst_ref=quarter_ref,
        send_sem=send_sem,
        recv_sem=recv_sem,
        device_id=across_mp,
        device_id_type=pl.DeviceIdType.MESH,
    )

    @pl.when(step == 0)
    def _():
        barrier = pltpu.get_barrier_semaphore()
        pl.semaphore_signal(
            barrier, inc=1, device_id=across_mp, device_id_type=pl.DeviceIdType.MESH
        )
        pl.semaphore_wait(barrier, 1)
        fetch.start()
        limit = jnp.where(flag_ref[0] > 0, LONG, SHORT)
        position = lax.broadcasted_iota(jnp.int32, (1, length), 1)
        row_ref[...] = jnp.zeros_like(row_ref)
        row_ref[0:1, :length] = jnp.where((mask_ref[...] > 0) & (position < limit), 1.0, 0.0)

    rows = token_ref.shape[0]
    keys = plane_ref.shape[1]
    place = pl.program_id(0) * rows + lax.broadcasted_iota(jnp.int32, token_ref.shape, 0)
    token = jnp.where(place < length, token_ref[...].astype(f32), 0.0).astype(bf16)
    token_out_ref[...] = token
    bias = bias_ref[...].astype(f32)
    query = (dot_f32(token, weight_ref[0]) + bias[0:1, :]).astype(bf16)
    query_ref[...] = (query.astype(f32) * 0.125).astype(bf16)
    key = dot_f32(token, weight_ref[1])
    value = dot_f32(token, weight_ref[2]) + bias[1:2, :]
    away = jnp.where(row_ref[0:1, :] > 0, 0, line_count)
    inside = pl.program_id(0) * rows + lax.broadcasted_iota(jnp.int32, (rows, length), 0) < length
    line = line_ref[...].reshape(rows, length)
    across = across_ref[...].reshape(rows, length)
    down = down_ref[...].reshape(rows, length)
    plane = jnp.where(inside, line | (across << 8), 0) | away[:, :length]
    plane_ref[:, :length] = plane.astype(jnp.int16)
    plane_ref[:, length:] = jnp.full((rows, keys - length), line_count, jnp.int16)
    here = pl.ds(pl.multiple_of(step * rows, LANES), rows)
    valid_ref[...] = jnp.broadcast_to(row_ref[0:1, here], (LANES, rows)).T
    down_out_ref[:, :length] = jnp.where(inside, down, 0).astype(jnp.int16)
    down_out_ref[:, length:] = jnp.zeros((rows, keys - length), jnp.int16)
    lane_first = lax.broadcasted_iota(jnp.int32, (rows, LANES), 1) < HEAD
    row_first = lax.broadcasted_iota(jnp.int32, (LANES, rows), 0) < HEAD
    for p in range(key.shape[1] // LANES):
        cols = slice(p * LANES, (p + 1) * LANES)
        key_pair, value_pair = key[:, cols], value[:, cols]
        key_turned, value_turned = key_pair.T, value_pair.T
        for u in range(2):
            h = 2 * p + u
            lane_own = lane_first if u == 0 else ~lane_first
            row_own = row_first if u == 0 else ~row_first
            key_ref[h] = jnp.where(lane_own, key_pair, 0.0).astype(bf16)
            value_ref[h] = jnp.where(lane_own, value_pair, 1.0).astype(bf16)
            key_turned_ref[h] = jnp.where(row_own, key_turned, 0.0).astype(bf16)
            value_turned_ref[h] = jnp.where(row_own, value_turned, 0.0).astype(bf16)
    pl.when(step == pl.num_programs(0) - 1)(fetch.wait)


def prepare(tokens, weight, bias, buckets, flag, token_mask, expand, row_count, keys, line_count):
    length, depth = tokens.shape
    width = weight.shape[2]
    heads = width // HEAD
    block = 3 * LANES
    row = pl.BlockSpec((block, width), lambda i: (i, 0))
    deep_row = pl.BlockSpec((block, depth), lambda i: (i, 0))
    wide = pl.BlockSpec((heads, block, LANES), lambda i: (0, i, 0))
    turned = pl.BlockSpec((heads, LANES, block), lambda i: (0, 0, i))
    bucket = pl.BlockSpec((block, 1, length), lambda i: (i, 0, 0))
    packed = pl.BlockSpec((block, keys), lambda i: (i, 0))
    wide_shape = jax.ShapeDtypeStruct((heads, keys, LANES), bf16)
    turned_shape = jax.ShapeDtypeStruct((heads, LANES, keys), bf16)
    packed_shape = jax.ShapeDtypeStruct((row_count, keys), jnp.int16)
    return pl.pallas_call(
        partial(prepare_kernel, length=length, line_count=line_count),
        grid=(keys // block,),
        in_specs=[
            deep_row,
            whole_spec(weight),
            whole_spec(bias),
            bucket,
            bucket,
            bucket,
            pl.BlockSpec(memory_space=pltpu.SMEM),
            whole_spec(token_mask),
            pl.BlockSpec(memory_space=pl.ANY),
        ],
        out_specs=[
            row,
            wide,
            turned,
            wide,
            turned,
            deep_row,
            packed,
            packed,
            pl.BlockSpec((block, LANES), lambda i: (i, 0)),
            pl.BlockSpec(memory_space=pl.ANY),
        ],
        out_shape=[
            jax.ShapeDtypeStruct((keys, width), bf16),
            wide_shape,
            turned_shape,
            wide_shape,
            turned_shape,
            jax.ShapeDtypeStruct((keys, depth), bf16),
            packed_shape,
            packed_shape,
            jax.ShapeDtypeStruct((keys, LANES), f32),
            jax.ShapeDtypeStruct((expand.shape[0] // 4, expand.shape[1]), bf16),
        ],
        scratch_shapes=[
            pltpu.VMEM((8, keys), f32),
            pltpu.SemaphoreType.DMA,
            pltpu.SemaphoreType.DMA,
        ],
        compiler_params=pltpu.CompilerParams(
            vmem_limit_bytes=vmem_limit, collective_id=2, has_side_effects=True
        ),
        name="prepare",
    )(
        tokens,
        weight,
        bias,
        *(index.reshape(length, 1, length) for index in buckets),
        flag,
        token_mask,
        expand,
    )


def attend_kernel(
    query_ref,
    key_ref,
    value_ref,
    plane_ref,
    down_ref,
    line_table_ref,
    across_table_ref,
    down_table_ref,
    expand_bias_ref,
    expand_quarter_ref,
    output_ref,
    reduce_ref,
    exp_out_ref,
    context_ref,
    inverse_ref,
    context_away_ref,
    expand_away_ref,
    output_away_ref,
    reduce_away_ref,
    bias_away_ref,
    score_ref,
    exp_ref,
    send_ref,
    table_ref,
    bias_ref,
    exp_sem,
    local_sem,
    send_sem,
    recv_sem,
):
    _, heads, rows, keys = exp_ref.shape
    step = pl.program_id(0)
    turn_rows = ATTEND_STRIPS * STRIP
    turns = rows // turn_rows
    place = lax.axis_index("dp")
    across_mp = {"mp": 1 - lax.axis_index("mp")}
    across = {bit: {"dp": place + bit * (1 - 2 * ((place // bit) % 2))} for bit in (1, 2)}

    def remote(src, dst, n, device):
        return pltpu.make_async_remote_copy(
            src_ref=src,
            dst_ref=dst,
            send_sem=send_sem.at[n],
            recv_sem=recv_sem.at[n],
            device_id=device,
            device_id_type=pl.DeviceIdType.MESH,
        )

    arrays = (
        (expand_quarter_ref, expand_away_ref),
        (output_ref, output_away_ref),
        (reduce_ref, reduce_away_ref),
    )
    quarter = place % 4
    other_chip = (place + 2) % 4
    other_core = quarter + 1 - 2 * (quarter % 2)
    third = (other_core + 2) % 4

    def rows_of(n, which):
        away = arrays[n][1]
        return away.at[quarter_rows(away, which), :]

    def fetch(n):
        ref = arrays[n][0]
        return remote(ref.at[quarter_rows(ref, quarter), :], rows_of(n, quarter), n, across_mp)

    def pass_on(n, stage):
        source = expand_quarter_ref if n == 0 and stage < 2 else rows_of(n, quarter)
        if stage == 0:
            return remote(source, rows_of(n, quarter), 3 + n, across[2])
        if stage == 1:
            return remote(source, rows_of(n, quarter), 6 + n, across[1])
        return remote(rows_of(n, other_chip), rows_of(n, other_chip), 9 + n, across[1])

    def arrival(n, stage):
        region = rows_of(n, (other_chip, other_core, third)[stage])
        return remote(region, region, 3 + 3 * stage + n, across_mp)

    def exp_copy(which, turn):
        half = lax.rem(which + 1 - lax.axis_index("mp"), 2)
        here = pl.ds(pl.multiple_of(turn * turn_rows, STRIP), turn_rows)
        there = pl.ds(pl.multiple_of(half * rows + turn * turn_rows, STRIP), turn_rows)
        return pltpu.make_async_copy(
            exp_ref.at[which, :, here, :], exp_out_ref.at[:, there, :], exp_sem.at[which, turn]
        )

    keep = pltpu.make_async_copy(expand_quarter_ref, rows_of(0, quarter), local_sem)
    context_swap = remote(send_ref, context_away_ref, 12, across_mp)
    bias_swap = remote(bias_ref, bias_away_ref, 13, across_mp)

    def event(n, stage):
        if stage == "fetched":
            fetch(n).wait_recv()
            pass_on(n, 0).start()
            pass_on(n, 1).start()
        else:
            arrival(n, 0).wait_recv()
            pass_on(n, 2).start()

    events = {
        (0, 2): ((1, "fetched"),),
        (1, 0): ((0, "passed"), (2, "fetched")),
        (1, 1): ((1, "passed"),),
    }

    @pl.when(step == 0)
    def _():
        barrier = pltpu.get_barrier_semaphore()
        for device in (across_mp, across[1], across[2]):
            pl.semaphore_signal(
                barrier, inc=1, device_id=device, device_id_type=pl.DeviceIdType.MESH
            )
        pl.semaphore_wait(barrier, 3)
        bias_ref[...] = jnp.broadcast_to(
            expand_bias_ref[...].astype(f32).reshape(1, -1), bias_ref.shape
        )
        bias_swap.start()
        for t, ref in enumerate((line_table_ref, across_table_ref, down_table_ref)):
            count = ref.shape[1]
            lanes = jnp.concatenate(
                [ref[...].astype(f32), jnp.full((heads, LANES - count), large_negative, f32)], axis=1
            )
            for h in range(heads):
                table_ref[t * heads + h] = jnp.broadcast_to(lanes[h : h + 1], (STRIP, LANES)).astype(
                    bf16
                )
        fetch(1).start()
        fetch(2).start()
        pass_on(0, 0).start()
        pass_on(0, 1).start()
        keep.start()

    for h in range(heads):
        pair = slice(h // 2 * LANES, (h // 2 + 1) * LANES)
        score_ref[h] = dot_f32(query_ref[:, pair], key_ref[h])

    lanes = [slice(c * LANES, (c + 1) * LANES) for c in range(keys // LANES)]

    def scores_of(at):
        scores = [[] for _ in range(heads)]
        for cols in lanes:
            packed = plane_ref[at, cols]
            bias = [None] * heads
            for t, index in enumerate(
                (packed & jnp.int16(255), packed >> jnp.int16(8), down_ref[at, cols])
            ):
                for h in range(heads):
                    found = gather_lanes(table_ref[t * heads + h], index).astype(f32)
                    bias[h] = found if t == 0 else bias[h] + found
            for h in range(heads):
                scores[h].append(score_ref[h, at, cols] + bias[h])
        return scores

    def exps_of(scores):
        exps = []
        for parts in scores:
            top = parts[0]
            for part in parts[1:]:
                top = jnp.maximum(top, part)
            top = jnp.max(top, axis=1, keepdims=True)
            exps.append([jnp.exp(part - top).astype(bf16) for part in parts])
        return exps

    def strips(n, carry):
        for (at_step, at_turn), pieces in events.items():

            @pl.when((step == at_step) & (n == at_turn))
            def _():
                for piece in pieces:
                    event(*piece)

        start = pl.multiple_of(n * turn_rows, STRIP)
        places = [pl.ds(start + k * STRIP, STRIP) for k in range(ATTEND_STRIPS)]
        scores = [scores_of(at) for at in places]
        exps = [exps_of(part) for part in scores]
        for at, part in zip(places, exps):
            for h in range(heads):
                for c, cols in enumerate(lanes):
                    exp_ref[step, h, at, cols] = part[h][c]
        exp_copy(step, n).start()
        return carry

    lax.fori_loop(0, turns, strips, 0)
    first = lax.broadcasted_iota(jnp.int32, (rows, LANES), 1) < HEAD
    for p in range(heads // 2):
        cols = slice(p * LANES, (p + 1) * LANES)
        even = dot_f32(exp_ref[step, 2 * p], value_ref[2 * p])
        odd = dot_f32(exp_ref[step, 2 * p + 1], value_ref[2 * p + 1])
        sums = jnp.where(first, pltpu.roll(even, HEAD, 1), pltpu.roll(odd, HEAD, 1))
        inverse = 1.0 / sums
        inverse_ref[:, cols] = inverse
        context = (jnp.where(first, even, odd) * inverse).astype(bf16)
        context_ref[:, cols] = context

        @pl.when(step == 0)
        def _():
            send_ref[:, cols] = context

    pl.when(step == 0)(context_swap.start)

    @pl.when(step == 1)
    def _():
        event(2, "passed")
        for which in range(2):
            for n in range(turns):
                exp_copy(which, n).wait()
        keep.wait()
        context_swap.wait()
        bias_swap.wait()
        for n in range(3):
            arrival(n, 1).wait_recv()
            arrival(n, 2).wait_recv()
            for stage in range(3):
                pass_on(n, stage).wait_send()
        fetch(1).wait_send()
        fetch(2).wait_send()


def attend(
    query,
    key_turned,
    value_ones,
    plane,
    down,
    tables,
    expand_bias,
    expand_quarter,
    output,
    reduce,
):
    heads, _, keys = key_turned.shape
    row_count = plane.shape[0]
    width = heads * HEAD
    half_rows = row_count // 2

    def half(i):
        return lax.rem(i + 1 - lax.axis_index("mp"), 2)

    anywhere = pl.BlockSpec(memory_space=pl.ANY)
    index_spec = pl.BlockSpec((half_rows, keys), lambda i: (half(i), 0))
    row_spec = pl.BlockSpec((half_rows, width), lambda i: (half(i), 0))
    return pl.pallas_call(
        attend_kernel,
        grid=(2,),
        in_specs=[
            row_spec,
            whole_spec(key_turned),
            whole_spec(value_ones),
            index_spec,
            index_spec,
            *(whole_spec(table) for table in tables),
            whole_spec(expand_bias),
            anywhere,
            anywhere,
            anywhere,
        ],
        out_specs=[
            anywhere,
            row_spec,
            row_spec,
            anywhere,
            anywhere,
            anywhere,
            anywhere,
            anywhere,
        ],
        out_shape=[
            jax.ShapeDtypeStruct((heads, row_count, keys), bf16),
            jax.ShapeDtypeStruct((row_count, width), bf16),
            jax.ShapeDtypeStruct((row_count, width), f32),
            jax.ShapeDtypeStruct((half_rows, width), bf16),
            jax.ShapeDtypeStruct((4 * expand_quarter.shape[0], expand_quarter.shape[1]), bf16),
            jax.ShapeDtypeStruct(output.shape, bf16),
            jax.ShapeDtypeStruct(reduce.shape, bf16),
            jax.ShapeDtypeStruct((8, expand_bias.size), f32),
        ],
        scratch_shapes=[
            pltpu.VMEM((heads, half_rows, keys), f32),
            pltpu.VMEM((2, heads, half_rows, keys), bf16),
            pltpu.VMEM((half_rows, width), bf16),
            pltpu.VMEM((3 * heads, STRIP, LANES), bf16),
            pltpu.VMEM((8, expand_bias.size), f32),
            pltpu.SemaphoreType.DMA((2, half_rows // (ATTEND_STRIPS * STRIP))),
            pltpu.SemaphoreType.DMA,
            pltpu.SemaphoreType.DMA((14,)),
            pltpu.SemaphoreType.DMA((14,)),
        ],
        compiler_params=pltpu.CompilerParams(
            vmem_limit_bytes=vmem_limit, collective_id=1, has_side_effects=True
        ),
        name="attend",
    )(
        query,
        key_turned,
        value_ones,
        plane,
        down,
        *tables,
        expand_bias,
        expand_quarter,
        output,
        reduce,
    )


def attend_back_kernel(
    exp_ref,
    grad_ref,
    context_ref,
    query_ref,
    value_ref,
    key_ref,
    grad_score_ref,
    grad_query_ref,
    grad_key_ref,
    grad_value_ref,
):
    heads, rows, _ = exp_ref.shape

    @pl.when(pl.program_id(0) == 0)
    def _():
        grad_key_ref[...] = jnp.zeros_like(grad_key_ref)
        grad_value_ref[...] = jnp.zeros_like(grad_value_ref)

    first = lax.broadcasted_iota(jnp.int32, (rows, LANES), 1) < HEAD
    for p in range(heads // 2):
        cols = slice(p * LANES, (p + 1) * LANES)
        grad = grad_ref[:, cols]
        product = grad.astype(f32) * context_ref[:, cols].astype(f32)
        query_turned = query_ref[:, cols].T
        grad_turned = grad.T
        grad_query = None
        for u in range(2):
            h = 2 * p + u
            half = slice(u * HEAD, (u + 1) * HEAD)
            own = first if u == 0 else ~first
            total = jnp.sum(jnp.where(own, product, 0.0), axis=1, keepdims=True)
            grad_exp = dot_f32(grad, value_ref[h])
            grad_score = (exp_ref[h].astype(f32) * (grad_exp - total)).astype(bf16)
            grad_score_ref[h] = grad_score
            part = dot_f32(grad_score, key_ref[h])
            grad_query = part if u == 0 else grad_query + part
            grad_key_ref[h] += dot_f32(query_turned[half], grad_score)
            grad_value_ref[h] += dot_f32(grad_turned[half], exp_ref[h])
        grad_query_ref[:, cols] = (grad_query * 0.125).astype(bf16)


def attend_back(exps, grad, context, query, value_turned, key_wide):
    heads, row_count, keys = exps.shape
    width = heads * HEAD
    row_spec = pl.BlockSpec((BLOCK_ROWS, width), lambda i: (i, 0))
    exp_spec = pl.BlockSpec((heads, BLOCK_ROWS, keys), lambda i: (0, i, 0))
    sum_spec = pl.BlockSpec((heads, HEAD, keys), lambda i: (0, 0, 0))
    return pl.pallas_call(
        attend_back_kernel,
        grid=(row_count // BLOCK_ROWS,),
        in_specs=[
            exp_spec,
            row_spec,
            row_spec,
            row_spec,
            whole_spec(value_turned),
            whole_spec(key_wide),
        ],
        out_specs=[exp_spec, row_spec, sum_spec, sum_spec],
        out_shape=[
            jax.ShapeDtypeStruct((heads, row_count, keys), bf16),
            jax.ShapeDtypeStruct((row_count, width), bf16),
            jax.ShapeDtypeStruct((heads, HEAD, keys), f32),
            jax.ShapeDtypeStruct((heads, HEAD, keys), f32),
        ],
        compiler_params=pltpu.CompilerParams(vmem_limit_bytes=vmem_limit),
        name="attend_back",
    )(exps, grad, context, query, value_turned, key_wide)


def table_strips(strips, sum_ref, heads, keys, high_counts):
    base = 0
    for t in range(3):
        shift = 8 if t == 1 else 0
        highs, lows = [], []
        for grad_of, plane_of, down_of in strips:
            for c in range(keys // LANES):
                cols = slice(c * LANES, (c + 1) * LANES)
                index = down_of(cols) if t == 2 else plane_of(cols)
                low = index & jnp.int16(15 << shift)
                high = index & jnp.int16(48 << shift)
                lows.append(
                    jnp.concatenate(
                        [
                            jnp.where(low == jnp.int16(x << shift), bf16(1), bf16(0))
                            for x in range(16)
                        ]
                    )
                )
                parts = []
                for x in range(high_counts[t]):
                    mask = high == jnp.int16(x << (4 + shift))
                    parts += [jnp.where(mask, grad_of(h, cols), bf16(0)) for h in range(heads)]
                highs.append(jnp.concatenate(parts))
        span = slice(base, base + high_counts[t] * heads * STRIP)
        sum_ref[span, :] += lax.dot_general(
            jnp.concatenate(highs, axis=1),
            jnp.concatenate(lows, axis=1),
            (((1,), (1,)), ((), ())),
            preferred_element_type=f32,
        )
        base = span.stop


def table_finish(sum_ref, out_ref, count):
    row_of_lane = lax.broadcasted_iota(jnp.int32, (STRIP, 16 * STRIP), 1) % STRIP
    same = row_of_lane == lax.broadcasted_iota(jnp.int32, (STRIP, 16 * STRIP), 0)
    for o in range(count):
        block = sum_ref[o * STRIP : (o + 1) * STRIP, :]
        out_ref[o : o + 1, :] = jnp.sum(jnp.where(same, block, 0.0), axis=0, keepdims=True)


def table_result(out, high_counts, heads):
    summed = jnp.sum(out.reshape(sum(high_counts), heads, 16, STRIP), axis=-1)
    return summed.transpose(0, 2, 1).reshape(-1, heads)


def table_kernel(grad_score_ref, plane_ref, down_ref, out_ref, sum_ref, *, high_counts):
    heads, rows, keys = grad_score_ref.shape
    step = pl.program_id(0)

    @pl.when(step == 0)
    def _():
        sum_ref[...] = jnp.zeros_like(sum_ref)

    def refs_at(start):
        at = pl.ds(pl.multiple_of(start, STRIP), STRIP)
        return (
            lambda h, cols: grad_score_ref[h, at, cols],
            lambda cols: plane_ref[at, cols],
            lambda cols: down_ref[at, cols],
        )

    def strips(r, carry):
        start = r * (TABLE_STRIPS * STRIP)
        table_strips(
            [refs_at(start + k * STRIP) for k in range(TABLE_STRIPS)],
            sum_ref,
            heads,
            keys,
            high_counts,
        )
        return carry

    lax.fori_loop(0, rows // (TABLE_STRIPS * STRIP), strips, 0)

    @pl.when(step == pl.num_programs(0) - 1)
    def _():
        table_finish(sum_ref, out_ref, out_ref.shape[0])


def table_sums(grad_scores, plane, down, counts):
    heads, row_count, keys = grad_scores.shape
    high_counts = (counts[0] // 16, counts[1] // 16, counts[1] // 16)
    high_rows = sum(high_counts) * heads
    index_spec = pl.BlockSpec((BLOCK_ROWS, keys), lambda i: (i, 0))
    out = pl.pallas_call(
        partial(table_kernel, high_counts=high_counts),
        grid=(row_count // BLOCK_ROWS,),
        in_specs=[
            pl.BlockSpec((heads, BLOCK_ROWS, keys), lambda i: (0, i, 0)),
            index_spec,
            index_spec,
        ],
        out_specs=pl.BlockSpec((high_rows, 16 * STRIP), lambda i: (0, 0)),
        out_shape=jax.ShapeDtypeStruct((high_rows, 16 * STRIP), f32),
        scratch_shapes=[pltpu.VMEM((high_rows * STRIP, 16 * STRIP), f32)],
        compiler_params=pltpu.CompilerParams(vmem_limit_bytes=vmem_limit),
        name="table_sums",
    )(grad_scores, plane, down)
    return table_result(out, high_counts, heads)


CHUNK = 768
CHUNKS = 6
LOCAL_CHUNKS = 2
PARTS = (CHUNK // 2, CHUNK // 4, CHUNK // 8, CHUNK // 16)
BITS = ((1, 2, 4, 8), (1, 4, 2, 8), (1, 2, 4, 8), (1, 4, 2, 8), (1, 2, 4, 8), (1, 4, 2, 8))
BACK_ROWS = 112
EXCHANGE = (
    ("b", 0, 0, 2), ("b", 0, 0, 3), ("b", 0, 0, 4), ("b", 1, 0, 5), ("b", 4, 1, 2), ("b", 6, 1, 3),
    ("b", 8, 1, 4), ("b", 9, 1, 5), ("b", 20, 2, 2), ("b", 22, 2, 3), ("p", 0, 3, 2), ("p", 2, 2, 4),
    ("p", 3, 2, 5), ("p", 3, 3, 3), ("p", 3, 0, 0), ("p", 3, 0, 1), ("t", 0, 4, 2), ("t", 1, 1, 0),
    ("t", 1, 1, 1), ("t", 2, 4, 3), ("t", 2, "small", 0), ("t", 3, 3, 4), ("t", 4, 5, 2),
    ("t", 6, 3, 5), ("t", 6, 2, 0), ("t", 6, 2, 1), ("t", 6, "small", 1), ("t", 8, 5, 3),
    ("t", 9, 4, 4), ("t", 10, 4, 5), ("t", 11, 6, 2), ("t", 11, "send", 0), ("t", 11, "small", 2),
    ("t", 12, 3, 1), ("t", 12, 3, 0), ("t", 13, 6, 3), ("t", 15, 5, 4), ("t", 16, "small", 3),
    ("t", 17, 5, 5), ("t", 17, 7, 3), ("t", 18, 7, 2), ("t", 19, 4, 1), ("t", 20, "small", 4),
    ("t", 21, 4, 0), ("t", 23, 6, 4), ("t", 24, 8, 2), ("t", 24, "input", 0), ("t", 25, 6, 5),
    ("t", 25, 9, 2), ("t", 25, "small", 5), ("t", 26, 8, 3), ("t", 26, "layer", 0), ("t", 27, 5, 1),
    ("t", 28, 9, 3), ("t", 29, 5, 0), ("t", 29, 7, 5), ("t", 29, 7, 4), ("t", 31, 6, 1),
    ("t", 33, 6, 0), ("e", 0, 8, 4), ("e", 0, 9, 4), ("e", 0, 8, 5), ("e", 0, 9, 5), ("e", 0, 7, 0),
    ("e", 0, 8, 0), ("e", 0, 7, 1), ("e", 0, 8, 1),
)


def plan_slots(phase, count):
    slots = [[] for _ in range(count)]
    for name, at, event, which in EXCHANGE:
        if name == phase:
            slots[at].append((event, which))
    return slots


def finish_kernel(
    exp_ref,
    inverse_ref,
    plane_ref,
    down_ref,
    context_ref,
    query_ref,
    token_ref,
    grad_ref,
    layer_ref,
    value_ref,
    key_ref,
    project_ref,
    output_ref,
    expand_ref,
    expand_away_ref,
    reduce_ref,
    reduce_away_ref,
    small_ref,
    total_ref,
    layer_out_ref,
    input_ref,
    small_out_ref,
    table_ref,
    score_ref,
    output_buf,
    grad_buf,
    value_buf,
    key_buf,
    context_buf,
    query_buf,
    token_buf,
    project_buf,
    ring_buf,
    inverse_buf,
    grad_key_buf,
    grad_value_buf,
    triple_buf,
    input_send_buf,
    input_recv_buf,
    input_buf,
    plane_buf,
    down_buf,
    sum_ref,
    own_buf,
    away_buf,
    core_buf,
    core_away_buf,
    first_buf,
    first_away_buf,
    y_buf,
    second_buf,
    third_buf,
    small_buf,
    small_recv_buf,
    table_buf,
    table_recv_buf,
    resident_sem,
    block_sem,
    ring_sem,
    load_sem,
    local_sem,
    out_sem,
    send_sem,
    recv_sem,
    wide_send_sem,
    wide_recv_sem,
    small_send_sem,
    small_recv_sem,
    table_send_sem,
    table_recv_sem,
    *,
    high_counts,
):
    heads, row_count, keys = exp_ref.shape
    width = heads * HEAD
    half_rows = row_count // 2
    rows = BACK_ROWS
    blocks = row_count // rows
    block_strips = rows // STRIP
    turns = row_count // (TABLE_STRIPS * STRIP)
    place = lax.axis_index("dp")
    mp_index = lax.axis_index("mp")
    side_of = {bit: (place // bit) % 2 for bit in (1, 2, 4, 8)}
    partner_of = {bit: {"dp": place + bit * (1 - 2 * side_of[bit])} for bit in (1, 2, 4, 8)}
    across_mp = {"mp": 1 - mp_index}

    def by_bits(*bits):
        return {"dp": place + sum(bit * (1 - 2 * side_of[bit]) for bit in bits)}

    diagonal = (by_bits(1, 2), by_bits(4, 8))
    barrier = pltpu.get_barrier_semaphore()
    for device in (*partner_of.values(), *diagonal, across_mp):
        pl.semaphore_signal(barrier, inc=1, device_id=device, device_id_type=pl.DeviceIdType.MESH)
    pl.semaphore_wait(barrier, 7)

    def rows_at(start, size):
        return pl.ds(pl.multiple_of(start, STRIP), size)

    def remote(src, dst, send, recv, device):
        return pltpu.make_async_remote_copy(
            src_ref=src,
            dst_ref=dst,
            send_sem=send,
            recv_sem=recv,
            device_id=device,
            device_id_type=pl.DeviceIdType.MESH,
        )

    mine = rows_at(mp_index * half_rows, half_rows)
    others = rows_at((1 - mp_index) * half_rows, half_rows)
    grad_swap = remote(
        grad_ref, grad_buf.at[1], wide_send_sem.at[0], wide_recv_sem.at[0], across_mp
    )
    input_swap = remote(
        input_send_buf, input_recv_buf, wide_send_sem.at[1], wide_recv_sem.at[1], across_mp
    )
    layer_swap = remote(
        layer_ref, layer_out_ref.at[mine, :], wide_send_sem.at[2], wide_recv_sem.at[2], across_mp
    )
    layer_arrival = remote(
        layer_out_ref.at[others, :],
        layer_out_ref.at[others, :],
        wide_send_sem.at[2],
        wide_recv_sem.at[2],
        across_mp,
    )
    layer_keep = pltpu.make_async_copy(layer_ref, layer_out_ref.at[mine, :], out_sem.at[2])
    grad_swap.start()

    residents = [
        pltpu.make_async_copy(src, dst, resident_sem.at[n])
        for n, (src, dst) in enumerate(
            (
                (grad_ref, grad_buf.at[0]),
                (output_ref, output_buf),
                (context_ref, context_buf),
                (query_ref, query_buf),
                (value_ref, value_buf),
                (key_ref, key_buf),
                (small_ref, small_buf.at[0]),
                (token_ref, token_buf),
                (project_ref, project_buf),
            )
        )
    ]

    def block_rows(block):
        start = (mp_index * (blocks // 2) + block) % blocks
        return rows_at(start * rows, rows)

    def block_copies(block, slot):
        at = block_rows(block)
        return (
            pltpu.make_async_copy(exp_ref.at[:, at, :], ring_buf.at[slot], block_sem.at[slot, 0]),
            pltpu.make_async_copy(inverse_ref.at[at, :], inverse_buf.at[slot], block_sem.at[slot, 1]),
        )

    def score_copy(block, slot):
        return pltpu.make_async_copy(
            ring_buf.at[2 + slot], score_ref.at[:, block_rows(block), :], out_sem.at[slot]
        )

    def ring_copies(block):
        slot = block % 4
        at = rows_at(block * rows, rows)
        return (
            pltpu.make_async_copy(score_ref.at[:, at, :], ring_buf.at[slot], ring_sem.at[slot, 0]),
            pltpu.make_async_copy(plane_ref.at[at, :], plane_buf.at[slot], ring_sem.at[slot, 1]),
            pltpu.make_async_copy(down_ref.at[at, :], down_buf.at[slot], ring_sem.at[slot, 2]),
        )

    def is_away(chunk):
        return chunk >= LOCAL_CHUNKS

    loads = {}
    for ref, away_ref, wide in (
        (expand_ref, expand_away_ref, True),
        (reduce_ref, reduce_away_ref, False),
    ):
        for k in range(2):
            piece = slice(k * CHUNK, (k + 1) * CHUNK)
            index = (slice(None), piece) if wide else (piece, slice(None))
            chunk = LOCAL_CHUNKS + len(loads)
            loads[chunk] = (
                pltpu.make_async_copy(ref.at[index], own_buf.at[chunk], load_sem.at[chunk, 0]),
                pltpu.make_async_copy(
                    away_ref.at[index], away_buf.at[chunk - LOCAL_CHUNKS], load_sem.at[chunk, 1]
                ),
            )

    for copy in loads[LOCAL_CHUNKS]:
        copy.start()
    for copy in residents[:2]:
        copy.start()
    for copy in block_copies(0, 0):
        copy.start()
    for copy in residents[2:6]:
        copy.start()
    for chunk in range(LOCAL_CHUNKS + 1, CHUNKS):
        for copy in loads[chunk]:
            copy.start()
    residents[6].start()
    for copy in residents[7:]:
        copy.start()

    keeps, leaves = [], []
    for bits in BITS:
        kept, left, base = [], [], 0
        for size, bit in zip(PARTS, bits):
            kept.append(base + side_of[bit] * size)
            left.append(base + (1 - side_of[bit]) * size)
            base = base + side_of[bit] * size
        keeps.append(kept)
        leaves.append(left)
    arrivals = (core_buf, first_buf, second_buf, third_buf)
    away_arrivals = (core_away_buf, first_away_buf)

    def staged(src, dst, chunk, stage, device):
        return remote(src, dst, send_sem.at[chunk, stage], recv_sem.at[chunk, stage], device)

    def scatter(chunk, level):
        return staged(
            own_buf.at[chunk, rows_at(leaves[chunk][level], PARTS[level]), :],
            arrivals[level].at[chunk],
            chunk,
            level,
            partner_of[BITS[chunk][level]],
        )

    def scatter_away(chunk, level):
        return staged(
            away_buf.at[chunk - LOCAL_CHUNKS, rows_at(leaves[chunk][level], PARTS[level]), :],
            away_arrivals[level].at[chunk - LOCAL_CHUNKS],
            chunk,
            4 + level,
            partner_of[BITS[chunk][level]],
        )

    def hand_over(chunk):
        return staged(
            away_buf.at[chunk - LOCAL_CHUNKS, rows_at(keeps[chunk][1], PARTS[1]), :],
            y_buf.at[chunk - LOCAL_CHUNKS],
            chunk,
            6,
            across_mp,
        )

    def total_rows(chunk, start, size):
        return total_ref.at[rows_at(chunk * CHUNK + start, size), :]

    def gather(chunk, level):
        kept, size = keeps[chunk][level], PARTS[level]
        if level == 3:
            src = own_buf.at[chunk, rows_at(kept, size), :]
        else:
            src = total_rows(chunk, kept, size)
        return staged(
            src, total_rows(chunk, kept, size), chunk, 7 + level, partner_of[BITS[chunk][level]]
        )

    def gathered(chunk, level):
        region = total_rows(chunk, leaves[chunk][level], PARTS[level])
        return staged(region, region, chunk, 7 + level, partner_of[BITS[chunk][level]])

    def store_own(chunk):
        return pltpu.make_async_copy(
            own_buf.at[chunk, rows_at(keeps[chunk][3], PARTS[3]), :],
            total_rows(chunk, keeps[chunk][3], PARTS[3]),
            local_sem.at[chunk],
        )

    def add(buf, chunk, start, size, arrived):
        piece = PARTS[3]

        def step(n, carry):
            here = rows_at(start + n * piece, piece)
            there = rows_at(n * piece, piece)
            buf[chunk, here, :] = buf[chunk, here, :] + arrived[there, :]
            return carry

        lax.fori_loop(0, size // piece, step, 0)

    def add_level(chunk, level):
        scatter(chunk, level).wait_recv()
        add(own_buf, chunk, keeps[chunk][level], PARTS[level], arrivals[level].at[chunk])

    def add_level_away(chunk, level):
        at = chunk - LOCAL_CHUNKS
        scatter_away(chunk, level).wait_recv()
        add(away_buf, at, keeps[chunk][level], PARTS[level], away_arrivals[level].at[at])

    def exchange(event, chunk):
        away = is_away(chunk)
        if event == 0:
            if away:
                for copy in loads[chunk]:
                    copy.wait()
                scatter_away(chunk, 0).start()
            scatter(chunk, 0).start()
            return
        if event == 1:
            if away:
                add_level_away(chunk, 0)
                scatter_away(chunk, 1).start()
            add_level(chunk, 0)
            scatter(chunk, 1).start()
            return
        if away and event == 2:
            add_level_away(chunk, 1)
            hand_over(chunk).start()
            add_level(chunk, 1)
            return
        if away:
            event -= 1
            if event == 2:
                hand_over(chunk).wait_recv()
                add(own_buf, chunk, keeps[chunk][1], PARTS[1], y_buf.at[chunk - LOCAL_CHUNKS])
        elif event == 2:
            add_level(chunk, 1)
        if event == 2:
            scatter(chunk, 2).start()
        elif event == 3:
            add_level(chunk, 2)
            scatter(chunk, 3).start()
        elif event == 4:
            add_level(chunk, 3)
            store_own(chunk).start()
            gather(chunk, 3).start()
        else:
            level = 8 - event
            if level == 3:
                store_own(chunk).wait()
            gathered(chunk, level).wait_recv()
            if level > 0:
                gather(chunk, level - 1).start()

    small_devices = (across_mp, *partner_of.values())

    def small_hop(n):
        return remote(
            small_buf.at[n],
            small_recv_buf.at[n],
            small_send_sem.at[n],
            small_recv_sem.at[n],
            small_devices[n],
        )

    def small_step(n):
        if n == 0:
            residents[6].wait()
        else:
            small_hop(n - 1).wait_recv()
            small_buf[n] = small_buf[n - 1] + small_recv_buf[n - 1]
        if n < 5:
            small_hop(n).start()
        else:
            small_out_ref[...] = small_buf[n]

    def input_rows(side):
        return mine if side == 0 else others

    def input_product(side, target):
        at = input_rows(side)
        part = None
        for k in range(3):
            product = lax.dot_general(
                triple_buf[k, at, :],
                project_buf[k, rows_at(target * width, width), :],
                (((1,), (1,)), ((), ())),
                preferred_element_type=f32,
            )
            part = product if part is None else part + product
        if side == 0:
            cols = pl.ds(pl.multiple_of(target * width, LANES), width)
            part = part + grad_buf[0, :, cols].astype(f32)
        return part

    def input_store(side):
        return pltpu.make_async_copy(
            input_buf.at[side], input_ref.at[input_rows(side), :], out_sem.at[3 + side]
        )

    def run(event, which):
        if event == "small":
            small_step(which)
        elif event == "send":
            input_swap.start()
        elif event == "layer":
            layer_swap.start()
            layer_keep.start()
        elif event == "input":
            input_swap.wait_recv()
            for side in range(2):
                part = input_product(side, mp_index)
                input_buf[side] = part + input_recv_buf[input_rows(side), :].astype(f32)
                input_store(side).start()
        else:
            exchange(event, which)

    pairs = heads // 2
    block_slots = plan_slots("b", blocks * pairs)
    part_slots = plan_slots("p", 4)
    turn_slots = plan_slots("t", turns)
    rest = plan_slots("e", 1)[0]

    def run_all(steps):
        for event, which in steps:
            run(event, which)

    def dispatch(slots, n, low, high):
        if not any(slots[low:high]):
            return
        if high - low == 1:
            for event, which in slots[low]:
                run(event, which)
            return
        middle = (low + high) // 2
        if any(slots[low:middle]):
            pl.when(n < middle)(lambda: dispatch(slots, n, low, middle))
        if any(slots[middle:high]):
            pl.when(n >= middle)(lambda: dispatch(slots, n, middle, high))

    grad_key_buf[...] = jnp.zeros_like(grad_key_buf)
    grad_value_buf[...] = jnp.zeros_like(grad_value_buf)
    sum_ref[...] = jnp.zeros_like(sum_ref)
    for copy in residents[:6]:
        copy.wait()
    first = lax.broadcasted_iota(jnp.int32, (rows, LANES), 1) < HEAD

    def back(block, carry):
        slot = block % 2
        at = block_rows(block)
        for copy in block_copies(block, slot):
            copy.wait()

        @pl.when(block + 1 < blocks)
        def _():
            for copy in block_copies(block + 1, 1 - slot):
                copy.start()

        pl.when(block == blocks // 2)(grad_swap.wait_recv)
        pl.when(block >= 2)(lambda: score_copy(block - 2, slot).wait())
        side = block // (blocks // 2)
        local = rows_at((block % (blocks // 2)) * rows, rows)
        grad_context = lax.dot_general(
            grad_buf[side, local, :],
            output_buf[...],
            (((1,), (1,)), ((), ())),
            preferred_element_type=f32,
        )
        scaled = (grad_context * inverse_buf[slot]).astype(bf16)
        for p in range(pairs):
            dispatch(block_slots, block * pairs + p, 0, blocks * pairs)
            cols = slice(p * LANES, (p + 1) * LANES)
            grad = scaled[:, cols]
            product = grad.astype(f32) * context_buf[at, cols].astype(f32)
            query_turned = query_buf[at, cols].T
            grad_turned = grad.T
            grad_query = None
            for u in range(2):
                h = 2 * p + u
                half = slice(u * HEAD, (u + 1) * HEAD)
                own = first if u == 0 else ~first
                total = jnp.sum(jnp.where(own, product, 0.0), axis=1, keepdims=True)
                exps = ring_buf[slot, h]
                grad_exp = dot_f32(grad, value_buf[h])
                grad_score = (exps.astype(f32) * (grad_exp - total)).astype(bf16)
                ring_buf[2 + slot, h] = grad_score
                part = dot_f32(grad_score, key_buf[h])
                grad_query = part if u == 0 else grad_query + part
                grad_key_buf[h] += dot_f32(query_turned[half], grad_score)
                grad_value_buf[h] += dot_f32(grad_turned[half], exps)
            triple_buf[0, at, cols] = (grad_query * 0.125).astype(bf16)
        score_copy(block, slot).start()
        return carry

    lax.fori_loop(0, blocks, back, 0)

    score_copy(blocks - 2, blocks % 2).wait()
    score_copy(blocks - 1, (blocks - 1) % 2).wait()
    for block in range(2):
        for copy in ring_copies(block):
            copy.start()
    run_all(part_slots[0])
    triple_buf[0, row_count:keys, :] = jnp.zeros((keys - row_count, width), bf16)
    for k, ref in ((1, grad_key_buf), (2, grad_value_buf)):
        for h in range(0, heads, 2):
            pair = ref[h : h + 2].reshape(LANES, keys)
            triple_buf[k, :, h * HEAD : (h + 2) * HEAD] = pair.T.astype(bf16)
    run_all(part_slots[1])
    for copy in residents[7:]:
        copy.wait()
    tokens_in = (((0,), (0,)), ((), ()))
    places = ((0, 0), (0, width), (1, 0))
    for k, (chunk, start) in enumerate(places):
        own_buf[chunk, start : start + width, :] = lax.dot_general(
            triple_buf[k], token_buf[...], tokens_in, preferred_element_type=f32
        ).astype(bf16)
    run_all(part_slots[2])
    own_buf[1, width : 2 * width, :] = (
        lax.dot_general(
            context_buf[mine, :], grad_buf[0], tokens_in, preferred_element_type=f32
        )
        + lax.dot_general(
            context_buf[others, :], grad_buf[1], tokens_in, preferred_element_type=f32
        )
    ).astype(bf16)
    run_all(part_slots[3])
    for side in range(2):
        input_send_buf[input_rows(side), :] = input_product(side, 1 - mp_index).astype(bf16)
    biases = jnp.concatenate(
        [
            jnp.sum(triple_buf[0].astype(f32), axis=0, keepdims=True),
            jnp.sum(triple_buf[2].astype(f32), axis=0, keepdims=True),
        ],
        axis=1,
    )

    def turn(n, carry):
        last = n * TABLE_STRIPS + TABLE_STRIPS - 1
        block = last // block_strips

        @pl.when(last % block_strips < TABLE_STRIPS)
        def _():
            for copy in ring_copies(block):
                copy.wait()

            @pl.when(block + 2 < blocks)
            def _():
                for copy in ring_copies(block + 2):
                    copy.start()

        dispatch(turn_slots, n, 0, turns)

        def refs_at(strip):
            slot = (strip // block_strips) % 4
            at = rows_at((strip % block_strips) * STRIP, STRIP)
            return (
                lambda h, cols: ring_buf[slot, h, at, cols],
                lambda cols: plane_buf[slot, at, cols],
                lambda cols: down_buf[slot, at, cols],
            )

        table_strips(
            [refs_at(n * TABLE_STRIPS + k) for k in range(TABLE_STRIPS)],
            sum_ref,
            heads,
            keys,
            high_counts,
        )
        return carry

    lax.fori_loop(0, turns, turn, 0)

    table_rows = sum(high_counts) * heads
    table_finish(sum_ref, table_buf.at[0], table_rows)
    lanes = table_buf.shape[2]
    pieces = 2 * width // lanes
    for n in range(pieces):
        table_buf[0, table_rows + n : table_rows + n + 1, :] = biases[:, n * lanes : (n + 1) * lanes]
    spare = table_buf.shape[1] - table_rows - pieces
    table_buf[0, table_rows + pieces :, :] = jnp.zeros((spare, lanes), f32)
    groups = ((1, 2), (4, 8))

    def table_hop(n, d):
        bits = [bit for k, bit in enumerate(groups[n]) if d >> k & 1]
        return remote(
            table_buf.at[n],
            table_recv_buf.at[n, d],
            table_send_sem.at[n, d],
            table_recv_sem.at[n, d],
            by_bits(*bits),
        )

    def table_step(n):
        if n > 0:
            for d in range(1, 4):
                table_hop(n - 1, d).wait_recv()
            table_recv_buf[n - 1, 0] = table_buf[n - 1]
            low, high = (side_of[bit] for bit in groups[n - 1])
            total = None
            for member in range(4):
                d = (low + member % 2) % 2 + 2 * ((high + member // 2) % 2)
                part = table_recv_buf[n - 1, d]
                total = part if member == 0 else total + part
            table_buf[n] = total
        if n < 2:
            for d in range(1, 4):
                table_hop(n, d).start()

    table_step(0)
    for n, (event, which) in enumerate(rest):
        if n in (3, 7):
            table_step(n // 3)
        run(event, which)
    for n in range(1, 3):
        if len(rest) <= 4 * n - 1:
            table_step(n)
    table_ref[...] = table_buf[2]

    layer_arrival.wait_recv()
    layer_keep.wait()
    grad_swap.wait_send()
    input_swap.wait_send()
    layer_swap.wait_send()
    for side in range(2):
        input_store(side).wait()
    for n in range(5):
        small_hop(n).wait_send()
    for n in range(2):
        for d in range(1, 4):
            table_hop(n, d).wait_send()
    for chunk in range(CHUNKS):
        for level in range(4):
            scatter(chunk, level).wait_send()
            gather(chunk, level).wait_send()
        if is_away(chunk):
            scatter_away(chunk, 0).wait_send()
            scatter_away(chunk, 1).wait_send()
            hand_over(chunk).wait_send()


def finish(
    exps,
    inverse,
    plane,
    down,
    context,
    query,
    tokens,
    grad,
    layer,
    value_turned,
    key_wide,
    project_weight,
    output_weight,
    expand,
    reduce,
    small,
    counts,
):
    heads, row_count, keys = exps.shape
    width = heads * HEAD
    depth = tokens.shape[1]
    half_rows = row_count // 2
    high_counts = (counts[0] // 16, counts[1] // 16, counts[1] // 16)
    high_rows = sum(high_counts) * heads
    low_lanes = 16 * STRIP
    table_shape = (round_up(high_rows + 2 * width // low_lanes, 8), low_lanes)
    away = CHUNKS - LOCAL_CHUNKS
    anywhere = pl.BlockSpec(memory_space=pl.ANY)
    in_vmem = pl.BlockSpec(memory_space=pltpu.VMEM)
    dma = pltpu.SemaphoreType.DMA
    total, layer_full, input_full, small_sum, table_sum, _ = pl.pallas_call(
        partial(finish_kernel, high_counts=high_counts),
        in_specs=[anywhere] * 18,
        out_specs=[anywhere, anywhere, anywhere, in_vmem, in_vmem, anywhere],
        out_shape=[
            jax.ShapeDtypeStruct((CHUNKS * CHUNK, CHUNK), bf16),
            jax.ShapeDtypeStruct((row_count, depth), bf16),
            jax.ShapeDtypeStruct((row_count, width), f32),
            jax.ShapeDtypeStruct(small.shape, f32),
            jax.ShapeDtypeStruct(table_shape, f32),
            jax.ShapeDtypeStruct(exps.shape, bf16),
        ],
        scratch_shapes=[
            pltpu.VMEM(output_weight.shape, bf16),
            pltpu.VMEM((2, half_rows, depth), bf16),
            pltpu.VMEM(value_turned.shape, bf16),
            pltpu.VMEM(key_wide.shape, bf16),
            pltpu.VMEM(context.shape, bf16),
            pltpu.VMEM(query.shape, bf16),
            pltpu.VMEM(tokens.shape, bf16),
            pltpu.VMEM(project_weight.shape, bf16),
            pltpu.VMEM((4, heads, BACK_ROWS, keys), bf16),
            pltpu.VMEM((2, BACK_ROWS, width), f32),
            pltpu.VMEM((heads, HEAD, keys), f32),
            pltpu.VMEM((heads, HEAD, keys), f32),
            pltpu.VMEM((3, keys, width), bf16),
            pltpu.VMEM((row_count, width), bf16),
            pltpu.VMEM((row_count, width), bf16),
            pltpu.VMEM((2, half_rows, width), f32),
            pltpu.VMEM((4, BACK_ROWS, keys), jnp.int16),
            pltpu.VMEM((4, BACK_ROWS, keys), jnp.int16),
            pltpu.VMEM((high_rows * STRIP, low_lanes), f32),
            pltpu.VMEM((CHUNKS, CHUNK, CHUNK), bf16),
            pltpu.VMEM((away, CHUNK, CHUNK), bf16),
            pltpu.VMEM((CHUNKS, PARTS[0], CHUNK), bf16),
            pltpu.VMEM((away, PARTS[0], CHUNK), bf16),
            pltpu.VMEM((CHUNKS, PARTS[1], CHUNK), bf16),
            pltpu.VMEM((away, PARTS[1], CHUNK), bf16),
            pltpu.VMEM((away, PARTS[1], CHUNK), bf16),
            pltpu.VMEM((CHUNKS, PARTS[2], CHUNK), bf16),
            pltpu.VMEM((CHUNKS, PARTS[3], CHUNK), bf16),
            pltpu.VMEM((6, *small.shape), f32),
            pltpu.VMEM((5, *small.shape), f32),
            pltpu.VMEM((3, *table_shape), f32),
            pltpu.VMEM((2, 4, *table_shape), f32),
            dma((9,)),
            dma((2, 2)),
            dma((4, 3)),
            dma((CHUNKS, 2)),
            dma((CHUNKS,)),
            dma((5,)),
            dma((CHUNKS, 11)),
            dma((CHUNKS, 11)),
            dma((3,)),
            dma((3,)),
            dma((5,)),
            dma((5,)),
            dma((2, 4)),
            dma((2, 4)),
        ],
        compiler_params=pltpu.CompilerParams(
            vmem_limit_bytes=FINISH_VMEM, collective_id=0, has_side_effects=True
        ),
        name="finish",
    )(
        exps,
        inverse,
        plane,
        down,
        context,
        query,
        tokens,
        grad,
        layer,
        value_turned,
        key_wide,
        project_weight,
        output_weight,
        *expand,
        *reduce,
        small,
    )
    return total, layer_full, input_full, table_sum, small_sum


UNPACK_ROWS = 192


def unpack_kernel(
    total_ref,
    layer_in_ref,
    input_in_ref,
    sum_ref,
    small_ref,
    layer_ref,
    input_ref,
    project_ref,
    output_ref,
    expand_ref,
    reduce_ref,
    line_ref,
    across_ref,
    down_ref,
    bias_ref,
    second_gain_ref,
    second_shift_ref,
    reduce_bias_ref,
    first_gain_ref,
    first_shift_ref,
    output_bias_ref,
    expand_bias_ref,
    *,
    high_counts,
):
    step = pl.program_id(0)
    layer_ref[...] = layer_in_ref[...]
    input_ref[...] = input_in_ref[...].reshape(input_ref.shape)
    values = total_ref[...].astype(f32)

    half = values.shape[0] // 2

    @pl.when(step < 2)
    def _():
        project_ref[0] = values[:half].T

    @pl.when(step == 0)
    def _():
        project_ref[1] = values[half:].T

    @pl.when(step == 1)
    def _():
        output_ref[...] = values[half:]

    @pl.when((step >= 2) & (step < 4))
    def _():
        expand_ref[...] = values

    @pl.when(step >= 4)
    def _():
        reduce_ref[...] = values

    @pl.when(step == 0)
    def _():
        lanes = sum_ref.shape[1]
        row = lax.broadcasted_iota(jnp.int32, (lanes, LANES), 0) // STRIP
        same = row == lax.broadcasted_iota(jnp.int32, (lanes, LANES), 1)
        folded = jnp.dot(
            sum_ref[...],
            jnp.where(same, 1.0, 0.0),
            precision=lax.Precision.HIGHEST,
            preferred_element_type=f32,
        )
        heads = line_ref.shape[0]
        start = 0
        for ref, count in zip((line_ref, across_ref, down_ref), high_counts):
            parts = []
            for _ in range(count):
                parts.append(folded[start : start + heads, : lanes // STRIP])
                start += heads
            ref[...] = jnp.concatenate(parts, axis=1)
        half = bias_ref.shape[1] - lanes
        middle = sum_ref[start + 1 : start + 2, :]
        bias_ref[0:1, :] = jnp.concatenate([sum_ref[start : start + 1, :], middle[:, :half]], axis=1)
        bias_ref[1:2, :] = jnp.concatenate([middle[:, half:], sum_ref[start + 2 : start + 3, :]], axis=1)
        lead = lax.axis_index("mp") == 0
        for n, ref in enumerate(
            (
                second_gain_ref,
                second_shift_ref,
                reduce_bias_ref,
                first_gain_ref,
                first_shift_ref,
                output_bias_ref,
            )
        ):
            row = small_ref[n : n + 1, :]
            if ref.shape[0] < row.shape[1]:
                cut = ref.shape[0]
                row = jnp.where(lead, row[:, :cut], row[:, cut:])
            ref[...] = row.reshape(ref.shape)
        pieces = expand_bias_ref.shape[0] // small_ref.shape[1]
        width = small_ref.shape[1]
        for k in range(pieces):
            even = small_ref[8 + k : 9 + k, :]
            odd = small_ref[8 + pieces + k : 9 + pieces + k, :]
            expand_bias_ref[k * width : (k + 1) * width] = jnp.where(lead, even, odd).reshape(width)


def unpack(total, layer, inputs, sums, small, length, heads, counts):
    width = inputs.shape[1]
    depth = layer.shape[1]
    high_counts = (counts[0] // 16, counts[1] // 16, counts[1] // 16)

    def whole(shape):
        return pl.BlockSpec(shape, lambda i: (0,) * len(shape))

    def rows(columns):
        return pl.BlockSpec((UNPACK_ROWS, columns), lambda i: (i, 0))

    shapes = [
        ((length, depth), bf16),
        ((length, 1, width), f32),
        ((3, depth, width), f32),
        ((width, depth), f32),
        ((CHUNK, 2 * CHUNK), f32),
        ((2 * CHUNK, CHUNK), f32),
        ((heads, counts[0]), f32),
        ((heads, counts[1]), f32),
        ((heads, counts[1]), f32),
        ((2, width), f32),
        ((depth,), f32),
        ((depth,), f32),
        ((depth,), f32),
        ((width,), f32),
        ((width,), f32),
        ((depth,), f32),
        ((2 * CHUNK,), f32),
    ]
    return pl.pallas_call(
        partial(unpack_kernel, high_counts=high_counts),
        grid=(CHUNKS,),
        in_specs=[
            pl.BlockSpec((CHUNK, CHUNK), lambda i: (i, 0)),
            rows(depth),
            rows(width),
            whole(sums.shape),
            whole(small.shape),
        ],
        out_specs=[
            rows(depth),
            pl.BlockSpec((UNPACK_ROWS, 1, width), lambda i: (i, 0, 0)),
            pl.BlockSpec((2, depth, width), lambda i: (jnp.minimum(i, 1), 0, 0)),
            whole((width, depth)),
            pl.BlockSpec((CHUNK, CHUNK), lambda i: (0, jnp.clip(i - 2, 0, 1))),
            pl.BlockSpec((CHUNK, CHUNK), lambda i: (jnp.clip(i - 4, 0, 1), 0)),
            *(whole(shape) for shape, _ in shapes[6:]),
        ],
        out_shape=[jax.ShapeDtypeStruct(shape, kind) for shape, kind in shapes],
        compiler_params=pltpu.CompilerParams(vmem_limit_bytes=vmem_limit),
        name="unpack",
    )(total, layer, inputs, sums, small)


def feed_kernel(
    context_ref,
    context_away_ref,
    token_ref,
    cotangent_ref,
    valid_ref,
    output_ref,
    output_away_ref,
    expand_ref,
    expand_away_ref,
    reduce_ref,
    reduce_away_ref,
    expand_bias_ref,
    expand_bias_away_ref,
    output_bias_ref,
    first_gain_ref,
    first_shift_ref,
    reduce_bias_ref,
    second_gain_ref,
    second_shift_ref,
    layer_ref,
    grad_ref,
    expand_grad_ref,
    expand_grad_away_ref,
    reduce_grad_ref,
    reduce_grad_away_ref,
    small_ref,
    input_buf,
    norm_buf,
    hat_buf,
    inverse_buf,
    total_buf,
    reduced_buf,
    active_buf,
    slope_buf,
    before_buf,
    vector_ref,
    bias_buf,
    *,
    pieces,
    tiles,
):
    rows, width = token_ref.shape
    step = pl.program_id(0)
    piece = step % (2 * pieces)
    strip_rows = FEED_STRIP
    strips = rows // strip_rows

    def vector(n):
        return vector_ref[n : n + 1, :]

    def for_strips(body, sums):
        def run(n, carry):
            at = pl.ds(pl.multiple_of(n * strip_rows, STRIP), strip_rows)
            return tuple(
                old + jnp.sum(new.reshape(strip_rows // 8, 8, width), axis=0)
                for old, new in zip(carry, body(at))
            )

        start = tuple(jnp.zeros((8, width), f32) for _ in range(sums))
        done = lax.fori_loop(0, strips, run, start)
        return [jnp.sum(part, axis=0, keepdims=True) for part in done]

    def mean(values):
        return jnp.sum(values, axis=-1, keepdims=True) * (1.0 / width)

    @pl.when(step == 0)
    def _():
        small_ref[...] = jnp.zeros_like(small_ref)
        for n, ref in enumerate(
            (
                output_bias_ref,
                first_gain_ref,
                first_shift_ref,
                reduce_bias_ref,
                second_gain_ref,
                second_shift_ref,
            )
        ):
            vector_ref[n : n + 1, :] = ref[...].astype(f32).reshape(1, width)
        bias = expand_bias_ref[...].astype(f32).reshape(1, -1)
        for k in range(pieces):
            cols = slice(k * expand_ref.shape[1], (k + 1) * expand_ref.shape[1])
            bias_buf[k : k + 1, :] = bias[:, cols]
            bias_buf[pieces + k : pieces + k + 1, :] = expand_bias_away_ref[0:1, cols]
        total_buf[...] = dot_f32(context_ref[...], output_ref[...]) + dot_f32(
            context_away_ref[...], output_away_ref[...]
        )

        def body(at):
            values = token_ref[at, :].astype(f32) + (total_buf[at, :] + vector(0))
            centered = values - mean(values)
            inverse = lax.rsqrt(mean(centered * centered) + norm_epsilon)
            hat = centered * inverse
            norm = hat * vector(1) + vector(2)
            hat_buf[at, :] = hat
            inverse_buf[at, :] = jnp.broadcast_to(inverse, (strip_rows, LANES))
            norm_buf[at, :] = norm
            input_buf[at, :] = norm.astype(bf16)
            total_buf[at, :] = norm + vector(3)
            return ()

        for_strips(body, 0)

    def forward(expand, reduce):
        for start, size in tiles:
            at = slice(start, start + size)
            before = dot_f32(input_buf[at, :], expand[...]) + bias_buf[pl.ds(piece, 1), :]
            phi = 0.5 * lax.erf(before * 0.7071067811865476) + 0.5
            slope_buf[piece, at, :] = phi + before * (
                0.3989422804014327 * jnp.exp(-0.5 * (before * before))
            )
            active = (before * phi).astype(bf16)
            active_buf[piece, at, :] = active
            total_buf[at, :] += dot_f32(active, reduce[...])

    pl.when(step < pieces)(lambda: forward(expand_ref, reduce_ref))
    pl.when((step >= pieces) & (step < 2 * pieces))(
        lambda: forward(expand_away_ref, reduce_away_ref)
    )

    @pl.when(step == 2 * pieces)
    def _():
        def body(at):
            values = total_buf[at, :]
            valid = valid_ref[at, 0:1]
            centered = values - mean(values)
            inverse = lax.rsqrt(mean(centered * centered) + norm_epsilon)
            hat = centered * inverse
            layer_ref[at, :] = (valid * (hat * vector(4) + vector(5))).astype(bf16)
            grad_out = jnp.where(valid > 0, cotangent_ref[at, :].astype(f32), 0.0)
            grad_hat = grad_out * vector(4)
            mixed = inverse * (grad_hat - mean(grad_hat) - hat * mean(grad_hat * hat))
            low = mixed.astype(bf16)
            reduced_buf[at, :] = low
            total_buf[at, :] = mixed
            return grad_out * hat, grad_out, low.astype(f32)

        for n, part in enumerate(for_strips(body, 3)):
            small_ref[n : n + 1, :] = part

    def backward(expand, reduce):
        sums = None
        for start, size in tiles:
            at = slice(start, start + size)
            grad_active = lax.dot_general(
                reduced_buf[at, :], reduce[...], (((1,), (1,)), ((), ())), preferred_element_type=f32
            )
            before = (grad_active * slope_buf[piece, at, :]).astype(bf16)
            before_buf[piece, at, :] = before
            part = jnp.sum(before.astype(f32), axis=0, keepdims=True)
            sums = part if sums is None else sums + part
            total_buf[at, :] += lax.dot_general(
                before, expand[...], (((1,), (1,)), ((), ())), preferred_element_type=f32
            )
        mp_index = lax.axis_index("mp")
        side = jnp.where(piece < pieces, mp_index, 1 - mp_index)
        small_ref[pl.ds(8 + side * pieces + lax.rem(piece, pieces), 1), :] = sums

    pl.when((step >= 2 * pieces) & (step < 3 * pieces))(lambda: backward(expand_ref, reduce_ref))
    pl.when((step >= 3 * pieces) & (step < 4 * pieces))(
        lambda: backward(expand_away_ref, reduce_away_ref)
    )

    @pl.when(step == 4 * pieces)
    def _():
        def body(at):
            grad_first = total_buf[at, :]
            hat = hat_buf[at, :]
            grad_hat = grad_first * vector(1)
            inverse = inverse_buf[at, 0:1]
            inner = inverse * (grad_hat - mean(grad_hat) - hat * mean(grad_hat * hat))
            low = inner.astype(bf16)
            grad_ref[at, :] = low
            return grad_first * hat, grad_first, low.astype(f32)

        for n, part in enumerate(for_strips(body, 3)):
            small_ref[n + 3 : n + 4, :] = part

    def weights(expand_grad, reduce_grad):
        reduce_grad[...] = lax.dot_general(
            active_buf[piece], reduced_buf[...], (((0,), (0,)), ((), ())), preferred_element_type=f32
        ).astype(bf16)
        expand_grad[...] = lax.dot_general(
            input_buf[...], before_buf[piece], (((0,), (0,)), ((), ())), preferred_element_type=f32
        ).astype(bf16)

    pl.when((step >= 4 * pieces) & (step < 5 * pieces))(
        lambda: weights(expand_grad_ref, reduce_grad_ref)
    )
    pl.when(step >= 5 * pieces)(lambda: weights(expand_grad_away_ref, reduce_grad_away_ref))


def feed(
    context,
    context_away,
    tokens,
    cotangent,
    valid,
    output,
    output_away,
    expand,
    expand_away,
    reduce,
    reduce_away,
    expand_bias,
    expand_bias_away,
    vectors,
):
    rows, width = context_away.shape[0], tokens.shape[1]
    hidden = expand.shape[1]
    size = FEED_PIECE
    pieces = hidden // size
    split = round_up(rows // 2, STRIP)
    tiles = ((0, split), (split, rows - split))

    def once(array):
        zeros = (0,) * array.ndim
        return pl.BlockSpec(array.shape, lambda i: zeros, pipeline_mode=pl.Buffered(1))

    def mine(array):
        return pl.BlockSpec(
            (rows, array.shape[1]),
            lambda i: (lax.axis_index("mp"), 0),
            pipeline_mode=pl.Buffered(1),
        )

    def place(first, i):
        at = lax.rem(i, 2 * pieces) - first
        at = jnp.clip(at, 0, pieces - 1)
        return jnp.where(i < 4 * pieces, at, pieces - 1)

    def grad_place(first, i):
        return jnp.clip(i - 4 * pieces - first, 0, pieces - 1)

    wide = lambda first: pl.BlockSpec((width, size), lambda i: (0, place(first, i)))
    tall = lambda first: pl.BlockSpec((size, width), lambda i: (place(first, i), 0))
    wide_grad = lambda first: pl.BlockSpec((width, size), lambda i: (0, grad_place(first, i)))
    tall_grad = lambda first: pl.BlockSpec((size, width), lambda i: (grad_place(first, i), 0))
    whole = lambda shape: pl.BlockSpec(
        shape, lambda i: (0,) * len(shape), pipeline_mode=pl.Buffered(1)
    )
    full = jax.ShapeDtypeStruct((rows, width), bf16)
    return pl.pallas_call(
        partial(feed_kernel, pieces=pieces, tiles=tiles),
        grid=(6 * pieces,),
        in_specs=[
            mine(context),
            once(context_away),
            mine(tokens),
            mine(cotangent),
            mine(valid),
            once(output),
            once(output_away),
            wide(0),
            wide(pieces),
            tall(0),
            tall(pieces),
            once(expand_bias),
            once(expand_bias_away),
            *(once(vector) for vector in vectors),
        ],
        out_specs=[
            whole((rows, width)),
            whole((rows, width)),
            wide_grad(0),
            wide_grad(pieces),
            tall_grad(0),
            tall_grad(pieces),
            whole((16, width)),
        ],
        out_shape=[
            full,
            full,
            jax.ShapeDtypeStruct((width, hidden), bf16),
            jax.ShapeDtypeStruct((width, hidden), bf16),
            jax.ShapeDtypeStruct((hidden, width), bf16),
            jax.ShapeDtypeStruct((hidden, width), bf16),
            jax.ShapeDtypeStruct((16, width), f32),
        ],
        scratch_shapes=[
            pltpu.VMEM((rows, width), bf16),
            pltpu.VMEM((rows, width), f32),
            pltpu.VMEM((rows, width), f32),
            pltpu.VMEM((rows, LANES), f32),
            pltpu.VMEM((rows, width), f32),
            pltpu.VMEM((rows, width), bf16),
            pltpu.VMEM((2 * pieces, rows, size), bf16),
            pltpu.VMEM((2 * pieces, rows, size), f32),
            pltpu.VMEM((2 * pieces, rows, size), bf16),
            pltpu.VMEM((8, width), f32),
            pltpu.VMEM((2 * pieces, size), f32),
        ],
        compiler_params=pltpu.CompilerParams(vmem_limit_bytes=vmem_limit),
        name="feed",
    )(
        context,
        context_away,
        tokens,
        cotangent,
        valid,
        output,
        output_away,
        expand,
        expand_away,
        reduce,
        reduce_away,
        expand_bias,
        expand_bias_away,
        *vectors,
    )


def swap(array):
    return lax.ppermute(array, "mp", [(0, 1), (1, 0)])


def partner(array, count, bit):
    return lax.ppermute(array, "dp", [(i, i ^ bit) for i in range(count)])


def sum_rows_over_dp(array, count):
    place = lax.axis_index("dp")
    bits = []
    bit = 1
    while bit < count:
        mine = (place // bit) % 2
        halves = array.reshape((2, array.shape[0] // 2) + array.shape[1:])
        sent = lax.dynamic_index_in_dim(halves, 1 - mine, 0, keepdims=False)
        kept = lax.dynamic_index_in_dim(halves, mine, 0, keepdims=False)
        array = kept + partner(sent, count, bit)
        bits.append(bit)
        bit *= 2
    for bit in reversed(bits):
        lead = (place // bit) % 2 == 0
        other = partner(array, count, bit)
        array = jnp.concatenate(
            [jnp.where(lead, array, other), jnp.where(lead, other, array)], axis=0
        )
    return array


def sum_small(arrays, count, over_mp):
    sizes = [a.size for a in arrays]
    total = sum(sizes)
    flat = jnp.concatenate([a.reshape(-1) for a in arrays])
    flat = jnp.pad(flat, (0, round_up(total, 1024) - total)).reshape(-1, LANES)
    if over_mp:
        flat = flat + swap(flat)
    bit = 1
    while bit < count:
        flat = flat + partner(flat, count, bit)
        bit *= 2
    flat = flat.reshape(-1)
    outs = []
    start = 0
    for array, size in zip(arrays, sizes):
        outs.append(flat[start : start + size].reshape(array.shape))
        start += size
    return outs


def per_device(
    dp_count,
    tokens,
    cotangent,
    long_flag,
    token_mask,
    bucket_line,
    bucket_across,
    bucket_down,
    project_weight,
    project_bias,
    table_line,
    table_across,
    table_down,
    output_weight,
    output_bias,
    first_gain,
    first_shift,
    expand_weight,
    expand_bias,
    reduce_weight,
    reduce_bias,
    second_gain,
    second_shift,
):
    length = tokens.shape[1]
    width = project_weight.shape[2]
    heads = table_line.shape[1]
    counts = (table_line.shape[0], table_across.shape[0])
    rows = round_up(length, BLOCK_ROWS)
    half_rows = rows // 2
    keys = round_up(length, 3 * LANES)
    mp_index = lax.axis_index("mp")
    lead = mp_index == 0

    def own_rows(array):
        return lax.dynamic_slice_in_dim(array, mp_index * half_rows, half_rows, 0)

    def in_order(mine, other):
        return jnp.where(lead, mine, other), jnp.where(lead, other, mine)


    (
        query,
        key_wide,
        key_turned,
        value_ones,
        value_turned,
        padded,
        plane,
        down,
        valid_rows,
        expand_quarter,
    ) = prepare(
        tokens[0],
        project_weight,
        project_bias,
        (bucket_line, bucket_across, bucket_down),
        long_flag,
        token_mask,
        expand_weight,
        rows,
        keys,
        counts[0],
    )
    (
        exps,
        context,
        inverse,
        context_away,
        expand_away,
        output_away,
        reduce_away,
        expand_bias_away,
    ) = attend(
        query,
        key_turned,
        value_ones,
        plane,
        down,
        (table_line.T, table_across.T, table_down.T),
        expand_bias,
        expand_quarter,
        output_weight,
        reduce_weight,
    )

    (
        layer_mine,
        grad_mine,
        expand_own,
        expand_sent,
        reduce_own,
        reduce_sent,
        small,
    ) = feed(
        context,
        context_away,
        padded,
        cotangent[0],
        valid_rows,
        output_weight,
        output_away,
        expand_weight,
        expand_away,
        reduce_weight,
        reduce_away,
        expand_bias,
        expand_bias_away,
        (output_bias, first_gain, first_shift, reduce_bias, second_gain, second_shift),
    )
    if dp_count == 16 and expand_own.shape == (CHUNK, 2 * CHUNK):
        total, layer_full, input_full, sums, small = finish(
            exps,
            inverse,
            plane,
            down,
            context,
            query,
            padded,
            grad_mine,
            layer_mine,
            value_turned,
            key_wide,
            project_weight,
            output_weight,
            (expand_own, expand_sent),
            (reduce_own, reduce_sent),
            small,
            counts,
        )
        (
            layer_out,
            input_grad,
            project_weight_grad,
            output_weight_grad,
            expand_weight_grad,
            reduce_weight_grad,
            line_grad,
            across_grad,
            down_grad,
            project_bias_grad,
            second_gain_grad,
            second_shift_grad,
            reduce_bias_grad,
            first_gain_grad,
            first_shift_grad,
            output_bias_grad,
            expand_bias_grad,
        ) = unpack(total, layer_full, input_full, sums, small, length, heads, counts)
        layer_out = layer_out[None]
        input_grad = input_grad.reshape(1, length, width)
        table_grads = (line_grad.T, across_grad.T, down_grad.T)
    else:
        layer_out = jnp.concatenate(in_order(layer_mine, swap(layer_mine)))[None, :length]
        grad_attended = jnp.concatenate(in_order(grad_mine, swap(grad_mine)))
        output_weight_grad = jnp.einsum(
            "le,lf->ef", context, grad_attended, preferred_element_type=f32
        ).astype(bf16)
        grad_context = jnp.einsum(
            "lf,ef->le", grad_attended, output_weight, preferred_element_type=f32
        )
        grad_scaled = (grad_context * inverse).astype(bf16)
        grad_scores, grad_query, grad_key, grad_value = attend_back(
            exps, grad_scaled, context, query, value_turned, key_wide
        )
        grad_key = grad_key.reshape(width, keys)[:, :rows].T.astype(bf16)
        grad_value = grad_value.reshape(width, keys)[:, :rows].T.astype(bf16)
        triple = jnp.stack([grad_query, grad_key, grad_value])
        project_weight_grad = jnp.einsum(
            "ld,kle->kde", padded[:rows], triple, preferred_element_type=f32
        ).astype(bf16)
        project_bias_grad = jnp.stack(
            [jnp.sum(grad_query, axis=0, dtype=f32), jnp.sum(grad_value, axis=0, dtype=f32)]
        )
        input_part = jnp.einsum("kle,kde->ld", triple, project_weight, preferred_element_type=f32)
        input_part = lax.dynamic_update_slice_in_dim(
            input_part,
            own_rows(input_part) + grad_mine.astype(f32),
            mp_index * half_rows,
            0,
        )
        sent = jnp.where(lead, input_part[:, width:], input_part[:, :width]).astype(bf16)
        own = jnp.where(lead, input_part[:, :width], input_part[:, width:])
        input_grad = (own + swap(sent).astype(f32))[None, :length]
        table_grads = table_sums(grad_scores, plane, down, counts)
        reduce_weight_grad = sum_rows_over_dp(reduce_own + swap(reduce_sent), dp_count)
        expand_weight_grad = sum_rows_over_dp(expand_own + swap(expand_sent), dp_count)
        output_weight_grad = sum_rows_over_dp(output_weight_grad, dp_count)
        project_weight_grad = sum_rows_over_dp(
            project_weight_grad.reshape(-1, width), dp_count
        ).reshape(project_weight.shape)
        (small,) = sum_small([small], dp_count, True)
        bias_rows = expand_bias.size // small.shape[1]
        bias_rows = lax.dynamic_slice_in_dim(small, 8 + mp_index * bias_rows, bias_rows, 0)
        expand_bias_grad = bias_rows.reshape(-1)
        (
            second_gain_grad,
            second_shift_grad,
            reduce_bias_grad,
            first_gain_grad,
            first_shift_grad,
            output_bias_grad,
        ) = (small[n] for n in range(6))
        first_gain_grad = lax.dynamic_slice_in_dim(first_gain_grad, mp_index * width, width, 0)
        first_shift_grad = lax.dynamic_slice_in_dim(first_shift_grad, mp_index * width, width, 0)
        table_grads, project_bias_grad = sum_small(
            [table_grads, project_bias_grad], dp_count, False
        )
        cuts = (counts[0], counts[0] + counts[1])
        table_grads = (
            table_grads[: cuts[0]],
            table_grads[cuts[0] : cuts[1]],
            table_grads[cuts[1] :],
        )
    return (
        layer_out,
        input_grad,
        project_weight_grad.astype(f32),
        project_bias_grad,
        *table_grads,
        output_weight_grad.astype(f32),
        output_bias_grad,
        first_gain_grad,
        first_shift_grad,
        expand_weight_grad.astype(f32),
        expand_bias_grad,
        reduce_weight_grad.astype(f32),
        reduce_bias_grad,
        second_gain_grad,
        second_shift_grad,
    )


def solution(mesh):
    placed = (
        P("dp", None, None),
        P("dp", None, None),
        P("dp"),
        P("dp", None),
        P("dp", None, None),
        P("dp", None, None),
        P("dp", None, None),
        P(None, None, "mp"),
        P(None, "mp"),
        P(None, "mp"),
        P(None, "mp"),
        P(None, "mp"),
        P("mp", None),
        P(),
        P(),
        P(),
        P(None, "mp"),
        P("mp"),
        P("mp", None),
        P(),
        P(),
        P(),
    )
    return jax.shard_map(
        partial(per_device, mesh.shape["dp"]),
        mesh=mesh,
        in_specs=placed,
        out_specs=(
            P("dp", None, None),
            P("dp", None, "mp"),
            P(None, None, "mp"),
            P(None, "mp"),
            P(None, "mp"),
            P(None, "mp"),
            P(None, "mp"),
            P("mp", None),
            P(),
            P("mp"),
            P("mp"),
            P(None, "mp"),
            P("mp"),
            P("mp", None),
            P(),
            P(),
            P(),
        ),
        check_vma=False,
    )
```

```python
from functools import partial

import jax
import jax.numpy as jnp
from jax import lax
from jax.experimental import pallas as pl
from jax.experimental.pallas import tpu as pltpu
from jax.sharding import PartitionSpec as P

LONG = 1089
SHORT = 709
HEAD = 64
LANES = 128
STRIP = 16
BLOCK_ROWS = 224
FEED_PIECE = 768
FEED_STRIP = 112
TABLE_STRIPS = 2
ATTEND_STRIPS = 7

large_negative = -1000000000.0
norm_epsilon = 1e-05
vmem_limit = 56 * 2**20
FINISH_VMEM = 62 * 2**20
bf16 = jnp.bfloat16
f32 = jnp.float32


def round_up(value, step):
    return (value + step - 1) // step * step


def whole_spec(array):
    zeros = (0,) * array.ndim
    return pl.BlockSpec(array.shape, lambda i: zeros)


def dot_f32(left, right):
    return jnp.dot(left, right, preferred_element_type=f32)


def gather_lanes(values, index):
    dims = lax.GatherDimensionNumbers(
        offset_dims=(),
        collapsed_slice_dims=(1,),
        start_index_map=(1,),
        operand_batching_dims=(0,),
        start_indices_batching_dims=(0,),
    )
    return lax.gather(
        values,
        index[..., None],
        dims,
        slice_sizes=(1, 1),
        mode=lax.GatherScatterMode.PROMISE_IN_BOUNDS,
    )


def quarter_rows(ref, quarter):
    count = ref.shape[0] // 4
    return pl.ds(pl.multiple_of(quarter * count, STRIP), count)


def prepare_kernel(
    token_ref,
    weight_ref,
    bias_ref,
    line_ref,
    across_ref,
    down_ref,
    flag_ref,
    mask_ref,
    expand_ref,
    query_ref,
    key_ref,
    key_turned_ref,
    value_ref,
    value_turned_ref,
    token_out_ref,
    plane_ref,
    down_out_ref,
    valid_ref,
    quarter_ref,
    row_ref,
    send_sem,
    recv_sem,
    *,
    length,
    line_count,
):
    step = pl.program_id(0)
    across_mp = {"mp": 1 - lax.axis_index("mp")}
    fetch = pltpu.make_async_remote_copy(
        src_ref=expand_ref.at[quarter_rows(expand_ref, lax.axis_index("dp") % 4), :],
        dst_ref=quarter_ref,
        send_sem=send_sem,
        recv_sem=recv_sem,
        device_id=across_mp,
        device_id_type=pl.DeviceIdType.MESH,
    )

    @pl.when(step == 0)
    def _():
        barrier = pltpu.get_barrier_semaphore()
        pl.semaphore_signal(
            barrier, inc=1, device_id=across_mp, device_id_type=pl.DeviceIdType.MESH
        )
        pl.semaphore_wait(barrier, 1)
        fetch.start()
        limit = jnp.where(flag_ref[0] > 0, LONG, SHORT)
        position = lax.broadcasted_iota(jnp.int32, (1, length), 1)
        row_ref[...] = jnp.zeros_like(row_ref)
        row_ref[0:1, :length] = jnp.where((mask_ref[...] > 0) & (position < limit), 1.0, 0.0)

    rows = token_ref.shape[0]
    keys = plane_ref.shape[1]
    place = pl.program_id(0) * rows + lax.broadcasted_iota(jnp.int32, token_ref.shape, 0)
    token = jnp.where(place < length, token_ref[...].astype(f32), 0.0).astype(bf16)
    token_out_ref[...] = token
    bias = bias_ref[...].astype(f32)
    query = (dot_f32(token, weight_ref[0]) + bias[0:1, :]).astype(bf16)
    query_ref[...] = (query.astype(f32) * 0.125).astype(bf16)
    key = dot_f32(token, weight_ref[1])
    value = dot_f32(token, weight_ref[2]) + bias[1:2, :]
    away = jnp.where(row_ref[0:1, :] > 0, 0, line_count)
    inside = pl.program_id(0) * rows + lax.broadcasted_iota(jnp.int32, (rows, length), 0) < length
    line = line_ref[...].reshape(rows, length)
    across = across_ref[...].reshape(rows, length)
    down = down_ref[...].reshape(rows, length)
    plane = jnp.where(inside, line | (across << 8), 0) | away[:, :length]
    plane_ref[:, :length] = plane.astype(jnp.int16)
    plane_ref[:, length:] = jnp.full((rows, keys - length), line_count, jnp.int16)
    here = pl.ds(pl.multiple_of(step * rows, LANES), rows)
    valid_ref[...] = jnp.broadcast_to(row_ref[0:1, here], (LANES, rows)).T
    down_out_ref[:, :length] = jnp.where(inside, down, 0).astype(jnp.int16)
    down_out_ref[:, length:] = jnp.zeros((rows, keys - length), jnp.int16)
    lane_first = lax.broadcasted_iota(jnp.int32, (rows, LANES), 1) < HEAD
    row_first = lax.broadcasted_iota(jnp.int32, (LANES, rows), 0) < HEAD
    for p in range(key.shape[1] // LANES):
        cols = slice(p * LANES, (p + 1) * LANES)
        key_pair, value_pair = key[:, cols], value[:, cols]
        key_turned, value_turned = key_pair.T, value_pair.T
        for u in range(2):
            h = 2 * p + u
            lane_own = lane_first if u == 0 else ~lane_first
            row_own = row_first if u == 0 else ~row_first
            key_ref[h] = jnp.where(lane_own, key_pair, 0.0).astype(bf16)
            value_ref[h] = jnp.where(lane_own, value_pair, 1.0).astype(bf16)
            key_turned_ref[h] = jnp.where(row_own, key_turned, 0.0).astype(bf16)
            value_turned_ref[h] = jnp.where(row_own, value_turned, 0.0).astype(bf16)
    pl.when(step == pl.num_programs(0) - 1)(fetch.wait)


def prepare(tokens, weight, bias, buckets, flag, token_mask, expand, row_count, keys, line_count):
    length, depth = tokens.shape
    width = weight.shape[2]
    heads = width // HEAD
    block = 3 * LANES
    row = pl.BlockSpec((block, width), lambda i: (i, 0))
    deep_row = pl.BlockSpec((block, depth), lambda i: (i, 0))
    wide = pl.BlockSpec((heads, block, LANES), lambda i: (0, i, 0))
    turned = pl.BlockSpec((heads, LANES, block), lambda i: (0, 0, i))
    bucket = pl.BlockSpec((block, 1, length), lambda i: (i, 0, 0))
    packed = pl.BlockSpec((block, keys), lambda i: (i, 0))
    wide_shape = jax.ShapeDtypeStruct((heads, keys, LANES), bf16)
    turned_shape = jax.ShapeDtypeStruct((heads, LANES, keys), bf16)
    packed_shape = jax.ShapeDtypeStruct((row_count, keys), jnp.int16)
    return pl.pallas_call(
        partial(prepare_kernel, length=length, line_count=line_count),
        grid=(keys // block,),
        in_specs=[
            deep_row,
            whole_spec(weight),
            whole_spec(bias),
            bucket,
            bucket,
            bucket,
            pl.BlockSpec(memory_space=pltpu.SMEM),
            whole_spec(token_mask),
            pl.BlockSpec(memory_space=pl.ANY),
        ],
        out_specs=[
            row,
            wide,
            turned,
            wide,
            turned,
            deep_row,
            packed,
            packed,
            pl.BlockSpec((block, LANES), lambda i: (i, 0)),
            pl.BlockSpec(memory_space=pl.ANY),
        ],
        out_shape=[
            jax.ShapeDtypeStruct((keys, width), bf16),
            wide_shape,
            turned_shape,
            wide_shape,
            turned_shape,
            jax.ShapeDtypeStruct((keys, depth), bf16),
            packed_shape,
            packed_shape,
            jax.ShapeDtypeStruct((keys, LANES), f32),
            jax.ShapeDtypeStruct((expand.shape[0] // 4, expand.shape[1]), bf16),
        ],
        scratch_shapes=[
            pltpu.VMEM((8, keys), f32),
            pltpu.SemaphoreType.DMA,
            pltpu.SemaphoreType.DMA,
        ],
        compiler_params=pltpu.CompilerParams(
            vmem_limit_bytes=vmem_limit, collective_id=2, has_side_effects=True
        ),
        name="prepare",
    )(
        tokens,
        weight,
        bias,
        *(index.reshape(length, 1, length) for index in buckets),
        flag,
        token_mask,
        expand,
    )


def attend_kernel(
    query_ref,
    key_ref,
    value_ref,
    plane_ref,
    down_ref,
    line_table_ref,
    across_table_ref,
    down_table_ref,
    expand_bias_ref,
    expand_quarter_ref,
    output_ref,
    reduce_ref,
    exp_out_ref,
    context_ref,
    inverse_ref,
    context_away_ref,
    expand_away_ref,
    output_away_ref,
    reduce_away_ref,
    bias_away_ref,
    score_ref,
    exp_ref,
    send_ref,
    table_ref,
    bias_ref,
    exp_sem,
    local_sem,
    send_sem,
    recv_sem,
):
    _, heads, rows, keys = exp_ref.shape
    step = pl.program_id(0)
    turn_rows = ATTEND_STRIPS * STRIP
    turns = rows // turn_rows
    place = lax.axis_index("dp")
    across_mp = {"mp": 1 - lax.axis_index("mp")}
    across = {bit: {"dp": place + bit * (1 - 2 * ((place // bit) % 2))} for bit in (1, 2)}

    def remote(src, dst, n, device):
        return pltpu.make_async_remote_copy(
            src_ref=src,
            dst_ref=dst,
            send_sem=send_sem.at[n],
            recv_sem=recv_sem.at[n],
            device_id=device,
            device_id_type=pl.DeviceIdType.MESH,
        )

    arrays = (
        (expand_quarter_ref, expand_away_ref),
        (output_ref, output_away_ref),
        (reduce_ref, reduce_away_ref),
    )
    quarter = place % 4
    other_chip = (place + 2) % 4
    other_core = quarter + 1 - 2 * (quarter % 2)
    third = (other_core + 2) % 4

    def rows_of(n, which):
        away = arrays[n][1]
        return away.at[quarter_rows(away, which), :]

    def fetch(n):
        ref = arrays[n][0]
        return remote(ref.at[quarter_rows(ref, quarter), :], rows_of(n, quarter), n, across_mp)

    def pass_on(n, stage):
        source = expand_quarter_ref if n == 0 and stage < 2 else rows_of(n, quarter)
        if stage == 0:
            return remote(source, rows_of(n, quarter), 3 + n, across[2])
        if stage == 1:
            return remote(source, rows_of(n, quarter), 6 + n, across[1])
        return remote(rows_of(n, other_chip), rows_of(n, other_chip), 9 + n, across[1])

    def arrival(n, stage):
        region = rows_of(n, (other_chip, other_core, third)[stage])
        return remote(region, region, 3 + 3 * stage + n, across_mp)

    def exp_copy(which, turn):
        half = lax.rem(which + 1 - lax.axis_index("mp"), 2)
        here = pl.ds(pl.multiple_of(turn * turn_rows, STRIP), turn_rows)
        there = pl.ds(pl.multiple_of(half * rows + turn * turn_rows, STRIP), turn_rows)
        return pltpu.make_async_copy(
            exp_ref.at[which, :, here, :], exp_out_ref.at[:, there, :], exp_sem.at[which, turn]
        )

    keep = pltpu.make_async_copy(expand_quarter_ref, rows_of(0, quarter), local_sem)
    context_swap = remote(send_ref, context_away_ref, 12, across_mp)
    bias_swap = remote(bias_ref, bias_away_ref, 13, across_mp)

    def event(n, stage):
        if stage == "fetched":
            fetch(n).wait_recv()
            pass_on(n, 0).start()
            pass_on(n, 1).start()
        else:
            arrival(n, 0).wait_recv()
            pass_on(n, 2).start()

    events = {
        (0, 2): ((1, "fetched"),),
        (1, 0): ((0, "passed"), (2, "fetched")),
        (1, 1): ((1, "passed"),),
    }

    @pl.when(step == 0)
    def _():
        barrier = pltpu.get_barrier_semaphore()
        for device in (across_mp, across[1], across[2]):
            pl.semaphore_signal(
                barrier, inc=1, device_id=device, device_id_type=pl.DeviceIdType.MESH
            )
        pl.semaphore_wait(barrier, 3)
        bias_ref[...] = jnp.broadcast_to(
            expand_bias_ref[...].astype(f32).reshape(1, -1), bias_ref.shape
        )
        bias_swap.start()
        for t, ref in enumerate((line_table_ref, across_table_ref, down_table_ref)):
            count = ref.shape[1]
            lanes = jnp.concatenate(
                [ref[...].astype(f32), jnp.full((heads, LANES - count), large_negative, f32)], axis=1
            )
            for h in range(heads):
                table_ref[t * heads + h] = jnp.broadcast_to(lanes[h : h + 1], (STRIP, LANES)).astype(
                    bf16
                )
        fetch(1).start()
        fetch(2).start()
        pass_on(0, 0).start()
        pass_on(0, 1).start()
        keep.start()

    for h in range(heads):
        pair = slice(h // 2 * LANES, (h // 2 + 1) * LANES)
        score_ref[h] = dot_f32(query_ref[:, pair], key_ref[h])

    lanes = [slice(c * LANES, (c + 1) * LANES) for c in range(keys // LANES)]

    def scores_of(at):
        scores = [[] for _ in range(heads)]
        for cols in lanes:
            packed = plane_ref[at, cols]
            bias = [None] * heads
            for t, index in enumerate(
                (packed & jnp.int16(255), packed >> jnp.int16(8), down_ref[at, cols])
            ):
                for h in range(heads):
                    found = gather_lanes(table_ref[t * heads + h], index).astype(f32)
                    bias[h] = found if t == 0 else bias[h] + found
            for h in range(heads):
                scores[h].append(score_ref[h, at, cols] + bias[h])
        return scores

    def exps_of(scores):
        exps = []
        for parts in scores:
            top = parts[0]
            for part in parts[1:]:
                top = jnp.maximum(top, part)
            top = jnp.max(top, axis=1, keepdims=True)
            exps.append([jnp.exp(part - top).astype(bf16) for part in parts])
        return exps

    def strips(n, carry):
        for (at_step, at_turn), pieces in events.items():

            @pl.when((step == at_step) & (n == at_turn))
            def _():
                for piece in pieces:
                    event(*piece)

        start = pl.multiple_of(n * turn_rows, STRIP)
        places = [pl.ds(start + k * STRIP, STRIP) for k in range(ATTEND_STRIPS)]
        scores = [scores_of(at) for at in places]
        exps = [exps_of(part) for part in scores]
        for at, part in zip(places, exps):
            for h in range(heads):
                for c, cols in enumerate(lanes):
                    exp_ref[step, h, at, cols] = part[h][c]
        exp_copy(step, n).start()
        return carry

    lax.fori_loop(0, turns, strips, 0)
    first = lax.broadcasted_iota(jnp.int32, (rows, LANES), 1) < HEAD
    for p in range(heads // 2):
        cols = slice(p * LANES, (p + 1) * LANES)
        even = dot_f32(exp_ref[step, 2 * p], value_ref[2 * p])
        odd = dot_f32(exp_ref[step, 2 * p + 1], value_ref[2 * p + 1])
        sums = jnp.where(first, pltpu.roll(even, HEAD, 1), pltpu.roll(odd, HEAD, 1))
        inverse = 1.0 / sums
        inverse_ref[:, cols] = inverse
        context = (jnp.where(first, even, odd) * inverse).astype(bf16)
        context_ref[:, cols] = context

        @pl.when(step == 0)
        def _():
            send_ref[:, cols] = context

    pl.when(step == 0)(context_swap.start)

    @pl.when(step == 1)
    def _():
        event(2, "passed")
        for which in range(2):
            for n in range(turns):
                exp_copy(which, n).wait()
        keep.wait()
        context_swap.wait()
        bias_swap.wait()
        for n in range(3):
            arrival(n, 1).wait_recv()
            arrival(n, 2).wait_recv()
            for stage in range(3):
                pass_on(n, stage).wait_send()
        fetch(1).wait_send()
        fetch(2).wait_send()


def attend(
    query,
    key_turned,
    value_ones,
    plane,
    down,
    tables,
    expand_bias,
    expand_quarter,
    output,
    reduce,
):
    heads, _, keys = key_turned.shape
    row_count = plane.shape[0]
    width = heads * HEAD
    half_rows = row_count // 2

    def half(i):
        return lax.rem(i + 1 - lax.axis_index("mp"), 2)

    anywhere = pl.BlockSpec(memory_space=pl.ANY)
    index_spec = pl.BlockSpec((half_rows, keys), lambda i: (half(i), 0))
    row_spec = pl.BlockSpec((half_rows, width), lambda i: (half(i), 0))
    return pl.pallas_call(
        attend_kernel,
        grid=(2,),
        in_specs=[
            row_spec,
            whole_spec(key_turned),
            whole_spec(value_ones),
            index_spec,
            index_spec,
            *(whole_spec(table) for table in tables),
            whole_spec(expand_bias),
            anywhere,
            anywhere,
            anywhere,
        ],
        out_specs=[
            anywhere,
            row_spec,
            row_spec,
            anywhere,
            anywhere,
            anywhere,
            anywhere,
            anywhere,
        ],
        out_shape=[
            jax.ShapeDtypeStruct((heads, row_count, keys), bf16),
            jax.ShapeDtypeStruct((row_count, width), bf16),
            jax.ShapeDtypeStruct((row_count, width), f32),
            jax.ShapeDtypeStruct((half_rows, width), bf16),
            jax.ShapeDtypeStruct((4 * expand_quarter.shape[0], expand_quarter.shape[1]), bf16),
            jax.ShapeDtypeStruct(output.shape, bf16),
            jax.ShapeDtypeStruct(reduce.shape, bf16),
            jax.ShapeDtypeStruct((8, expand_bias.size), f32),
        ],
        scratch_shapes=[
            pltpu.VMEM((heads, half_rows, keys), f32),
            pltpu.VMEM((2, heads, half_rows, keys), bf16),
            pltpu.VMEM((half_rows, width), bf16),
            pltpu.VMEM((3 * heads, STRIP, LANES), bf16),
            pltpu.VMEM((8, expand_bias.size), f32),
            pltpu.SemaphoreType.DMA((2, half_rows // (ATTEND_STRIPS * STRIP))),
            pltpu.SemaphoreType.DMA,
            pltpu.SemaphoreType.DMA((14,)),
            pltpu.SemaphoreType.DMA((14,)),
        ],
        compiler_params=pltpu.CompilerParams(
            vmem_limit_bytes=vmem_limit, collective_id=1, has_side_effects=True
        ),
        name="attend",
    )(
        query,
        key_turned,
        value_ones,
        plane,
        down,
        *tables,
        expand_bias,
        expand_quarter,
        output,
        reduce,
    )


def attend_back_kernel(
    exp_ref,
    grad_ref,
    context_ref,
    query_ref,
    value_ref,
    key_ref,
    grad_score_ref,
    grad_query_ref,
    grad_key_ref,
    grad_value_ref,
):
    heads, rows, _ = exp_ref.shape

    @pl.when(pl.program_id(0) == 0)
    def _():
        grad_key_ref[...] = jnp.zeros_like(grad_key_ref)
        grad_value_ref[...] = jnp.zeros_like(grad_value_ref)

    first = lax.broadcasted_iota(jnp.int32, (rows, LANES), 1) < HEAD
    for p in range(heads // 2):
        cols = slice(p * LANES, (p + 1) * LANES)
        grad = grad_ref[:, cols]
        product = grad.astype(f32) * context_ref[:, cols].astype(f32)
        query_turned = query_ref[:, cols].T
        grad_turned = grad.T
        grad_query = None
        for u in range(2):
            h = 2 * p + u
            half = slice(u * HEAD, (u + 1) * HEAD)
            own = first if u == 0 else ~first
            total = jnp.sum(jnp.where(own, product, 0.0), axis=1, keepdims=True)
            grad_exp = dot_f32(grad, value_ref[h])
            grad_score = (exp_ref[h].astype(f32) * (grad_exp - total)).astype(bf16)
            grad_score_ref[h] = grad_score
            part = dot_f32(grad_score, key_ref[h])
            grad_query = part if u == 0 else grad_query + part
            grad_key_ref[h] += dot_f32(query_turned[half], grad_score)
            grad_value_ref[h] += dot_f32(grad_turned[half], exp_ref[h])
        grad_query_ref[:, cols] = (grad_query * 0.125).astype(bf16)


def attend_back(exps, grad, context, query, value_turned, key_wide):
    heads, row_count, keys = exps.shape
    width = heads * HEAD
    row_spec = pl.BlockSpec((BLOCK_ROWS, width), lambda i: (i, 0))
    exp_spec = pl.BlockSpec((heads, BLOCK_ROWS, keys), lambda i: (0, i, 0))
    sum_spec = pl.BlockSpec((heads, HEAD, keys), lambda i: (0, 0, 0))
    return pl.pallas_call(
        attend_back_kernel,
        grid=(row_count // BLOCK_ROWS,),
        in_specs=[
            exp_spec,
            row_spec,
            row_spec,
            row_spec,
            whole_spec(value_turned),
            whole_spec(key_wide),
        ],
        out_specs=[exp_spec, row_spec, sum_spec, sum_spec],
        out_shape=[
            jax.ShapeDtypeStruct((heads, row_count, keys), bf16),
            jax.ShapeDtypeStruct((row_count, width), bf16),
            jax.ShapeDtypeStruct((heads, HEAD, keys), f32),
            jax.ShapeDtypeStruct((heads, HEAD, keys), f32),
        ],
        compiler_params=pltpu.CompilerParams(vmem_limit_bytes=vmem_limit),
        name="attend_back",
    )(exps, grad, context, query, value_turned, key_wide)


def table_strips(strips, sum_ref, heads, keys, high_counts):
    base = 0
    for t in range(3):
        shift = 8 if t == 1 else 0
        highs, lows = [], []
        for grad_of, plane_of, down_of in strips:
            for c in range(keys // LANES):
                cols = slice(c * LANES, (c + 1) * LANES)
                index = down_of(cols) if t == 2 else plane_of(cols)
                low = index & jnp.int16(15 << shift)
                high = index & jnp.int16(48 << shift)
                lows.append(
                    jnp.concatenate(
                        [
                            jnp.where(low == jnp.int16(x << shift), bf16(1), bf16(0))
                            for x in range(16)
                        ]
                    )
                )
                parts = []
                for x in range(high_counts[t]):
                    mask = high == jnp.int16(x << (4 + shift))
                    parts += [jnp.where(mask, grad_of(h, cols), bf16(0)) for h in range(heads)]
                highs.append(jnp.concatenate(parts))
        span = slice(base, base + high_counts[t] * heads * STRIP)
        sum_ref[span, :] += lax.dot_general(
            jnp.concatenate(highs, axis=1),
            jnp.concatenate(lows, axis=1),
            (((1,), (1,)), ((), ())),
            preferred_element_type=f32,
        )
        base = span.stop


def table_finish(sum_ref, out_ref, count):
    row_of_lane = lax.broadcasted_iota(jnp.int32, (STRIP, 16 * STRIP), 1) % STRIP
    same = row_of_lane == lax.broadcasted_iota(jnp.int32, (STRIP, 16 * STRIP), 0)
    for o in range(count):
        block = sum_ref[o * STRIP : (o + 1) * STRIP, :]
        out_ref[o : o + 1, :] = jnp.sum(jnp.where(same, block, 0.0), axis=0, keepdims=True)


def table_result(out, high_counts, heads):
    summed = jnp.sum(out.reshape(sum(high_counts), heads, 16, STRIP), axis=-1)
    return summed.transpose(0, 2, 1).reshape(-1, heads)


def table_kernel(grad_score_ref, plane_ref, down_ref, out_ref, sum_ref, *, high_counts):
    heads, rows, keys = grad_score_ref.shape
    step = pl.program_id(0)

    @pl.when(step == 0)
    def _():
        sum_ref[...] = jnp.zeros_like(sum_ref)

    def refs_at(start):
        at = pl.ds(pl.multiple_of(start, STRIP), STRIP)
        return (
            lambda h, cols: grad_score_ref[h, at, cols],
            lambda cols: plane_ref[at, cols],
            lambda cols: down_ref[at, cols],
        )

    def strips(r, carry):
        start = r * (TABLE_STRIPS * STRIP)
        table_strips(
            [refs_at(start + k * STRIP) for k in range(TABLE_STRIPS)],
            sum_ref,
            heads,
            keys,
            high_counts,
        )
        return carry

    lax.fori_loop(0, rows // (TABLE_STRIPS * STRIP), strips, 0)

    @pl.when(step == pl.num_programs(0) - 1)
    def _():
        table_finish(sum_ref, out_ref, out_ref.shape[0])


def table_sums(grad_scores, plane, down, counts):
    heads, row_count, keys = grad_scores.shape
    high_counts = (counts[0] // 16, counts[1] // 16, counts[1] // 16)
    high_rows = sum(high_counts) * heads
    index_spec = pl.BlockSpec((BLOCK_ROWS, keys), lambda i: (i, 0))
    out = pl.pallas_call(
        partial(table_kernel, high_counts=high_counts),
        grid=(row_count // BLOCK_ROWS,),
        in_specs=[
            pl.BlockSpec((heads, BLOCK_ROWS, keys), lambda i: (0, i, 0)),
            index_spec,
            index_spec,
        ],
        out_specs=pl.BlockSpec((high_rows, 16 * STRIP), lambda i: (0, 0)),
        out_shape=jax.ShapeDtypeStruct((high_rows, 16 * STRIP), f32),
        scratch_shapes=[pltpu.VMEM((high_rows * STRIP, 16 * STRIP), f32)],
        compiler_params=pltpu.CompilerParams(vmem_limit_bytes=vmem_limit),
        name="table_sums",
    )(grad_scores, plane, down)
    return table_result(out, high_counts, heads)


CHUNK = 768
CHUNKS = 6
LOCAL_CHUNKS = 2
PARTS = (CHUNK // 2, CHUNK // 4, CHUNK // 8, CHUNK // 16)
BITS = ((1, 2, 4, 8), (1, 4, 2, 8), (1, 2, 4, 8), (1, 4, 2, 8), (1, 2, 4, 8), (1, 4, 2, 8))
BACK_ROWS = 112
EXCHANGE = (
    ("b", 0, 0, 2), ("b", 0, 0, 3), ("b", 0, 0, 4), ("b", 1, 0, 5), ("b", 4, 1, 2), ("b", 6, 1, 3),
    ("b", 8, 1, 4), ("b", 9, 1, 5), ("b", 20, 2, 2), ("b", 22, 2, 3), ("p", 0, 3, 2), ("p", 2, 2, 4),
    ("p", 3, 2, 5), ("p", 3, 3, 3), ("p", 3, 0, 0), ("p", 3, 0, 1), ("t", 0, 4, 2), ("t", 1, 1, 0),
    ("t", 1, 1, 1), ("t", 2, 4, 3), ("t", 2, "small", 0), ("t", 3, 3, 4), ("t", 4, 5, 2),
    ("t", 6, 3, 5), ("t", 6, 2, 0), ("t", 6, 2, 1), ("t", 6, "small", 1), ("t", 8, 5, 3),
    ("t", 9, 4, 4), ("t", 10, 4, 5), ("t", 11, 6, 2), ("t", 11, "send", 0), ("t", 11, "small", 2),
    ("t", 12, 3, 1), ("t", 12, 3, 0), ("t", 13, 6, 3), ("t", 15, 5, 4), ("t", 16, "small", 3),
    ("t", 17, 5, 5), ("t", 17, 7, 3), ("t", 18, 7, 2), ("t", 19, 4, 1), ("t", 20, "small", 4),
    ("t", 21, 4, 0), ("t", 23, 6, 4), ("t", 24, 8, 2), ("t", 24, "input", 0), ("t", 25, 6, 5),
    ("t", 25, 9, 2), ("t", 25, "small", 5), ("t", 26, 8, 3), ("t", 26, "layer", 0), ("t", 27, 5, 1),
    ("t", 28, 9, 3), ("t", 29, 5, 0), ("t", 29, 7, 5), ("t", 29, 7, 4), ("t", 31, 6, 1),
    ("t", 33, 6, 0), ("e", 0, 8, 4), ("e", 0, 9, 4), ("e", 0, 8, 5), ("e", 0, 9, 5), ("e", 0, 7, 0),
    ("e", 0, 8, 0), ("e", 0, 7, 1), ("e", 0, 8, 1),
)


def plan_slots(phase, count):
    slots = [[] for _ in range(count)]
    for name, at, event, which in EXCHANGE:
        if name == phase:
            slots[at].append((event, which))
    return slots


def finish_kernel(
    exp_ref,
    inverse_ref,
    plane_ref,
    down_ref,
    context_ref,
    query_ref,
    token_ref,
    grad_ref,
    layer_ref,
    value_ref,
    key_ref,
    project_ref,
    output_ref,
    expand_ref,
    expand_away_ref,
    reduce_ref,
    reduce_away_ref,
    small_ref,
    total_ref,
    layer_out_ref,
    input_ref,
    small_out_ref,
    table_ref,
    score_ref,
    output_buf,
    grad_buf,
    value_buf,
    key_buf,
    context_buf,
    query_buf,
    token_buf,
    project_buf,
    ring_buf,
    inverse_buf,
    grad_key_buf,
    grad_value_buf,
    triple_buf,
    input_send_buf,
    input_recv_buf,
    input_buf,
    plane_buf,
    down_buf,
    sum_ref,
    own_buf,
    away_buf,
    core_buf,
    core_away_buf,
    first_buf,
    first_away_buf,
    y_buf,
    second_buf,
    third_buf,
    small_buf,
    small_recv_buf,
    table_buf,
    table_recv_buf,
    resident_sem,
    block_sem,
    ring_sem,
    load_sem,
    local_sem,
    out_sem,
    send_sem,
    recv_sem,
    wide_send_sem,
    wide_recv_sem,
    small_send_sem,
    small_recv_sem,
    table_send_sem,
    table_recv_sem,
    *,
    high_counts,
):
    heads, row_count, keys = exp_ref.shape
    width = heads * HEAD
    half_rows = row_count // 2
    rows = BACK_ROWS
    blocks = row_count // rows
    block_strips = rows // STRIP
    turns = row_count // (TABLE_STRIPS * STRIP)
    place = lax.axis_index("dp")
    mp_index = lax.axis_index("mp")
    side_of = {bit: (place // bit) % 2 for bit in (1, 2, 4, 8)}
    partner_of = {bit: {"dp": place + bit * (1 - 2 * side_of[bit])} for bit in (1, 2, 4, 8)}
    across_mp = {"mp": 1 - mp_index}

    def by_bits(*bits):
        return {"dp": place + sum(bit * (1 - 2 * side_of[bit]) for bit in bits)}

    diagonal = (by_bits(1, 2), by_bits(4, 8))
    barrier = pltpu.get_barrier_semaphore()
    for device in (*partner_of.values(), *diagonal, across_mp):
        pl.semaphore_signal(barrier, inc=1, device_id=device, device_id_type=pl.DeviceIdType.MESH)
    pl.semaphore_wait(barrier, 7)

    def rows_at(start, size):
        return pl.ds(pl.multiple_of(start, STRIP), size)

    def remote(src, dst, send, recv, device):
        return pltpu.make_async_remote_copy(
            src_ref=src,
            dst_ref=dst,
            send_sem=send,
            recv_sem=recv,
            device_id=device,
            device_id_type=pl.DeviceIdType.MESH,
        )

    mine = rows_at(mp_index * half_rows, half_rows)
    others = rows_at((1 - mp_index) * half_rows, half_rows)
    grad_swap = remote(
        grad_ref, grad_buf.at[1], wide_send_sem.at[0], wide_recv_sem.at[0], across_mp
    )
    input_swap = remote(
        input_send_buf, input_recv_buf, wide_send_sem.at[1], wide_recv_sem.at[1], across_mp
    )
    layer_swap = remote(
        layer_ref, layer_out_ref.at[mine, :], wide_send_sem.at[2], wide_recv_sem.at[2], across_mp
    )
    layer_arrival = remote(
        layer_out_ref.at[others, :],
        layer_out_ref.at[others, :],
        wide_send_sem.at[2],
        wide_recv_sem.at[2],
        across_mp,
    )
    layer_keep = pltpu.make_async_copy(layer_ref, layer_out_ref.at[mine, :], out_sem.at[2])
    grad_swap.start()

    residents = [
        pltpu.make_async_copy(src, dst, resident_sem.at[n])
        for n, (src, dst) in enumerate(
            (
                (grad_ref, grad_buf.at[0]),
                (output_ref, output_buf),
                (context_ref, context_buf),
                (query_ref, query_buf),
                (value_ref, value_buf),
                (key_ref, key_buf),
                (small_ref, small_buf.at[0]),
                (token_ref, token_buf),
                (project_ref, project_buf),
            )
        )
    ]

    def block_rows(block):
        start = (mp_index * (blocks // 2) + block) % blocks
        return rows_at(start * rows, rows)

    def block_copies(block, slot):
        at = block_rows(block)
        return (
            pltpu.make_async_copy(exp_ref.at[:, at, :], ring_buf.at[slot], block_sem.at[slot, 0]),
            pltpu.make_async_copy(inverse_ref.at[at, :], inverse_buf.at[slot], block_sem.at[slot, 1]),
        )

    def score_copy(block, slot):
        return pltpu.make_async_copy(
            ring_buf.at[2 + slot], score_ref.at[:, block_rows(block), :], out_sem.at[slot]
        )

    def ring_copies(block):
        slot = block % 4
        at = rows_at(block * rows, rows)
        return (
            pltpu.make_async_copy(score_ref.at[:, at, :], ring_buf.at[slot], ring_sem.at[slot, 0]),
            pltpu.make_async_copy(plane_ref.at[at, :], plane_buf.at[slot], ring_sem.at[slot, 1]),
            pltpu.make_async_copy(down_ref.at[at, :], down_buf.at[slot], ring_sem.at[slot, 2]),
        )

    def is_away(chunk):
        return chunk >= LOCAL_CHUNKS

    loads = {}
    for ref, away_ref, wide in (
        (expand_ref, expand_away_ref, True),
        (reduce_ref, reduce_away_ref, False),
    ):
        for k in range(2):
            piece = slice(k * CHUNK, (k + 1) * CHUNK)
            index = (slice(None), piece) if wide else (piece, slice(None))
            chunk = LOCAL_CHUNKS + len(loads)
            loads[chunk] = (
                pltpu.make_async_copy(ref.at[index], own_buf.at[chunk], load_sem.at[chunk, 0]),
                pltpu.make_async_copy(
                    away_ref.at[index], away_buf.at[chunk - LOCAL_CHUNKS], load_sem.at[chunk, 1]
                ),
            )

    for copy in loads[LOCAL_CHUNKS]:
        copy.start()
    for copy in residents[:2]:
        copy.start()
    for copy in block_copies(0, 0):
        copy.start()
    for copy in residents[2:6]:
        copy.start()
    for chunk in range(LOCAL_CHUNKS + 1, CHUNKS):
        for copy in loads[chunk]:
            copy.start()
    residents[6].start()
    for copy in residents[7:]:
        copy.start()

    keeps, leaves = [], []
    for bits in BITS:
        kept, left, base = [], [], 0
        for size, bit in zip(PARTS, bits):
            kept.append(base + side_of[bit] * size)
            left.append(base + (1 - side_of[bit]) * size)
            base = base + side_of[bit] * size
        keeps.append(kept)
        leaves.append(left)
    arrivals = (core_buf, first_buf, second_buf, third_buf)
    away_arrivals = (core_away_buf, first_away_buf)

    def staged(src, dst, chunk, stage, device):
        return remote(src, dst, send_sem.at[chunk, stage], recv_sem.at[chunk, stage], device)

    def scatter(chunk, level):
        return staged(
            own_buf.at[chunk, rows_at(leaves[chunk][level], PARTS[level]), :],
            arrivals[level].at[chunk],
            chunk,
            level,
            partner_of[BITS[chunk][level]],
        )

    def scatter_away(chunk, level):
        return staged(
            away_buf.at[chunk - LOCAL_CHUNKS, rows_at(leaves[chunk][level], PARTS[level]), :],
            away_arrivals[level].at[chunk - LOCAL_CHUNKS],
            chunk,
            4 + level,
            partner_of[BITS[chunk][level]],
        )

    def hand_over(chunk):
        return staged(
            away_buf.at[chunk - LOCAL_CHUNKS, rows_at(keeps[chunk][1], PARTS[1]), :],
            y_buf.at[chunk - LOCAL_CHUNKS],
            chunk,
            6,
            across_mp,
        )

    def total_rows(chunk, start, size):
        return total_ref.at[rows_at(chunk * CHUNK + start, size), :]

    def gather(chunk, level):
        kept, size = keeps[chunk][level], PARTS[level]
        if level == 3:
            src = own_buf.at[chunk, rows_at(kept, size), :]
        else:
            src = total_rows(chunk, kept, size)
        return staged(
            src, total_rows(chunk, kept, size), chunk, 7 + level, partner_of[BITS[chunk][level]]
        )

    def gathered(chunk, level):
        region = total_rows(chunk, leaves[chunk][level], PARTS[level])
        return staged(region, region, chunk, 7 + level, partner_of[BITS[chunk][level]])

    def store_own(chunk):
        return pltpu.make_async_copy(
            own_buf.at[chunk, rows_at(keeps[chunk][3], PARTS[3]), :],
            total_rows(chunk, keeps[chunk][3], PARTS[3]),
            local_sem.at[chunk],
        )

    def add(buf, chunk, start, size, arrived):
        piece = PARTS[3]

        def step(n, carry):
            here = rows_at(start + n * piece, piece)
            there = rows_at(n * piece, piece)
            buf[chunk, here, :] = buf[chunk, here, :] + arrived[there, :]
            return carry

        lax.fori_loop(0, size // piece, step, 0)

    def add_level(chunk, level):
        scatter(chunk, level).wait_recv()
        add(own_buf, chunk, keeps[chunk][level], PARTS[level], arrivals[level].at[chunk])

    def add_level_away(chunk, level):
        at = chunk - LOCAL_CHUNKS
        scatter_away(chunk, level).wait_recv()
        add(away_buf, at, keeps[chunk][level], PARTS[level], away_arrivals[level].at[at])

    def exchange(event, chunk):
        away = is_away(chunk)
        if event == 0:
            if away:
                for copy in loads[chunk]:
                    copy.wait()
                scatter_away(chunk, 0).start()
            scatter(chunk, 0).start()
            return
        if event == 1:
            if away:
                add_level_away(chunk, 0)
                scatter_away(chunk, 1).start()
            add_level(chunk, 0)
            scatter(chunk, 1).start()
            return
        if away and event == 2:
            add_level_away(chunk, 1)
            hand_over(chunk).start()
            add_level(chunk, 1)
            return
        if away:
            event -= 1
            if event == 2:
                hand_over(chunk).wait_recv()
                add(own_buf, chunk, keeps[chunk][1], PARTS[1], y_buf.at[chunk - LOCAL_CHUNKS])
        elif event == 2:
            add_level(chunk, 1)
        if event == 2:
            scatter(chunk, 2).start()
        elif event == 3:
            add_level(chunk, 2)
            scatter(chunk, 3).start()
        elif event == 4:
            add_level(chunk, 3)
            store_own(chunk).start()
            gather(chunk, 3).start()
        else:
            level = 8 - event
            if level == 3:
                store_own(chunk).wait()
            gathered(chunk, level).wait_recv()
            if level > 0:
                gather(chunk, level - 1).start()

    small_devices = (across_mp, *partner_of.values())

    def small_hop(n):
        return remote(
            small_buf.at[n],
            small_recv_buf.at[n],
            small_send_sem.at[n],
            small_recv_sem.at[n],
            small_devices[n],
        )

    def small_step(n):
        if n == 0:
            residents[6].wait()
        else:
            small_hop(n - 1).wait_recv()
            small_buf[n] = small_buf[n - 1] + small_recv_buf[n - 1]
        if n < 5:
            small_hop(n).start()
        else:
            small_out_ref[...] = small_buf[n]

    def input_rows(side):
        return mine if side == 0 else others

    def input_product(side, target):
        at = input_rows(side)
        part = None
        for k in range(3):
            product = lax.dot_general(
                triple_buf[k, at, :],
                project_buf[k, rows_at(target * width, width), :],
                (((1,), (1,)), ((), ())),
                preferred_element_type=f32,
            )
            part = product if part is None else part + product
        if side == 0:
            cols = pl.ds(pl.multiple_of(target * width, LANES), width)
            part = part + grad_buf[0, :, cols].astype(f32)
        return part

    def input_store(side):
        return pltpu.make_async_copy(
            input_buf.at[side], input_ref.at[input_rows(side), :], out_sem.at[3 + side]
        )

    def run(event, which):
        if event == "small":
            small_step(which)
        elif event == "send":
            input_swap.start()
        elif event == "layer":
            layer_swap.start()
            layer_keep.start()
        elif event == "input":
            input_swap.wait_recv()
            for side in range(2):
                part = input_product(side, mp_index)
                input_buf[side] = part + input_recv_buf[input_rows(side), :].astype(f32)
                input_store(side).start()
        else:
            exchange(event, which)

    pairs = heads // 2
    block_slots = plan_slots("b", blocks * pairs)
    part_slots = plan_slots("p", 4)
    turn_slots = plan_slots("t", turns)
    rest = plan_slots("e", 1)[0]

    def run_all(steps):
        for event, which in steps:
            run(event, which)

    def dispatch(slots, n, low, high):
        if not any(slots[low:high]):
            return
        if high - low == 1:
            for event, which in slots[low]:
                run(event, which)
            return
        middle = (low + high) // 2
        if any(slots[low:middle]):
            pl.when(n < middle)(lambda: dispatch(slots, n, low, middle))
        if any(slots[middle:high]):
            pl.when(n >= middle)(lambda: dispatch(slots, n, middle, high))

    grad_key_buf[...] = jnp.zeros_like(grad_key_buf)
    grad_value_buf[...] = jnp.zeros_like(grad_value_buf)
    sum_ref[...] = jnp.zeros_like(sum_ref)
    for copy in residents[:6]:
        copy.wait()
    first = lax.broadcasted_iota(jnp.int32, (rows, LANES), 1) < HEAD

    def back(block, carry):
        slot = block % 2
        at = block_rows(block)
        for copy in block_copies(block, slot):
            copy.wait()

        @pl.when(block + 1 < blocks)
        def _():
            for copy in block_copies(block + 1, 1 - slot):
                copy.start()

        pl.when(block == blocks // 2)(grad_swap.wait_recv)
        pl.when(block >= 2)(lambda: score_copy(block - 2, slot).wait())
        side = block // (blocks // 2)
        local = rows_at((block % (blocks // 2)) * rows, rows)
        grad_context = lax.dot_general(
            grad_buf[side, local, :],
            output_buf[...],
            (((1,), (1,)), ((), ())),
            preferred_element_type=f32,
        )
        scaled = (grad_context * inverse_buf[slot]).astype(bf16)
        for p in range(pairs):
            dispatch(block_slots, block * pairs + p, 0, blocks * pairs)
            cols = slice(p * LANES, (p + 1) * LANES)
            grad = scaled[:, cols]
            product = grad.astype(f32) * context_buf[at, cols].astype(f32)
            query_turned = query_buf[at, cols].T
            grad_turned = grad.T
            grad_query = None
            for u in range(2):
                h = 2 * p + u
                half = slice(u * HEAD, (u + 1) * HEAD)
                own = first if u == 0 else ~first
                total = jnp.sum(jnp.where(own, product, 0.0), axis=1, keepdims=True)
                exps = ring_buf[slot, h]
                grad_exp = dot_f32(grad, value_buf[h])
                grad_score = (exps.astype(f32) * (grad_exp - total)).astype(bf16)
                ring_buf[2 + slot, h] = grad_score
                part = dot_f32(grad_score, key_buf[h])
                grad_query = part if u == 0 else grad_query + part
                grad_key_buf[h] += dot_f32(query_turned[half], grad_score)
                grad_value_buf[h] += dot_f32(grad_turned[half], exps)
            triple_buf[0, at, cols] = (grad_query * 0.125).astype(bf16)
        score_copy(block, slot).start()
        return carry

    lax.fori_loop(0, blocks, back, 0)

    score_copy(blocks - 2, blocks % 2).wait()
    score_copy(blocks - 1, (blocks - 1) % 2).wait()
    for block in range(2):
        for copy in ring_copies(block):
            copy.start()
    run_all(part_slots[0])
    triple_buf[0, row_count:keys, :] = jnp.zeros((keys - row_count, width), bf16)
    for k, ref in ((1, grad_key_buf), (2, grad_value_buf)):
        for h in range(0, heads, 2):
            pair = ref[h : h + 2].reshape(LANES, keys)
            triple_buf[k, :, h * HEAD : (h + 2) * HEAD] = pair.T.astype(bf16)
    run_all(part_slots[1])
    for copy in residents[7:]:
        copy.wait()
    tokens_in = (((0,), (0,)), ((), ()))
    places = ((0, 0), (0, width), (1, 0))
    for k, (chunk, start) in enumerate(places):
        own_buf[chunk, start : start + width, :] = lax.dot_general(
            triple_buf[k], token_buf[...], tokens_in, preferred_element_type=f32
        ).astype(bf16)
    run_all(part_slots[2])
    own_buf[1, width : 2 * width, :] = (
        lax.dot_general(
            context_buf[mine, :], grad_buf[0], tokens_in, preferred_element_type=f32
        )
        + lax.dot_general(
            context_buf[others, :], grad_buf[1], tokens_in, preferred_element_type=f32
        )
    ).astype(bf16)
    run_all(part_slots[3])
    for side in range(2):
        input_send_buf[input_rows(side), :] = input_product(side, 1 - mp_index).astype(bf16)
    biases = jnp.concatenate(
        [
            jnp.sum(triple_buf[0].astype(f32), axis=0, keepdims=True),
            jnp.sum(triple_buf[2].astype(f32), axis=0, keepdims=True),
        ],
        axis=1,
    )

    def turn(n, carry):
        last = n * TABLE_STRIPS + TABLE_STRIPS - 1
        block = last // block_strips

        @pl.when(last % block_strips < TABLE_STRIPS)
        def _():
            for copy in ring_copies(block):
                copy.wait()

            @pl.when(block + 2 < blocks)
            def _():
                for copy in ring_copies(block + 2):
                    copy.start()

        dispatch(turn_slots, n, 0, turns)

        def refs_at(strip):
            slot = (strip // block_strips) % 4
            at = rows_at((strip % block_strips) * STRIP, STRIP)
            return (
                lambda h, cols: ring_buf[slot, h, at, cols],
                lambda cols: plane_buf[slot, at, cols],
                lambda cols: down_buf[slot, at, cols],
            )

        table_strips(
            [refs_at(n * TABLE_STRIPS + k) for k in range(TABLE_STRIPS)],
            sum_ref,
            heads,
            keys,
            high_counts,
        )
        return carry

    lax.fori_loop(0, turns, turn, 0)

    table_rows = sum(high_counts) * heads
    table_finish(sum_ref, table_buf.at[0], table_rows)
    lanes = table_buf.shape[2]
    pieces = 2 * width // lanes
    for n in range(pieces):
        table_buf[0, table_rows + n : table_rows + n + 1, :] = biases[:, n * lanes : (n + 1) * lanes]
    spare = table_buf.shape[1] - table_rows - pieces
    table_buf[0, table_rows + pieces :, :] = jnp.zeros((spare, lanes), f32)
    groups = ((1, 2), (4, 8))

    def table_hop(n, d):
        bits = [bit for k, bit in enumerate(groups[n]) if d >> k & 1]
        return remote(
            table_buf.at[n],
            table_recv_buf.at[n, d],
            table_send_sem.at[n, d],
            table_recv_sem.at[n, d],
            by_bits(*bits),
        )

    def table_step(n):
        if n > 0:
            for d in range(1, 4):
                table_hop(n - 1, d).wait_recv()
            table_recv_buf[n - 1, 0] = table_buf[n - 1]
            low, high = (side_of[bit] for bit in groups[n - 1])
            total = None
            for member in range(4):
                d = (low + member % 2) % 2 + 2 * ((high + member // 2) % 2)
                part = table_recv_buf[n - 1, d]
                total = part if member == 0 else total + part
            table_buf[n] = total
        if n < 2:
            for d in range(1, 4):
                table_hop(n, d).start()

    table_step(0)
    for n, (event, which) in enumerate(rest):
        if n in (3, 7):
            table_step(n // 3)
        run(event, which)
    for n in range(1, 3):
        if len(rest) <= 4 * n - 1:
            table_step(n)
    table_ref[...] = table_buf[2]

    layer_arrival.wait_recv()
    layer_keep.wait()
    grad_swap.wait_send()
    input_swap.wait_send()
    layer_swap.wait_send()
    for side in range(2):
        input_store(side).wait()
    for n in range(5):
        small_hop(n).wait_send()
    for n in range(2):
        for d in range(1, 4):
            table_hop(n, d).wait_send()
    for chunk in range(CHUNKS):
        for level in range(4):
            scatter(chunk, level).wait_send()
            gather(chunk, level).wait_send()
        if is_away(chunk):
            scatter_away(chunk, 0).wait_send()
            scatter_away(chunk, 1).wait_send()
            hand_over(chunk).wait_send()


def finish(
    exps,
    inverse,
    plane,
    down,
    context,
    query,
    tokens,
    grad,
    layer,
    value_turned,
    key_wide,
    project_weight,
    output_weight,
    expand,
    reduce,
    small,
    counts,
):
    heads, row_count, keys = exps.shape
    width = heads * HEAD
    depth = tokens.shape[1]
    half_rows = row_count // 2
    high_counts = (counts[0] // 16, counts[1] // 16, counts[1] // 16)
    high_rows = sum(high_counts) * heads
    low_lanes = 16 * STRIP
    table_shape = (round_up(high_rows + 2 * width // low_lanes, 8), low_lanes)
    away = CHUNKS - LOCAL_CHUNKS
    anywhere = pl.BlockSpec(memory_space=pl.ANY)
    in_vmem = pl.BlockSpec(memory_space=pltpu.VMEM)
    dma = pltpu.SemaphoreType.DMA
    total, layer_full, input_full, small_sum, table_sum, _ = pl.pallas_call(
        partial(finish_kernel, high_counts=high_counts),
        in_specs=[anywhere] * 18,
        out_specs=[anywhere, anywhere, anywhere, in_vmem, in_vmem, anywhere],
        out_shape=[
            jax.ShapeDtypeStruct((CHUNKS * CHUNK, CHUNK), bf16),
            jax.ShapeDtypeStruct((row_count, depth), bf16),
            jax.ShapeDtypeStruct((row_count, width), f32),
            jax.ShapeDtypeStruct(small.shape, f32),
            jax.ShapeDtypeStruct(table_shape, f32),
            jax.ShapeDtypeStruct(exps.shape, bf16),
        ],
        scratch_shapes=[
            pltpu.VMEM(output_weight.shape, bf16),
            pltpu.VMEM((2, half_rows, depth), bf16),
            pltpu.VMEM(value_turned.shape, bf16),
            pltpu.VMEM(key_wide.shape, bf16),
            pltpu.VMEM(context.shape, bf16),
            pltpu.VMEM(query.shape, bf16),
            pltpu.VMEM(tokens.shape, bf16),
            pltpu.VMEM(project_weight.shape, bf16),
            pltpu.VMEM((4, heads, BACK_ROWS, keys), bf16),
            pltpu.VMEM((2, BACK_ROWS, width), f32),
            pltpu.VMEM((heads, HEAD, keys), f32),
            pltpu.VMEM((heads, HEAD, keys), f32),
            pltpu.VMEM((3, keys, width), bf16),
            pltpu.VMEM((row_count, width), bf16),
            pltpu.VMEM((row_count, width), bf16),
            pltpu.VMEM((2, half_rows, width), f32),
            pltpu.VMEM((4, BACK_ROWS, keys), jnp.int16),
            pltpu.VMEM((4, BACK_ROWS, keys), jnp.int16),
            pltpu.VMEM((high_rows * STRIP, low_lanes), f32),
            pltpu.VMEM((CHUNKS, CHUNK, CHUNK), bf16),
            pltpu.VMEM((away, CHUNK, CHUNK), bf16),
            pltpu.VMEM((CHUNKS, PARTS[0], CHUNK), bf16),
            pltpu.VMEM((away, PARTS[0], CHUNK), bf16),
            pltpu.VMEM((CHUNKS, PARTS[1], CHUNK), bf16),
            pltpu.VMEM((away, PARTS[1], CHUNK), bf16),
            pltpu.VMEM((away, PARTS[1], CHUNK), bf16),
            pltpu.VMEM((CHUNKS, PARTS[2], CHUNK), bf16),
            pltpu.VMEM((CHUNKS, PARTS[3], CHUNK), bf16),
            pltpu.VMEM((6, *small.shape), f32),
            pltpu.VMEM((5, *small.shape), f32),
            pltpu.VMEM((3, *table_shape), f32),
            pltpu.VMEM((2, 4, *table_shape), f32),
            dma((9,)),
            dma((2, 2)),
            dma((4, 3)),
            dma((CHUNKS, 2)),
            dma((CHUNKS,)),
            dma((5,)),
            dma((CHUNKS, 11)),
            dma((CHUNKS, 11)),
            dma((3,)),
            dma((3,)),
            dma((5,)),
            dma((5,)),
            dma((2, 4)),
            dma((2, 4)),
        ],
        compiler_params=pltpu.CompilerParams(
            vmem_limit_bytes=FINISH_VMEM, collective_id=0, has_side_effects=True
        ),
        name="finish",
    )(
        exps,
        inverse,
        plane,
        down,
        context,
        query,
        tokens,
        grad,
        layer,
        value_turned,
        key_wide,
        project_weight,
        output_weight,
        *expand,
        *reduce,
        small,
    )
    return total, layer_full, input_full, table_sum, small_sum


UNPACK_ROWS = 192


def unpack_kernel(
    total_ref,
    layer_in_ref,
    input_in_ref,
    sum_ref,
    small_ref,
    layer_ref,
    input_ref,
    project_ref,
    output_ref,
    expand_ref,
    reduce_ref,
    line_ref,
    across_ref,
    down_ref,
    bias_ref,
    second_gain_ref,
    second_shift_ref,
    reduce_bias_ref,
    first_gain_ref,
    first_shift_ref,
    output_bias_ref,
    expand_bias_ref,
    *,
    high_counts,
):
    step = pl.program_id(0)
    layer_ref[...] = layer_in_ref[...]
    input_ref[...] = input_in_ref[...].reshape(input_ref.shape)
    values = total_ref[...].astype(f32)

    half = values.shape[0] // 2

    @pl.when(step < 2)
    def _():
        project_ref[0] = values[:half].T

    @pl.when(step == 0)
    def _():
        project_ref[1] = values[half:].T

    @pl.when(step == 1)
    def _():
        output_ref[...] = values[half:]

    @pl.when((step >= 2) & (step < 4))
    def _():
        expand_ref[...] = values

    @pl.when(step >= 4)
    def _():
        reduce_ref[...] = values

    @pl.when(step == 0)
    def _():
        lanes = sum_ref.shape[1]
        row = lax.broadcasted_iota(jnp.int32, (lanes, LANES), 0) // STRIP
        same = row == lax.broadcasted_iota(jnp.int32, (lanes, LANES), 1)
        folded = jnp.dot(
            sum_ref[...],
            jnp.where(same, 1.0, 0.0),
            precision=lax.Precision.HIGHEST,
            preferred_element_type=f32,
        )
        heads = line_ref.shape[0]
        start = 0
        for ref, count in zip((line_ref, across_ref, down_ref), high_counts):
            parts = []
            for _ in range(count):
                parts.append(folded[start : start + heads, : lanes // STRIP])
                start += heads
            ref[...] = jnp.concatenate(parts, axis=1)
        half = bias_ref.shape[1] - lanes
        middle = sum_ref[start + 1 : start + 2, :]
        bias_ref[0:1, :] = jnp.concatenate([sum_ref[start : start + 1, :], middle[:, :half]], axis=1)
        bias_ref[1:2, :] = jnp.concatenate([middle[:, half:], sum_ref[start + 2 : start + 3, :]], axis=1)
        lead = lax.axis_index("mp") == 0
        for n, ref in enumerate(
            (
                second_gain_ref,
                second_shift_ref,
                reduce_bias_ref,
                first_gain_ref,
                first_shift_ref,
                output_bias_ref,
            )
        ):
            row = small_ref[n : n + 1, :]
            if ref.shape[0] < row.shape[1]:
                cut = ref.shape[0]
                row = jnp.where(lead, row[:, :cut], row[:, cut:])
            ref[...] = row.reshape(ref.shape)
        pieces = expand_bias_ref.shape[0] // small_ref.shape[1]
        width = small_ref.shape[1]
        for k in range(pieces):
            even = small_ref[8 + k : 9 + k, :]
            odd = small_ref[8 + pieces + k : 9 + pieces + k, :]
            expand_bias_ref[k * width : (k + 1) * width] = jnp.where(lead, even, odd).reshape(width)


def unpack(total, layer, inputs, sums, small, length, heads, counts):
    width = inputs.shape[1]
    depth = layer.shape[1]
    high_counts = (counts[0] // 16, counts[1] // 16, counts[1] // 16)

    def whole(shape):
        return pl.BlockSpec(shape, lambda i: (0,) * len(shape))

    def rows(columns):
        return pl.BlockSpec((UNPACK_ROWS, columns), lambda i: (i, 0))

    shapes = [
        ((length, depth), bf16),
        ((length, 1, width), f32),
        ((3, depth, width), f32),
        ((width, depth), f32),
        ((CHUNK, 2 * CHUNK), f32),
        ((2 * CHUNK, CHUNK), f32),
        ((heads, counts[0]), f32),
        ((heads, counts[1]), f32),
        ((heads, counts[1]), f32),
        ((2, width), f32),
        ((depth,), f32),
        ((depth,), f32),
        ((depth,), f32),
        ((width,), f32),
        ((width,), f32),
        ((depth,), f32),
        ((2 * CHUNK,), f32),
    ]
    return pl.pallas_call(
        partial(unpack_kernel, high_counts=high_counts),
        grid=(CHUNKS,),
        in_specs=[
            pl.BlockSpec((CHUNK, CHUNK), lambda i: (i, 0)),
            rows(depth),
            rows(width),
            whole(sums.shape),
            whole(small.shape),
        ],
        out_specs=[
            rows(depth),
            pl.BlockSpec((UNPACK_ROWS, 1, width), lambda i: (i, 0, 0)),
            pl.BlockSpec((2, depth, width), lambda i: (jnp.minimum(i, 1), 0, 0)),
            whole((width, depth)),
            pl.BlockSpec((CHUNK, CHUNK), lambda i: (0, jnp.clip(i - 2, 0, 1))),
            pl.BlockSpec((CHUNK, CHUNK), lambda i: (jnp.clip(i - 4, 0, 1), 0)),
            *(whole(shape) for shape, _ in shapes[6:]),
        ],
        out_shape=[jax.ShapeDtypeStruct(shape, kind) for shape, kind in shapes],
        compiler_params=pltpu.CompilerParams(vmem_limit_bytes=vmem_limit),
        name="unpack",
    )(total, layer, inputs, sums, small)


def feed_kernel(
    context_ref,
    context_away_ref,
    token_ref,
    cotangent_ref,
    valid_ref,
    output_ref,
    output_away_ref,
    expand_ref,
    expand_away_ref,
    reduce_ref,
    reduce_away_ref,
    expand_bias_ref,
    expand_bias_away_ref,
    output_bias_ref,
    first_gain_ref,
    first_shift_ref,
    reduce_bias_ref,
    second_gain_ref,
    second_shift_ref,
    layer_ref,
    grad_ref,
    expand_grad_ref,
    expand_grad_away_ref,
    reduce_grad_ref,
    reduce_grad_away_ref,
    small_ref,
    input_buf,
    norm_buf,
    hat_buf,
    inverse_buf,
    total_buf,
    reduced_buf,
    active_buf,
    slope_buf,
    before_buf,
    vector_ref,
    bias_buf,
    *,
    pieces,
    tiles,
):
    rows, width = token_ref.shape
    step = pl.program_id(0)
    piece = step % (2 * pieces)

    def vector(n):
        return vector_ref[n : n + 1, :]

    def for_strips(body, sums, strip_rows):
        def run(n, carry):
            at = pl.ds(pl.multiple_of(n * strip_rows, STRIP), strip_rows)
            return tuple(
                old + jnp.sum(new.reshape(strip_rows // 8, 8, width), axis=0)
                for old, new in zip(carry, body(at))
            )

        start = tuple(jnp.zeros((8, width), f32) for _ in range(sums))
        done = lax.fori_loop(0, rows // strip_rows, run, start)
        return [jnp.sum(part, axis=0, keepdims=True) for part in done]

    def mean(values):
        return jnp.sum(values, axis=-1, keepdims=True) * (1.0 / width)

    @pl.when(step == 0)
    def _():
        small_ref[...] = jnp.zeros_like(small_ref)
        for n, ref in enumerate(
            (
                output_bias_ref,
                first_gain_ref,
                first_shift_ref,
                reduce_bias_ref,
                second_gain_ref,
                second_shift_ref,
            )
        ):
            vector_ref[n : n + 1, :] = ref[...].astype(f32).reshape(1, width)
        bias = expand_bias_ref[...].astype(f32).reshape(1, -1)
        for k in range(pieces):
            cols = slice(k * expand_ref.shape[1], (k + 1) * expand_ref.shape[1])
            bias_buf[k : k + 1, :] = bias[:, cols]
            bias_buf[pieces + k : pieces + k + 1, :] = expand_bias_away_ref[0:1, cols]
        total_buf[...] = dot_f32(context_ref[...], output_ref[...]) + dot_f32(
            context_away_ref[...], output_away_ref[...]
        )

        def body(at):
            values = token_ref[at, :].astype(f32) + (total_buf[at, :] + vector(0))
            centered = values - mean(values)
            inverse = lax.rsqrt(mean(centered * centered) + norm_epsilon)
            hat = centered * inverse
            norm = hat * vector(1) + vector(2)
            hat_buf[at, :] = hat
            inverse_buf[at, :] = jnp.broadcast_to(inverse, (rows, LANES))
            norm_buf[at, :] = norm
            input_buf[at, :] = norm.astype(bf16)
            total_buf[at, :] = norm + vector(3)
            return ()

        for_strips(body, 0, rows)

    def forward(expand, reduce):
        for start, size in tiles:
            at = slice(start, start + size)
            before = dot_f32(input_buf[at, :], expand[...]) + bias_buf[pl.ds(piece, 1), :]
            phi = 0.5 * lax.erf(before * 0.7071067811865476) + 0.5
            slope_buf[piece, at, :] = phi + before * (
                0.3989422804014327 * jnp.exp(-0.5 * (before * before))
            )
            active = (before * phi).astype(bf16)
            active_buf[piece, at, :] = active
            total_buf[at, :] += dot_f32(active, reduce[...])

    pl.when(step < pieces)(lambda: forward(expand_ref, reduce_ref))
    pl.when((step >= pieces) & (step < 2 * pieces))(
        lambda: forward(expand_away_ref, reduce_away_ref)
    )

    @pl.when(step == 2 * pieces)
    def _():
        def body(at):
            values = total_buf[at, :]
            valid = valid_ref[at, 0:1]
            centered = values - mean(values)
            inverse = lax.rsqrt(mean(centered * centered) + norm_epsilon)
            hat = centered * inverse
            layer_ref[at, :] = (valid * (hat * vector(4) + vector(5))).astype(bf16)
            grad_out = jnp.where(valid > 0, cotangent_ref[at, :].astype(f32), 0.0)
            grad_hat = grad_out * vector(4)
            mixed = inverse * (grad_hat - mean(grad_hat) - hat * mean(grad_hat * hat))
            low = mixed.astype(bf16)
            reduced_buf[at, :] = low
            total_buf[at, :] = mixed
            return grad_out * hat, grad_out, low.astype(f32)

        for n, part in enumerate(for_strips(body, 3, FEED_STRIP)):
            small_ref[n : n + 1, :] = part

    def backward(expand, reduce):
        sums = None
        for start, size in tiles:
            at = slice(start, start + size)
            grad_active = lax.dot_general(
                reduced_buf[at, :], reduce[...], (((1,), (1,)), ((), ())), preferred_element_type=f32
            )
            before = (grad_active * slope_buf[piece, at, :]).astype(bf16)
            before_buf[piece, at, :] = before
            part = jnp.sum(before.astype(f32), axis=0, keepdims=True)
            sums = part if sums is None else sums + part
            total_buf[at, :] += lax.dot_general(
                before, expand[...], (((1,), (1,)), ((), ())), preferred_element_type=f32
            )
        mp_index = lax.axis_index("mp")
        side = jnp.where(piece < pieces, mp_index, 1 - mp_index)
        small_ref[pl.ds(8 + side * pieces + lax.rem(piece, pieces), 1), :] = sums

    pl.when((step >= 2 * pieces) & (step < 3 * pieces))(lambda: backward(expand_ref, reduce_ref))
    pl.when((step >= 3 * pieces) & (step < 4 * pieces))(
        lambda: backward(expand_away_ref, reduce_away_ref)
    )

    @pl.when(step == 4 * pieces)
    def _():
        def body(at):
            grad_first = total_buf[at, :]
            hat = hat_buf[at, :]
            grad_hat = grad_first * vector(1)
            inverse = inverse_buf[at, 0:1]
            inner = inverse * (grad_hat - mean(grad_hat) - hat * mean(grad_hat * hat))
            low = inner.astype(bf16)
            grad_ref[at, :] = low
            return grad_first * hat, grad_first, low.astype(f32)

        for n, part in enumerate(for_strips(body, 3, rows)):
            small_ref[n + 3 : n + 4, :] = part

    def weights(expand_grad, reduce_grad):
        reduce_grad[...] = lax.dot_general(
            active_buf[piece], reduced_buf[...], (((0,), (0,)), ((), ())), preferred_element_type=f32
        ).astype(bf16)
        expand_grad[...] = lax.dot_general(
            input_buf[...], before_buf[piece], (((0,), (0,)), ((), ())), preferred_element_type=f32
        ).astype(bf16)

    pl.when((step >= 4 * pieces) & (step < 5 * pieces))(
        lambda: weights(expand_grad_ref, reduce_grad_ref)
    )
    pl.when(step >= 5 * pieces)(lambda: weights(expand_grad_away_ref, reduce_grad_away_ref))


def feed(
    context,
    context_away,
    tokens,
    cotangent,
    valid,
    output,
    output_away,
    expand,
    expand_away,
    reduce,
    reduce_away,
    expand_bias,
    expand_bias_away,
    vectors,
):
    rows, width = context_away.shape[0], tokens.shape[1]
    hidden = expand.shape[1]
    size = FEED_PIECE
    pieces = hidden // size
    split = round_up(rows // 2, STRIP)
    tiles = ((0, rows),)

    def once(array):
        zeros = (0,) * array.ndim
        return pl.BlockSpec(array.shape, lambda i: zeros, pipeline_mode=pl.Buffered(1))

    def mine(array):
        return pl.BlockSpec(
            (rows, array.shape[1]),
            lambda i: (lax.axis_index("mp"), 0),
            pipeline_mode=pl.Buffered(1),
        )

    def place(first, i):
        at = lax.rem(i, 2 * pieces) - first
        at = jnp.clip(at, 0, pieces - 1)
        return jnp.where(i < 4 * pieces, at, pieces - 1)

    def grad_place(first, i):
        return jnp.clip(i - 4 * pieces - first, 0, pieces - 1)

    wide = lambda first: pl.BlockSpec((width, size), lambda i: (0, place(first, i)))
    tall = lambda first: pl.BlockSpec((size, width), lambda i: (place(first, i), 0))
    wide_grad = lambda first: pl.BlockSpec((width, size), lambda i: (0, grad_place(first, i)))
    tall_grad = lambda first: pl.BlockSpec((size, width), lambda i: (grad_place(first, i), 0))
    whole = lambda shape: pl.BlockSpec(
        shape, lambda i: (0,) * len(shape), pipeline_mode=pl.Buffered(1)
    )
    full = jax.ShapeDtypeStruct((rows, width), bf16)
    return pl.pallas_call(
        partial(feed_kernel, pieces=pieces, tiles=tiles),
        grid=(6 * pieces,),
        in_specs=[
            mine(context),
            once(context_away),
            mine(tokens),
            mine(cotangent),
            mine(valid),
            once(output),
            once(output_away),
            wide(0),
            wide(pieces),
            tall(0),
            tall(pieces),
            once(expand_bias),
            once(expand_bias_away),
            *(once(vector) for vector in vectors),
        ],
        out_specs=[
            whole((rows, width)),
            whole((rows, width)),
            wide_grad(0),
            wide_grad(pieces),
            tall_grad(0),
            tall_grad(pieces),
            whole((16, width)),
        ],
        out_shape=[
            full,
            full,
            jax.ShapeDtypeStruct((width, hidden), bf16),
            jax.ShapeDtypeStruct((width, hidden), bf16),
            jax.ShapeDtypeStruct((hidden, width), bf16),
            jax.ShapeDtypeStruct((hidden, width), bf16),
            jax.ShapeDtypeStruct((16, width), f32),
        ],
        scratch_shapes=[
            pltpu.VMEM((rows, width), bf16),
            pltpu.VMEM((rows, width), f32),
            pltpu.VMEM((rows, width), f32),
            pltpu.VMEM((rows, LANES), f32),
            pltpu.VMEM((rows, width), f32),
            pltpu.VMEM((rows, width), bf16),
            pltpu.VMEM((2 * pieces, rows, size), bf16),
            pltpu.VMEM((2 * pieces, rows, size), f32),
            pltpu.VMEM((2 * pieces, rows, size), bf16),
            pltpu.VMEM((8, width), f32),
            pltpu.VMEM((2 * pieces, size), f32),
        ],
        compiler_params=pltpu.CompilerParams(vmem_limit_bytes=vmem_limit),
        name="feed",
    )(
        context,
        context_away,
        tokens,
        cotangent,
        valid,
        output,
        output_away,
        expand,
        expand_away,
        reduce,
        reduce_away,
        expand_bias,
        expand_bias_away,
        *vectors,
    )


def swap(array):
    return lax.ppermute(array, "mp", [(0, 1), (1, 0)])


def partner(array, count, bit):
    return lax.ppermute(array, "dp", [(i, i ^ bit) for i in range(count)])


def sum_rows_over_dp(array, count):
    place = lax.axis_index("dp")
    bits = []
    bit = 1
    while bit < count:
        mine = (place // bit) % 2
        halves = array.reshape((2, array.shape[0] // 2) + array.shape[1:])
        sent = lax.dynamic_index_in_dim(halves, 1 - mine, 0, keepdims=False)
        kept = lax.dynamic_index_in_dim(halves, mine, 0, keepdims=False)
        array = kept + partner(sent, count, bit)
        bits.append(bit)
        bit *= 2
    for bit in reversed(bits):
        lead = (place // bit) % 2 == 0
        other = partner(array, count, bit)
        array = jnp.concatenate(
            [jnp.where(lead, array, other), jnp.where(lead, other, array)], axis=0
        )
    return array


def sum_small(arrays, count, over_mp):
    sizes = [a.size for a in arrays]
    total = sum(sizes)
    flat = jnp.concatenate([a.reshape(-1) for a in arrays])
    flat = jnp.pad(flat, (0, round_up(total, 1024) - total)).reshape(-1, LANES)
    if over_mp:
        flat = flat + swap(flat)
    bit = 1
    while bit < count:
        flat = flat + partner(flat, count, bit)
        bit *= 2
    flat = flat.reshape(-1)
    outs = []
    start = 0
    for array, size in zip(arrays, sizes):
        outs.append(flat[start : start + size].reshape(array.shape))
        start += size
    return outs


def per_device(
    dp_count,
    tokens,
    cotangent,
    long_flag,
    token_mask,
    bucket_line,
    bucket_across,
    bucket_down,
    project_weight,
    project_bias,
    table_line,
    table_across,
    table_down,
    output_weight,
    output_bias,
    first_gain,
    first_shift,
    expand_weight,
    expand_bias,
    reduce_weight,
    reduce_bias,
    second_gain,
    second_shift,
):
    length = tokens.shape[1]
    width = project_weight.shape[2]
    heads = table_line.shape[1]
    counts = (table_line.shape[0], table_across.shape[0])
    rows = round_up(length, BLOCK_ROWS)
    half_rows = rows // 2
    keys = round_up(length, 3 * LANES)
    mp_index = lax.axis_index("mp")
    lead = mp_index == 0

    def own_rows(array):
        return lax.dynamic_slice_in_dim(array, mp_index * half_rows, half_rows, 0)

    def in_order(mine, other):
        return jnp.where(lead, mine, other), jnp.where(lead, other, mine)


    (
        query,
        key_wide,
        key_turned,
        value_ones,
        value_turned,
        padded,
        plane,
        down,
        valid_rows,
        expand_quarter,
    ) = prepare(
        tokens[0],
        project_weight,
        project_bias,
        (bucket_line, bucket_across, bucket_down),
        long_flag,
        token_mask,
        expand_weight,
        rows,
        keys,
        counts[0],
    )
    (
        exps,
        context,
        inverse,
        context_away,
        expand_away,
        output_away,
        reduce_away,
        expand_bias_away,
    ) = attend(
        query,
        key_turned,
        value_ones,
        plane,
        down,
        (table_line.T, table_across.T, table_down.T),
        expand_bias,
        expand_quarter,
        output_weight,
        reduce_weight,
    )

    (
        layer_mine,
        grad_mine,
        expand_own,
        expand_sent,
        reduce_own,
        reduce_sent,
        small,
    ) = feed(
        context,
        context_away,
        padded,
        cotangent[0],
        valid_rows,
        output_weight,
        output_away,
        expand_weight,
        expand_away,
        reduce_weight,
        reduce_away,
        expand_bias,
        expand_bias_away,
        (output_bias, first_gain, first_shift, reduce_bias, second_gain, second_shift),
    )
    if dp_count == 16 and expand_own.shape == (CHUNK, 2 * CHUNK):
        total, layer_full, input_full, sums, small = finish(
            exps,
            inverse,
            plane,
            down,
            context,
            query,
            padded,
            grad_mine,
            layer_mine,
            value_turned,
            key_wide,
            project_weight,
            output_weight,
            (expand_own, expand_sent),
            (reduce_own, reduce_sent),
            small,
            counts,
        )
        (
            layer_out,
            input_grad,
            project_weight_grad,
            output_weight_grad,
            expand_weight_grad,
            reduce_weight_grad,
            line_grad,
            across_grad,
            down_grad,
            project_bias_grad,
            second_gain_grad,
            second_shift_grad,
            reduce_bias_grad,
            first_gain_grad,
            first_shift_grad,
            output_bias_grad,
            expand_bias_grad,
        ) = unpack(total, layer_full, input_full, sums, small, length, heads, counts)
        layer_out = layer_out[None]
        input_grad = input_grad.reshape(1, length, width)
        table_grads = (line_grad.T, across_grad.T, down_grad.T)
    else:
        layer_out = jnp.concatenate(in_order(layer_mine, swap(layer_mine)))[None, :length]
        grad_attended = jnp.concatenate(in_order(grad_mine, swap(grad_mine)))
        output_weight_grad = jnp.einsum(
            "le,lf->ef", context, grad_attended, preferred_element_type=f32
        ).astype(bf16)
        grad_context = jnp.einsum(
            "lf,ef->le", grad_attended, output_weight, preferred_element_type=f32
        )
        grad_scaled = (grad_context * inverse).astype(bf16)
        grad_scores, grad_query, grad_key, grad_value = attend_back(
            exps, grad_scaled, context, query, value_turned, key_wide
        )
        grad_key = grad_key.reshape(width, keys)[:, :rows].T.astype(bf16)
        grad_value = grad_value.reshape(width, keys)[:, :rows].T.astype(bf16)
        triple = jnp.stack([grad_query, grad_key, grad_value])
        project_weight_grad = jnp.einsum(
            "ld,kle->kde", padded[:rows], triple, preferred_element_type=f32
        ).astype(bf16)
        project_bias_grad = jnp.stack(
            [jnp.sum(grad_query, axis=0, dtype=f32), jnp.sum(grad_value, axis=0, dtype=f32)]
        )
        input_part = jnp.einsum("kle,kde->ld", triple, project_weight, preferred_element_type=f32)
        input_part = lax.dynamic_update_slice_in_dim(
            input_part,
            own_rows(input_part) + grad_mine.astype(f32),
            mp_index * half_rows,
            0,
        )
        sent = jnp.where(lead, input_part[:, width:], input_part[:, :width]).astype(bf16)
        own = jnp.where(lead, input_part[:, :width], input_part[:, width:])
        input_grad = (own + swap(sent).astype(f32))[None, :length]
        table_grads = table_sums(grad_scores, plane, down, counts)
        reduce_weight_grad = sum_rows_over_dp(reduce_own + swap(reduce_sent), dp_count)
        expand_weight_grad = sum_rows_over_dp(expand_own + swap(expand_sent), dp_count)
        output_weight_grad = sum_rows_over_dp(output_weight_grad, dp_count)
        project_weight_grad = sum_rows_over_dp(
            project_weight_grad.reshape(-1, width), dp_count
        ).reshape(project_weight.shape)
        (small,) = sum_small([small], dp_count, True)
        bias_rows = expand_bias.size // small.shape[1]
        bias_rows = lax.dynamic_slice_in_dim(small, 8 + mp_index * bias_rows, bias_rows, 0)
        expand_bias_grad = bias_rows.reshape(-1)
        (
            second_gain_grad,
            second_shift_grad,
            reduce_bias_grad,
            first_gain_grad,
            first_shift_grad,
            output_bias_grad,
        ) = (small[n] for n in range(6))
        first_gain_grad = lax.dynamic_slice_in_dim(first_gain_grad, mp_index * width, width, 0)
        first_shift_grad = lax.dynamic_slice_in_dim(first_shift_grad, mp_index * width, width, 0)
        table_grads, project_bias_grad = sum_small(
            [table_grads, project_bias_grad], dp_count, False
        )
        cuts = (counts[0], counts[0] + counts[1])
        table_grads = (
            table_grads[: cuts[0]],
            table_grads[cuts[0] : cuts[1]],
            table_grads[cuts[1] :],
        )
    return (
        layer_out,
        input_grad,
        project_weight_grad.astype(f32),
        project_bias_grad,
        *table_grads,
        output_weight_grad.astype(f32),
        output_bias_grad,
        first_gain_grad,
        first_shift_grad,
        expand_weight_grad.astype(f32),
        expand_bias_grad,
        reduce_weight_grad.astype(f32),
        reduce_bias_grad,
        second_gain_grad,
        second_shift_grad,
    )


def solution(mesh):
    placed = (
        P("dp", None, None),
        P("dp", None, None),
        P("dp"),
        P("dp", None),
        P("dp", None, None),
        P("dp", None, None),
        P("dp", None, None),
        P(None, None, "mp"),
        P(None, "mp"),
        P(None, "mp"),
        P(None, "mp"),
        P(None, "mp"),
        P("mp", None),
        P(),
        P(),
        P(),
        P(None, "mp"),
        P("mp"),
        P("mp", None),
        P(),
        P(),
        P(),
    )
    return jax.shard_map(
        partial(per_device, mesh.shape["dp"]),
        mesh=mesh,
        in_specs=placed,
        out_specs=(
            P("dp", None, None),
            P("dp", None, "mp"),
            P(None, None, "mp"),
            P(None, "mp"),
            P(None, "mp"),
            P(None, "mp"),
            P(None, "mp"),
            P("mp", None),
            P(),
            P("mp"),
            P("mp"),
            P(None, "mp"),
            P("mp"),
            P("mp", None),
            P(),
            P(),
            P(),
        ),
        check_vma=False,
    )
```

```python
from functools import partial

import jax
import jax.numpy as jnp
from jax import lax
from jax.experimental import pallas as pl
from jax.experimental.pallas import tpu as pltpu
from jax.sharding import PartitionSpec as P

LONG = 1089
SHORT = 709
HEAD = 64
LANES = 128
STRIP = 16
BLOCK_ROWS = 224
FEED_PIECE = 768
FEED_STRIP = 112
TABLE_STRIPS = 2
ATTEND_STRIPS = 7

large_negative = -1000000000.0
norm_epsilon = 1e-05
vmem_limit = 56 * 2**20
FINISH_VMEM = 62 * 2**20
bf16 = jnp.bfloat16
f32 = jnp.float32


def round_up(value, step):
    return (value + step - 1) // step * step


def whole_spec(array):
    zeros = (0,) * array.ndim
    return pl.BlockSpec(array.shape, lambda i: zeros)


def dot_f32(left, right):
    return jnp.dot(left, right, preferred_element_type=f32)


def gather_lanes(values, index):
    dims = lax.GatherDimensionNumbers(
        offset_dims=(),
        collapsed_slice_dims=(1,),
        start_index_map=(1,),
        operand_batching_dims=(0,),
        start_indices_batching_dims=(0,),
    )
    return lax.gather(
        values,
        index[..., None],
        dims,
        slice_sizes=(1, 1),
        mode=lax.GatherScatterMode.PROMISE_IN_BOUNDS,
    )


def quarter_rows(ref, quarter):
    count = ref.shape[0] // 4
    return pl.ds(pl.multiple_of(quarter * count, STRIP), count)


def prepare_kernel(
    token_ref,
    weight_ref,
    bias_ref,
    line_ref,
    across_ref,
    down_ref,
    flag_ref,
    mask_ref,
    expand_ref,
    query_ref,
    key_ref,
    key_turned_ref,
    value_ref,
    value_turned_ref,
    token_out_ref,
    plane_ref,
    down_out_ref,
    valid_ref,
    quarter_ref,
    row_ref,
    send_sem,
    recv_sem,
    *,
    length,
    line_count,
):
    step = pl.program_id(0)
    across_mp = {"mp": 1 - lax.axis_index("mp")}
    fetch = pltpu.make_async_remote_copy(
        src_ref=expand_ref.at[quarter_rows(expand_ref, lax.axis_index("dp") % 4), :],
        dst_ref=quarter_ref,
        send_sem=send_sem,
        recv_sem=recv_sem,
        device_id=across_mp,
        device_id_type=pl.DeviceIdType.MESH,
    )

    @pl.when(step == 0)
    def _():
        barrier = pltpu.get_barrier_semaphore()
        pl.semaphore_signal(
            barrier, inc=1, device_id=across_mp, device_id_type=pl.DeviceIdType.MESH
        )
        pl.semaphore_wait(barrier, 1)
        fetch.start()
        limit = jnp.where(flag_ref[0] > 0, LONG, SHORT)
        position = lax.broadcasted_iota(jnp.int32, (1, length), 1)
        row_ref[...] = jnp.zeros_like(row_ref)
        row_ref[0:1, :length] = jnp.where((mask_ref[...] > 0) & (position < limit), 1.0, 0.0)

    rows = token_ref.shape[0]
    keys = plane_ref.shape[1]
    place = pl.program_id(0) * rows + lax.broadcasted_iota(jnp.int32, token_ref.shape, 0)
    token = jnp.where(place < length, token_ref[...].astype(f32), 0.0).astype(bf16)
    token_out_ref[...] = token
    bias = bias_ref[...].astype(f32)
    query = (dot_f32(token, weight_ref[0]) + bias[0:1, :]).astype(bf16)
    query_ref[...] = (query.astype(f32) * 0.125).astype(bf16)
    key = dot_f32(token, weight_ref[1])
    value = dot_f32(token, weight_ref[2]) + bias[1:2, :]
    away = jnp.where(row_ref[0:1, :] > 0, 0, line_count)
    inside = pl.program_id(0) * rows + lax.broadcasted_iota(jnp.int32, (rows, length), 0) < length
    line = line_ref[...].reshape(rows, length)
    across = across_ref[...].reshape(rows, length)
    down = down_ref[...].reshape(rows, length)
    plane = jnp.where(inside, line | (across << 8), 0) | away[:, :length]
    plane_ref[:, :length] = plane.astype(jnp.int16)
    plane_ref[:, length:] = jnp.full((rows, keys - length), line_count, jnp.int16)
    here = pl.ds(pl.multiple_of(step * rows, LANES), rows)
    valid_ref[...] = jnp.broadcast_to(row_ref[0:1, here], (LANES, rows)).T
    down_out_ref[:, :length] = jnp.where(inside, down, 0).astype(jnp.int16)
    down_out_ref[:, length:] = jnp.zeros((rows, keys - length), jnp.int16)
    lane_first = lax.broadcasted_iota(jnp.int32, (rows, LANES), 1) < HEAD
    row_first = lax.broadcasted_iota(jnp.int32, (LANES, rows), 0) < HEAD
    for p in range(key.shape[1] // LANES):
        cols = slice(p * LANES, (p + 1) * LANES)
        key_pair, value_pair = key[:, cols], value[:, cols]
        key_turned, value_turned = key_pair.T, value_pair.T
        for u in range(2):
            h = 2 * p + u
            lane_own = lane_first if u == 0 else ~lane_first
            row_own = row_first if u == 0 else ~row_first
            key_ref[h] = jnp.where(lane_own, key_pair, 0.0).astype(bf16)
            value_ref[h] = jnp.where(lane_own, value_pair, 1.0).astype(bf16)
            key_turned_ref[h] = jnp.where(row_own, key_turned, 0.0).astype(bf16)
            value_turned_ref[h] = jnp.where(row_own, value_turned, 0.0).astype(bf16)
    pl.when(step == pl.num_programs(0) - 1)(fetch.wait)


def prepare(tokens, weight, bias, buckets, flag, token_mask, expand, row_count, keys, line_count):
    length, depth = tokens.shape
    width = weight.shape[2]
    heads = width // HEAD
    block = 3 * LANES
    row = pl.BlockSpec((block, width), lambda i: (i, 0))
    deep_row = pl.BlockSpec((block, depth), lambda i: (i, 0))
    wide = pl.BlockSpec((heads, block, LANES), lambda i: (0, i, 0))
    turned = pl.BlockSpec((heads, LANES, block), lambda i: (0, 0, i))
    bucket = pl.BlockSpec((block, 1, length), lambda i: (i, 0, 0))
    packed = pl.BlockSpec((block, keys), lambda i: (i, 0))
    wide_shape = jax.ShapeDtypeStruct((heads, keys, LANES), bf16)
    turned_shape = jax.ShapeDtypeStruct((heads, LANES, keys), bf16)
    packed_shape = jax.ShapeDtypeStruct((row_count, keys), jnp.int16)
    return pl.pallas_call(
        partial(prepare_kernel, length=length, line_count=line_count),
        grid=(keys // block,),
        in_specs=[
            deep_row,
            whole_spec(weight),
            whole_spec(bias),
            bucket,
            bucket,
            bucket,
            pl.BlockSpec(memory_space=pltpu.SMEM),
            whole_spec(token_mask),
            pl.BlockSpec(memory_space=pl.ANY),
        ],
        out_specs=[
            row,
            wide,
            turned,
            wide,
            turned,
            deep_row,
            packed,
            packed,
            pl.BlockSpec((block, LANES), lambda i: (i, 0)),
            pl.BlockSpec(memory_space=pl.ANY),
        ],
        out_shape=[
            jax.ShapeDtypeStruct((keys, width), bf16),
            wide_shape,
            turned_shape,
            wide_shape,
            turned_shape,
            jax.ShapeDtypeStruct((keys, depth), bf16),
            packed_shape,
            packed_shape,
            jax.ShapeDtypeStruct((keys, LANES), f32),
            jax.ShapeDtypeStruct((expand.shape[0] // 4, expand.shape[1]), bf16),
        ],
        scratch_shapes=[
            pltpu.VMEM((8, keys), f32),
            pltpu.SemaphoreType.DMA,
            pltpu.SemaphoreType.DMA,
        ],
        compiler_params=pltpu.CompilerParams(
            vmem_limit_bytes=vmem_limit, collective_id=2, has_side_effects=True
        ),
        name="prepare",
    )(
        tokens,
        weight,
        bias,
        *(index.reshape(length, 1, length) for index in buckets),
        flag,
        token_mask,
        expand,
    )


def attend_kernel(
    query_ref,
    key_ref,
    value_ref,
    plane_ref,
    down_ref,
    line_table_ref,
    across_table_ref,
    down_table_ref,
    expand_bias_ref,
    expand_quarter_ref,
    output_ref,
    reduce_ref,
    exp_out_ref,
    context_ref,
    inverse_ref,
    context_away_ref,
    expand_away_ref,
    output_away_ref,
    reduce_away_ref,
    bias_away_ref,
    score_ref,
    exp_ref,
    send_ref,
    table_ref,
    bias_ref,
    exp_sem,
    local_sem,
    send_sem,
    recv_sem,
):
    _, heads, rows, keys = exp_ref.shape
    step = pl.program_id(0)
    turn_rows = ATTEND_STRIPS * STRIP
    turns = rows // turn_rows
    place = lax.axis_index("dp")
    across_mp = {"mp": 1 - lax.axis_index("mp")}
    across = {bit: {"dp": place + bit * (1 - 2 * ((place // bit) % 2))} for bit in (1, 2)}

    def remote(src, dst, n, device):
        return pltpu.make_async_remote_copy(
            src_ref=src,
            dst_ref=dst,
            send_sem=send_sem.at[n],
            recv_sem=recv_sem.at[n],
            device_id=device,
            device_id_type=pl.DeviceIdType.MESH,
        )

    arrays = (
        (expand_quarter_ref, expand_away_ref),
        (output_ref, output_away_ref),
        (reduce_ref, reduce_away_ref),
    )
    quarter = place % 4
    other_chip = (place + 2) % 4
    other_core = quarter + 1 - 2 * (quarter % 2)
    third = (other_core + 2) % 4

    def rows_of(n, which):
        away = arrays[n][1]
        return away.at[quarter_rows(away, which), :]

    def fetch(n):
        ref = arrays[n][0]
        return remote(ref.at[quarter_rows(ref, quarter), :], rows_of(n, quarter), n, across_mp)

    def pass_on(n, stage):
        source = expand_quarter_ref if n == 0 and stage < 2 else rows_of(n, quarter)
        if stage == 0:
            return remote(source, rows_of(n, quarter), 3 + n, across[2])
        if stage == 1:
            return remote(source, rows_of(n, quarter), 6 + n, across[1])
        return remote(rows_of(n, other_chip), rows_of(n, other_chip), 9 + n, across[1])

    def arrival(n, stage):
        region = rows_of(n, (other_chip, other_core, third)[stage])
        return remote(region, region, 3 + 3 * stage + n, across_mp)

    def exp_copy(which, turn):
        half = lax.rem(which + 1 - lax.axis_index("mp"), 2)
        here = pl.ds(pl.multiple_of(turn * turn_rows, STRIP), turn_rows)
        there = pl.ds(pl.multiple_of(half * rows + turn * turn_rows, STRIP), turn_rows)
        return pltpu.make_async_copy(
            exp_ref.at[which, :, here, :], exp_out_ref.at[:, there, :], exp_sem.at[which, turn]
        )

    keep = pltpu.make_async_copy(expand_quarter_ref, rows_of(0, quarter), local_sem)
    context_swap = remote(send_ref, context_away_ref, 12, across_mp)
    bias_swap = remote(bias_ref, bias_away_ref, 13, across_mp)

    def event(n, stage):
        if stage == "fetched":
            fetch(n).wait_recv()
            pass_on(n, 0).start()
            pass_on(n, 1).start()
        else:
            arrival(n, 0).wait_recv()
            pass_on(n, 2).start()

    events = {
        (0, 2): ((1, "fetched"),),
        (1, 0): ((0, "passed"), (2, "fetched")),
        (1, 1): ((1, "passed"),),
    }

    @pl.when(step == 0)
    def _():
        barrier = pltpu.get_barrier_semaphore()
        for device in (across_mp, across[1], across[2]):
            pl.semaphore_signal(
                barrier, inc=1, device_id=device, device_id_type=pl.DeviceIdType.MESH
            )
        pl.semaphore_wait(barrier, 3)
        bias_ref[...] = jnp.broadcast_to(
            expand_bias_ref[...].astype(f32).reshape(1, -1), bias_ref.shape
        )
        bias_swap.start()
        for t, ref in enumerate((line_table_ref, across_table_ref, down_table_ref)):
            count = ref.shape[1]
            lanes = jnp.concatenate(
                [ref[...].astype(f32), jnp.full((heads, LANES - count), large_negative, f32)], axis=1
            )
            for h in range(heads):
                table_ref[t * heads + h] = jnp.broadcast_to(lanes[h : h + 1], (STRIP, LANES)).astype(
                    bf16
                )
        fetch(1).start()
        fetch(2).start()
        pass_on(0, 0).start()
        pass_on(0, 1).start()
        keep.start()

    for h in range(heads):
        pair = slice(h // 2 * LANES, (h // 2 + 1) * LANES)
        score_ref[h] = dot_f32(query_ref[:, pair], key_ref[h])

    lanes = [slice(c * LANES, (c + 1) * LANES) for c in range(keys // LANES)]

    def scores_of(at):
        scores = [[] for _ in range(heads)]
        for cols in lanes:
            packed = plane_ref[at, cols]
            bias = [None] * heads
            for t, index in enumerate(
                (packed & jnp.int16(255), packed >> jnp.int16(8), down_ref[at, cols])
            ):
                for h in range(heads):
                    found = gather_lanes(table_ref[t * heads + h], index).astype(f32)
                    bias[h] = found if t == 0 else bias[h] + found
            for h in range(heads):
                scores[h].append(score_ref[h, at, cols] + bias[h])
        return scores

    def exps_of(scores):
        exps = []
        for parts in scores:
            top = parts[0]
            for part in parts[1:]:
                top = jnp.maximum(top, part)
            top = jnp.max(top, axis=1, keepdims=True)
            exps.append([jnp.exp(part - top).astype(bf16) for part in parts])
        return exps

    def strips(n, carry):
        for (at_step, at_turn), pieces in events.items():

            @pl.when((step == at_step) & (n == at_turn))
            def _():
                for piece in pieces:
                    event(*piece)

        start = pl.multiple_of(n * turn_rows, STRIP)
        places = [pl.ds(start + k * STRIP, STRIP) for k in range(ATTEND_STRIPS)]
        scores = [scores_of(at) for at in places]
        exps = [exps_of(part) for part in scores]
        for at, part in zip(places, exps):
            for h in range(heads):
                for c, cols in enumerate(lanes):
                    exp_ref[step, h, at, cols] = part[h][c]
        exp_copy(step, n).start()
        return carry

    lax.fori_loop(0, turns, strips, 0)
    first = lax.broadcasted_iota(jnp.int32, (rows, LANES), 1) < HEAD
    for p in range(heads // 2):
        cols = slice(p * LANES, (p + 1) * LANES)
        even = dot_f32(exp_ref[step, 2 * p], value_ref[2 * p])
        odd = dot_f32(exp_ref[step, 2 * p + 1], value_ref[2 * p + 1])
        sums = jnp.where(first, pltpu.roll(even, HEAD, 1), pltpu.roll(odd, HEAD, 1))
        inverse = 1.0 / sums
        inverse_ref[:, cols] = inverse
        context = (jnp.where(first, even, odd) * inverse).astype(bf16)
        context_ref[:, cols] = context

        @pl.when(step == 0)
        def _():
            send_ref[:, cols] = context

    pl.when(step == 0)(context_swap.start)

    @pl.when(step == 1)
    def _():
        event(2, "passed")
        for which in range(2):
            for n in range(turns):
                exp_copy(which, n).wait()
        keep.wait()
        context_swap.wait()
        bias_swap.wait()
        for n in range(3):
            arrival(n, 1).wait_recv()
            arrival(n, 2).wait_recv()
            for stage in range(3):
                pass_on(n, stage).wait_send()
        fetch(1).wait_send()
        fetch(2).wait_send()


def attend(
    query,
    key_turned,
    value_ones,
    plane,
    down,
    tables,
    expand_bias,
    expand_quarter,
    output,
    reduce,
):
    heads, _, keys = key_turned.shape
    row_count = plane.shape[0]
    width = heads * HEAD
    half_rows = row_count // 2

    def half(i):
        return lax.rem(i + 1 - lax.axis_index("mp"), 2)

    anywhere = pl.BlockSpec(memory_space=pl.ANY)
    index_spec = pl.BlockSpec((half_rows, keys), lambda i: (half(i), 0))
    row_spec = pl.BlockSpec((half_rows, width), lambda i: (half(i), 0))
    return pl.pallas_call(
        attend_kernel,
        grid=(2,),
        in_specs=[
            row_spec,
            whole_spec(key_turned),
            whole_spec(value_ones),
            index_spec,
            index_spec,
            *(whole_spec(table) for table in tables),
            whole_spec(expand_bias),
            anywhere,
            anywhere,
            anywhere,
        ],
        out_specs=[
            anywhere,
            row_spec,
            row_spec,
            anywhere,
            anywhere,
            anywhere,
            anywhere,
            anywhere,
        ],
        out_shape=[
            jax.ShapeDtypeStruct((heads, row_count, keys), bf16),
            jax.ShapeDtypeStruct((row_count, width), bf16),
            jax.ShapeDtypeStruct((row_count, width), f32),
            jax.ShapeDtypeStruct((half_rows, width), bf16),
            jax.ShapeDtypeStruct((4 * expand_quarter.shape[0], expand_quarter.shape[1]), bf16),
            jax.ShapeDtypeStruct(output.shape, bf16),
            jax.ShapeDtypeStruct(reduce.shape, bf16),
            jax.ShapeDtypeStruct((8, expand_bias.size), f32),
        ],
        scratch_shapes=[
            pltpu.VMEM((heads, half_rows, keys), f32),
            pltpu.VMEM((2, heads, half_rows, keys), bf16),
            pltpu.VMEM((half_rows, width), bf16),
            pltpu.VMEM((3 * heads, STRIP, LANES), bf16),
            pltpu.VMEM((8, expand_bias.size), f32),
            pltpu.SemaphoreType.DMA((2, half_rows // (ATTEND_STRIPS * STRIP))),
            pltpu.SemaphoreType.DMA,
            pltpu.SemaphoreType.DMA((14,)),
            pltpu.SemaphoreType.DMA((14,)),
        ],
        compiler_params=pltpu.CompilerParams(
            vmem_limit_bytes=vmem_limit, collective_id=1, has_side_effects=True
        ),
        name="attend",
    )(
        query,
        key_turned,
        value_ones,
        plane,
        down,
        *tables,
        expand_bias,
        expand_quarter,
        output,
        reduce,
    )


def attend_back_kernel(
    exp_ref,
    grad_ref,
    context_ref,
    query_ref,
    value_ref,
    key_ref,
    grad_score_ref,
    grad_query_ref,
    grad_key_ref,
    grad_value_ref,
):
    heads, rows, _ = exp_ref.shape

    @pl.when(pl.program_id(0) == 0)
    def _():
        grad_key_ref[...] = jnp.zeros_like(grad_key_ref)
        grad_value_ref[...] = jnp.zeros_like(grad_value_ref)

    first = lax.broadcasted_iota(jnp.int32, (rows, LANES), 1) < HEAD
    for p in range(heads // 2):
        cols = slice(p * LANES, (p + 1) * LANES)
        grad = grad_ref[:, cols]
        product = grad.astype(f32) * context_ref[:, cols].astype(f32)
        query_turned = query_ref[:, cols].T
        grad_turned = grad.T
        grad_query = None
        for u in range(2):
            h = 2 * p + u
            half = slice(u * HEAD, (u + 1) * HEAD)
            own = first if u == 0 else ~first
            total = jnp.sum(jnp.where(own, product, 0.0), axis=1, keepdims=True)
            grad_exp = dot_f32(grad, value_ref[h])
            grad_score = (exp_ref[h].astype(f32) * (grad_exp - total)).astype(bf16)
            grad_score_ref[h] = grad_score
            part = dot_f32(grad_score, key_ref[h])
            grad_query = part if u == 0 else grad_query + part
            grad_key_ref[h] += dot_f32(query_turned[half], grad_score)
            grad_value_ref[h] += dot_f32(grad_turned[half], exp_ref[h])
        grad_query_ref[:, cols] = (grad_query * 0.125).astype(bf16)


def attend_back(exps, grad, context, query, value_turned, key_wide):
    heads, row_count, keys = exps.shape
    width = heads * HEAD
    row_spec = pl.BlockSpec((BLOCK_ROWS, width), lambda i: (i, 0))
    exp_spec = pl.BlockSpec((heads, BLOCK_ROWS, keys), lambda i: (0, i, 0))
    sum_spec = pl.BlockSpec((heads, HEAD, keys), lambda i: (0, 0, 0))
    return pl.pallas_call(
        attend_back_kernel,
        grid=(row_count // BLOCK_ROWS,),
        in_specs=[
            exp_spec,
            row_spec,
            row_spec,
            row_spec,
            whole_spec(value_turned),
            whole_spec(key_wide),
        ],
        out_specs=[exp_spec, row_spec, sum_spec, sum_spec],
        out_shape=[
            jax.ShapeDtypeStruct((heads, row_count, keys), bf16),
            jax.ShapeDtypeStruct((row_count, width), bf16),
            jax.ShapeDtypeStruct((heads, HEAD, keys), f32),
            jax.ShapeDtypeStruct((heads, HEAD, keys), f32),
        ],
        compiler_params=pltpu.CompilerParams(vmem_limit_bytes=vmem_limit),
        name="attend_back",
    )(exps, grad, context, query, value_turned, key_wide)


def table_strips(strips, sum_ref, heads, keys, high_counts):
    base = 0
    for t in range(3):
        shift = 8 if t == 1 else 0
        highs, lows = [], []
        for grad_of, plane_of, down_of in strips:
            for c in range(keys // LANES):
                cols = slice(c * LANES, (c + 1) * LANES)
                index = down_of(cols) if t == 2 else plane_of(cols)
                low = index & jnp.int16(15 << shift)
                high = index & jnp.int16(48 << shift)
                lows.append(
                    jnp.concatenate(
                        [
                            jnp.where(low == jnp.int16(x << shift), bf16(1), bf16(0))
                            for x in range(16)
                        ]
                    )
                )
                parts = []
                for x in range(high_counts[t]):
                    mask = high == jnp.int16(x << (4 + shift))
                    parts += [jnp.where(mask, grad_of(h, cols), bf16(0)) for h in range(heads)]
                highs.append(jnp.concatenate(parts))
        span = slice(base, base + high_counts[t] * heads * STRIP)
        sum_ref[span, :] += lax.dot_general(
            jnp.concatenate(highs, axis=1),
            jnp.concatenate(lows, axis=1),
            (((1,), (1,)), ((), ())),
            preferred_element_type=f32,
        )
        base = span.stop


def table_finish(sum_ref, out_ref, count):
    row_of_lane = lax.broadcasted_iota(jnp.int32, (STRIP, 16 * STRIP), 1) % STRIP
    same = row_of_lane == lax.broadcasted_iota(jnp.int32, (STRIP, 16 * STRIP), 0)
    for o in range(count):
        block = sum_ref[o * STRIP : (o + 1) * STRIP, :]
        out_ref[o : o + 1, :] = jnp.sum(jnp.where(same, block, 0.0), axis=0, keepdims=True)


def table_result(out, high_counts, heads):
    summed = jnp.sum(out.reshape(sum(high_counts), heads, 16, STRIP), axis=-1)
    return summed.transpose(0, 2, 1).reshape(-1, heads)


def table_kernel(grad_score_ref, plane_ref, down_ref, out_ref, sum_ref, *, high_counts):
    heads, rows, keys = grad_score_ref.shape
    step = pl.program_id(0)

    @pl.when(step == 0)
    def _():
        sum_ref[...] = jnp.zeros_like(sum_ref)

    def refs_at(start):
        at = pl.ds(pl.multiple_of(start, STRIP), STRIP)
        return (
            lambda h, cols: grad_score_ref[h, at, cols],
            lambda cols: plane_ref[at, cols],
            lambda cols: down_ref[at, cols],
        )

    def strips(r, carry):
        start = r * (TABLE_STRIPS * STRIP)
        table_strips(
            [refs_at(start + k * STRIP) for k in range(TABLE_STRIPS)],
            sum_ref,
            heads,
            keys,
            high_counts,
        )
        return carry

    lax.fori_loop(0, rows // (TABLE_STRIPS * STRIP), strips, 0)

    @pl.when(step == pl.num_programs(0) - 1)
    def _():
        table_finish(sum_ref, out_ref, out_ref.shape[0])


def table_sums(grad_scores, plane, down, counts):
    heads, row_count, keys = grad_scores.shape
    high_counts = (counts[0] // 16, counts[1] // 16, counts[1] // 16)
    high_rows = sum(high_counts) * heads
    index_spec = pl.BlockSpec((BLOCK_ROWS, keys), lambda i: (i, 0))
    out = pl.pallas_call(
        partial(table_kernel, high_counts=high_counts),
        grid=(row_count // BLOCK_ROWS,),
        in_specs=[
            pl.BlockSpec((heads, BLOCK_ROWS, keys), lambda i: (0, i, 0)),
            index_spec,
            index_spec,
        ],
        out_specs=pl.BlockSpec((high_rows, 16 * STRIP), lambda i: (0, 0)),
        out_shape=jax.ShapeDtypeStruct((high_rows, 16 * STRIP), f32),
        scratch_shapes=[pltpu.VMEM((high_rows * STRIP, 16 * STRIP), f32)],
        compiler_params=pltpu.CompilerParams(vmem_limit_bytes=vmem_limit),
        name="table_sums",
    )(grad_scores, plane, down)
    return table_result(out, high_counts, heads)


CHUNK = 768
CHUNKS = 6
LOCAL_CHUNKS = 2
PARTS = (CHUNK // 2, CHUNK // 4, CHUNK // 8, CHUNK // 16)
BITS = ((1, 2, 4, 8), (1, 4, 2, 8), (1, 2, 4, 8), (1, 4, 2, 8), (1, 2, 4, 8), (1, 4, 2, 8))
BACK_ROWS = 112
EXCHANGE = (
    ("b", 0, 0, 2), ("b", 0, 0, 3), ("b", 0, 0, 4), ("b", 1, 0, 5), ("b", 4, 1, 2), ("b", 6, 1, 3),
    ("b", 8, 1, 4), ("b", 9, 1, 5), ("b", 20, 2, 2), ("b", 22, 2, 3), ("p", 0, 3, 2), ("p", 2, 2, 4),
    ("p", 3, 2, 5), ("p", 3, 3, 3), ("p", 3, 0, 0), ("p", 3, 0, 1), ("t", 0, 4, 2), ("t", 1, 1, 0),
    ("t", 1, 1, 1), ("t", 2, 4, 3), ("t", 2, "small", 0), ("t", 3, 3, 4), ("t", 4, 5, 2),
    ("t", 6, 3, 5), ("t", 6, 2, 0), ("t", 6, 2, 1), ("t", 6, "small", 1), ("t", 8, 5, 3),
    ("t", 9, 4, 4), ("t", 10, 4, 5), ("t", 11, 6, 2), ("t", 11, "send", 0), ("t", 11, "small", 2),
    ("t", 12, 3, 1), ("t", 12, 3, 0), ("t", 13, 6, 3), ("t", 15, 5, 4), ("t", 16, "small", 3),
    ("t", 17, 5, 5), ("t", 17, 7, 3), ("t", 18, 7, 2), ("t", 19, 4, 1), ("t", 20, "small", 4),
    ("t", 21, 4, 0), ("t", 23, 6, 4), ("t", 24, 8, 2), ("t", 24, "input", 0), ("t", 25, 6, 5),
    ("t", 25, 9, 2), ("t", 25, "small", 5), ("t", 26, 8, 3), ("t", 26, "layer", 0), ("t", 27, 5, 1),
    ("t", 28, 9, 3), ("t", 29, 5, 0), ("t", 29, 7, 5), ("t", 29, 7, 4), ("t", 31, 6, 1),
    ("t", 33, 6, 0), ("e", 0, 8, 4), ("e", 0, 9, 4), ("e", 0, 8, 5), ("e", 0, 9, 5), ("e", 0, 7, 0),
    ("e", 0, 8, 0), ("e", 0, 7, 1), ("e", 0, 8, 1),
)


def plan_slots(phase, count):
    slots = [[] for _ in range(count)]
    for name, at, event, which in EXCHANGE:
        if name == phase:
            slots[at].append((event, which))
    return slots


def finish_kernel(
    exp_ref,
    inverse_ref,
    plane_ref,
    down_ref,
    context_ref,
    query_ref,
    token_ref,
    grad_ref,
    layer_ref,
    value_ref,
    key_ref,
    project_ref,
    output_ref,
    expand_ref,
    expand_away_ref,
    reduce_ref,
    reduce_away_ref,
    small_ref,
    total_ref,
    layer_out_ref,
    input_ref,
    small_out_ref,
    table_ref,
    score_ref,
    output_buf,
    grad_buf,
    value_buf,
    key_buf,
    context_buf,
    query_buf,
    token_buf,
    project_buf,
    ring_buf,
    inverse_buf,
    grad_key_buf,
    grad_value_buf,
    triple_buf,
    input_send_buf,
    input_recv_buf,
    input_buf,
    plane_buf,
    down_buf,
    sum_ref,
    own_buf,
    away_buf,
    core_buf,
    core_away_buf,
    first_buf,
    first_away_buf,
    y_buf,
    second_buf,
    third_buf,
    small_buf,
    small_recv_buf,
    table_buf,
    table_recv_buf,
    resident_sem,
    block_sem,
    ring_sem,
    load_sem,
    local_sem,
    out_sem,
    send_sem,
    recv_sem,
    wide_send_sem,
    wide_recv_sem,
    small_send_sem,
    small_recv_sem,
    table_send_sem,
    table_recv_sem,
    *,
    high_counts,
):
    heads, row_count, keys = exp_ref.shape
    width = heads * HEAD
    half_rows = row_count // 2
    rows = BACK_ROWS
    blocks = row_count // rows
    block_strips = rows // STRIP
    turns = row_count // (TABLE_STRIPS * STRIP)
    place = lax.axis_index("dp")
    mp_index = lax.axis_index("mp")
    side_of = {bit: (place // bit) % 2 for bit in (1, 2, 4, 8)}
    partner_of = {bit: {"dp": place + bit * (1 - 2 * side_of[bit])} for bit in (1, 2, 4, 8)}
    across_mp = {"mp": 1 - mp_index}

    def by_bits(*bits):
        return {"dp": place + sum(bit * (1 - 2 * side_of[bit]) for bit in bits)}

    diagonal = (by_bits(1, 2), by_bits(4, 8))
    barrier = pltpu.get_barrier_semaphore()
    for device in (*partner_of.values(), *diagonal, across_mp):
        pl.semaphore_signal(barrier, inc=1, device_id=device, device_id_type=pl.DeviceIdType.MESH)
    pl.semaphore_wait(barrier, 7)

    def rows_at(start, size):
        return pl.ds(pl.multiple_of(start, STRIP), size)

    def remote(src, dst, send, recv, device):
        return pltpu.make_async_remote_copy(
            src_ref=src,
            dst_ref=dst,
            send_sem=send,
            recv_sem=recv,
            device_id=device,
            device_id_type=pl.DeviceIdType.MESH,
        )

    mine = rows_at(mp_index * half_rows, half_rows)
    others = rows_at((1 - mp_index) * half_rows, half_rows)
    grad_swap = remote(
        grad_ref, grad_buf.at[1], wide_send_sem.at[0], wide_recv_sem.at[0], across_mp
    )
    input_swap = remote(
        input_send_buf, input_recv_buf, wide_send_sem.at[1], wide_recv_sem.at[1], across_mp
    )
    layer_swap = remote(
        layer_ref, layer_out_ref.at[mine, :], wide_send_sem.at[2], wide_recv_sem.at[2], across_mp
    )
    layer_arrival = remote(
        layer_out_ref.at[others, :],
        layer_out_ref.at[others, :],
        wide_send_sem.at[2],
        wide_recv_sem.at[2],
        across_mp,
    )
    layer_keep = pltpu.make_async_copy(layer_ref, layer_out_ref.at[mine, :], out_sem.at[2])
    grad_swap.start()

    residents = [
        pltpu.make_async_copy(src, dst, resident_sem.at[n])
        for n, (src, dst) in enumerate(
            (
                (grad_ref, grad_buf.at[0]),
                (output_ref, output_buf),
                (context_ref, context_buf),
                (query_ref, query_buf),
                (value_ref, value_buf),
                (key_ref, key_buf),
                (small_ref, small_buf.at[0]),
                (token_ref, token_buf),
                (project_ref, project_buf),
            )
        )
    ]

    def block_rows(block):
        start = (mp_index * (blocks // 2) + block) % blocks
        return rows_at(start * rows, rows)

    def block_copies(block, slot):
        at = block_rows(block)
        return (
            pltpu.make_async_copy(exp_ref.at[:, at, :], ring_buf.at[slot], block_sem.at[slot, 0]),
            pltpu.make_async_copy(inverse_ref.at[at, :], inverse_buf.at[slot], block_sem.at[slot, 1]),
        )

    def score_copy(block, slot):
        return pltpu.make_async_copy(
            ring_buf.at[2 + slot], score_ref.at[:, block_rows(block), :], out_sem.at[slot]
        )

    def ring_copies(block):
        slot = block % 4
        at = rows_at(block * rows, rows)
        return (
            pltpu.make_async_copy(score_ref.at[:, at, :], ring_buf.at[slot], ring_sem.at[slot, 0]),
            pltpu.make_async_copy(plane_ref.at[at, :], plane_buf.at[slot], ring_sem.at[slot, 1]),
            pltpu.make_async_copy(down_ref.at[at, :], down_buf.at[slot], ring_sem.at[slot, 2]),
        )

    def is_away(chunk):
        return chunk >= LOCAL_CHUNKS

    loads = {}
    for ref, away_ref, wide in (
        (expand_ref, expand_away_ref, True),
        (reduce_ref, reduce_away_ref, False),
    ):
        for k in range(2):
            piece = slice(k * CHUNK, (k + 1) * CHUNK)
            index = (slice(None), piece) if wide else (piece, slice(None))
            chunk = LOCAL_CHUNKS + len(loads)
            loads[chunk] = (
                pltpu.make_async_copy(ref.at[index], own_buf.at[chunk], load_sem.at[chunk, 0]),
                pltpu.make_async_copy(
                    away_ref.at[index], away_buf.at[chunk - LOCAL_CHUNKS], load_sem.at[chunk, 1]
                ),
            )

    for copy in loads[LOCAL_CHUNKS]:
        copy.start()
    for copy in residents[:2]:
        copy.start()
    for copy in block_copies(0, 0):
        copy.start()
    for copy in residents[2:6]:
        copy.start()
    for chunk in range(LOCAL_CHUNKS + 1, CHUNKS):
        for copy in loads[chunk]:
            copy.start()
    residents[6].start()
    for copy in residents[7:]:
        copy.start()

    keeps, leaves = [], []
    for bits in BITS:
        kept, left, base = [], [], 0
        for size, bit in zip(PARTS, bits):
            kept.append(base + side_of[bit] * size)
            left.append(base + (1 - side_of[bit]) * size)
            base = base + side_of[bit] * size
        keeps.append(kept)
        leaves.append(left)
    arrivals = (core_buf, first_buf, second_buf, third_buf)
    away_arrivals = (core_away_buf, first_away_buf)

    def staged(src, dst, chunk, stage, device):
        return remote(src, dst, send_sem.at[chunk, stage], recv_sem.at[chunk, stage], device)

    def scatter(chunk, level):
        return staged(
            own_buf.at[chunk, rows_at(leaves[chunk][level], PARTS[level]), :],
            arrivals[level].at[chunk],
            chunk,
            level,
            partner_of[BITS[chunk][level]],
        )

    def scatter_away(chunk, level):
        return staged(
            away_buf.at[chunk - LOCAL_CHUNKS, rows_at(leaves[chunk][level], PARTS[level]), :],
            away_arrivals[level].at[chunk - LOCAL_CHUNKS],
            chunk,
            4 + level,
            partner_of[BITS[chunk][level]],
        )

    def hand_over(chunk):
        return staged(
            away_buf.at[chunk - LOCAL_CHUNKS, rows_at(keeps[chunk][1], PARTS[1]), :],
            y_buf.at[chunk - LOCAL_CHUNKS],
            chunk,
            6,
            across_mp,
        )

    def total_rows(chunk, start, size):
        return total_ref.at[rows_at(chunk * CHUNK + start, size), :]

    def gather(chunk, level):
        kept, size = keeps[chunk][level], PARTS[level]
        if level == 3:
            src = own_buf.at[chunk, rows_at(kept, size), :]
        else:
            src = total_rows(chunk, kept, size)
        return staged(
            src, total_rows(chunk, kept, size), chunk, 7 + level, partner_of[BITS[chunk][level]]
        )

    def gathered(chunk, level):
        region = total_rows(chunk, leaves[chunk][level], PARTS[level])
        return staged(region, region, chunk, 7 + level, partner_of[BITS[chunk][level]])

    def store_own(chunk):
        return pltpu.make_async_copy(
            own_buf.at[chunk, rows_at(keeps[chunk][3], PARTS[3]), :],
            total_rows(chunk, keeps[chunk][3], PARTS[3]),
            local_sem.at[chunk],
        )

    def add(buf, chunk, start, size, arrived):
        piece = PARTS[3]

        def step(n, carry):
            here = rows_at(start + n * piece, piece)
            there = rows_at(n * piece, piece)
            buf[chunk, here, :] = buf[chunk, here, :] + arrived[there, :]
            return carry

        lax.fori_loop(0, size // piece, step, 0)

    def add_level(chunk, level):
        scatter(chunk, level).wait_recv()
        add(own_buf, chunk, keeps[chunk][level], PARTS[level], arrivals[level].at[chunk])

    def add_level_away(chunk, level):
        at = chunk - LOCAL_CHUNKS
        scatter_away(chunk, level).wait_recv()
        add(away_buf, at, keeps[chunk][level], PARTS[level], away_arrivals[level].at[at])

    def exchange(event, chunk):
        away = is_away(chunk)
        if event == 0:
            if away:
                for copy in loads[chunk]:
                    copy.wait()
                scatter_away(chunk, 0).start()
            scatter(chunk, 0).start()
            return
        if event == 1:
            if away:
                add_level_away(chunk, 0)
                scatter_away(chunk, 1).start()
            add_level(chunk, 0)
            scatter(chunk, 1).start()
            return
        if away and event == 2:
            add_level_away(chunk, 1)
            hand_over(chunk).start()
            add_level(chunk, 1)
            return
        if away:
            event -= 1
            if event == 2:
                hand_over(chunk).wait_recv()
                add(own_buf, chunk, keeps[chunk][1], PARTS[1], y_buf.at[chunk - LOCAL_CHUNKS])
        elif event == 2:
            add_level(chunk, 1)
        if event == 2:
            scatter(chunk, 2).start()
        elif event == 3:
            add_level(chunk, 2)
            scatter(chunk, 3).start()
        elif event == 4:
            add_level(chunk, 3)
            store_own(chunk).start()
            gather(chunk, 3).start()
        else:
            level = 8 - event
            if level == 3:
                store_own(chunk).wait()
            gathered(chunk, level).wait_recv()
            if level > 0:
                gather(chunk, level - 1).start()

    small_devices = (across_mp, *partner_of.values())

    def small_hop(n):
        return remote(
            small_buf.at[n],
            small_recv_buf.at[n],
            small_send_sem.at[n],
            small_recv_sem.at[n],
            small_devices[n],
        )

    def small_step(n):
        if n == 0:
            residents[6].wait()
        else:
            small_hop(n - 1).wait_recv()
            small_buf[n] = small_buf[n - 1] + small_recv_buf[n - 1]
        if n < 5:
            small_hop(n).start()
        else:
            small_out_ref[...] = small_buf[n]

    def input_rows(side):
        return mine if side == 0 else others

    def input_product(side, target):
        at = input_rows(side)
        part = None
        for k in range(3):
            product = lax.dot_general(
                triple_buf[k, at, :],
                project_buf[k, rows_at(target * width, width), :],
                (((1,), (1,)), ((), ())),
                preferred_element_type=f32,
            )
            part = product if part is None else part + product
        if side == 0:
            cols = pl.ds(pl.multiple_of(target * width, LANES), width)
            part = part + grad_buf[0, :, cols].astype(f32)
        return part

    def input_store(side):
        return pltpu.make_async_copy(
            input_buf.at[side], input_ref.at[input_rows(side), :], out_sem.at[3 + side]
        )

    def run(event, which):
        if event == "small":
            small_step(which)
        elif event == "send":
            input_swap.start()
        elif event == "layer":
            layer_swap.start()
            layer_keep.start()
        elif event == "input":
            input_swap.wait_recv()
            for side in range(2):
                part = input_product(side, mp_index)
                input_buf[side] = part + input_recv_buf[input_rows(side), :].astype(f32)
                input_store(side).start()
        else:
            exchange(event, which)

    pairs = heads // 2
    block_slots = plan_slots("b", blocks * pairs)
    part_slots = plan_slots("p", 4)
    turn_slots = plan_slots("t", turns)
    rest = plan_slots("e", 1)[0]

    def run_all(steps):
        for event, which in steps:
            run(event, which)

    def dispatch(slots, n, low, high):
        if not any(slots[low:high]):
            return
        if high - low == 1:
            for event, which in slots[low]:
                run(event, which)
            return
        middle = (low + high) // 2
        if any(slots[low:middle]):
            pl.when(n < middle)(lambda: dispatch(slots, n, low, middle))
        if any(slots[middle:high]):
            pl.when(n >= middle)(lambda: dispatch(slots, n, middle, high))

    grad_key_buf[...] = jnp.zeros_like(grad_key_buf)
    grad_value_buf[...] = jnp.zeros_like(grad_value_buf)
    sum_ref[...] = jnp.zeros_like(sum_ref)
    for copy in residents[:6]:
        copy.wait()
    first = lax.broadcasted_iota(jnp.int32, (rows, LANES), 1) < HEAD

    def back(block, carry):
        slot = block % 2
        at = block_rows(block)
        for copy in block_copies(block, slot):
            copy.wait()

        @pl.when(block + 1 < blocks)
        def _():
            for copy in block_copies(block + 1, 1 - slot):
                copy.start()

        pl.when(block == blocks // 2)(grad_swap.wait_recv)
        pl.when(block >= 2)(lambda: score_copy(block - 2, slot).wait())
        side = block // (blocks // 2)
        local = rows_at((block % (blocks // 2)) * rows, rows)
        grad_context = lax.dot_general(
            grad_buf[side, local, :],
            output_buf[...],
            (((1,), (1,)), ((), ())),
            preferred_element_type=f32,
        )
        scaled = (grad_context * inverse_buf[slot]).astype(bf16)
        for p in range(pairs):
            dispatch(block_slots, block * pairs + p, 0, blocks * pairs)
            cols = slice(p * LANES, (p + 1) * LANES)
            grad = scaled[:, cols]
            product = grad.astype(f32) * context_buf[at, cols].astype(f32)
            query_turned = query_buf[at, cols].T
            grad_turned = grad.T
            grad_query = None
            for u in range(2):
                h = 2 * p + u
                half = slice(u * HEAD, (u + 1) * HEAD)
                own = first if u == 0 else ~first
                total = jnp.sum(jnp.where(own, product, 0.0), axis=1, keepdims=True)
                exps = ring_buf[slot, h]
                grad_exp = dot_f32(grad, value_buf[h])
                grad_score = (exps.astype(f32) * (grad_exp - total)).astype(bf16)
                ring_buf[2 + slot, h] = grad_score
                part = dot_f32(grad_score, key_buf[h])
                grad_query = part if u == 0 else grad_query + part
                grad_key_buf[h] += dot_f32(query_turned[half], grad_score)
                grad_value_buf[h] += dot_f32(grad_turned[half], exps)
            triple_buf[0, at, cols] = (grad_query * 0.125).astype(bf16)
        score_copy(block, slot).start()
        return carry

    lax.fori_loop(0, blocks, back, 0)

    score_copy(blocks - 2, blocks % 2).wait()
    score_copy(blocks - 1, (blocks - 1) % 2).wait()
    for block in range(2):
        for copy in ring_copies(block):
            copy.start()
    run_all(part_slots[0])
    triple_buf[0, row_count:keys, :] = jnp.zeros((keys - row_count, width), bf16)
    for k, ref in ((1, grad_key_buf), (2, grad_value_buf)):
        for h in range(0, heads, 2):
            pair = ref[h : h + 2].reshape(LANES, keys)
            triple_buf[k, :, h * HEAD : (h + 2) * HEAD] = pair.T.astype(bf16)
    run_all(part_slots[1])
    for copy in residents[7:]:
        copy.wait()
    tokens_in = (((0,), (0,)), ((), ()))
    places = ((0, 0), (0, width), (1, 0))
    for k, (chunk, start) in enumerate(places):
        own_buf[chunk, start : start + width, :] = lax.dot_general(
            triple_buf[k], token_buf[...], tokens_in, preferred_element_type=f32
        ).astype(bf16)
    run_all(part_slots[2])
    own_buf[1, width : 2 * width, :] = (
        lax.dot_general(
            context_buf[mine, :], grad_buf[0], tokens_in, preferred_element_type=f32
        )
        + lax.dot_general(
            context_buf[others, :], grad_buf[1], tokens_in, preferred_element_type=f32
        )
    ).astype(bf16)
    run_all(part_slots[3])
    for side in range(2):
        input_send_buf[input_rows(side), :] = input_product(side, 1 - mp_index).astype(bf16)
    biases = jnp.concatenate(
        [
            jnp.sum(triple_buf[0].astype(f32), axis=0, keepdims=True),
            jnp.sum(triple_buf[2].astype(f32), axis=0, keepdims=True),
        ],
        axis=1,
    )

    def turn(n, carry):
        last = n * TABLE_STRIPS + TABLE_STRIPS - 1
        block = last // block_strips

        @pl.when(last % block_strips < TABLE_STRIPS)
        def _():
            for copy in ring_copies(block):
                copy.wait()

            @pl.when(block + 2 < blocks)
            def _():
                for copy in ring_copies(block + 2):
                    copy.start()

        dispatch(turn_slots, n, 0, turns)

        def refs_at(strip):
            slot = (strip // block_strips) % 4
            at = rows_at((strip % block_strips) * STRIP, STRIP)
            return (
                lambda h, cols: ring_buf[slot, h, at, cols],
                lambda cols: plane_buf[slot, at, cols],
                lambda cols: down_buf[slot, at, cols],
            )

        table_strips(
            [refs_at(n * TABLE_STRIPS + k) for k in range(TABLE_STRIPS)],
            sum_ref,
            heads,
            keys,
            high_counts,
        )
        return carry

    lax.fori_loop(0, turns, turn, 0)

    table_rows = sum(high_counts) * heads
    table_finish(sum_ref, table_buf.at[0], table_rows)
    lanes = table_buf.shape[2]
    pieces = 2 * width // lanes
    for n in range(pieces):
        table_buf[0, table_rows + n : table_rows + n + 1, :] = biases[:, n * lanes : (n + 1) * lanes]
    spare = table_buf.shape[1] - table_rows - pieces
    table_buf[0, table_rows + pieces :, :] = jnp.zeros((spare, lanes), f32)
    groups = ((1, 2), (4, 8))

    def table_hop(n, d):
        bits = [bit for k, bit in enumerate(groups[n]) if d >> k & 1]
        return remote(
            table_buf.at[n],
            table_recv_buf.at[n, d],
            table_send_sem.at[n, d],
            table_recv_sem.at[n, d],
            by_bits(*bits),
        )

    def table_step(n):
        if n > 0:
            for d in range(1, 4):
                table_hop(n - 1, d).wait_recv()
            table_recv_buf[n - 1, 0] = table_buf[n - 1]
            low, high = (side_of[bit] for bit in groups[n - 1])
            total = None
            for member in range(4):
                d = (low + member % 2) % 2 + 2 * ((high + member // 2) % 2)
                part = table_recv_buf[n - 1, d]
                total = part if member == 0 else total + part
            table_buf[n] = total
        if n < 2:
            for d in range(1, 4):
                table_hop(n, d).start()

    table_step(0)
    for n, (event, which) in enumerate(rest):
        if n in (3, 7):
            table_step(n // 3)
        run(event, which)
    for n in range(1, 3):
        if len(rest) <= 4 * n - 1:
            table_step(n)
    table_ref[...] = table_buf[2]

    layer_arrival.wait_recv()
    layer_keep.wait()
    grad_swap.wait_send()
    input_swap.wait_send()
    layer_swap.wait_send()
    for side in range(2):
        input_store(side).wait()
    for n in range(5):
        small_hop(n).wait_send()
    for n in range(2):
        for d in range(1, 4):
            table_hop(n, d).wait_send()
    for chunk in range(CHUNKS):
        for level in range(4):
            scatter(chunk, level).wait_send()
            gather(chunk, level).wait_send()
        if is_away(chunk):
            scatter_away(chunk, 0).wait_send()
            scatter_away(chunk, 1).wait_send()
            hand_over(chunk).wait_send()


def finish(
    exps,
    inverse,
    plane,
    down,
    context,
    query,
    tokens,
    grad,
    layer,
    value_turned,
    key_wide,
    project_weight,
    output_weight,
    expand,
    reduce,
    small,
    counts,
):
    heads, row_count, keys = exps.shape
    width = heads * HEAD
    depth = tokens.shape[1]
    half_rows = row_count // 2
    high_counts = (counts[0] // 16, counts[1] // 16, counts[1] // 16)
    high_rows = sum(high_counts) * heads
    low_lanes = 16 * STRIP
    table_shape = (round_up(high_rows + 2 * width // low_lanes, 8), low_lanes)
    away = CHUNKS - LOCAL_CHUNKS
    anywhere = pl.BlockSpec(memory_space=pl.ANY)
    in_vmem = pl.BlockSpec(memory_space=pltpu.VMEM)
    dma = pltpu.SemaphoreType.DMA
    total, layer_full, input_full, small_sum, table_sum, _ = pl.pallas_call(
        partial(finish_kernel, high_counts=high_counts),
        in_specs=[anywhere] * 18,
        out_specs=[anywhere, anywhere, anywhere, in_vmem, in_vmem, anywhere],
        out_shape=[
            jax.ShapeDtypeStruct((CHUNKS * CHUNK, CHUNK), bf16),
            jax.ShapeDtypeStruct((row_count, depth), bf16),
            jax.ShapeDtypeStruct((row_count, width), f32),
            jax.ShapeDtypeStruct(small.shape, f32),
            jax.ShapeDtypeStruct(table_shape, f32),
            jax.ShapeDtypeStruct(exps.shape, bf16),
        ],
        scratch_shapes=[
            pltpu.VMEM(output_weight.shape, bf16),
            pltpu.VMEM((2, half_rows, depth), bf16),
            pltpu.VMEM(value_turned.shape, bf16),
            pltpu.VMEM(key_wide.shape, bf16),
            pltpu.VMEM(context.shape, bf16),
            pltpu.VMEM(query.shape, bf16),
            pltpu.VMEM(tokens.shape, bf16),
            pltpu.VMEM(project_weight.shape, bf16),
            pltpu.VMEM((4, heads, BACK_ROWS, keys), bf16),
            pltpu.VMEM((2, BACK_ROWS, width), f32),
            pltpu.VMEM((heads, HEAD, keys), f32),
            pltpu.VMEM((heads, HEAD, keys), f32),
            pltpu.VMEM((3, keys, width), bf16),
            pltpu.VMEM((row_count, width), bf16),
            pltpu.VMEM((row_count, width), bf16),
            pltpu.VMEM((2, half_rows, width), f32),
            pltpu.VMEM((4, BACK_ROWS, keys), jnp.int16),
            pltpu.VMEM((4, BACK_ROWS, keys), jnp.int16),
            pltpu.VMEM((high_rows * STRIP, low_lanes), f32),
            pltpu.VMEM((CHUNKS, CHUNK, CHUNK), bf16),
            pltpu.VMEM((away, CHUNK, CHUNK), bf16),
            pltpu.VMEM((CHUNKS, PARTS[0], CHUNK), bf16),
            pltpu.VMEM((away, PARTS[0], CHUNK), bf16),
            pltpu.VMEM((CHUNKS, PARTS[1], CHUNK), bf16),
            pltpu.VMEM((away, PARTS[1], CHUNK), bf16),
            pltpu.VMEM((away, PARTS[1], CHUNK), bf16),
            pltpu.VMEM((CHUNKS, PARTS[2], CHUNK), bf16),
            pltpu.VMEM((CHUNKS, PARTS[3], CHUNK), bf16),
            pltpu.VMEM((6, *small.shape), f32),
            pltpu.VMEM((5, *small.shape), f32),
            pltpu.VMEM((3, *table_shape), f32),
            pltpu.VMEM((2, 4, *table_shape), f32),
            dma((9,)),
            dma((2, 2)),
            dma((4, 3)),
            dma((CHUNKS, 2)),
            dma((CHUNKS,)),
            dma((5,)),
            dma((CHUNKS, 11)),
            dma((CHUNKS, 11)),
            dma((3,)),
            dma((3,)),
            dma((5,)),
            dma((5,)),
            dma((2, 4)),
            dma((2, 4)),
        ],
        compiler_params=pltpu.CompilerParams(
            vmem_limit_bytes=FINISH_VMEM, collective_id=0, has_side_effects=True
        ),
        name="finish",
    )(
        exps,
        inverse,
        plane,
        down,
        context,
        query,
        tokens,
        grad,
        layer,
        value_turned,
        key_wide,
        project_weight,
        output_weight,
        *expand,
        *reduce,
        small,
    )
    return total, layer_full, input_full, table_sum, small_sum


UNPACK_ROWS = 192


def unpack_kernel(
    total_ref,
    layer_in_ref,
    input_in_ref,
    sum_ref,
    small_ref,
    layer_ref,
    input_ref,
    project_ref,
    output_ref,
    expand_ref,
    reduce_ref,
    line_ref,
    across_ref,
    down_ref,
    bias_ref,
    second_gain_ref,
    second_shift_ref,
    reduce_bias_ref,
    first_gain_ref,
    first_shift_ref,
    output_bias_ref,
    expand_bias_ref,
    *,
    high_counts,
):
    step = pl.program_id(0)
    layer_ref[...] = layer_in_ref[...]
    input_ref[...] = input_in_ref[...].reshape(input_ref.shape)
    values = total_ref[...].astype(f32)

    half = values.shape[0] // 2

    @pl.when(step < 2)
    def _():
        project_ref[0] = values[:half].T

    @pl.when(step == 0)
    def _():
        project_ref[1] = values[half:].T

    @pl.when(step == 1)
    def _():
        output_ref[...] = values[half:]

    @pl.when((step >= 2) & (step < 4))
    def _():
        expand_ref[...] = values

    @pl.when(step >= 4)
    def _():
        reduce_ref[...] = values

    @pl.when(step == 3)
    def _():
        lanes = sum_ref.shape[1]
        row = lax.broadcasted_iota(jnp.int32, (lanes, LANES), 0) // STRIP
        same = row == lax.broadcasted_iota(jnp.int32, (lanes, LANES), 1)
        folded = jnp.dot(
            sum_ref[...],
            jnp.where(same, 1.0, 0.0),
            precision=lax.Precision.HIGHEST,
            preferred_element_type=f32,
        )
        heads = line_ref.shape[0]
        start = 0
        for ref, count in zip((line_ref, across_ref, down_ref), high_counts):
            parts = []
            for _ in range(count):
                parts.append(folded[start : start + heads, : lanes // STRIP])
                start += heads
            ref[...] = jnp.concatenate(parts, axis=1)
        half = bias_ref.shape[1] - lanes
        middle = sum_ref[start + 1 : start + 2, :]
        bias_ref[0:1, :] = jnp.concatenate([sum_ref[start : start + 1, :], middle[:, :half]], axis=1)
        bias_ref[1:2, :] = jnp.concatenate([middle[:, half:], sum_ref[start + 2 : start + 3, :]], axis=1)
        lead = lax.axis_index("mp") == 0
        for n, ref in enumerate(
            (
                second_gain_ref,
                second_shift_ref,
                reduce_bias_ref,
                first_gain_ref,
                first_shift_ref,
                output_bias_ref,
            )
        ):
            row = small_ref[n : n + 1, :]
            if ref.shape[0] < row.shape[1]:
                cut = ref.shape[0]
                row = jnp.where(lead, row[:, :cut], row[:, cut:])
            ref[...] = row.reshape(ref.shape)
        pieces = expand_bias_ref.shape[0] // small_ref.shape[1]
        width = small_ref.shape[1]
        for k in range(pieces):
            even = small_ref[8 + k : 9 + k, :]
            odd = small_ref[8 + pieces + k : 9 + pieces + k, :]
            expand_bias_ref[k * width : (k + 1) * width] = jnp.where(lead, even, odd).reshape(width)


def unpack(total, layer, inputs, sums, small, length, heads, counts):
    width = inputs.shape[1]
    depth = layer.shape[1]
    high_counts = (counts[0] // 16, counts[1] // 16, counts[1] // 16)

    def whole(shape):
        return pl.BlockSpec(shape, lambda i: (0,) * len(shape))

    def rows(columns):
        return pl.BlockSpec((UNPACK_ROWS, columns), lambda i: (i, 0))

    shapes = [
        ((length, depth), bf16),
        ((length, 1, width), f32),
        ((3, depth, width), f32),
        ((width, depth), f32),
        ((CHUNK, 2 * CHUNK), f32),
        ((2 * CHUNK, CHUNK), f32),
        ((heads, counts[0]), f32),
        ((heads, counts[1]), f32),
        ((heads, counts[1]), f32),
        ((2, width), f32),
        ((depth,), f32),
        ((depth,), f32),
        ((depth,), f32),
        ((width,), f32),
        ((width,), f32),
        ((depth,), f32),
        ((2 * CHUNK,), f32),
    ]
    return pl.pallas_call(
        partial(unpack_kernel, high_counts=high_counts),
        grid=(CHUNKS,),
        in_specs=[
            pl.BlockSpec((CHUNK, CHUNK), lambda i: (i, 0)),
            rows(depth),
            rows(width),
            whole(sums.shape),
            whole(small.shape),
        ],
        out_specs=[
            rows(depth),
            pl.BlockSpec((UNPACK_ROWS, 1, width), lambda i: (i, 0, 0)),
            pl.BlockSpec((2, depth, width), lambda i: (jnp.minimum(i, 1), 0, 0)),
            whole((width, depth)),
            pl.BlockSpec((CHUNK, CHUNK), lambda i: (0, jnp.clip(i - 2, 0, 1))),
            pl.BlockSpec((CHUNK, CHUNK), lambda i: (jnp.clip(i - 4, 0, 1), 0)),
            *(whole(shape) for shape, _ in shapes[6:]),
        ],
        out_shape=[jax.ShapeDtypeStruct(shape, kind) for shape, kind in shapes],
        compiler_params=pltpu.CompilerParams(vmem_limit_bytes=vmem_limit),
        name="unpack",
    )(total, layer, inputs, sums, small)


def feed_kernel(
    context_ref,
    context_away_ref,
    token_ref,
    cotangent_ref,
    valid_ref,
    output_ref,
    output_away_ref,
    expand_ref,
    expand_away_ref,
    reduce_ref,
    reduce_away_ref,
    expand_bias_ref,
    expand_bias_away_ref,
    output_bias_ref,
    first_gain_ref,
    first_shift_ref,
    reduce_bias_ref,
    second_gain_ref,
    second_shift_ref,
    layer_ref,
    grad_ref,
    expand_grad_ref,
    expand_grad_away_ref,
    reduce_grad_ref,
    reduce_grad_away_ref,
    small_ref,
    input_buf,
    norm_buf,
    hat_buf,
    inverse_buf,
    total_buf,
    reduced_buf,
    active_buf,
    slope_buf,
    before_buf,
    vector_ref,
    bias_buf,
    *,
    pieces,
    tiles,
):
    rows, width = token_ref.shape
    step = pl.program_id(0)
    piece = step % (2 * pieces)

    def vector(n):
        return vector_ref[n : n + 1, :]

    def for_strips(body, sums, strip_rows):
        def run(n, carry):
            at = pl.ds(pl.multiple_of(n * strip_rows, STRIP), strip_rows)
            return tuple(
                old + jnp.sum(new.reshape(strip_rows // 8, 8, width), axis=0)
                for old, new in zip(carry, body(at))
            )

        start = tuple(jnp.zeros((8, width), f32) for _ in range(sums))
        done = lax.fori_loop(0, rows // strip_rows, run, start)
        return [jnp.sum(part, axis=0, keepdims=True) for part in done]

    def mean(values):
        return jnp.sum(values, axis=-1, keepdims=True) * (1.0 / width)

    @pl.when(step == 0)
    def _():
        small_ref[...] = jnp.zeros_like(small_ref)
        for n, ref in enumerate(
            (
                output_bias_ref,
                first_gain_ref,
                first_shift_ref,
                reduce_bias_ref,
                second_gain_ref,
                second_shift_ref,
            )
        ):
            vector_ref[n : n + 1, :] = ref[...].astype(f32).reshape(1, width)
        bias = expand_bias_ref[...].astype(f32).reshape(1, -1)
        for k in range(pieces):
            cols = slice(k * expand_ref.shape[1], (k + 1) * expand_ref.shape[1])
            bias_buf[k : k + 1, :] = bias[:, cols]
            bias_buf[pieces + k : pieces + k + 1, :] = expand_bias_away_ref[0:1, cols]
        total_buf[...] = dot_f32(context_ref[...], output_ref[...]) + dot_f32(
            context_away_ref[...], output_away_ref[...]
        )

        def body(at):
            values = token_ref[at, :].astype(f32) + (total_buf[at, :] + vector(0))
            centered = values - mean(values)
            inverse = lax.rsqrt(mean(centered * centered) + norm_epsilon)
            hat = centered * inverse
            norm = hat * vector(1) + vector(2)
            hat_buf[at, :] = hat
            inverse_buf[at, :] = jnp.broadcast_to(inverse, (rows, LANES))
            norm_buf[at, :] = norm
            input_buf[at, :] = norm.astype(bf16)
            total_buf[at, :] = norm + vector(3)
            return ()

        for_strips(body, 0, rows)

    def forward(expand, reduce):
        for start, size in tiles:
            at = slice(start, start + size)
            before = dot_f32(input_buf[at, :], expand[...]) + bias_buf[pl.ds(piece, 1), :]
            phi = 0.5 * lax.erf(before * 0.7071067811865476) + 0.5
            slope_buf[piece, at, :] = phi + before * (
                0.3989422804014327 * jnp.exp(-0.5 * (before * before))
            )
            active = (before * phi).astype(bf16)
            active_buf[piece, at, :] = active
            total_buf[at, :] += dot_f32(active, reduce[...])

    pl.when(step < pieces)(lambda: forward(expand_ref, reduce_ref))
    pl.when((step >= pieces) & (step < 2 * pieces))(
        lambda: forward(expand_away_ref, reduce_away_ref)
    )

    @pl.when(step == 2 * pieces)
    def _():
        def body(at):
            values = total_buf[at, :]
            valid = valid_ref[at, 0:1]
            centered = values - mean(values)
            inverse = lax.rsqrt(mean(centered * centered) + norm_epsilon)
            hat = centered * inverse
            layer_ref[at, :] = (valid * (hat * vector(4) + vector(5))).astype(bf16)
            grad_out = jnp.where(valid > 0, cotangent_ref[at, :].astype(f32), 0.0)
            grad_hat = grad_out * vector(4)
            mixed = inverse * (grad_hat - mean(grad_hat) - hat * mean(grad_hat * hat))
            low = mixed.astype(bf16)
            reduced_buf[at, :] = low
            total_buf[at, :] = mixed
            return grad_out * hat, grad_out, low.astype(f32)

        for n, part in enumerate(for_strips(body, 3, FEED_STRIP)):
            small_ref[n : n + 1, :] = part

    def backward(expand, reduce):
        sums = None
        for start, size in tiles:
            at = slice(start, start + size)
            grad_active = lax.dot_general(
                reduced_buf[at, :], reduce[...], (((1,), (1,)), ((), ())), preferred_element_type=f32
            )
            before = (grad_active * slope_buf[piece, at, :]).astype(bf16)
            before_buf[piece, at, :] = before
            part = jnp.sum(before.astype(f32), axis=0, keepdims=True)
            sums = part if sums is None else sums + part
            total_buf[at, :] += lax.dot_general(
                before, expand[...], (((1,), (1,)), ((), ())), preferred_element_type=f32
            )
        mp_index = lax.axis_index("mp")
        side = jnp.where(piece < pieces, mp_index, 1 - mp_index)
        small_ref[pl.ds(8 + side * pieces + lax.rem(piece, pieces), 1), :] = sums

    pl.when((step >= 2 * pieces) & (step < 3 * pieces))(lambda: backward(expand_ref, reduce_ref))
    pl.when((step >= 3 * pieces) & (step < 4 * pieces))(
        lambda: backward(expand_away_ref, reduce_away_ref)
    )

    @pl.when(step == 4 * pieces)
    def _():
        def body(at):
            grad_first = total_buf[at, :]
            hat = hat_buf[at, :]
            grad_hat = grad_first * vector(1)
            inverse = inverse_buf[at, 0:1]
            inner = inverse * (grad_hat - mean(grad_hat) - hat * mean(grad_hat * hat))
            low = inner.astype(bf16)
            grad_ref[at, :] = low
            return grad_first * hat, grad_first, low.astype(f32)

        for n, part in enumerate(for_strips(body, 3, rows)):
            small_ref[n + 3 : n + 4, :] = part

    def weights(expand_grad, reduce_grad):
        reduce_grad[...] = lax.dot_general(
            active_buf[piece], reduced_buf[...], (((0,), (0,)), ((), ())), preferred_element_type=f32
        ).astype(bf16)
        expand_grad[...] = lax.dot_general(
            input_buf[...], before_buf[piece], (((0,), (0,)), ((), ())), preferred_element_type=f32
        ).astype(bf16)

    pl.when((step >= 4 * pieces) & (step < 5 * pieces))(
        lambda: weights(expand_grad_ref, reduce_grad_ref)
    )
    pl.when(step >= 5 * pieces)(lambda: weights(expand_grad_away_ref, reduce_grad_away_ref))


def feed(
    context,
    context_away,
    tokens,
    cotangent,
    valid,
    output,
    output_away,
    expand,
    expand_away,
    reduce,
    reduce_away,
    expand_bias,
    expand_bias_away,
    vectors,
):
    rows, width = context_away.shape[0], tokens.shape[1]
    hidden = expand.shape[1]
    size = FEED_PIECE
    pieces = hidden // size
    split = round_up(rows // 2, STRIP)
    tiles = ((0, rows),)

    def once(array):
        zeros = (0,) * array.ndim
        return pl.BlockSpec(array.shape, lambda i: zeros, pipeline_mode=pl.Buffered(1))

    def mine(array):
        return pl.BlockSpec(
            (rows, array.shape[1]),
            lambda i: (lax.axis_index("mp"), 0),
            pipeline_mode=pl.Buffered(1),
        )

    def place(first, i):
        at = lax.rem(i, 2 * pieces) - first
        at = jnp.clip(at, 0, pieces - 1)
        return jnp.where(i < 4 * pieces, at, pieces - 1)

    def grad_place(first, i):
        return jnp.clip(i - 4 * pieces - first, 0, pieces - 1)

    wide = lambda first: pl.BlockSpec((width, size), lambda i: (0, place(first, i)))
    tall = lambda first: pl.BlockSpec((size, width), lambda i: (place(first, i), 0))
    wide_grad = lambda first: pl.BlockSpec((width, size), lambda i: (0, grad_place(first, i)))
    tall_grad = lambda first: pl.BlockSpec((size, width), lambda i: (grad_place(first, i), 0))
    whole = lambda shape: pl.BlockSpec(
        shape, lambda i: (0,) * len(shape), pipeline_mode=pl.Buffered(1)
    )
    full = jax.ShapeDtypeStruct((rows, width), bf16)
    return pl.pallas_call(
        partial(feed_kernel, pieces=pieces, tiles=tiles),
        grid=(6 * pieces,),
        in_specs=[
            mine(context),
            once(context_away),
            mine(tokens),
            mine(cotangent),
            mine(valid),
            once(output),
            once(output_away),
            wide(0),
            wide(pieces),
            tall(0),
            tall(pieces),
            once(expand_bias),
            once(expand_bias_away),
            *(once(vector) for vector in vectors),
        ],
        out_specs=[
            whole((rows, width)),
            whole((rows, width)),
            wide_grad(0),
            wide_grad(pieces),
            tall_grad(0),
            tall_grad(pieces),
            whole((16, width)),
        ],
        out_shape=[
            full,
            full,
            jax.ShapeDtypeStruct((width, hidden), bf16),
            jax.ShapeDtypeStruct((width, hidden), bf16),
            jax.ShapeDtypeStruct((hidden, width), bf16),
            jax.ShapeDtypeStruct((hidden, width), bf16),
            jax.ShapeDtypeStruct((16, width), f32),
        ],
        scratch_shapes=[
            pltpu.VMEM((rows, width), bf16),
            pltpu.VMEM((rows, width), f32),
            pltpu.VMEM((rows, width), f32),
            pltpu.VMEM((rows, LANES), f32),
            pltpu.VMEM((rows, width), f32),
            pltpu.VMEM((rows, width), bf16),
            pltpu.VMEM((2 * pieces, rows, size), bf16),
            pltpu.VMEM((2 * pieces, rows, size), f32),
            pltpu.VMEM((2 * pieces, rows, size), bf16),
            pltpu.VMEM((8, width), f32),
            pltpu.VMEM((2 * pieces, size), f32),
        ],
        compiler_params=pltpu.CompilerParams(vmem_limit_bytes=vmem_limit),
        name="feed",
    )(
        context,
        context_away,
        tokens,
        cotangent,
        valid,
        output,
        output_away,
        expand,
        expand_away,
        reduce,
        reduce_away,
        expand_bias,
        expand_bias_away,
        *vectors,
    )


def swap(array):
    return lax.ppermute(array, "mp", [(0, 1), (1, 0)])


def partner(array, count, bit):
    return lax.ppermute(array, "dp", [(i, i ^ bit) for i in range(count)])


def sum_rows_over_dp(array, count):
    place = lax.axis_index("dp")
    bits = []
    bit = 1
    while bit < count:
        mine = (place // bit) % 2
        halves = array.reshape((2, array.shape[0] // 2) + array.shape[1:])
        sent = lax.dynamic_index_in_dim(halves, 1 - mine, 0, keepdims=False)
        kept = lax.dynamic_index_in_dim(halves, mine, 0, keepdims=False)
        array = kept + partner(sent, count, bit)
        bits.append(bit)
        bit *= 2
    for bit in reversed(bits):
        lead = (place // bit) % 2 == 0
        other = partner(array, count, bit)
        array = jnp.concatenate(
            [jnp.where(lead, array, other), jnp.where(lead, other, array)], axis=0
        )
    return array


def sum_small(arrays, count, over_mp):
    sizes = [a.size for a in arrays]
    total = sum(sizes)
    flat = jnp.concatenate([a.reshape(-1) for a in arrays])
    flat = jnp.pad(flat, (0, round_up(total, 1024) - total)).reshape(-1, LANES)
    if over_mp:
        flat = flat + swap(flat)
    bit = 1
    while bit < count:
        flat = flat + partner(flat, count, bit)
        bit *= 2
    flat = flat.reshape(-1)
    outs = []
    start = 0
    for array, size in zip(arrays, sizes):
        outs.append(flat[start : start + size].reshape(array.shape))
        start += size
    return outs


def per_device(
    dp_count,
    tokens,
    cotangent,
    long_flag,
    token_mask,
    bucket_line,
    bucket_across,
    bucket_down,
    project_weight,
    project_bias,
    table_line,
    table_across,
    table_down,
    output_weight,
    output_bias,
    first_gain,
    first_shift,
    expand_weight,
    expand_bias,
    reduce_weight,
    reduce_bias,
    second_gain,
    second_shift,
):
    length = tokens.shape[1]
    width = project_weight.shape[2]
    heads = table_line.shape[1]
    counts = (table_line.shape[0], table_across.shape[0])
    rows = round_up(length, BLOCK_ROWS)
    half_rows = rows // 2
    keys = round_up(length, 3 * LANES)
    mp_index = lax.axis_index("mp")
    lead = mp_index == 0

    def own_rows(array):
        return lax.dynamic_slice_in_dim(array, mp_index * half_rows, half_rows, 0)

    def in_order(mine, other):
        return jnp.where(lead, mine, other), jnp.where(lead, other, mine)


    (
        query,
        key_wide,
        key_turned,
        value_ones,
        value_turned,
        padded,
        plane,
        down,
        valid_rows,
        expand_quarter,
    ) = prepare(
        tokens[0],
        project_weight,
        project_bias,
        (bucket_line, bucket_across, bucket_down),
        long_flag,
        token_mask,
        expand_weight,
        rows,
        keys,
        counts[0],
    )
    (
        exps,
        context,
        inverse,
        context_away,
        expand_away,
        output_away,
        reduce_away,
        expand_bias_away,
    ) = attend(
        query,
        key_turned,
        value_ones,
        plane,
        down,
        (table_line.T, table_across.T, table_down.T),
        expand_bias,
        expand_quarter,
        output_weight,
        reduce_weight,
    )

    (
        layer_mine,
        grad_mine,
        expand_own,
        expand_sent,
        reduce_own,
        reduce_sent,
        small,
    ) = feed(
        context,
        context_away,
        padded,
        cotangent[0],
        valid_rows,
        output_weight,
        output_away,
        expand_weight,
        expand_away,
        reduce_weight,
        reduce_away,
        expand_bias,
        expand_bias_away,
        (output_bias, first_gain, first_shift, reduce_bias, second_gain, second_shift),
    )
    if dp_count == 16 and expand_own.shape == (CHUNK, 2 * CHUNK):
        total, layer_full, input_full, sums, small = finish(
            exps,
            inverse,
            plane,
            down,
            context,
            query,
            padded,
            grad_mine,
            layer_mine,
            value_turned,
            key_wide,
            project_weight,
            output_weight,
            (expand_own, expand_sent),
            (reduce_own, reduce_sent),
            small,
            counts,
        )
        (
            layer_out,
            input_grad,
            project_weight_grad,
            output_weight_grad,
            expand_weight_grad,
            reduce_weight_grad,
            line_grad,
            across_grad,
            down_grad,
            project_bias_grad,
            second_gain_grad,
            second_shift_grad,
            reduce_bias_grad,
            first_gain_grad,
            first_shift_grad,
            output_bias_grad,
            expand_bias_grad,
        ) = unpack(total, layer_full, input_full, sums, small, length, heads, counts)
        layer_out = layer_out[None]
        input_grad = input_grad.reshape(1, length, width)
        table_grads = (line_grad.T, across_grad.T, down_grad.T)
    else:
        layer_out = jnp.concatenate(in_order(layer_mine, swap(layer_mine)))[None, :length]
        grad_attended = jnp.concatenate(in_order(grad_mine, swap(grad_mine)))
        output_weight_grad = jnp.einsum(
            "le,lf->ef", context, grad_attended, preferred_element_type=f32
        ).astype(bf16)
        grad_context = jnp.einsum(
            "lf,ef->le", grad_attended, output_weight, preferred_element_type=f32
        )
        grad_scaled = (grad_context * inverse).astype(bf16)
        grad_scores, grad_query, grad_key, grad_value = attend_back(
            exps, grad_scaled, context, query, value_turned, key_wide
        )
        grad_key = grad_key.reshape(width, keys)[:, :rows].T.astype(bf16)
        grad_value = grad_value.reshape(width, keys)[:, :rows].T.astype(bf16)
        triple = jnp.stack([grad_query, grad_key, grad_value])
        project_weight_grad = jnp.einsum(
            "ld,kle->kde", padded[:rows], triple, preferred_element_type=f32
        ).astype(bf16)
        project_bias_grad = jnp.stack(
            [jnp.sum(grad_query, axis=0, dtype=f32), jnp.sum(grad_value, axis=0, dtype=f32)]
        )
        input_part = jnp.einsum("kle,kde->ld", triple, project_weight, preferred_element_type=f32)
        input_part = lax.dynamic_update_slice_in_dim(
            input_part,
            own_rows(input_part) + grad_mine.astype(f32),
            mp_index * half_rows,
            0,
        )
        sent = jnp.where(lead, input_part[:, width:], input_part[:, :width]).astype(bf16)
        own = jnp.where(lead, input_part[:, :width], input_part[:, width:])
        input_grad = (own + swap(sent).astype(f32))[None, :length]
        table_grads = table_sums(grad_scores, plane, down, counts)
        reduce_weight_grad = sum_rows_over_dp(reduce_own + swap(reduce_sent), dp_count)
        expand_weight_grad = sum_rows_over_dp(expand_own + swap(expand_sent), dp_count)
        output_weight_grad = sum_rows_over_dp(output_weight_grad, dp_count)
        project_weight_grad = sum_rows_over_dp(
            project_weight_grad.reshape(-1, width), dp_count
        ).reshape(project_weight.shape)
        (small,) = sum_small([small], dp_count, True)
        bias_rows = expand_bias.size // small.shape[1]
        bias_rows = lax.dynamic_slice_in_dim(small, 8 + mp_index * bias_rows, bias_rows, 0)
        expand_bias_grad = bias_rows.reshape(-1)
        (
            second_gain_grad,
            second_shift_grad,
            reduce_bias_grad,
            first_gain_grad,
            first_shift_grad,
            output_bias_grad,
        ) = (small[n] for n in range(6))
        first_gain_grad = lax.dynamic_slice_in_dim(first_gain_grad, mp_index * width, width, 0)
        first_shift_grad = lax.dynamic_slice_in_dim(first_shift_grad, mp_index * width, width, 0)
        table_grads, project_bias_grad = sum_small(
            [table_grads, project_bias_grad], dp_count, False
        )
        cuts = (counts[0], counts[0] + counts[1])
        table_grads = (
            table_grads[: cuts[0]],
            table_grads[cuts[0] : cuts[1]],
            table_grads[cuts[1] :],
        )
    return (
        layer_out,
        input_grad,
        project_weight_grad.astype(f32),
        project_bias_grad,
        *table_grads,
        output_weight_grad.astype(f32),
        output_bias_grad,
        first_gain_grad,
        first_shift_grad,
        expand_weight_grad.astype(f32),
        expand_bias_grad,
        reduce_weight_grad.astype(f32),
        reduce_bias_grad,
        second_gain_grad,
        second_shift_grad,
    )


def solution(mesh):
    placed = (
        P("dp", None, None),
        P("dp", None, None),
        P("dp"),
        P("dp", None),
        P("dp", None, None),
        P("dp", None, None),
        P("dp", None, None),
        P(None, None, "mp"),
        P(None, "mp"),
        P(None, "mp"),
        P(None, "mp"),
        P(None, "mp"),
        P("mp", None),
        P(),
        P(),
        P(),
        P(None, "mp"),
        P("mp"),
        P("mp", None),
        P(),
        P(),
        P(),
    )
    return jax.shard_map(
        partial(per_device, mesh.shape["dp"]),
        mesh=mesh,
        in_specs=placed,
        out_specs=(
            P("dp", None, None),
            P("dp", None, "mp"),
            P(None, None, "mp"),
            P(None, "mp"),
            P(None, "mp"),
            P(None, "mp"),
            P(None, "mp"),
            P("mp", None),
            P(),
            P("mp"),
            P("mp"),
            P(None, "mp"),
            P("mp"),
            P("mp", None),
            P(),
            P(),
            P(),
        ),
        check_vma=False,
    )
```
